32 devices in a mesh: batch: 4 (over x, core), seq: 8 (over z, y).
Axes of the slice: x: 2, y: 2, z: 4, core: 2. Of those that a mesh axis runs over, the one named last changes fastest.
Arguments:
- activations: bfloat16 [8, 1024, 768], P('batch', 'seq'), may hold values from -6 to 6
- cotangent: bfloat16 [8, 1024, 768], P('batch', 'seq'), may hold values from -6 to 6
- w_in: float32 [1, 768, 3072], P(None, ('batch', 'seq')), may hold values from -0.21875 to 0.21875
- w_out: float32 [1, 3072, 768], P(None, None, ('batch', 'seq')), may hold values from -0.109375 to 0.109375
- b_in: float32 [1, 3072], P(None, ('batch', 'seq')), may hold values from -3 to 3
- vec_params: float32 [1, 5, 768], P(None, None, ('batch', 'seq')), may hold values from -0.9 to 4.5, as said below
- first_w_in: float32 [1, 768, 3072], P(None, ('batch', 'seq')), may hold values from -0.0068359375 to 0.0068359375
- second_w_in: float32 [1, 768, 3072], P(None, ('batch', 'seq')), may hold values from 1.0580882e-07 to 1.6929412e-06
- first_w_out: float32 [1, 3072, 768], P(None, None, ('batch', 'seq')), may hold values from -0.0068359375 to 0.0068359375
- second_w_out: float32 [1, 3072, 768], P(None, None, ('batch', 'seq')), may hold values from 1.0580882e-07 to 1.6929412e-06
- first_b_in: float32 [1, 3072], P(None, ('batch', 'seq')), may hold values from -0.0068359375 to 0.0068359375
- second_b_in: float32 [1, 3072], P(None, ('batch', 'seq')), may hold values from 1.0580882e-07 to 1.6929412e-06
- first_vec: float32 [1, 5, 768], P(None, None, ('batch', 'seq')), may hold values from -0.0068359375 to 0.0068359375
- second_vec: float32 [1, 5, 768], P(None, None, ('batch', 'seq')), may hold values from 1.0580882e-07 to 1.6929412e-06
Outputs:
- block_output: bfloat16 [8, 1024, 768], P('batch', 'seq')
- input_grad: float32 [8, 1024, 768], P('batch', 'seq')
- grad_norm: float32 [], replicated
- new_first_w_in: float32 [1, 768, 3072], P(None, ('batch', 'seq'))
- new_second_w_in: float32 [1, 768, 3072], P(None, ('batch', 'seq'))
- new_w_in: float32 [1, 768, 3072], P(None, ('batch', 'seq'))
- new_first_w_out: float32 [1, 3072, 768], P(None, None, ('batch', 'seq'))
- new_second_w_out: float32 [1, 3072, 768], P(None, None, ('batch', 'seq'))
- new_w_out: float32 [1, 3072, 768], P(None, None, ('batch', 'seq'))
- new_first_b_in: float32 [1, 3072], P(None, ('batch', 'seq'))
- new_second_b_in: float32 [1, 3072], P(None, ('batch', 'seq'))
- new_b_in: float32 [1, 3072], P(None, ('batch', 'seq'))
- new_first_vec: float32 [1, 5, 768], P(None, None, ('batch', 'seq'))
- new_second_vec: float32 [1, 5, 768], P(None, None, ('batch', 'seq'))
- new_vec: float32 [1, 5, 768], P(None, None, ('batch', 'seq'))
The draws below stay inside these ranges and needn't reach their ends.
Inputs may be any that keep to these rules, and one draw needn't show every extreme that they name: `vec_params`: rows 0 and 3 of every layer are positive norm gains; rows 1, 2 and 4 are shifts and biases of both signs.
All inputs are finite; a program needn't handle non-finite values.
Results may differ from the reference program's by a relative error of at most 0.0079.
Values may be sent and summed in bfloat16 or wider, within the bound.
A program may use at most 192 MiB of HBM per device.

```python
import math
import jax
import jax.numpy as jnp
from jax import lax

D = 768
FF = 3072
LAYERS = 1
STEP_COUNT = 10
LENGTH = 1024
SEQS_ALL = 8
DSHARD = 24
SEQ_DEVS = 8
BATCH_DEVS = 4
PARAMS = 4725504


def draw_vec_params(key, part):
    key = jax.random.fold_in(key, 11)
    key_rough, key_shift = jax.random.split(key, 2)
    feature = jnp.arange(D, dtype=jnp.int32)
    owner = feature // DSHARD
    batch_place = (owner // SEQ_DEVS).astype(jnp.float32) / max(BATCH_DEVS - 1, 1)
    seq_place = (owner % SEQ_DEVS).astype(jnp.float32) / max(SEQ_DEVS - 1, 1)
    climb = 0.732
    rising = (1.0 + climb * batch_place) * (1.0 + climb * seq_place)
    rough = jnp.exp(jax.random.uniform(key_rough, (LAYERS, 2, D), jnp.float32, -0.22, 0.22))
    gains = 0.7 * rising * rough
    shifts = 0.3 * jnp.clip(jax.random.normal(key_shift, (LAYERS, 3, D), jnp.float32), -3.0, 3.0)
    return jnp.stack([gains[:, 0], shifts[:, 0], shifts[:, 1], gains[:, 1], shifts[:, 2]], axis=1)


def steps_of(key, shape, pieces, low, top_value):
    def one(position, blocks):
        steps = jax.random.uniform(jax.random.fold_in(jax.random.fold_in(key, 6), position), (blocks,), jnp.float32, low / len(pieces), top_value / len(pieces))
        return jnp.repeat(jnp.exp(steps), shape[position] // blocks).reshape((-1,) + (1,) * (len(shape) - position - 1))

    level = one(*pieces[0])
    for cut in pieces[1:]:
        level = level * one(*cut)
    return level


def normal_values(stream_key, extent, width, bound, cuts=(), held_as=jnp.bfloat16):
    array = width * jax.random.normal(stream_key, extent, jnp.float32)
    if cuts:
        array = array * steps_of(stream_key, extent, cuts, -0.22, 0.18)
    return jnp.clip(array, -bound, bound).astype(held_as)


def setup_inputs(seed: int = 0) -> dict:
    arg_keys = jax.random.split(jax.random.key(seed), 15)
    return {
        "activations": normal_values(arg_keys[0], (SEQS_ALL, LENGTH, D), 1.0, 6.0, ((0, 4), (1, 8))),
        "cotangent": normal_values(arg_keys[1], (SEQS_ALL, LENGTH, D), 1.0, 6.0, ((0, 4), (1, 8))),
        "w_in": normal_values(arg_keys[2], (LAYERS, D, FF), D ** -0.5, 0.21875, ((1, 32),), jnp.float32),
        "w_out": normal_values(arg_keys[3], (LAYERS, FF, D), FF ** -0.5, 0.109375, ((2, 32),), jnp.float32),
        "b_in": normal_values(arg_keys[4], (LAYERS, FF), 0.3, 3.0, ((1, 32),), jnp.float32),
        "vec_params": draw_vec_params(jax.random.fold_in(arg_keys[14], 71), 0),
        "first_w_in": normal_values(arg_keys[6], (LAYERS, D, FF), (PARAMS ** -0.5), 0.0068359375, ((1, 32),), jnp.float32),
        "second_w_in": jnp.clip(jnp.exp(math.log(1.6929411685850937e-06) - 2.7725887 * jax.random.uniform(arg_keys[7], (LAYERS, D, FF), jnp.float32) ** steps_of(arg_keys[7], (LAYERS, D, FF), ((1, 32),), -0.2, 0.2)), 1.0580882303656836e-07, 1.6929411685850937e-06),
        "first_w_out": normal_values(arg_keys[8], (LAYERS, FF, D), (PARAMS ** -0.5), 0.0068359375, ((2, 32),), jnp.float32),
        "second_w_out": jnp.clip(jnp.exp(math.log(1.6929411685850937e-06) - 2.7725887 * jax.random.uniform(arg_keys[9], (LAYERS, FF, D), jnp.float32) ** steps_of(arg_keys[9], (LAYERS, FF, D), ((2, 32),), -0.2, 0.2)), 1.0580882303656836e-07, 1.6929411685850937e-06),
        "first_b_in": normal_values(arg_keys[10], (LAYERS, FF), (PARAMS ** -0.5), 0.0068359375, ((1, 32),), jnp.float32),
        "second_b_in": jnp.clip(jnp.exp(math.log(1.6929411685850937e-06) - 2.7725887 * jax.random.uniform(arg_keys[11], (LAYERS, FF), jnp.float32) ** steps_of(arg_keys[11], (LAYERS, FF), ((1, 32),), -0.2, 0.2)), 1.0580882303656836e-07, 1.6929411685850937e-06),
        "first_vec": normal_values(arg_keys[12], (LAYERS, 5, D), (PARAMS ** -0.5), 0.0068359375, ((2, 32),), jnp.float32),
        "second_vec": jnp.clip(jnp.exp(math.log(1.6929411685850937e-06) - 2.7725887 * jax.random.uniform(arg_keys[13], (LAYERS, 5, D), jnp.float32) ** steps_of(arg_keys[13], (LAYERS, 5, D), ((2, 32),), -0.2, 0.2)), 1.0580882303656836e-07, 1.6929411685850937e-06),
    }


@jax.custom_vjp
def low(v):
    return lax.optimization_barrier(v.astype(jnp.bfloat16)).astype(jnp.float32)

@jax.custom_vjp
def low_back(v):
    return v

def low_keep(v):
    return (low(v), None)

def low_pass(kept, grad):
    return (grad,)

def back_keep(v):
    return (v, None)

def back_low(kept, grad):
    return (low(grad),)
low.defvjp(low_keep, low_pass)
low_back.defvjp(back_keep, back_low)
beta_first = 0.5
beta_second = 0.5
rate_matrix = 0.03
rate_vector = 0.2
weight_decay = 0.01
adam_epsilon = 1e-08
norm_epsilon = 1e-06
clip_limit = 1.0
highest = lax.Precision.HIGHEST

def dft_pair(count):
    index_line = jnp.arange(count, dtype=jnp.int32)
    product = index_line[:, None] * index_line[None, :] % count
    angle = product.astype(jnp.float32) * (2.0 * math.pi / count)
    return (low(jnp.cos(angle)), low(jnp.sin(angle)))

def layer_norm(values, gain, shift):
    centre = lax.optimization_barrier(jnp.mean(values, axis=-1, keepdims=True))
    centred = values - centre
    spread = lax.optimization_barrier(jnp.mean(centred * centred, axis=-1, keepdims=True))
    return centred * lax.rsqrt(spread + norm_epsilon) * gain + shift

def fnet_layer(stream, weight_in, weight_out, bias_in, vectors, tables):
    cos_model, sin_model, cos_seq, sin_seq = tables
    seq_len, model_width = (stream.shape[1], stream.shape[2])
    stream_low = low(stream)
    part_cos = low_back(low(jnp.einsum('gld,de->gle', stream_low, cos_model, precision=highest)))
    part_sin = low_back(low(jnp.einsum('gld,de->gle', stream_low, sin_model, precision=highest)))
    mixed = jnp.einsum('ml,gld->gmd', cos_seq, part_cos, precision=highest)
    mixed = mixed - jnp.einsum('ml,gld->gmd', sin_seq, part_sin, precision=highest)
    mixed = low_back(mixed * (1.0 / math.sqrt(seq_len * model_width)))
    vec_low = low(vectors)
    normed = layer_norm(stream + mixed, vec_low[0], vec_low[1])
    pre_act = jnp.einsum('gld,df->glf', low(normed), low(weight_in), precision=highest) + low(bias_in)
    pre_act = low_back(pre_act)
    activated = low(jax.nn.gelu(pre_act, approximate=True))
    feed = jnp.einsum('glf,fd->gld', activated, low(weight_out), precision=highest) + vec_low[2]
    feed = low_back(feed)
    return layer_norm(normed + feed, vec_low[3], vec_low[4])

def adam_update(weight, gradient, first, second, rate):
    first_new = beta_first * first + (1.0 - beta_first) * gradient
    second_new = beta_second * second + (1.0 - beta_second) * gradient * gradient
    first_hat = first_new / (1.0 - beta_first ** STEP_COUNT)
    second_hat = second_new / (1.0 - beta_second ** STEP_COUNT)
    updated = weight - rate * (first_hat / (jnp.sqrt(second_hat) + adam_epsilon) + weight_decay * weight)
    return (first_new, second_new, updated)

def reference(activations, cotangent, w_in, w_out, b_in, vec_params, first_w_in, second_w_in, first_w_out, second_w_out, first_b_in, second_b_in, first_vec, second_vec):
    cos_model, sin_model = dft_pair(D)
    cos_seq, sin_seq = dft_pair(LENGTH)
    tables = (cos_model, sin_model, cos_seq, sin_seq)
    group_size = math.gcd(SEQS_ALL, max(1, 4096 // LENGTH))

    def whole_block(inputs, weight_in, weight_out, bias_in, vectors):

        def one_group(group):
            stream = group
            for layer_index in range(LAYERS):
                stream = fnet_layer(stream, weight_in[layer_index], weight_out[layer_index], bias_in[layer_index], vectors[layer_index], tables)
            return stream
        grouped = inputs.reshape(SEQS_ALL // group_size, group_size, LENGTH, D)
        return lax.map(jax.checkpoint(one_group), grouped).reshape(SEQS_ALL, LENGTH, D)
    stream = activations.astype(jnp.float32)
    result, pullback = jax.vjp(whole_block, stream, w_in, w_out, b_in, vec_params)
    grads = pullback(cotangent.astype(jnp.float32))
    grad_stream, grad_w_in, grad_w_out, grad_b_in, grad_vec = grads
    squares = jnp.sum(grad_w_in * grad_w_in) + jnp.sum(grad_w_out * grad_w_out)
    squares = squares + jnp.sum(grad_b_in * grad_b_in) + jnp.sum(grad_vec * grad_vec)
    norm_value = jnp.sqrt(squares)
    factor = clip_limit / jnp.maximum(norm_value, clip_limit)
    upd_w_in = adam_update(w_in, factor * grad_w_in, first_w_in, second_w_in, rate_matrix)
    upd_w_out = adam_update(w_out, factor * grad_w_out, first_w_out, second_w_out, rate_matrix)
    upd_b_in = adam_update(b_in, factor * grad_b_in, first_b_in, second_b_in, rate_vector)
    upd_vec = adam_update(vec_params, factor * grad_vec, first_vec, second_vec, rate_vector)
    return (result.astype(jnp.bfloat16), grad_stream, norm_value, upd_w_in[0], upd_w_in[1], upd_w_in[2], upd_w_out[0], upd_w_out[1], upd_w_out[2], upd_b_in[0], upd_b_in[1], upd_b_in[2], upd_vec[0], upd_vec[1], upd_vec[2])
```

```python
import functools
import math
import types

import jax
import jax.numpy as jnp
import ml_dtypes
import numpy as np
from jax import lax
from jax.experimental import pallas as pl
from jax.experimental.pallas import tpu as pltpu
from jax.sharding import PartitionSpec as P

STEP_COUNT = 10


beta_first = 0.5
beta_second = 0.5
rate_matrix = 0.03
rate_vector = 0.2
weight_decay = 0.01
adam_epsilon = 1e-08
norm_epsilon = 1e-06
clip_limit = 1.0


def dft_tables(row_index, column_index, seq_len):
    product = row_index[:, None] * column_index[None, :] % seq_len
    angle = product.astype(jnp.float32) * (2.0 * math.pi / seq_len)
    return (jnp.cos(angle).astype(jnp.bfloat16), jnp.sin(angle).astype(jnp.bfloat16))


def layer_norm(values, gain, shift):
    centre = jnp.mean(values, axis=-1, keepdims=True)
    centred = values - centre
    spread = jnp.mean(centred * centred, axis=-1, keepdims=True)
    return centred * lax.rsqrt(spread + norm_epsilon) * gain + shift


def gelu_tanh(values):
    return jax.nn.gelu(values, approximate=True)


def adam_update(weight, gradient, first, second, rate, step_count):
    first_new = beta_first * first + (1.0 - beta_first) * gradient
    second_new = beta_second * second + (1.0 - beta_second) * gradient * gradient
    first_hat = first_new / (1.0 - beta_first**step_count)
    second_hat = second_new / (1.0 - beta_second**step_count)
    updated = weight - rate * (
        first_hat / (jnp.sqrt(second_hat) + adam_epsilon) + weight_decay * weight
    )
    return (first_new, second_new, updated)


def general_layer(
    activations,
    cotangent,
    w_in,
    w_out,
    b_in,
    vec_params,
    first_w_in,
    second_w_in,
    first_w_out,
    second_w_out,
    first_b_in,
    second_b_in,
    first_vec,
    second_vec,
):
    layers = w_in.shape[0]
    seq_count, block_len, model_width = activations.shape
    seq_devices = lax.axis_size(BOTH[1])
    seq_len = block_len * seq_devices
    dft_scale = 1.0 / math.sqrt(seq_len * model_width)
    first_row = lax.axis_index(BOTH[1]) * block_len
    my_rows = first_row + jnp.arange(block_len, dtype=jnp.int32)
    feature_line = jnp.arange(model_width, dtype=jnp.int32)
    cos_model, sin_model = dft_tables(feature_line, feature_line, model_width)
    table_fwd = jnp.concatenate([cos_model, sin_model], axis=1)
    table_back = jnp.transpose(table_fwd)
    layer_index = 0
    pieces = (
        w_in[layer_index].astype(jnp.bfloat16),
        w_out[layer_index].astype(jnp.bfloat16),
        b_in[layer_index].astype(jnp.bfloat16),
        vec_params[layer_index].astype(jnp.bfloat16),
    )
    gathered = [
        (
            lax.all_gather(pieces[0], BOTH, axis=0, tiled=True),
            lax.all_gather(pieces[1], BOTH, axis=1, tiled=True),
            lax.all_gather(pieces[2], BOTH, axis=0, tiled=True),
            lax.all_gather(pieces[3], BOTH, axis=1, tiled=True),
        )
    ]
    zeros_block = jnp.zeros((seq_count, block_len, model_width), jnp.float32)
    stream = activations.astype(jnp.float32)
    layer_index = 0
    weight_first, weight_second, bias_low, vec_low = gathered[layer_index]
    vec_float = vec_low.astype(jnp.float32)
    bias_float = bias_low.astype(jnp.float32)
    joined = jnp.dot(
        stream.astype(jnp.bfloat16), table_fwd, preferred_element_type=jnp.float32
    ).astype(jnp.bfloat16)
    halves = (joined[..., :model_width], joined[..., model_width:])
    shard_piece = (
        lax.all_gather(halves[0], BOTH[1], axis=1, tiled=True),
        lax.all_gather(halves[1], BOTH[1], axis=1, tiled=True),
    )
    piece_len = shard_piece[0].shape[1]
    cos_block, sin_block = dft_tables(my_rows, jnp.arange(piece_len, dtype=jnp.int32), seq_len)
    running = jnp.einsum(
        "ij,sjd->sid", cos_block, shard_piece[0], preferred_element_type=jnp.float32
    )
    mixed = (
        running
        - jnp.einsum("ij,sjd->sid", sin_block, shard_piece[1], preferred_element_type=jnp.float32)
    ) * dft_scale
    normed, norm_first_back = jax.vjp(layer_norm, stream + mixed, vec_float[0], vec_float[1])
    normed_low = normed.astype(jnp.bfloat16)
    pre_act = jnp.dot(normed_low, weight_first, preferred_element_type=jnp.float32) + bias_float
    activated, gelu_back = jax.vjp(gelu_tanh, pre_act)
    act_low = activated.astype(jnp.bfloat16)
    feed = jnp.dot(act_low, weight_second, preferred_element_type=jnp.float32) + vec_float[2]
    stream, norm_second_back = jax.vjp(layer_norm, normed + feed, vec_float[3], vec_float[4])
    saved = [(norm_first_back, normed_low, gelu_back, act_low, norm_second_back)]
    block_output = stream.astype(jnp.bfloat16)
    grad_now = cotangent.astype(jnp.float32)
    raw_grads = [None] * layers
    for layer_index in reversed(range(layers)):
        weight_first, weight_second, bias_low, vec_low = gathered[layer_index]
        norm_first_back, normed_low, gelu_back, act_low, norm_second_back = saved[layer_index]
        grad_sum2, grad_gain2, grad_shift2 = norm_second_back(grad_now)
        grad_z = grad_sum2.astype(jnp.bfloat16)
        grad_weight_second = jnp.einsum(
            "stf,std->fd", act_low, grad_z, preferred_element_type=jnp.float32
        )
        grad_bias_out = jnp.sum(grad_z.astype(jnp.float32), axis=(0, 1))
        grad_act = jnp.einsum(
            "std,fd->stf", grad_z, weight_second, preferred_element_type=jnp.float32
        )
        (grad_pre,) = gelu_back(grad_act)
        grad_pre_low = grad_pre.astype(jnp.bfloat16)
        grad_weight_first = jnp.einsum(
            "std,stf->df", normed_low, grad_pre_low, preferred_element_type=jnp.float32
        )
        grad_bias_in = jnp.sum(grad_pre_low.astype(jnp.float32), axis=(0, 1))
        grad_normed = (
            jnp.einsum(
                "stf,df->std", grad_pre_low, weight_first, preferred_element_type=jnp.float32
            )
            + grad_sum2
        )
        grad_sum1, grad_gain1, grad_shift1 = norm_first_back(grad_normed)
        grad_mix_low = grad_sum1.astype(jnp.bfloat16)
        add_shard_piece = lax.all_gather(grad_mix_low, BOTH[1], axis=1, tiled=True)
        add_piece_len = add_shard_piece.shape[1]
        add_cos_block, add_sin_block = dft_tables(
            my_rows, jnp.arange(add_piece_len, dtype=jnp.int32), seq_len
        )
        with_cos = jnp.einsum(
            "ij,sjd->sid", add_cos_block, add_shard_piece, preferred_element_type=jnp.float32
        )
        with_sin = (zeros_block, zeros_block)[1] - jnp.einsum(
            "ij,sjd->sid", add_sin_block, add_shard_piece, preferred_element_type=jnp.float32
        )
        with_cos, with_sin = (with_cos, with_sin)
        with_cos = (with_cos * dft_scale).astype(jnp.bfloat16)
        with_sin = (with_sin * dft_scale).astype(jnp.bfloat16)
        grad_halves = jnp.concatenate([with_cos, with_sin], axis=-1)
        grad_now = grad_sum1 + jnp.dot(grad_halves, table_back, preferred_element_type=jnp.float32)
        grad_vec = jnp.stack([grad_gain1, grad_shift1, grad_bias_out, grad_gain2, grad_shift2])
        layer_terms = (grad_weight_first, grad_weight_second, grad_bias_in, grad_vec)
        raw_grads[layer_index] = (
            lax.psum_scatter(layer_terms[0], BOTH, scatter_dimension=0, tiled=True),
            lax.psum_scatter(layer_terms[1], BOTH, scatter_dimension=1, tiled=True),
            lax.psum_scatter(layer_terms[2], BOTH, scatter_dimension=0, tiled=True),
            lax.psum_scatter(layer_terms[3], BOTH, scatter_dimension=1, tiled=True),
        )
    shard_w_in = jnp.stack([entry[0] for entry in raw_grads])
    shard_w_out = jnp.stack([entry[1] for entry in raw_grads])
    shard_b_in = jnp.stack([entry[2] for entry in raw_grads])
    shard_vec = jnp.stack([entry[3] for entry in raw_grads])
    local_squares = jnp.sum(shard_w_in * shard_w_in) + jnp.sum(shard_w_out * shard_w_out)
    local_squares = (
        local_squares + jnp.sum(shard_b_in * shard_b_in) + jnp.sum(shard_vec * shard_vec)
    )
    norm_value = jnp.sqrt(lax.psum(local_squares, BOTH))
    factor = clip_limit / jnp.maximum(norm_value, clip_limit)
    upd_w_in = adam_update(
        w_in, factor * shard_w_in, first_w_in, second_w_in, rate_matrix, STEP_COUNT
    )
    upd_w_out = adam_update(
        w_out, factor * shard_w_out, first_w_out, second_w_out, rate_matrix, STEP_COUNT
    )
    upd_b_in = adam_update(
        b_in, factor * shard_b_in, first_b_in, second_b_in, rate_vector, STEP_COUNT
    )
    upd_vec = adam_update(
        vec_params, factor * shard_vec, first_vec, second_vec, rate_vector, STEP_COUNT
    )
    return (
        block_output,
        grad_now,
        norm_value,
        upd_w_in[0],
        upd_w_in[1],
        upd_w_in[2],
        upd_w_out[0],
        upd_w_out[1],
        upd_w_out[2],
        upd_b_in[0],
        upd_b_in[1],
        upd_b_in[2],
        upd_vec[0],
        upd_vec[1],
        upd_vec[2],
    )


MESH = pl.DeviceIdType.MESH
F32 = jnp.float32
BF16 = jnp.bfloat16
NN = (((1,), (0,)), ((), ()))
NT = (((1,), (1,)), ((), ()))
TN = (((0,), (0,)), ((), ()))


def dot(a, b, dims=NN):
    return lax.dot_general(a, b, dims, preferred_element_type=F32)


class Sizes:
    def __init__(self, mesh, seqs, block, width, hidden):
        self.batch, self.seq = mesh.shape["batch"], mesh.shape["seq"]
        self.xs, self.ys, self.zs = self.batch // 2, 2, self.seq // 2
        self.devices = self.batch * self.seq
        self.seqs, self.block, self.width, self.hidden = seqs, block, width, hidden
        self.length = block * self.seq
        self.rows = width // self.devices
        self.slab = 2 * self.rows
        self.segment = self.zs * self.slab
        self.half = hidden // 2
        self.chunks = 4
        self.cols = self.half // self.chunks
        self.packed = width // self.seq
        self.tokens = seqs * block
        self.bias = hidden // self.devices

    def fits(self):
        return (
            self.batch == 4
            and self.seq % 2 == 0
            and self.width % self.devices == 0
            and self.slab % 16 == 0
            and self.packed % 32 == 0
            and self.block % 128 == 0
            and self.half % (128 * self.chunks) == 0
            and self.rows <= 128
            and self.bias <= 128
            and 5 * self.rows <= self.width
        )

    def owner(self, x, core, z, y):
        return (2 * x + core) * self.seq + 2 * z + y

    def place_owner(self):
        return [
            self.owner(x, core, z, y)
            for y in range(self.ys)
            for x in range(self.xs)
            for z in range(self.zs)
            for core in range(2)
        ]


def cos_sin(rows, columns, count):
    angle = (rows[:, None] * columns[None, :] % count) * (2.0 * math.pi / count)
    return np.cos(angle), np.sin(angle)


def host_tables(n):
    width, half = n.width, n.packed // 2
    owners = np.array(n.place_owner())
    order = (owners[:, None] * n.rows + np.arange(n.rows)[None, :]).reshape(-1)
    line = np.arange(width)
    cosine, sine = cos_sin(line, line, width)
    pack = np.zeros((width, width))
    unpack = np.zeros((width, width))
    for k in range(width // 2):
        device, inner = divmod(k, half)
        at_cos = device * n.packed + inner
        at_sin = at_cos + half
        pack[at_cos] = cosine[k]
        unpack[at_cos, k] = 1.0
        if k:
            unpack[at_cos, width - k] = 1.0
            pack[at_sin] = sine[k]
            unpack[at_sin, k] = -1.0
            unpack[at_sin, width - k] = 1.0
    pack[half] = cosine[width // 2]
    unpack[half, width // 2] = 1.0
    perm = np.zeros((width, width))
    perm[order, np.arange(width)] = 1.0
    positions = np.arange(n.length)
    by_length = np.stack(cos_sin(positions, positions, n.length))
    vec_mask = np.zeros((n.devices, width))
    vec_mask[np.repeat(owners, n.rows), np.arange(width)] = 1.0
    vec_spread = np.zeros((128, width))
    vec_spread[np.arange(width) % n.rows, np.arange(width)] = 1.0
    bias_spread = np.zeros((128, n.half))
    bias_spread[np.arange(n.half) % n.bias, np.arange(n.half)] = 1.0

    def low(a):
        return jnp.asarray(a.astype(np.float32).astype(ml_dtypes.bfloat16))

    return types.SimpleNamespace(
        tt_f=low(pack),
        by_length=low(by_length),
        un_f=low(unpack[:, order]),
        perm=low(perm),
        tt_b=low(pack[:, order]),
        un_b=low(unpack),
        vec_mask=jnp.asarray(vec_mask.astype(np.float32)),
        vec_spread=low(vec_spread),
        bias_spread=low(bias_spread),
    )


TABLES = ("tt_f", "by_length", "un_f", "perm", "tt_b", "un_b")


def layer_kernel(n, names, *refs):
    r = types.SimpleNamespace(**dict(zip(names, refs)))
    batch_at, seq_at = lax.axis_index("batch"), lax.axis_index("seq")
    x, core = batch_at // 2, batch_at % 2
    z, y = seq_at // 2, seq_at % 2
    tokens, width, seg, slab = n.tokens, n.width, n.segment, n.slab
    started = []

    def aligned(at, by):
        return pl.multiple_of(at * by, by)

    def rows_of(at, by):
        return pl.ds(aligned(at, by), by)

    def remote(src, dst, send, recv, batch_to, seq_to):
        return pltpu.make_async_remote_copy(
            src_ref=src,
            dst_ref=dst,
            send_sem=send,
            recv_sem=recv,
            device_id=(batch_to, seq_to),
            device_id_type=MESH,
        )

    def go(copy):
        copy.start()
        started.append(copy)
        return copy

    other_core = 2 * x + 1 - core
    other_x = 2 * (1 - x) + core
    other_y = 2 * z + 1 - y

    def plane(k):
        return (seq_at + k) % n.seq

    def plane_from(k):
        return (seq_at + n.seq - k) % n.seq

    def across(k):
        return (batch_at + k) % n.batch

    def across_from(k):
        return (batch_at + n.batch - k) % n.batch

    loads = types.SimpleNamespace()
    for i, name in enumerate(TABLES):
        load = pltpu.make_async_copy(getattr(r, name), getattr(r, name + "_v"), r.load_sem.at[i])
        setattr(loads, name, load)
        load.start()

    barrier = pltpu.get_barrier_semaphore()
    for k in range(1, n.seq):
        pl.semaphore_signal(barrier, inc=1, device_id=(batch_at, plane(k)), device_id_type=MESH)
    for k in range(1, n.batch):
        pl.semaphore_signal(barrier, inc=1, device_id=(across(k), seq_at), device_id_type=MESH)
    pl.semaphore_wait(barrier, n.seq + n.batch - 2)

    weights = (r.w1, r.w2)
    give = pl.ds(aligned(1 - core, n.half), n.half)
    keep = pl.ds(aligned(core, n.half), n.half)
    core_rows = pl.ds(aligned(core, n.rows), n.rows)
    swaps = [
        go(
            remote(
                weights[m].at[:, give],
                r.stage.at[m, core_rows],
                r.swap_send.at[m],
                r.swap_recv.at[m],
                other_core,
                seq_at,
            )
        )
        for m in range(2)
    ]

    tile = r.tile
    tile[...] = jnp.zeros(tile.shape, F32)
    tile[0:5, 0 : n.rows] = r.vec[...]
    tile[5:6, 0 : n.bias] = r.bias[...]
    small = r.small
    small_one = [
        go(
            remote(
                tile,
                small.at[batch_at, seq_at],
                r.small_send.at[k - 1],
                r.small_recv.at[k - 1],
                batch_at,
                plane(k),
            )
        )
        for k in range(1, n.seq)
    ]
    small[batch_at, seq_at] = tile[...]

    def mix_start(t, source, table):
        y_ref, l_ref = r.y_buf.at[t], r.l_buf.at[t]
        y_ref[...] = dot(table[...], source, NT).astype(BF16)
        for k in range(1, n.seq):
            go(
                remote(
                    y_ref.at[rows_of(plane(k), n.packed)],
                    l_ref.at[seq_at],
                    r.mix_send.at[2 * t, k - 1],
                    r.mix_recv.at[2 * t, k - 1],
                    batch_at,
                    plane(k),
                )
            )
        l_ref[seq_at] = y_ref[rows_of(seq_at, n.packed), :]

    def mix_turn(t):
        l_ref, z_ref, r_ref = r.l_buf.at[t], r.z_buf.at[t], r.r_buf.at[t]
        for k in range(1, n.seq):
            remote(
                r.y_buf.at[t, rows_of(plane(k), n.packed)],
                l_ref.at[plane_from(k)],
                r.mix_send.at[2 * t, k - 1],
                r.mix_recv.at[2 * t, k - 1],
                batch_at,
                plane(k),
            ).wait_recv()
        left = jnp.concatenate(
            [
                jnp.concatenate(
                    [l_ref[d, :, g * n.block : (g + 1) * n.block] for d in range(n.seq)], axis=1
                )
                for g in range(n.seqs)
            ],
            axis=0,
        )
        r.left[...] = left
        inner = lax.broadcasted_iota(jnp.int32, (n.seqs * n.packed, 1), 0) % n.packed
        first = (inner < n.packed // 2) | ((inner == n.packed // 2) & (seq_at == 0))
        scale = 1.0 / math.sqrt(n.length * n.width)
        for e in range(n.seq):
            at = slice(e * n.block, (e + 1) * n.block)
            by_cos = dot(r.left[...], r.by_length_v[0, :, at])
            by_sin = dot(r.left[...], r.by_length_v[1, :, at])
            z_ref[e] = (jnp.where(first, by_cos, by_sin) * scale).astype(BF16)
        for k in range(1, n.seq):
            go(
                remote(
                    z_ref.at[plane(k)],
                    r_ref.at[seq_at],
                    r.mix_send.at[2 * t + 1, k - 1],
                    r.mix_recv.at[2 * t + 1, k - 1],
                    batch_at,
                    plane(k),
                )
            )
        r_ref[seq_at] = z_ref[seq_at]

    def mix_finish(t, table):
        r_ref = r.r_buf.at[t]
        for k in range(1, n.seq):
            remote(
                r.z_buf.at[t, plane(k)],
                r_ref.at[plane_from(k)],
                r.mix_send.at[2 * t + 1, k - 1],
                r.mix_recv.at[2 * t + 1, k - 1],
                batch_at,
                plane(k),
            ).wait_recv()
        parts = [
            r_ref[:, g * n.packed : (g + 1) * n.packed, :].reshape(width, n.block)
            for g in range(n.seqs)
        ]
        r.mixed[...] = dot(jnp.concatenate(parts, axis=1), table[...], TN)

    loads.tt_f.wait()
    mix_start(0, r.x[...], r.tt_f_v)

    full = r.full

    def seg_rows(sx, sy):
        return rows_of(sy * n.xs + sx, seg)

    def slab_rows(sx, sy, sz):
        return rows_of((sy * n.xs + sx) * n.zs + sz, slab)

    for m in range(2):
        r.stage[m, core_rows, :] = weights[m][:, keep]
        remote(
            weights[m].at[:, give],
            r.stage.at[m, pl.ds(aligned(1 - core, n.rows), n.rows)],
            r.swap_send.at[m],
            r.swap_recv.at[m],
            other_core,
            seq_at,
        ).wait_recv()
        for q in range(n.chunks):
            full[m, q, slab_rows(x, y, z), :] = r.stage[m, :, q * n.cols : (q + 1) * n.cols].astype(
                BF16
            )

    def z_copy(m, q, d, source_z):
        at = slab_rows(x, y, source_z)
        return remote(
            full.at[m, q, at],
            full.at[m, q, at],
            r.z_send.at[m, q, d - 1],
            r.z_recv.at[m, q, d - 1],
            batch_at,
            2 * ((z + d) % n.zs) + y,
        )

    def weights_along_z(q):
        for m in range(2):
            for d in range(1, n.zs):
                go(z_copy(m, q, d, z))

    def turn_of(m, q):
        return (m + q) % 2

    def peer(t):
        return (
            batch_at + (1 - t) * (other_x - batch_at),
            seq_at + t * (other_y - seq_at),
        )

    def away(t):
        return x + (1 - t) * (1 - 2 * x), y + t * (1 - 2 * y)

    def seg_copy(m, q, i, t, sx, sy):
        at = seg_rows(sx, sy)
        return remote(
            full.at[m, q, at],
            full.at[m, q, at],
            r.seg_send.at[m, q, i],
            r.seg_recv.at[m, q, i],
            *peer(t),
        )

    def weights_one(q):
        for m in range(2):
            t = turn_of(m, q)
            for d in range(1, n.zs):
                z_copy(m, q, d, (z + n.zs - d) % n.zs).wait_recv()
            go(seg_copy(m, q, 0, t, x, y))
            go(seg_copy(m, q, 1, 1 - t, x, y))

    def weights_two(q):
        for m in range(2):
            t = turn_of(m, q)
            ax, ay = away(t)
            seg_copy(m, q, 0, t, ax, ay).wait_recv()
            go(seg_copy(m, q, 2, 1 - t, ax, ay))

    def weights_here(m, q):
        t = (m + q) % 2
        bx, by = away(1 - t)
        seg_copy(m, q, 1, 1 - t, bx, by).wait_recv()
        seg_copy(m, q, 2, 1 - t, 1 - x, 1 - y).wait_recv()

    weights_along_z(0)
    weights_along_z(1)

    for k in range(1, n.seq):
        remote(
            tile,
            small.at[batch_at, plane_from(k)],
            r.small_send.at[k - 1],
            r.small_recv.at[k - 1],
            batch_at,
            plane(k),
        ).wait_recv()
    for k in range(1, n.batch):
        go(
            remote(
                small.at[batch_at],
                small.at[batch_at],
                r.row_send.at[k - 1],
                r.row_recv.at[k - 1],
                across(k),
                seq_at,
            )
        )

    loads.by_length.wait()
    mix_turn(0)
    weights_along_z(2)
    weights_along_z(3)
    weights_one(0)

    loads.perm.wait()
    r.x_place[...] = dot(r.x[...], r.perm_v[...])
    r.dy_place[...] = dot(r.dy[...], r.perm_v[...])
    for k in range(1, n.batch):
        remote(
            small.at[batch_at],
            small.at[across_from(k)],
            r.row_send.at[k - 1],
            r.row_recv.at[k - 1],
            across(k),
            seq_at,
        ).wait_recv()
    vec_rows = []
    for i in range(5):
        held = small[:, :, i, :].reshape(n.devices, 128).astype(BF16)
        spread = dot(held, r.vec_spread[...]) * r.vec_mask[...]
        vec_rows.append(jnp.sum(spread, axis=0, keepdims=True))
    for i in range(5):
        r.vecs[i : i + 1, :] = vec_rows[i]
    half_owners = n.devices // 2
    held = small[pl.ds(core * (n.batch // 2), n.batch // 2), :, 5, :]
    held = held.reshape(half_owners, 128).astype(BF16)
    bias_mask = (
        lax.broadcasted_iota(jnp.int32, (half_owners, n.half), 0)
        == lax.broadcasted_iota(jnp.int32, (half_owners, n.half), 1) // n.bias
    )
    biases = jnp.sum(
        jnp.where(bias_mask, dot(held, r.bias_spread[...]), 0.0), axis=0, keepdims=True
    )
    for q in range(n.chunks):
        r.biases[q] = biases[:, q * n.cols : (q + 1) * n.cols]

    weights_one(1)
    weights_two(0)
    loads.un_f.wait()
    mix_finish(0, r.un_f_v)

    step = 32

    def row_loop(body):
        @pl.loop(0, tokens // step)
        def _(i):
            body(pl.ds(pl.multiple_of(i * step, step), step))

    def mean(v):
        return jnp.mean(v, axis=-1, keepdims=True)

    def first_norm(at):
        v = r.x_place[at, :] + r.mixed[at, :]
        centred = v - mean(v)
        scale = lax.rsqrt(mean(centred * centred) + norm_epsilon)
        unit = centred * scale
        h = unit * r.vecs[0:1, :] + r.vecs[1:2, :]
        r.unit1[at, :] = unit
        r.scale1[at, :] = jnp.broadcast_to(scale, (step, 128))
        r.h[at, :] = h
        r.h_low[at, :] = h.astype(BF16)

    row_loop(first_norm)

    mine, theirs = pl.ds(0, tokens), pl.ds(tokens, tokens)

    def swap(i, src, dst):
        return remote(
            src, dst, r.core_send.at[i], r.core_recv.at[i], other_core, seq_at
        )

    swap_h = go(swap(0, r.h_low.at[mine], r.h_low.at[theirs]))
    weights_one(2)
    weights_two(1)
    weights_one(3)
    weights_two(2)
    weights_two(3)
    swap_h.wait_recv()

    r.total[...] = jnp.zeros(r.total.shape, F32)
    root = math.sqrt(2.0 / math.pi)
    part = 128

    @pl.loop(0, n.chunks)
    def _(q):
        weights_here(0, q)
        weights_here(1, q)

        @pl.loop(0, 2 * tokens // part)
        def _(i):
            at = pl.ds(pl.multiple_of(i * part, part), part)
            u = dot(r.h_low[at, :], full[0, q]) + r.biases[q]
            square = u * u
            bent = jnp.tanh(root * u * (1.0 + 0.044715 * square))
            half_up = 0.5 * (1.0 + bent)
            act = (u * half_up).astype(BF16)
            r.slope[q, at, :] = half_up + 0.5 * u * (1.0 - bent * bent) * (
                root * (1.0 + 3.0 * 0.044715 * square)
            )
            r.act[q, at, :] = act
            r.total[at, :] = r.total[at, :] + dot(act, full[1, q], NT)

    r.part_low[...] = r.total[theirs, :].astype(BF16)
    swap_ff = go(swap(1, r.part_low, r.part_in))
    swap_ff.wait_recv()

    r.sums[...] = jnp.zeros(r.sums.shape, F32)

    def fold(v):
        return jnp.sum(v.reshape(step // 8, 8, width), axis=0)

    def second_norm(at):
        v = (
            r.h[at, :]
            + r.total[at, :]
            + r.part_in[at, :].astype(F32)
            + r.vecs[2:3, :]
        )
        centred = v - mean(v)
        scale = lax.rsqrt(mean(centred * centred) + norm_epsilon)
        unit = centred * scale
        gain = r.vecs[3:4, :]
        r.out_low[at, :] = (unit * gain + r.vecs[4:5, :]).astype(BF16)
        dy = r.dy_place[at, :]
        r.sums[3] += fold(dy * unit)
        r.sums[4] += fold(dy)
        du = dy * gain
        dv = scale * (du - mean(du) - unit * mean(du * unit))
        r.dr2[at, :] = dv
        low = dv.astype(BF16)
        r.dz[at, :] = low
        r.sums[2] += fold(low.astype(F32))

    row_loop(second_norm)
    swap_dz = go(swap(2, r.dz.at[mine], r.dz.at[theirs]))
    r.h_turned[...] = jnp.transpose(r.h_low[...])
    swap_dz.wait_recv()
    r.dz_turned[...] = jnp.transpose(r.dz[...])

    acc, out_low, in_one, in_two, in_three = (
        r.acc,
        r.give,
        r.in_one,
        r.in_two,
        r.in_three,
    )

    def first_parts(m, q, t):
        ax, ay = away(t)
        return [(j, ax * (1 - t) + j * t, ay * t + j * (1 - t)) for j in range(2)]

    def grad_copy_one(m, q, t, j, sx, sy):
        return remote(
            out_low.at[m, q, seg_rows(sx, sy)],
            in_one.at[m, q, j],
            r.one_send.at[m, q, j],
            r.one_recv.at[m, q, j],
            *peer(t),
        )

    def grads_one(m, q):
        t = 1 - (m + q) % 2
        for j, sx, sy in first_parts(m, q, t):
            at = seg_rows(sx, sy)
            out_low[m, q, at, :] = acc[m, q, at, :].astype(BF16)
            grad_copy_one(m, q, t, j, sx, sy).start()

    def grad_copy_two(m, q, t, sx, sy):
        return remote(
            out_low.at[m, q, seg_rows(sx, sy)],
            in_two.at[m, q],
            r.two_send.at[m, q],
            r.two_recv.at[m, q],
            *peer(t),
        )

    def grads_two(m, q):
        t = 1 - (m + q) % 2
        for j, sx, sy in first_parts(m, q, t):
            grad_copy_one(m, q, t, j, sx, sy).wait_recv()
        bx, by = away(1 - t)
        at = seg_rows(bx, by)
        away_j = bx * t + by * (1 - t)
        out_low[m, q, at, :] = (acc[m, q, at, :] + in_one[m, q, away_j].astype(F32)).astype(BF16)
        grad_copy_two(m, q, 1 - t, bx, by).start()
        at = seg_rows(x, y)
        here_j = x * t + y * (1 - t)
        acc[m, q, at, :] = acc[m, q, at, :] + in_one[m, q, here_j].astype(F32)

    def grad_copy_three(m, q, d):
        to_z = (z + d) % n.zs
        return remote(
            out_low.at[m, q, slab_rows(x, y, to_z)],
            in_three.at[m, q, d - 1],
            r.three_send.at[m, q, d - 1],
            r.three_recv.at[m, q, d - 1],
            batch_at,
            2 * to_z + y,
        )

    def grads_three(m, q):
        t = 1 - (m + q) % 2
        bx, by = away(1 - t)
        grad_copy_two(m, q, 1 - t, bx, by).wait_recv()
        at = seg_rows(x, y)
        acc[m, q, at, :] = acc[m, q, at, :] + in_two[m, q].astype(F32)
        for d in range(1, n.zs):
            at = slab_rows(x, y, (z + d) % n.zs)
            out_low[m, q, at, :] = acc[m, q, at, :].astype(BF16)
            grad_copy_three(m, q, d).start()

    def grads_four(m, q):
        at = slab_rows(x, y, z)
        value = acc[m, q, at, :]
        for d in range(1, n.zs):
            grad_copy_three(m, q, d).wait_recv()
            value = value + in_three[m, q, d - 1].astype(F32)
        r.final[m, q] = value

    @pl.loop(0, n.chunks)
    def _(q):
        acc[1, q] = dot(r.dz_turned[...], r.act[q])
        grads_one(1, q)

    r.total[...] = jnp.zeros(r.total.shape, F32)

    @pl.loop(0, n.chunks)
    def _(q):
        r.bias_sum[q] = jnp.zeros((8, n.cols), F32)

        @pl.loop(0, 2 * tokens // part)
        def _(i):
            at = pl.ds(pl.multiple_of(i * part, part), part)
            low = (dot(r.dz[at, :], full[1, q]) * r.slope[q, at, :]).astype(BF16)
            r.dpre[q, at, :] = low
            r.bias_sum[q] += jnp.sum(low.astype(F32).reshape(part // 8, 8, n.cols), axis=0)
            r.total[at, :] = r.total[at, :] + dot(low, full[0, q], NT)

    swap_ff.wait_send()
    started[:] = [copy for copy in started if copy is not swap_ff]
    r.part_low[...] = r.total[theirs, :].astype(BF16)
    swap_dh = go(swap(3, r.part_low, r.part_in2))
    swap_dh.wait_recv()

    def first_norm_back(at):
        dh = r.total[at, :] + r.part_in2[at, :].astype(F32) + r.dr2[at, :]
        unit = r.unit1[at, :]
        r.sums[0] += fold(dh * unit)
        r.sums[1] += fold(dh)
        du = dh * r.vecs[0:1, :]
        dv = r.scale1[at, 0:1] * (du - mean(du) - unit * mean(du * unit))
        low = dv.astype(BF16)
        r.dm[at, :] = low
        r.rest[at, :] = (dv - low.astype(F32)).astype(BF16)

    row_loop(first_norm_back)
    loads.tt_b.wait()
    mix_start(1, r.dm[...], r.tt_b_v)

    @pl.loop(0, n.chunks)
    def _(q):
        acc[0, q] = dot(r.h_turned[...], r.dpre[q])
        grads_one(0, q)

    for i in range(5):
        line = jnp.sum(r.sums[i], axis=0, keepdims=True)
        masked = line * r.vec_mask[...]
        high = masked.astype(BF16)
        left = masked - high.astype(F32)
        mid = left.astype(BF16)
        low = (left - mid.astype(F32)).astype(BF16)
        spread = r.vec_spread[...]
        tiles = dot(high, spread, NT) + dot(mid, spread, NT) + dot(low, spread, NT)
        r.small_out[:, :, i, :] = tiles.reshape(n.batch, n.seq, 128)
    line = jnp.concatenate(
        [jnp.sum(r.bias_sum[q], axis=0, keepdims=True) for q in range(n.chunks)], axis=1
    )
    masked = jnp.where(bias_mask, line, 0.0)
    high = masked.astype(BF16)
    left = masked - high.astype(F32)
    mid = left.astype(BF16)
    low = (left - mid.astype(F32)).astype(BF16)
    spread = r.bias_spread[...]
    tiles = dot(high, spread, NT) + dot(mid, spread, NT) + dot(low, spread, NT)
    r.small_out[:, :, 5, :] = jnp.zeros((n.batch, n.seq, 128), F32)
    r.small_out[pl.ds(core * (n.batch // 2), n.batch // 2), :, 5, :] = tiles.reshape(
        n.batch // 2, n.seq, 128
    )
    r.small_out[:, :, 6:8, :] = jnp.zeros((n.batch, n.seq, 2, 128), F32)
    for k in range(1, n.batch):
        go(
            remote(
                r.small_out.at[across(k)],
                r.small_in.at[k - 1],
                r.row_send2.at[k - 1],
                r.row_recv2.at[k - 1],
                across(k),
                seq_at,
            )
        )

    @pl.loop(0, n.chunks)
    def _(q):
        grads_two(1, q)

    mix_turn(1)

    total_small = r.small_out[batch_at]
    for k in range(1, n.batch):
        remote(
            r.small_out.at[across(k)],
            r.small_in.at[k - 1],
            r.row_send2.at[k - 1],
            r.row_recv2.at[k - 1],
            across(k),
            seq_at,
        ).wait_recv()
        total_small = total_small + r.small_in[k - 1]
    r.small_mid[...] = total_small
    for k in range(1, n.seq):
        go(
            remote(
                r.small_mid.at[plane(k)],
                r.small_last.at[k - 1],
                r.small_send2.at[k - 1],
                r.small_recv2.at[k - 1],
                batch_at,
                plane(k),
            )
        )

    @pl.loop(0, n.chunks)
    def _(q):
        grads_three(1, q)

    @pl.loop(0, n.chunks)
    def _(q):
        grads_two(0, q)

    r.out[...] = dot(r.out_low[...], r.perm_v[...], NT).astype(BF16)
    r.dx[...] = dot(r.dm[...], r.perm_v[...], NT) + dot(
        r.rest[...], r.perm_v[...], NT
    )
    loads.un_b.wait()
    mix_finish(1, r.un_b_v)
    r.dx[...] = r.dx[...] + r.mixed[...]

    value = r.small_mid[seq_at]
    for k in range(1, n.seq):
        remote(
            r.small_mid.at[plane(k)],
            r.small_last.at[k - 1],
            r.small_send2.at[k - 1],
            r.small_recv2.at[k - 1],
            batch_at,
            plane(k),
        ).wait_recv()
        value = value + r.small_last[k - 1]
    r.g_small[...] = value

    @pl.loop(0, n.chunks)
    def _(q):
        grads_four(1, q)

    @pl.loop(0, n.chunks)
    def _(q):
        grads_three(0, q)

    @pl.loop(0, n.chunks)
    def _(q):
        grads_four(0, q)

    grads = (r.g1, r.g2)
    for m in range(2):
        r.final_turn[m] = jnp.concatenate([r.final[m, q] for q in range(n.chunks)], axis=1)
    their_rows = pl.ds(aligned(1 - core, n.rows), n.rows)
    back = [
        go(
            remote(
                r.final_turn.at[m, their_rows],
                r.final_in.at[m],
                r.back_send.at[m],
                r.back_recv.at[m],
                other_core,
                seq_at,
            )
        )
        for m in range(2)
    ]
    squares = jnp.zeros((8, 128), F32)

    def squares_of(v):
        v = v * v
        v = jnp.sum(v.reshape(v.shape[0] // 8, 8, v.shape[1]), axis=0)
        return sum(v[:, i : i + 128] for i in range(0, v.shape[1], 128))

    squares = squares + value * value
    for m in range(2):
        grads[m][:, keep] = r.final_turn[m, core_rows, :]
        back[m].wait_recv()
        grads[m][:, give] = r.final_in[m]
        squares = squares + squares_of(grads[m][...])
    r.norm_own[...] = squares
    r.norm_plane[seq_at] = squares
    for k in range(1, n.seq):
        go(
            remote(
                r.norm_own,
                r.norm_plane.at[seq_at],
                r.norm_send.at[k - 1],
                r.norm_recv.at[k - 1],
                batch_at,
                plane(k),
            )
        )
    for k in range(1, n.seq):
        remote(
            r.norm_own,
            r.norm_plane.at[plane_from(k)],
            r.norm_send.at[k - 1],
            r.norm_recv.at[k - 1],
            batch_at,
            plane(k),
        ).wait_recv()
    squares = r.norm_plane[0]
    for k in range(1, n.seq):
        squares = squares + r.norm_plane[k]
    r.norm_sum[...] = squares
    r.norm_all[batch_at] = squares
    for k in range(1, n.batch):
        go(
            remote(
                r.norm_sum,
                r.norm_all.at[batch_at],
                r.norm_send2.at[k - 1],
                r.norm_recv2.at[k - 1],
                across(k),
                seq_at,
            )
        )
    for k in range(1, n.batch):
        remote(
            r.norm_sum,
            r.norm_all.at[across_from(k)],
            r.norm_send2.at[k - 1],
            r.norm_recv2.at[k - 1],
            across(k),
            seq_at,
        ).wait_recv()
    squares = r.norm_all[0]
    for k in range(1, n.batch):
        squares = squares + r.norm_all[k]
    whole = jnp.sum(jnp.sum(squares, axis=1, keepdims=True), axis=0, keepdims=True)
    r.norm[...] = jnp.broadcast_to(jnp.sqrt(whole), (8, 128))

    for copy in started:
        copy.wait_send()

    @pl.loop(0, n.chunks)
    def _(q):
        for m in range(2):
            t = 1 - (m + q) % 2
            for j, sx, sy in first_parts(m, q, t):
                grad_copy_one(m, q, t, j, sx, sy).wait_send()
            bx, by = away(1 - t)
            grad_copy_two(m, q, 1 - t, bx, by).wait_send()
            for d in range(1, n.zs):
                grad_copy_three(m, q, d).wait_send()


def run_layer(n, x, dy, w1, w2, bias, vec):
    tables = host_tables(n)
    tokens, width, cols, q = n.tokens, n.width, n.cols, n.chunks
    dma = pltpu.SemaphoreType.DMA
    vmem = pltpu.VMEM
    inputs = dict(
        x=x,
        dy=dy,
        w1=w1,
        w2=w2,
        bias=bias,
        vec=vec,
        vec_mask=tables.vec_mask,
        vec_spread=tables.vec_spread,
        bias_spread=tables.bias_spread,
    )
    inputs.update({name: getattr(tables, name) for name in TABLES})
    outputs = dict(
        out=((tokens, width), BF16),
        dx=((tokens, width), F32),
        g1=((n.rows, n.hidden), F32),
        g2=((n.rows, n.hidden), F32),
        g_small=((8, 128), F32),
        norm=((8, 128), F32),
    )
    scratch = {name + "_v": vmem(getattr(tables, name).shape, BF16) for name in TABLES}
    scratch.update(
        load_sem=dma((len(TABLES),)),
        stage=vmem((2, n.slab, n.half), F32),
        swap_send=dma((2,)),
        swap_recv=dma((2,)),
        tile=vmem((8, 128), F32),
        small=vmem((n.batch, n.seq, 8, 128), F32),
        small_send=dma((n.seq - 1,)),
        small_recv=dma((n.seq - 1,)),
        row_send=dma((n.batch - 1,)),
        row_recv=dma((n.batch - 1,)),
        y_buf=vmem((2, width, tokens), BF16),
        l_buf=vmem((2, n.seq, n.packed, tokens), BF16),
        left=vmem((n.seqs * n.packed, n.length), BF16),
        z_buf=vmem((2, n.seq, n.seqs * n.packed, n.block), BF16),
        r_buf=vmem((2, n.seq, n.seqs * n.packed, n.block), BF16),
        mix_send=dma((4, n.seq - 1)),
        mix_recv=dma((4, n.seq - 1)),
        mixed=vmem((tokens, width), F32),
        full=vmem((2, q, width, cols), BF16),
        z_send=dma((2, q, n.zs - 1)),
        z_recv=dma((2, q, n.zs - 1)),
        seg_send=dma((2, q, 3)),
        seg_recv=dma((2, q, 3)),
        x_place=vmem((tokens, width), F32),
        dy_place=vmem((tokens, width), F32),
        vecs=vmem((8, width), F32),
        biases=vmem((q, 1, cols), F32),
        unit1=vmem((tokens, width), F32),
        scale1=vmem((tokens, 128), F32),
        h=vmem((tokens, width), F32),
        h_low=vmem((2 * tokens, width), BF16),
        core_send=dma((4,)),
        core_recv=dma((4,)),
        total=vmem((2 * tokens, width), F32),
        act=vmem((q, 2 * tokens, cols), BF16),
        slope=vmem((q, 2 * tokens, cols), F32),
        part_low=vmem((tokens, width), BF16),
        part_in=vmem((tokens, width), BF16),
        part_in2=vmem((tokens, width), BF16),
        sums=vmem((5, 8, width), F32),
        out_low=vmem((tokens, width), BF16),
        dr2=vmem((tokens, width), F32),
        dz=vmem((2 * tokens, width), BF16),
        h_turned=vmem((width, 2 * tokens), BF16),
        dz_turned=vmem((width, 2 * tokens), BF16),
        acc=vmem((2, q, width, cols), F32),
        give=vmem((2, q, width, cols), BF16),
        in_one=vmem((2, q, 2, n.segment, cols), BF16),
        in_two=vmem((2, q, n.segment, cols), BF16),
        in_three=vmem((2, q, n.zs - 1, n.slab, cols), BF16),
        one_send=dma((2, q, 2)),
        one_recv=dma((2, q, 2)),
        two_send=dma((2, q)),
        two_recv=dma((2, q)),
        three_send=dma((2, q, n.zs - 1)),
        three_recv=dma((2, q, n.zs - 1)),
        bias_sum=vmem((q, 8, cols), F32),
        dpre=vmem((q, 2 * tokens, cols), BF16),
        dm=vmem((tokens, width), BF16),
        rest=vmem((tokens, width), BF16),
        small_out=vmem((n.batch, n.seq, 8, 128), F32),
        small_in=vmem((n.batch - 1, n.seq, 8, 128), F32),
        row_send2=dma((n.batch - 1,)),
        row_recv2=dma((n.batch - 1,)),
        small_mid=vmem((n.seq, 8, 128), F32),
        small_last=vmem((n.seq - 1, 8, 128), F32),
        small_send2=dma((n.seq - 1,)),
        small_recv2=dma((n.seq - 1,)),
        final=vmem((2, q, n.slab, cols), F32),
        final_turn=vmem((2, n.slab, n.half), F32),
        final_in=vmem((2, n.rows, n.half), F32),
        back_send=dma((2,)),
        back_recv=dma((2,)),
        norm_own=vmem((8, 128), F32),
        norm_plane=vmem((n.seq, 8, 128), F32),
        norm_sum=vmem((8, 128), F32),
        norm_all=vmem((n.batch, 8, 128), F32),
        norm_send=dma((n.seq - 1,)),
        norm_recv=dma((n.seq - 1,)),
        norm_send2=dma((n.batch - 1,)),
        norm_recv2=dma((n.batch - 1,)),
    )
    names = tuple(inputs) + tuple(outputs) + tuple(scratch)
    in_vmem = pl.BlockSpec(memory_space=pltpu.VMEM)
    anywhere = pl.BlockSpec(memory_space=pl.ANY)
    values = pl.pallas_call(
        functools.partial(layer_kernel, n, names),
        out_shape=[jax.ShapeDtypeStruct(*shape) for shape in outputs.values()],
        in_specs=[anywhere if name in TABLES else in_vmem for name in inputs],
        out_specs=[in_vmem] * len(outputs),
        scratch_shapes=list(scratch.values()),
        compiler_params=pltpu.CompilerParams(
            collective_id=0, has_side_effects=True, vmem_limit_bytes=62 * 2**20
        ),
        name="fused_layer",
    )(*inputs.values())
    return types.SimpleNamespace(**dict(zip(outputs, values)))


def fused_layer(
    n,
    activations,
    cotangent,
    w_in,
    w_out,
    b_in,
    vec_params,
    first_w_in,
    second_w_in,
    first_w_out,
    second_w_out,
    first_b_in,
    second_b_in,
    first_vec,
    second_vec,
):
    got = run_layer(
        n,
        activations.reshape(n.tokens, n.width),
        cotangent.reshape(n.tokens, n.width),
        w_in[0],
        jnp.swapaxes(w_out[0], 0, 1),
        b_in,
        vec_params[0],
    )
    norm_value = got.norm[0, 0]
    factor = clip_limit / jnp.maximum(norm_value, clip_limit)
    grad_w_in = got.g1[None]
    grad_w_out = jnp.swapaxes(got.g2, 0, 1)[None]
    grad_b_in = got.g_small[5:6, : n.bias]
    grad_vec = got.g_small[None, :5, : n.rows]
    upd_w_in = adam_update(
        w_in, factor * grad_w_in, first_w_in, second_w_in, rate_matrix, STEP_COUNT
    )
    upd_w_out = adam_update(
        w_out, factor * grad_w_out, first_w_out, second_w_out, rate_matrix, STEP_COUNT
    )
    upd_b_in = adam_update(
        b_in, factor * grad_b_in, first_b_in, second_b_in, rate_vector, STEP_COUNT
    )
    upd_vec = adam_update(
        vec_params, factor * grad_vec, first_vec, second_vec, rate_vector, STEP_COUNT
    )
    return (
        got.out.reshape(activations.shape),
        got.dx.reshape(activations.shape),
        norm_value,
        *upd_w_in,
        *upd_w_out,
        *upd_b_in,
        *upd_vec,
    )


def local_layer(mesh, activations, cotangent, w_in, *rest):
    seqs, block, width = activations.shape
    n = Sizes(mesh, seqs, block, width, w_in.shape[2])
    if w_in.shape[0] == 1 and n.fits():
        return fused_layer(n, activations, cotangent, w_in, *rest)
    return general_layer(activations, cotangent, w_in, *rest)


BOTH = ("batch", "seq")


def solution(mesh):
    in_specs = (
        P(*BOTH, None),
        P(*BOTH, None),
        P(None, BOTH, None),
        P(None, None, BOTH),
        P(None, BOTH),
        P(None, None, BOTH),
        P(None, BOTH, None),
        P(None, BOTH, None),
        P(None, None, BOTH),
        P(None, None, BOTH),
        P(None, BOTH),
        P(None, BOTH),
        P(None, None, BOTH),
        P(None, None, BOTH),
    )
    out_specs = (
        P(*BOTH, None),
        P(*BOTH, None),
        P(),
        P(None, BOTH, None),
        P(None, BOTH, None),
        P(None, BOTH, None),
        P(None, None, BOTH),
        P(None, None, BOTH),
        P(None, None, BOTH),
        P(None, BOTH),
        P(None, BOTH),
        P(None, BOTH),
        P(None, None, BOTH),
        P(None, None, BOTH),
        P(None, None, BOTH),
    )
    return jax.shard_map(
        functools.partial(local_layer, mesh), mesh=mesh, in_specs=in_specs, out_specs=out_specs, check_vma=False)
```

```python
import functools
import math
import types

import jax
import jax.numpy as jnp
import ml_dtypes
import numpy as np
from jax import lax
from jax.experimental import pallas as pl
from jax.experimental.pallas import tpu as pltpu
from jax.sharding import PartitionSpec as P

STEP_COUNT = 10


beta_first = 0.5
beta_second = 0.5
rate_matrix = 0.03
rate_vector = 0.2
weight_decay = 0.01
adam_epsilon = 1e-08
norm_epsilon = 1e-06
clip_limit = 1.0


def dft_tables(row_index, column_index, seq_len):
    product = row_index[:, None] * column_index[None, :] % seq_len
    angle = product.astype(jnp.float32) * (2.0 * math.pi / seq_len)
    return (jnp.cos(angle).astype(jnp.bfloat16), jnp.sin(angle).astype(jnp.bfloat16))


def layer_norm(values, gain, shift):
    centre = jnp.mean(values, axis=-1, keepdims=True)
    centred = values - centre
    spread = jnp.mean(centred * centred, axis=-1, keepdims=True)
    return centred * lax.rsqrt(spread + norm_epsilon) * gain + shift


def gelu_tanh(values):
    return jax.nn.gelu(values, approximate=True)


def adam_update(weight, gradient, first, second, rate, step_count):
    first_new = beta_first * first + (1.0 - beta_first) * gradient
    second_new = beta_second * second + (1.0 - beta_second) * gradient * gradient
    first_hat = first_new / (1.0 - beta_first**step_count)
    second_hat = second_new / (1.0 - beta_second**step_count)
    updated = weight - rate * (
        first_hat / (jnp.sqrt(second_hat) + adam_epsilon) + weight_decay * weight
    )
    return (first_new, second_new, updated)


def general_layer(
    activations,
    cotangent,
    w_in,
    w_out,
    b_in,
    vec_params,
    first_w_in,
    second_w_in,
    first_w_out,
    second_w_out,
    first_b_in,
    second_b_in,
    first_vec,
    second_vec,
):
    layers = w_in.shape[0]
    seq_count, block_len, model_width = activations.shape
    seq_devices = lax.axis_size(BOTH[1])
    seq_len = block_len * seq_devices
    dft_scale = 1.0 / math.sqrt(seq_len * model_width)
    first_row = lax.axis_index(BOTH[1]) * block_len
    my_rows = first_row + jnp.arange(block_len, dtype=jnp.int32)
    feature_line = jnp.arange(model_width, dtype=jnp.int32)
    cos_model, sin_model = dft_tables(feature_line, feature_line, model_width)
    table_fwd = jnp.concatenate([cos_model, sin_model], axis=1)
    table_back = jnp.transpose(table_fwd)
    layer_index = 0
    pieces = (
        w_in[layer_index].astype(jnp.bfloat16),
        w_out[layer_index].astype(jnp.bfloat16),
        b_in[layer_index].astype(jnp.bfloat16),
        vec_params[layer_index].astype(jnp.bfloat16),
    )
    gathered = [
        (
            lax.all_gather(pieces[0], BOTH, axis=0, tiled=True),
            lax.all_gather(pieces[1], BOTH, axis=1, tiled=True),
            lax.all_gather(pieces[2], BOTH, axis=0, tiled=True),
            lax.all_gather(pieces[3], BOTH, axis=1, tiled=True),
        )
    ]
    zeros_block = jnp.zeros((seq_count, block_len, model_width), jnp.float32)
    stream = activations.astype(jnp.float32)
    layer_index = 0
    weight_first, weight_second, bias_low, vec_low = gathered[layer_index]
    vec_float = vec_low.astype(jnp.float32)
    bias_float = bias_low.astype(jnp.float32)
    joined = jnp.dot(
        stream.astype(jnp.bfloat16), table_fwd, preferred_element_type=jnp.float32
    ).astype(jnp.bfloat16)
    halves = (joined[..., :model_width], joined[..., model_width:])
    shard_piece = (
        lax.all_gather(halves[0], BOTH[1], axis=1, tiled=True),
        lax.all_gather(halves[1], BOTH[1], axis=1, tiled=True),
    )
    piece_len = shard_piece[0].shape[1]
    cos_block, sin_block = dft_tables(my_rows, jnp.arange(piece_len, dtype=jnp.int32), seq_len)
    running = jnp.einsum(
        "ij,sjd->sid", cos_block, shard_piece[0], preferred_element_type=jnp.float32
    )
    mixed = (
        running
        - jnp.einsum("ij,sjd->sid", sin_block, shard_piece[1], preferred_element_type=jnp.float32)
    ) * dft_scale
    normed, norm_first_back = jax.vjp(layer_norm, stream + mixed, vec_float[0], vec_float[1])
    normed_low = normed.astype(jnp.bfloat16)
    pre_act = jnp.dot(normed_low, weight_first, preferred_element_type=jnp.float32) + bias_float
    activated, gelu_back = jax.vjp(gelu_tanh, pre_act)
    act_low = activated.astype(jnp.bfloat16)
    feed = jnp.dot(act_low, weight_second, preferred_element_type=jnp.float32) + vec_float[2]
    stream, norm_second_back = jax.vjp(layer_norm, normed + feed, vec_float[3], vec_float[4])
    saved = [(norm_first_back, normed_low, gelu_back, act_low, norm_second_back)]
    block_output = stream.astype(jnp.bfloat16)
    grad_now = cotangent.astype(jnp.float32)
    raw_grads = [None] * layers
    for layer_index in reversed(range(layers)):
        weight_first, weight_second, bias_low, vec_low = gathered[layer_index]
        norm_first_back, normed_low, gelu_back, act_low, norm_second_back = saved[layer_index]
        grad_sum2, grad_gain2, grad_shift2 = norm_second_back(grad_now)
        grad_z = grad_sum2.astype(jnp.bfloat16)
        grad_weight_second = jnp.einsum(
            "stf,std->fd", act_low, grad_z, preferred_element_type=jnp.float32
        )
        grad_bias_out = jnp.sum(grad_z.astype(jnp.float32), axis=(0, 1))
        grad_act = jnp.einsum(
            "std,fd->stf", grad_z, weight_second, preferred_element_type=jnp.float32
        )
        (grad_pre,) = gelu_back(grad_act)
        grad_pre_low = grad_pre.astype(jnp.bfloat16)
        grad_weight_first = jnp.einsum(
            "std,stf->df", normed_low, grad_pre_low, preferred_element_type=jnp.float32
        )
        grad_bias_in = jnp.sum(grad_pre_low.astype(jnp.float32), axis=(0, 1))
        grad_normed = (
            jnp.einsum(
                "stf,df->std", grad_pre_low, weight_first, preferred_element_type=jnp.float32
            )
            + grad_sum2
        )
        grad_sum1, grad_gain1, grad_shift1 = norm_first_back(grad_normed)
        grad_mix_low = grad_sum1.astype(jnp.bfloat16)
        add_shard_piece = lax.all_gather(grad_mix_low, BOTH[1], axis=1, tiled=True)
        add_piece_len = add_shard_piece.shape[1]
        add_cos_block, add_sin_block = dft_tables(
            my_rows, jnp.arange(add_piece_len, dtype=jnp.int32), seq_len
        )
        with_cos = jnp.einsum(
            "ij,sjd->sid", add_cos_block, add_shard_piece, preferred_element_type=jnp.float32
        )
        with_sin = (zeros_block, zeros_block)[1] - jnp.einsum(
            "ij,sjd->sid", add_sin_block, add_shard_piece, preferred_element_type=jnp.float32
        )
        with_cos, with_sin = (with_cos, with_sin)
        with_cos = (with_cos * dft_scale).astype(jnp.bfloat16)
        with_sin = (with_sin * dft_scale).astype(jnp.bfloat16)
        grad_halves = jnp.concatenate([with_cos, with_sin], axis=-1)
        grad_now = grad_sum1 + jnp.dot(grad_halves, table_back, preferred_element_type=jnp.float32)
        grad_vec = jnp.stack([grad_gain1, grad_shift1, grad_bias_out, grad_gain2, grad_shift2])
        layer_terms = (grad_weight_first, grad_weight_second, grad_bias_in, grad_vec)
        raw_grads[layer_index] = (
            lax.psum_scatter(layer_terms[0], BOTH, scatter_dimension=0, tiled=True),
            lax.psum_scatter(layer_terms[1], BOTH, scatter_dimension=1, tiled=True),
            lax.psum_scatter(layer_terms[2], BOTH, scatter_dimension=0, tiled=True),
            lax.psum_scatter(layer_terms[3], BOTH, scatter_dimension=1, tiled=True),
        )
    shard_w_in = jnp.stack([entry[0] for entry in raw_grads])
    shard_w_out = jnp.stack([entry[1] for entry in raw_grads])
    shard_b_in = jnp.stack([entry[2] for entry in raw_grads])
    shard_vec = jnp.stack([entry[3] for entry in raw_grads])
    local_squares = jnp.sum(shard_w_in * shard_w_in) + jnp.sum(shard_w_out * shard_w_out)
    local_squares = (
        local_squares + jnp.sum(shard_b_in * shard_b_in) + jnp.sum(shard_vec * shard_vec)
    )
    norm_value = jnp.sqrt(lax.psum(local_squares, BOTH))
    factor = clip_limit / jnp.maximum(norm_value, clip_limit)
    upd_w_in = adam_update(
        w_in, factor * shard_w_in, first_w_in, second_w_in, rate_matrix, STEP_COUNT
    )
    upd_w_out = adam_update(
        w_out, factor * shard_w_out, first_w_out, second_w_out, rate_matrix, STEP_COUNT
    )
    upd_b_in = adam_update(
        b_in, factor * shard_b_in, first_b_in, second_b_in, rate_vector, STEP_COUNT
    )
    upd_vec = adam_update(
        vec_params, factor * shard_vec, first_vec, second_vec, rate_vector, STEP_COUNT
    )
    return (
        block_output,
        grad_now,
        norm_value,
        upd_w_in[0],
        upd_w_in[1],
        upd_w_in[2],
        upd_w_out[0],
        upd_w_out[1],
        upd_w_out[2],
        upd_b_in[0],
        upd_b_in[1],
        upd_b_in[2],
        upd_vec[0],
        upd_vec[1],
        upd_vec[2],
    )


MESH = pl.DeviceIdType.MESH
F32 = jnp.float32
BF16 = jnp.bfloat16
NN = (((1,), (0,)), ((), ()))
NT = (((1,), (1,)), ((), ()))
TN = (((0,), (0,)), ((), ()))


def dot(a, b, dims=NN):
    return lax.dot_general(a, b, dims, preferred_element_type=F32)


class Sizes:
    def __init__(self, mesh, seqs, block, width, hidden):
        self.batch, self.seq = mesh.shape["batch"], mesh.shape["seq"]
        self.xs, self.ys, self.zs = self.batch // 2, 2, self.seq // 2
        self.devices = self.batch * self.seq
        self.seqs, self.block, self.width, self.hidden = seqs, block, width, hidden
        self.length = block * self.seq
        self.rows = width // self.devices
        self.slab = 2 * self.rows
        self.segment = self.zs * self.slab
        self.half = hidden // 2
        self.cols = 512
        self.chunks = self.half // self.cols
        self.parts = 2
        self.thin = self.cols // self.parts
        self.packed = width // self.seq
        self.tokens = seqs * block
        self.bias = hidden // self.devices

    def fits(self):
        return (
            self.batch == 4
            and self.seq % 2 == 0
            and self.width % self.devices == 0
            and self.slab % 16 == 0
            and self.packed % 32 == 0
            and self.block % 128 == 0
            and self.zs == 4
            and self.half % self.cols == 0
            and self.rows <= 128
            and self.bias <= 128
            and 5 * self.rows <= self.width
        )

    def owner(self, x, core, z, y):
        return (2 * x + core) * self.seq + 2 * z + y

    def place_owner(self):
        return [
            self.owner(x, core, z, y)
            for y in range(self.ys)
            for x in range(self.xs)
            for z in range(self.zs)
            for core in range(2)
        ]


def cos_sin(rows, columns, count):
    angle = (rows[:, None] * columns[None, :] % count) * (2.0 * math.pi / count)
    return np.cos(angle), np.sin(angle)


def host_tables(n):
    width, half = n.width, n.packed // 2
    owners = np.array(n.place_owner())
    order = (owners[:, None] * n.rows + np.arange(n.rows)[None, :]).reshape(-1)
    line = np.arange(width)
    cosine, sine = cos_sin(line, line, width)
    pack = np.zeros((width, width))
    unpack = np.zeros((width, width))
    for k in range(width // 2):
        device, inner = divmod(k, half)
        at_cos = device * n.packed + inner
        at_sin = at_cos + half
        pack[at_cos] = cosine[k]
        unpack[at_cos, k] = 1.0
        if k:
            unpack[at_cos, width - k] = 1.0
            pack[at_sin] = sine[k]
            unpack[at_sin, k] = -1.0
            unpack[at_sin, width - k] = 1.0
    pack[half] = cosine[width // 2]
    unpack[half, width // 2] = 1.0
    perm = np.zeros((width, width))
    perm[order, np.arange(width)] = 1.0
    positions = np.arange(n.length)
    by_length = np.stack(cos_sin(positions, positions, n.length))
    vec_mask = np.zeros((n.devices, width))
    vec_mask[np.repeat(owners, n.rows), np.arange(width)] = 1.0
    vec_spread = np.zeros((128, width))
    vec_spread[np.arange(width) % n.rows, np.arange(width)] = 1.0
    bias_spread = np.zeros((128, n.half))
    bias_spread[np.arange(n.half) % n.bias, np.arange(n.half)] = 1.0

    def low(a):
        return jnp.asarray(a.astype(np.float32).astype(ml_dtypes.bfloat16))

    return types.SimpleNamespace(
        tt_f=low(pack),
        by_length=low(by_length),
        un_f=low(unpack[:, order]),
        perm=low(perm),
        tt_b=low(pack[:, order]),
        un_b=low(unpack),
        vec_mask=jnp.asarray(vec_mask.astype(np.float32)),
        vec_spread=low(vec_spread),
        bias_spread=low(bias_spread),
    )


TABLES = ("tt_f", "by_length", "un_f", "perm", "tt_b", "un_b")


FORWARD_TURNS = (0, 1, 1, 1, 0, 1)
BACK_TURNS = (0, 1, 1, 0, 1, 1, 0, 1, 1, 0, 1, 1)


def layer_kernel(n, names, *refs):
    r = types.SimpleNamespace(**dict(zip(names, refs)))
    batch_at, seq_at = lax.axis_index("batch"), lax.axis_index("seq")
    x, core = batch_at // 2, batch_at % 2
    z, y = seq_at // 2, seq_at % 2
    tokens, width, seg, slab = n.tokens, n.width, n.segment, n.slab
    started = []

    def aligned(at, by):
        return pl.multiple_of(at * by, by)

    def rows_of(at, by):
        return pl.ds(aligned(at, by), by)

    def remote(src, dst, send, recv, batch_to, seq_to):
        return pltpu.make_async_remote_copy(
            src_ref=src,
            dst_ref=dst,
            send_sem=send,
            recv_sem=recv,
            device_id=(batch_to, seq_to),
            device_id_type=MESH,
        )

    def go(copy):
        copy.start()
        started.append(copy)
        return copy

    other_core = 2 * x + 1 - core
    other_x = 2 * (1 - x) + core
    other_y = 2 * z + 1 - y

    def plane(k):
        return (seq_at + k) % n.seq

    def plane_from(k):
        return (seq_at + n.seq - k) % n.seq

    def across(k):
        return (batch_at + k) % n.batch

    def across_from(k):
        return (batch_at + n.batch - k) % n.batch

    loads = types.SimpleNamespace()
    for i, name in enumerate(TABLES):
        load = pltpu.make_async_copy(getattr(r, name), getattr(r, name + "_v"), r.load_sem.at[i])
        setattr(loads, name, load)
        load.start()

    barrier = pltpu.get_barrier_semaphore()
    for k in range(1, n.seq):
        pl.semaphore_signal(barrier, inc=1, device_id=(batch_at, plane(k)), device_id_type=MESH)
    for k in range(1, n.batch):
        pl.semaphore_signal(barrier, inc=1, device_id=(across(k), seq_at), device_id_type=MESH)
    pl.semaphore_wait(barrier, n.seq + n.batch - 2)

    weights = (r.w1, r.w2)
    give = pl.ds(aligned(1 - core, n.half), n.half)
    keep = pl.ds(aligned(core, n.half), n.half)
    core_rows = pl.ds(aligned(core, n.rows), n.rows)
    swaps = [
        go(
            remote(
                weights[m].at[:, give],
                r.stage.at[m, core_rows],
                r.swap_send.at[m],
                r.swap_recv.at[m],
                other_core,
                seq_at,
            )
        )
        for m in range(2)
    ]

    def mix_start(t, source, table):
        y_ref, l_ref = r.y_buf.at[t], r.l_buf.at[t]
        y_ref[...] = dot(table[...], source, NT).astype(BF16)
        l_ref[seq_at] = y_ref[rows_of(seq_at, n.packed), :]

    def mix_send(t):
        y_ref, l_ref = r.y_buf.at[t], r.l_buf.at[t]
        for k in range(1, n.seq):
            go(
                remote(
                    y_ref.at[rows_of(plane(k), n.packed)],
                    l_ref.at[seq_at],
                    r.mix_send.at[2 * t, k - 1],
                    r.mix_recv.at[2 * t, k - 1],
                    batch_at,
                    plane(k),
                )
            )

    def mix_turn(t):
        l_ref, z_ref, r_ref = r.l_buf.at[t], r.z_buf.at[t], r.r_buf.at[t]
        for k in range(1, n.seq):
            remote(
                r.y_buf.at[t, rows_of(plane(k), n.packed)],
                l_ref.at[plane_from(k)],
                r.mix_send.at[2 * t, k - 1],
                r.mix_recv.at[2 * t, k - 1],
                batch_at,
                plane(k),
            ).wait_recv()
        left = jnp.concatenate(
            [
                jnp.concatenate(
                    [l_ref[d, :, g * n.block : (g + 1) * n.block] for d in range(n.seq)], axis=1
                )
                for g in range(n.seqs)
            ],
            axis=0,
        )
        r.left[...] = left
        inner = lax.broadcasted_iota(jnp.int32, (n.seqs * n.packed, 1), 0) % n.packed
        first = (inner < n.packed // 2) | ((inner == n.packed // 2) & (seq_at == 0))
        scale = 1.0 / math.sqrt(n.length * n.width)
        for e in range(n.seq):
            at = slice(e * n.block, (e + 1) * n.block)
            by_cos = dot(r.left[...], r.by_length_v[0, :, at])
            by_sin = dot(r.left[...], r.by_length_v[1, :, at])
            z_ref[e] = (jnp.where(first, by_cos, by_sin) * scale).astype(BF16)
        for k in range(1, n.seq):
            go(
                remote(
                    z_ref.at[plane(k)],
                    r_ref.at[seq_at],
                    r.mix_send.at[2 * t + 1, k - 1],
                    r.mix_recv.at[2 * t + 1, k - 1],
                    batch_at,
                    plane(k),
                )
            )
        r_ref[seq_at] = z_ref[seq_at]

    def mix_finish(t, table):
        r_ref = r.r_buf.at[t]
        for k in range(1, n.seq):
            remote(
                r.z_buf.at[t, plane(k)],
                r_ref.at[plane_from(k)],
                r.mix_send.at[2 * t + 1, k - 1],
                r.mix_recv.at[2 * t + 1, k - 1],
                batch_at,
                plane(k),
            ).wait_recv()
        parts = [
            r_ref[:, g * n.packed : (g + 1) * n.packed, :].reshape(width, n.block)
            for g in range(n.seqs)
        ]
        r.mixed[...] = dot(jnp.concatenate(parts, axis=1), table[...], TN)

    loads.tt_f.wait()
    mix_start(0, r.x[...], r.tt_f_v)

    full = r.full
    mate_z = z + 1 - 2 * (z % 2)
    pair_z = z // 2
    inner = (z > 0) & (z < n.zs - 1)

    def line(to_z):
        return batch_at, 2 * to_z + y

    def seg_rows(sx, sy):
        return rows_of(sy * n.xs + sx, seg)

    def pair_rows(sx, sy, sp):
        return rows_of((sy * n.xs + sx) * 2 + sp, 2 * slab)

    def slab_rows(sx, sy, sz):
        return rows_of((sy * n.xs + sx) * n.zs + sz, slab)

    def peer(t):
        return (other_y_at, other_x_at)[t == 0]

    other_x_at = (other_x, seq_at)
    other_y_at = (batch_at, other_y)

    def away(t):
        return (1 - x, y) if t == 0 else (x, 1 - y)

    def turn_of(c):
        return FORWARD_TURNS[c]

    def place(c):
        return c // n.chunks, c % n.chunks

    def stage_weights():
        for m in range(2):
            r.stage[m, core_rows, :] = weights[m][:, keep]
            remote(
                weights[m].at[:, give],
                r.stage.at[m, pl.ds(aligned(1 - core, n.rows), n.rows)],
                r.swap_send.at[m],
                r.swap_recv.at[m],
                other_core,
                seq_at,
            ).wait_recv()
            for q in range(n.chunks):
                full[m, q, slab_rows(x, y, z), :] = r.stage[
                    m, :, q * n.cols : (q + 1) * n.cols
                ].astype(BF16)

    def full_copy(c, at, send, recv, to):
        m, q = place(c)
        return remote(full.at[m, q, at], full.at[m, q, at], send.at[m, q], recv.at[m, q], *to)

    def rows_at(sx, sy, i):
        return (slab_rows(sx, sy, z), slab_rows(sx, sy, mate_z), pair_rows(sx, sy, 1 - pair_z))[i]

    def side_copy(c, i, sx, sy, first):
        t = turn_of(c)
        recv = r.first_recv.at[i] if first else r.second_recv
        return full_copy(c, rows_at(sx, sy, i), r.side_send, recv, peer(t if first else 1 - t))

    def to_sides(c, i):
        side_copy(c, i, x, y, True).start()
        side_copy(c, i, x, y, False).start()

    def own_to_mate(c):
        return full_copy(c, rows_at(x, y, 0), r.mate_send, r.mate_recv, line(mate_z))

    def pair_across(c):
        at = pair_rows(x, y, pair_z)
        return full_copy(c, at, r.across_send, r.pair_recv, line(n.zs - 1 - z))

    def pair_out(c):
        return full_copy(c, rows_at(x, y, 2), r.out_send, r.pair_recv, line(mate_z))

    def own_sides(c):
        to_sides(c, 0)

    def own_line(c):
        own_to_mate(c).start()

    def mate_in(c):
        full_copy(c, rows_at(x, y, 1), r.mate_send, r.mate_recv, line(mate_z)).wait_recv()

        @pl.when(inner)
        def _():
            pair_across(c).start()

        to_sides(c, 1)

    def pair_in(c):
        pair_out(c).wait_recv()

        @pl.when(inner)
        def _():
            pair_out(c).start()

        to_sides(c, 2)

    def pass_on(c, i):
        t = turn_of(c)
        ax, ay = away(t)
        side_copy(c, i, ax, ay, True).wait_recv()
        side_copy(c, i, ax, ay, False).start()

    def slabs_of(c, count, recv):
        return full_copy(c, pl.ds(0, count * slab), r.side_send, recv, other_x_at)

    def weights_here(c):
        slabs_of(c, 2 * n.zs, r.second_recv).wait_recv()

    def small_tiles():
        tile = r.tile
        tile[...] = jnp.zeros(tile.shape, F32)
        for i in range(5):
            tile[i : i + 1, 0 : n.rows] = r.vec[i]
        tile[5:6, 0 : n.bias] = r.bias[...]
        small[batch_at, seq_at] = tile[...]
        for k in range(1, n.seq):
            go(small_copy(k, seq_at))

    def small_copy(k, at):
        return remote(
            r.tile,
            small.at[batch_at, at],
            r.small_send.at[k - 1],
            r.small_recv.at[k - 1],
            batch_at,
            plane(k),
        )

    def row_copy(k, at):
        return remote(
            small.at[batch_at],
            small.at[at],
            r.row_send.at[k - 1],
            r.row_recv.at[k - 1],
            across(k),
            seq_at,
        )

    small = r.small

    def small_rows():
        for k in range(1, n.seq):
            small_copy(k, plane_from(k)).wait_recv()
        for k in range(1, n.batch):
            go(row_copy(k, batch_at))

    half_owners = n.devices // 2
    bias_mask = (
        lax.broadcasted_iota(jnp.int32, (half_owners, n.half), 0)
        == lax.broadcasted_iota(jnp.int32, (half_owners, n.half), 1) // n.bias
    )

    def small_vectors():
        for k in range(1, n.batch):
            row_copy(k, across_from(k)).wait_recv()
        for i in range(5):
            held = small[:, :, i, :].reshape(n.devices, 128).astype(BF16)
            spread = dot(held, r.vec_spread[...]) * r.vec_mask[...]
            r.vecs[i : i + 1, :] = jnp.sum(spread, axis=0, keepdims=True)
        held = small[pl.ds(core * (n.batch // 2), n.batch // 2), :, 5, :]
        held = held.reshape(half_owners, 128).astype(BF16)
        spread = jnp.where(bias_mask, dot(held, r.bias_spread[...]), 0.0)
        biases = jnp.sum(spread, axis=0, keepdims=True)
        for q in range(n.chunks):
            r.biases[q] = biases[:, q * n.cols : (q + 1) * n.cols]

    def place_inputs():
        loads.perm.wait()
        r.x_place[...] = dot(r.x[...], r.perm_v[...])
        r.dy_place[...] = dot(r.dy[...], r.perm_v[...])

    def turn_forward():
        loads.by_length.wait()
        mix_turn(0)

    step = 32
    mine, theirs = pl.ds(0, tokens), pl.ds(tokens, tokens)

    def row_loop(body):
        @pl.loop(0, tokens // step)
        def _(i):
            body(pl.ds(pl.multiple_of(i * step, step), step))

    def mean(v):
        return jnp.mean(v, axis=-1, keepdims=True)

    def first_norm(at):
        v = r.x_place[at, :] + r.mixed[at, :]
        centred = v - mean(v)
        scale = lax.rsqrt(mean(centred * centred) + norm_epsilon)
        unit = centred * scale
        h = unit * r.vecs[0:1, :] + r.vecs[1:2, :]
        r.unit1[at, :] = unit
        r.scale1[at, :] = jnp.broadcast_to(scale, (step, 128))
        r.h[at, :] = h
        r.h_low[at, :] = h.astype(BF16)

    def swap(i, src, dst):
        return remote(src, dst, r.core_send.at[i], r.core_recv.at[i], other_core, seq_at)

    def swap_h():
        return swap(0, r.h_low.at[mine], r.h_low.at[theirs])

    def norm_forward():
        loads.un_f.wait()
        mix_finish(0, r.un_f_v)
        row_loop(first_norm)
        go(swap_h())

    root = math.sqrt(2.0 / math.pi)

    lifted_parts = []

    def lift(q):
        if not lifted_parts:
            swap_h().wait_recv()
        lifted_parts.append(q)
        weights_here(q)
        r.lift[...] = dot(r.h_low[...], full[0, q]) + r.biases[q]

        @pl.loop(0, 2 * tokens // step)
        def _(i):
            at = pl.ds(pl.multiple_of(i * step, step), step)
            u = r.lift[at, :]
            square = u * u
            bent = jnp.tanh(u * (root + (root * 0.044715) * square))
            half_up = 0.5 + 0.5 * bent
            r.act[q, at, :] = (u * half_up).astype(BF16)
            r.slope[q, at, :] = half_up + (u * (1.0 - bent * bent)) * (
                0.5 * root + (1.5 * root * 0.044715) * square
            )

    gathered_parts = []

    def drop(q):
        weights_here(n.chunks + q)
        part = dot(r.act[q], full[1, q], NT)
        r.total[...] = r.total[...] + part if gathered_parts else part
        gathered_parts.append(q)

    def send_forward():
        mix_send(0)

    forward_steps = (
        (stage_weights,), (own_line, 1), (small_tiles,), (own_sides, 5), (own_line, 2),
        (own_line, 4), (own_sides, 2), (own_sides, 1), (own_line, 3), (own_line, 0),
        (mate_in, 1), (own_line, 5), (pass_on, 5, 0), (own_sides, 0), (mate_in, 2),
        (own_sides, 4), (pass_on, 2, 0), (pass_on, 1, 0), (mate_in, 4), (mate_in, 0),
        (send_forward,), (own_sides, 3), (pair_in, 1), (pair_in, 2), (mate_in, 3),
        (small_rows,), (pass_on, 4, 1), (pair_in, 0), (pair_in, 3), (mate_in, 5),
        (turn_forward,), (pass_on, 2, 2), (pass_on, 1, 1), (pass_on, 0, 1), (pass_on, 0, 2),
        (pass_on, 0, 0), (pass_on, 3, 1), (pass_on, 1, 2), (pair_in, 5), (small_vectors,),
        (pair_in, 4), (pass_on, 5, 1), (place_inputs,), (pass_on, 4, 0), (pass_on, 2, 1),
        (norm_forward,), (pass_on, 5, 2), (pass_on, 3, 2), (pass_on, 4, 2), (lift, 0),
        (pass_on, 3, 0), (lift, 1), (lift, 2), (drop, 2), (drop, 1), (drop, 0),
    )
    for task, *which in forward_steps:
        task(*which)
    r.part_low[...] = r.total[theirs, :].astype(BF16)
    swap_ff = go(swap(1, r.part_low, r.part_in))
    swap_ff.wait_recv()

    r.sums[...] = jnp.zeros(r.sums.shape, F32)

    def fold(v):
        return jnp.sum(v.reshape(step // 8, 8, width), axis=0)

    def second_norm(at):
        v = (
            r.h[at, :]
            + r.total[at, :]
            + r.part_in[at, :].astype(F32)
            + r.vecs[2:3, :]
        )
        centred = v - mean(v)
        scale = lax.rsqrt(mean(centred * centred) + norm_epsilon)
        unit = centred * scale
        gain = r.vecs[3:4, :]
        r.out_low[at, :] = (unit * gain + r.vecs[4:5, :]).astype(BF16)
        dy = r.dy_place[at, :]
        r.sums[3] += fold(dy * unit)
        r.sums[4] += fold(dy)
        du = dy * gain
        dv = scale * (du - mean(du) - unit * mean(du * unit))
        r.dr2[at, :] = dv
        low = dv.astype(BF16)
        r.dz[at, :] = low
        r.sums[2] += fold(low.astype(F32))

    row_loop(second_norm)
    swap_dz = go(swap(2, r.dz.at[mine], r.dz.at[theirs]))
    r.h_turned[...] = jnp.transpose(r.h_low[...])
    swap_dz.wait_recv()
    r.dz_turned[...] = jnp.transpose(r.dz[...])

    acc, out_low = r.acc, r.give

    def wide(c):
        m, q = c // (n.chunks * n.parts), c % (n.chunks * n.parts)
        return 1 - m, q // n.parts, pl.ds((q % n.parts) * n.thin, n.thin)

    def grad_copy(c, at, into, i, to):
        return remote(
            out_low.at[c, at],
            into.at[c],
            r.grad_send.at[i, c],
            r.grad_recv.at[i, c],
            *to,
        )

    def back_turn(c):
        return BACK_TURNS[c]

    def copy_diagonal(c):
        return grad_copy(c, seg_rows(1 - x, 1 - y), r.in_diagonal, 0, peer(1 - back_turn(c)))

    def copy_near(c):
        t = 1 - back_turn(c)
        return grad_copy(c, seg_rows(*away(t)), r.in_near, 1, peer(t))

    def copy_side(c):
        t = back_turn(c)
        return grad_copy(c, seg_rows(*away(t)), r.in_side, 2, peer(t))

    def copy_mate(c):
        return grad_copy(c, slab_rows(x, y, mate_z), r.in_mate, 3, line(mate_z))

    def copy_pair_in(c):
        return grad_copy(c, pair_rows(x, y, 1 - pair_z), r.in_pair, 4, line(mate_z))

    def copy_pair_across(c):
        return grad_copy(c, pair_rows(x, y, 1 - pair_z), r.in_across, 5, line(n.zs - 1 - z))

    def round_out(c, at, *more):
        value = acc[c, at, :]
        for ref in more:
            value = value + ref[c].astype(F32)
        out_low[c, at, :] = value.astype(BF16)

    def grad_product(c):
        m, q, at = wide(c)
        if m:
            acc[c] = dot(r.dz_turned[...], r.act[q, :, at])
        else:
            acc[c] = dot(r.h_turned[...], r.dpre[q, :, at])
        round_out(c, seg_rows(1 - x, 1 - y))
        copy_diagonal(c).start()
        round_out(c, seg_rows(*away(1 - back_turn(c))))
        copy_near(c).start()

    def grad_side(c):
        copy_diagonal(c).wait_recv()
        round_out(c, seg_rows(*away(back_turn(c))), r.in_diagonal)
        copy_side(c).start()

    def grad_line(c):
        copy_near(c).wait_recv()
        copy_side(c).wait_recv()
        at = seg_rows(x, y)
        acc[c, at, :] = acc[c, at, :] + (r.in_near[c].astype(F32) + r.in_side[c].astype(F32))

        @pl.when(jnp.logical_not(inner))
        def _():
            round_out(c, pair_rows(x, y, 1 - pair_z))
            copy_pair_in(c).start()
            round_out(c, slab_rows(x, y, mate_z))
            copy_mate(c).start()

    def grad_across(c):
        @pl.when(inner)
        def _():
            copy_pair_in(c).wait_recv()
            round_out(c, pair_rows(x, y, 1 - pair_z), r.in_pair)
            copy_pair_across(c).start()

    def grad_out(c):
        @pl.when(inner)
        def _():
            copy_pair_across(c).wait_recv()
            at = pair_rows(x, y, pair_z)
            acc[c, at, :] = acc[c, at, :] + r.in_across[c].astype(F32)
            round_out(c, slab_rows(x, y, mate_z))
            copy_mate(c).start()

    def grad_end(c):
        m, q, at = wide(c)
        copy_mate(c).wait_recv()
        r.final[m, q, :, at] = acc[c, slab_rows(x, y, z), :] + r.in_mate[c].astype(F32)

    back_parts = []

    def slope_back(q):
        r.lift[...] = dot(r.dz[...], full[1, q])
        r.bias_sum[q] = jnp.zeros((8, n.cols), F32)

        @pl.loop(0, 2 * tokens // step)
        def _(i):
            at = pl.ds(pl.multiple_of(i * step, step), step)
            low = (r.lift[at, :] * r.slope[q, at, :]).astype(BF16)
            r.dpre[q, at, :] = low
            r.bias_sum[q] += jnp.sum(low.astype(F32).reshape(step // 8, 8, n.cols), axis=0)

        part = dot(r.dpre[q], full[0, q], NT)
        r.total[...] = r.total[...] + part if back_parts else part
        back_parts.append(q)

    def swap_dh():
        return swap(3, r.part_low2, r.part_in2)

    def send_dh():
        r.part_low2[...] = r.total[theirs, :].astype(BF16)
        go(swap_dh())

    def first_norm_back(at):
        dh = r.total[at, :] + r.part_in2[at, :].astype(F32) + r.dr2[at, :]
        unit = r.unit1[at, :]
        r.sums[0] += fold(dh * unit)
        r.sums[1] += fold(dh)
        du = dh * r.vecs[0:1, :]
        dv = r.scale1[at, 0:1] * (du - mean(du) - unit * mean(du * unit))
        low = dv.astype(BF16)
        r.dm[at, :] = low
        r.rest[at, :] = (dv - low.astype(F32)).astype(BF16)

    def norm_back():
        swap_dh().wait_recv()
        row_loop(first_norm_back)
        loads.tt_b.wait()
        mix_start(1, r.dm[...], r.tt_b_v)
        mix_send(1)

    def thirds(v):
        high = v.astype(BF16)
        left = v - high.astype(F32)
        mid = left.astype(BF16)
        return high, mid, (left - mid.astype(F32)).astype(BF16)

    def small_gather(v, spread):
        return sum(dot(part, spread, NT) for part in thirds(v))

    def row_sums(k):
        return remote(
            r.small_out.at[across(k)],
            r.small_in.at[k - 1],
            r.row_send2.at[k - 1],
            r.row_recv2.at[k - 1],
            across(k),
            seq_at,
        )

    def tile_sums(k):
        return remote(
            r.small_mid.at[plane(k)],
            r.small_last.at[k - 1],
            r.small_send2.at[k - 1],
            r.small_recv2.at[k - 1],
            batch_at,
            plane(k),
        )

    def small_grads():
        for i in range(5):
            line_sum = jnp.sum(r.sums[i], axis=0, keepdims=True)
            tiles = small_gather(line_sum * r.vec_mask[...], r.vec_spread[...])
            r.small_out[:, :, i, :] = tiles.reshape(n.batch, n.seq, 128)
        line_sum = jnp.concatenate(
            [jnp.sum(r.bias_sum[q], axis=0, keepdims=True) for q in range(n.chunks)], axis=1
        )
        tiles = small_gather(jnp.where(bias_mask, line_sum, 0.0), r.bias_spread[...])
        r.small_out[:, :, 5:8, :] = jnp.zeros((n.batch, n.seq, 3, 128), F32)
        r.small_out[pl.ds(core * (n.batch // 2), n.batch // 2), :, 5, :] = tiles.reshape(
            n.batch // 2, n.seq, 128
        )
        for k in range(1, n.batch):
            go(row_sums(k))

    def small_rows_back():
        value = r.small_out[batch_at]
        for k in range(1, n.batch):
            row_sums(k).wait_recv()
            value = value + r.small_in[k - 1]
        r.small_mid[...] = value
        for k in range(1, n.seq):
            go(tile_sums(k))

    def small_end():
        value = r.small_mid[seq_at]
        for k in range(1, n.seq):
            tile_sums(k).wait_recv()
            value = value + r.small_last[k - 1]
        r.g_small[...] = value

    def turn_back():
        mix_turn(1)

    def outputs():
        r.out[...] = dot(r.out_low[...], r.perm_v[...], NT).astype(BF16)
        r.dx[...] = dot(r.dm[...], r.perm_v[...], NT) + dot(r.rest[...], r.perm_v[...], NT)

    def mix_back():
        loads.un_b.wait()
        mix_finish(1, r.un_b_v)
        r.dx[...] = r.dx[...] + r.mixed[...]

    for task, *which in (
        (grad_product, 0), (grad_product, 2), (grad_product, 1), (slope_back, 1),
        (grad_side, 2), (slope_back, 2), (grad_product, 9), (slope_back, 0), (grad_side, 1),
        (send_dh,), (grad_line, 2), (grad_product, 4), (norm_back,), (grad_side, 9),
        (grad_side, 0), (grad_product, 10), (grad_side, 4), (grad_product, 3),
        (grad_product, 5), (grad_side, 10), (grad_line, 4), (grad_product, 7), (grad_across, 2),
        (grad_line, 0), (grad_across, 0), (grad_side, 3), (grad_product, 6), (grad_out, 2),
        (grad_across, 4), (grad_line, 1), (grad_across, 1), (grad_product, 8), (turn_back,),
        (grad_side, 5), (grad_out, 1), (grad_line, 10), (grad_product, 11), (grad_out, 4),
        (grad_side, 7), (grad_line, 3), (grad_end, 2), (grad_across, 3), (outputs,),
        (grad_end, 1), (grad_side, 8), (grad_across, 10), (grad_out, 0), (grad_line, 5),
        (mix_back,), (grad_line, 9), (grad_side, 11), (grad_across, 9), (grad_line, 7),
        (grad_side, 6), (grad_across, 5), (grad_end, 4), (grad_out, 10), (small_grads,),
        (grad_line, 8), (grad_across, 7), (grad_line, 11), (grad_out, 9), (grad_out, 5),
        (grad_across, 8), (grad_across, 11), (grad_line, 6), (grad_out, 3), (grad_end, 3),
        (grad_end, 0), (grad_across, 6), (grad_end, 5), (grad_out, 8), (small_rows_back,),
        (grad_end, 9), (grad_end, 10), (grad_out, 11), (grad_out, 7), (grad_end, 8),
        (grad_end, 7), (grad_out, 6), (grad_end, 11), (small_end,), (grad_end, 6),
    ):
        task(*which)

    grads = (r.g1, r.g2)
    for m in range(2):
        r.final_turn[m] = jnp.concatenate([r.final[m, q] for q in range(n.chunks)], axis=1)
    their_rows = pl.ds(aligned(1 - core, n.rows), n.rows)
    back = [
        go(
            remote(
                r.final_turn.at[m, their_rows],
                r.final_in.at[m],
                r.back_send.at[m],
                r.back_recv.at[m],
                other_core,
                seq_at,
            )
        )
        for m in range(2)
    ]
    squares = jnp.zeros((8, 128), F32)

    def squares_of(v):
        v = v * v
        v = jnp.sum(v.reshape(v.shape[0] // 8, 8, v.shape[1]), axis=0)
        return sum(v[:, i : i + 128] for i in range(0, v.shape[1], 128))

    squares = squares + r.g_small[...] * r.g_small[...]
    for m in range(2):
        grads[m][:, keep] = r.final_turn[m, core_rows, :]
        back[m].wait_recv()
        grads[m][:, give] = r.final_in[m]
        squares = squares + squares_of(grads[m][...])
    r.norm_own[...] = squares
    r.norm_plane[seq_at] = squares
    for k in range(1, n.seq):
        go(
            remote(
                r.norm_own,
                r.norm_plane.at[seq_at],
                r.norm_send.at[k - 1],
                r.norm_recv.at[k - 1],
                batch_at,
                plane(k),
            )
        )
    for k in range(1, n.seq):
        remote(
            r.norm_own,
            r.norm_plane.at[plane_from(k)],
            r.norm_send.at[k - 1],
            r.norm_recv.at[k - 1],
            batch_at,
            plane(k),
        ).wait_recv()
    squares = r.norm_plane[0]
    for k in range(1, n.seq):
        squares = squares + r.norm_plane[k]
    r.norm_sum[...] = squares
    r.norm_all[batch_at] = squares
    for k in range(1, n.batch):
        go(
            remote(
                r.norm_sum,
                r.norm_all.at[batch_at],
                r.norm_send2.at[k - 1],
                r.norm_recv2.at[k - 1],
                across(k),
                seq_at,
            )
        )
    for k in range(1, n.batch):
        remote(
            r.norm_sum,
            r.norm_all.at[across_from(k)],
            r.norm_send2.at[k - 1],
            r.norm_recv2.at[k - 1],
            across(k),
            seq_at,
        ).wait_recv()
    squares = r.norm_all[0]
    for k in range(1, n.batch):
        squares = squares + r.norm_all[k]
    whole = jnp.sum(jnp.sum(squares, axis=1, keepdims=True), axis=0, keepdims=True)
    r.norm[...] = jnp.broadcast_to(jnp.sqrt(whole), (8, 128))

    for copy in started:
        copy.wait_send()

    for c in range(2 * n.chunks):
        own_to_mate(c).wait_send()
        slabs_of(c, 3 * n.zs, r.second_recv).wait_send()

    for c in range(2 * n.chunks * n.parts):
        for copy in (copy_diagonal(c), copy_near(c), copy_side(c), copy_mate(c)):
            copy.wait_send()

    @pl.when(inner)
    def _():
        for c in range(2 * n.chunks):
            pair_across(c).wait_send()
            pair_out(c).wait_send()
        for c in range(2 * n.chunks * n.parts):
            copy_pair_across(c).wait_send()

    @pl.when(jnp.logical_not(inner))
    def _():
        for c in range(2 * n.chunks * n.parts):
            copy_pair_in(c).wait_send()


def run_layer(n, x, dy, w1, w2, bias, vec):
    tables = host_tables(n)
    tokens, width, cols, q = n.tokens, n.width, n.cols, n.chunks
    grads = 2 * q * n.parts
    dma = pltpu.SemaphoreType.DMA
    vmem = pltpu.VMEM
    inputs = dict(
        x=x,
        dy=dy,
        w1=w1,
        w2=w2,
        bias=bias,
        vec=vec,
        vec_mask=tables.vec_mask,
        vec_spread=tables.vec_spread,
        bias_spread=tables.bias_spread,
    )
    inputs.update({name: getattr(tables, name) for name in TABLES})
    outputs = dict(
        out=((tokens, width), BF16),
        dx=((tokens, width), F32),
        g1=((n.rows, n.hidden), F32),
        g2=((n.rows, n.hidden), F32),
        g_small=((8, 128), F32),
        norm=((8, 128), F32),
    )
    scratch = {name + "_v": vmem(getattr(tables, name).shape, BF16) for name in TABLES}
    scratch.update(
        load_sem=dma((len(TABLES),)),
        stage=vmem((2, n.slab, n.half), F32),
        swap_send=dma((2,)),
        swap_recv=dma((2,)),
        tile=vmem((8, 128), F32),
        small=vmem((n.batch, n.seq, 8, 128), F32),
        small_send=dma((n.seq - 1,)),
        small_recv=dma((n.seq - 1,)),
        row_send=dma((n.batch - 1,)),
        row_recv=dma((n.batch - 1,)),
        y_buf=vmem((2, width, tokens), BF16),
        l_buf=vmem((2, n.seq, n.packed, tokens), BF16),
        left=vmem((n.seqs * n.packed, n.length), BF16),
        z_buf=vmem((2, n.seq, n.seqs * n.packed, n.block), BF16),
        r_buf=vmem((2, n.seq, n.seqs * n.packed, n.block), BF16),
        mix_send=dma((4, n.seq - 1)),
        mix_recv=dma((4, n.seq - 1)),
        mixed=vmem((tokens, width), F32),
        full=vmem((2, q, width, cols), BF16),
        mate_send=dma((2, q)),
        mate_recv=dma((2, q)),
        across_send=dma((2, q)),
        out_send=dma((2, q)),
        pair_recv=dma((2, q)),
        side_send=dma((2, q)),
        first_recv=dma((3, 2, q)),
        second_recv=dma((2, q)),
        x_place=vmem((tokens, width), F32),
        dy_place=vmem((tokens, width), F32),
        vecs=vmem((8, width), F32),
        biases=vmem((q, 1, cols), F32),
        unit1=vmem((tokens, width), F32),
        scale1=vmem((tokens, 128), F32),
        h=vmem((tokens, width), F32),
        h_low=vmem((2 * tokens, width), BF16),
        core_send=dma((4,)),
        core_recv=dma((4,)),
        total=vmem((2 * tokens, width), F32),
        act=vmem((q, 2 * tokens, cols), BF16),
        lift=vmem((2 * tokens, cols), F32),
        slope=vmem((q, 2 * tokens, cols), F32),
        part_low=vmem((tokens, width), BF16),
        part_low2=vmem((tokens, width), BF16),
        part_in=vmem((tokens, width), BF16),
        part_in2=vmem((tokens, width), BF16),
        sums=vmem((5, 8, width), F32),
        out_low=vmem((tokens, width), BF16),
        dr2=vmem((tokens, width), F32),
        dz=vmem((2 * tokens, width), BF16),
        h_turned=vmem((width, 2 * tokens), BF16),
        dz_turned=vmem((width, 2 * tokens), BF16),
        acc=vmem((grads, width, n.thin), F32),
        give=vmem((grads, width, n.thin), BF16),
        in_diagonal=vmem((grads, n.segment, n.thin), BF16),
        in_near=vmem((grads, n.segment, n.thin), BF16),
        in_side=vmem((grads, n.segment, n.thin), BF16),
        in_mate=vmem((grads, n.slab, n.thin), BF16),
        in_pair=vmem((grads, 2 * n.slab, n.thin), BF16),
        in_across=vmem((grads, 2 * n.slab, n.thin), BF16),
        grad_send=dma((6, grads)),
        grad_recv=dma((6, grads)),
        bias_sum=vmem((q, 8, cols), F32),
        dpre=vmem((q, 2 * tokens, cols), BF16),
        dm=vmem((tokens, width), BF16),
        rest=vmem((tokens, width), BF16),
        small_out=vmem((n.batch, n.seq, 8, 128), F32),
        small_in=vmem((n.batch - 1, n.seq, 8, 128), F32),
        row_send2=dma((n.batch - 1,)),
        row_recv2=dma((n.batch - 1,)),
        small_mid=vmem((n.seq, 8, 128), F32),
        small_last=vmem((n.seq - 1, 8, 128), F32),
        small_send2=dma((n.seq - 1,)),
        small_recv2=dma((n.seq - 1,)),
        final=vmem((2, q, n.slab, cols), F32),
        final_turn=vmem((2, n.slab, n.half), F32),
        final_in=vmem((2, n.rows, n.half), F32),
        back_send=dma((2,)),
        back_recv=dma((2,)),
        norm_own=vmem((8, 128), F32),
        norm_plane=vmem((n.seq, 8, 128), F32),
        norm_sum=vmem((8, 128), F32),
        norm_all=vmem((n.batch, 8, 128), F32),
        norm_send=dma((n.seq - 1,)),
        norm_recv=dma((n.seq - 1,)),
        norm_send2=dma((n.batch - 1,)),
        norm_recv2=dma((n.batch - 1,)),
    )
    names = tuple(inputs) + tuple(outputs) + tuple(scratch)
    in_vmem = pl.BlockSpec(memory_space=pltpu.VMEM)
    anywhere = pl.BlockSpec(memory_space=pl.ANY)
    values = pl.pallas_call(
        functools.partial(layer_kernel, n, names),
        out_shape=[jax.ShapeDtypeStruct(*shape) for shape in outputs.values()],
        in_specs=[anywhere if name in TABLES else in_vmem for name in inputs],
        out_specs=[in_vmem] * len(outputs),
        scratch_shapes=list(scratch.values()),
        compiler_params=pltpu.CompilerParams(
            collective_id=0, has_side_effects=True, vmem_limit_bytes=62 * 2**20
        ),
        name="fused_layer",
    )(*inputs.values())
    return types.SimpleNamespace(**dict(zip(outputs, values)))


def adam_kernel(n, names, *refs):
    r = types.SimpleNamespace(**dict(zip(names, refs)))
    passed = [
        pltpu.make_async_copy(r.out, r.out_there, r.sem.at[0]),
        pltpu.make_async_copy(r.dx, r.dx_there, r.sem.at[1]),
    ]
    for copy in passed:
        copy.start()
    norm_value = r.norm[0:1, 0:1]
    r.norm_out[...] = norm_value
    factor = clip_limit / jnp.maximum(norm_value, clip_limit)
    lanes = n.cols

    def update(gradient, given, made, at, rate):
        weight, first, second = (ref[at] for ref in given)
        new = adam_update(weight, factor * gradient, first, second, rate, STEP_COUNT)
        for ref, value in zip(made, new):
            ref[at] = value

    weight_in, weight_out = refs[4:7], refs[7:10]
    made_in, made_out = refs[19:22], refs[22:25]

    @pl.loop(0, n.hidden // lanes)
    def _(i):
        at = (slice(None), pl.ds(pl.multiple_of(i * lanes, lanes), lanes))
        update(r.g1[at], weight_in, made_in, at, rate_matrix)
        update(r.g2[at], weight_out, made_out, at, rate_matrix)

    update(r.g_small[5:6, 0 : n.bias], refs[10:13], refs[25:28], ..., rate_vector)
    for i in range(5):
        update(r.g_small[i : i + 1, 0 : n.rows], refs[13:16], refs[28:31], i, rate_vector)
    for copy in passed:
        copy.wait()


def run_adam(n, got, given):
    f32 = functools.partial(jax.ShapeDtypeStruct, dtype=F32)
    matrix, bias, vec = f32((n.rows, n.hidden)), f32((1, n.bias)), f32((5, 1, n.rows))
    inputs = dict(g1=got.g1, g2=got.g2, g_small=got.g_small, norm=got.norm)
    inputs.update({chr(97 + i): array for i, array in enumerate(given)})
    inputs.update(out=got.out, dx=got.dx)
    outputs = dict(norm_out=f32((1, 1)))
    outputs.update({chr(110 + i): matrix for i in range(6)})
    outputs.update({chr(65 + i): bias for i in range(3)})
    outputs.update({chr(70 + i): vec for i in range(3)})
    outputs.update(
        out_there=jax.ShapeDtypeStruct(got.out.shape, BF16),
        dx_there=jax.ShapeDtypeStruct(got.dx.shape, F32),
    )
    names = tuple(inputs) + tuple(outputs) + ("sem",)
    in_vmem = pl.BlockSpec(memory_space=pltpu.VMEM)
    anywhere = pl.BlockSpec(memory_space=pl.ANY)
    return pl.pallas_call(
        functools.partial(adam_kernel, n, names),
        out_shape=list(outputs.values()),
        in_specs=[in_vmem] * (len(inputs) - 2) + [anywhere] * 2,
        out_specs=[in_vmem] * (len(outputs) - 2) + [anywhere] * 2,
        scratch_shapes=[pltpu.SemaphoreType.DMA((2,))],
        compiler_params=pltpu.CompilerParams(vmem_limit_bytes=32 * 2**20),
        name="adam",
    )(*inputs.values())


def turned(a):
    return jnp.swapaxes(a[0], 0, 1)


def lined(a):
    return jnp.transpose(a, (1, 0, 2))


def fused_layer(
    n,
    activations,
    cotangent,
    w_in,
    w_out,
    b_in,
    vec_params,
    first_w_in,
    second_w_in,
    first_w_out,
    second_w_out,
    first_b_in,
    second_b_in,
    first_vec,
    second_vec,
):
    got = run_layer(
        n,
        activations.reshape(n.tokens, n.width),
        cotangent.reshape(n.tokens, n.width),
        w_in[0],
        turned(w_out),
        b_in,
        lined(vec_params),
    )
    given = (
        *(a[0] for a in (w_in, first_w_in, second_w_in)),
        *(turned(a) for a in (w_out, first_w_out, second_w_out)),
        *(b_in, first_b_in, second_b_in),
        *(lined(a) for a in (vec_params, first_vec, second_vec)),
    )
    norm_value, *made, out, dx = run_adam(n, got, given)
    return (
        out.reshape(activations.shape),
        dx.reshape(activations.shape),
        norm_value.reshape(()),
        *(a[None] for a in made[:3]),
        *(jnp.swapaxes(a, 0, 1)[None] for a in made[3:6]),
        *made[6:9],
        *(lined(a) for a in made[9:]),
    )


def local_layer(mesh, activations, cotangent, w_in, *rest):
    seqs, block, width = activations.shape
    n = Sizes(mesh, seqs, block, width, w_in.shape[2])
    if w_in.shape[0] == 1 and n.fits():
        return fused_layer(n, activations, cotangent, w_in, *rest)
    return general_layer(activations, cotangent, w_in, *rest)


BOTH = ("batch", "seq")


def solution(mesh):
    in_specs = (
        P(*BOTH, None),
        P(*BOTH, None),
        P(None, BOTH, None),
        P(None, None, BOTH),
        P(None, BOTH),
        P(None, None, BOTH),
        P(None, BOTH, None),
        P(None, BOTH, None),
        P(None, None, BOTH),
        P(None, None, BOTH),
        P(None, BOTH),
        P(None, BOTH),
        P(None, None, BOTH),
        P(None, None, BOTH),
    )
    out_specs = (
        P(*BOTH, None),
        P(*BOTH, None),
        P(),
        P(None, BOTH, None),
        P(None, BOTH, None),
        P(None, BOTH, None),
        P(None, None, BOTH),
        P(None, None, BOTH),
        P(None, None, BOTH),
        P(None, BOTH),
        P(None, BOTH),
        P(None, BOTH),
        P(None, None, BOTH),
        P(None, None, BOTH),
        P(None, None, BOTH),
    )
    return jax.shard_map(
        functools.partial(local_layer, mesh), mesh=mesh, in_specs=in_specs, out_specs=out_specs, check_vma=False)
```

```python
import functools
import math
import types

import jax
import jax.numpy as jnp
import ml_dtypes
import numpy as np
from jax import lax
from jax.experimental import pallas as pl
from jax.experimental.pallas import tpu as pltpu
from jax.sharding import PartitionSpec as P

STEP_COUNT = 10


beta_first = 0.5
beta_second = 0.5
rate_matrix = 0.03
rate_vector = 0.2
weight_decay = 0.01
adam_epsilon = 1e-08
norm_epsilon = 1e-06
clip_limit = 1.0


def dft_tables(row_index, column_index, seq_len):
    product = row_index[:, None] * column_index[None, :] % seq_len
    angle = product.astype(jnp.float32) * (2.0 * math.pi / seq_len)
    return (jnp.cos(angle).astype(jnp.bfloat16), jnp.sin(angle).astype(jnp.bfloat16))


def layer_norm(values, gain, shift):
    centre = jnp.mean(values, axis=-1, keepdims=True)
    centred = values - centre
    spread = jnp.mean(centred * centred, axis=-1, keepdims=True)
    return centred * lax.rsqrt(spread + norm_epsilon) * gain + shift


def gelu_tanh(values):
    return jax.nn.gelu(values, approximate=True)


def adam_update(weight, gradient, first, second, rate, step_count):
    first_new = beta_first * first + (1.0 - beta_first) * gradient
    second_new = beta_second * second + (1.0 - beta_second) * gradient * gradient
    first_hat = first_new / (1.0 - beta_first**step_count)
    second_hat = second_new / (1.0 - beta_second**step_count)
    updated = weight - rate * (
        first_hat / (jnp.sqrt(second_hat) + adam_epsilon) + weight_decay * weight
    )
    return (first_new, second_new, updated)


def general_layer(
    activations,
    cotangent,
    w_in,
    w_out,
    b_in,
    vec_params,
    first_w_in,
    second_w_in,
    first_w_out,
    second_w_out,
    first_b_in,
    second_b_in,
    first_vec,
    second_vec,
):
    layers = w_in.shape[0]
    seq_count, block_len, model_width = activations.shape
    seq_devices = lax.axis_size(BOTH[1])
    seq_len = block_len * seq_devices
    dft_scale = 1.0 / math.sqrt(seq_len * model_width)
    first_row = lax.axis_index(BOTH[1]) * block_len
    my_rows = first_row + jnp.arange(block_len, dtype=jnp.int32)
    feature_line = jnp.arange(model_width, dtype=jnp.int32)
    cos_model, sin_model = dft_tables(feature_line, feature_line, model_width)
    table_fwd = jnp.concatenate([cos_model, sin_model], axis=1)
    table_back = jnp.transpose(table_fwd)
    layer_index = 0
    pieces = (
        w_in[layer_index].astype(jnp.bfloat16),
        w_out[layer_index].astype(jnp.bfloat16),
        b_in[layer_index].astype(jnp.bfloat16),
        vec_params[layer_index].astype(jnp.bfloat16),
    )
    gathered = [
        (
            lax.all_gather(pieces[0], BOTH, axis=0, tiled=True),
            lax.all_gather(pieces[1], BOTH, axis=1, tiled=True),
            lax.all_gather(pieces[2], BOTH, axis=0, tiled=True),
            lax.all_gather(pieces[3], BOTH, axis=1, tiled=True),
        )
    ]
    zeros_block = jnp.zeros((seq_count, block_len, model_width), jnp.float32)
    stream = activations.astype(jnp.float32)
    layer_index = 0
    weight_first, weight_second, bias_low, vec_low = gathered[layer_index]
    vec_float = vec_low.astype(jnp.float32)
    bias_float = bias_low.astype(jnp.float32)
    joined = jnp.dot(
        stream.astype(jnp.bfloat16), table_fwd, preferred_element_type=jnp.float32
    ).astype(jnp.bfloat16)
    halves = (joined[..., :model_width], joined[..., model_width:])
    shard_piece = (
        lax.all_gather(halves[0], BOTH[1], axis=1, tiled=True),
        lax.all_gather(halves[1], BOTH[1], axis=1, tiled=True),
    )
    piece_len = shard_piece[0].shape[1]
    cos_block, sin_block = dft_tables(my_rows, jnp.arange(piece_len, dtype=jnp.int32), seq_len)
    running = jnp.einsum(
        "ij,sjd->sid", cos_block, shard_piece[0], preferred_element_type=jnp.float32
    )
    mixed = (
        running
        - jnp.einsum("ij,sjd->sid", sin_block, shard_piece[1], preferred_element_type=jnp.float32)
    ) * dft_scale
    normed, norm_first_back = jax.vjp(layer_norm, stream + mixed, vec_float[0], vec_float[1])
    normed_low = normed.astype(jnp.bfloat16)
    pre_act = jnp.dot(normed_low, weight_first, preferred_element_type=jnp.float32) + bias_float
    activated, gelu_back = jax.vjp(gelu_tanh, pre_act)
    act_low = activated.astype(jnp.bfloat16)
    feed = jnp.dot(act_low, weight_second, preferred_element_type=jnp.float32) + vec_float[2]
    stream, norm_second_back = jax.vjp(layer_norm, normed + feed, vec_float[3], vec_float[4])
    saved = [(norm_first_back, normed_low, gelu_back, act_low, norm_second_back)]
    block_output = stream.astype(jnp.bfloat16)
    grad_now = cotangent.astype(jnp.float32)
    raw_grads = [None] * layers
    for layer_index in reversed(range(layers)):
        weight_first, weight_second, bias_low, vec_low = gathered[layer_index]
        norm_first_back, normed_low, gelu_back, act_low, norm_second_back = saved[layer_index]
        grad_sum2, grad_gain2, grad_shift2 = norm_second_back(grad_now)
        grad_z = grad_sum2.astype(jnp.bfloat16)
        grad_weight_second = jnp.einsum(
            "stf,std->fd", act_low, grad_z, preferred_element_type=jnp.float32
        )
        grad_bias_out = jnp.sum(grad_z.astype(jnp.float32), axis=(0, 1))
        grad_act = jnp.einsum(
            "std,fd->stf", grad_z, weight_second, preferred_element_type=jnp.float32
        )
        (grad_pre,) = gelu_back(grad_act)
        grad_pre_low = grad_pre.astype(jnp.bfloat16)
        grad_weight_first = jnp.einsum(
            "std,stf->df", normed_low, grad_pre_low, preferred_element_type=jnp.float32
        )
        grad_bias_in = jnp.sum(grad_pre_low.astype(jnp.float32), axis=(0, 1))
        grad_normed = (
            jnp.einsum(
                "stf,df->std", grad_pre_low, weight_first, preferred_element_type=jnp.float32
            )
            + grad_sum2
        )
        grad_sum1, grad_gain1, grad_shift1 = norm_first_back(grad_normed)
        grad_mix_low = grad_sum1.astype(jnp.bfloat16)
        add_shard_piece = lax.all_gather(grad_mix_low, BOTH[1], axis=1, tiled=True)
        add_piece_len = add_shard_piece.shape[1]
        add_cos_block, add_sin_block = dft_tables(
            my_rows, jnp.arange(add_piece_len, dtype=jnp.int32), seq_len
        )
        with_cos = jnp.einsum(
            "ij,sjd->sid", add_cos_block, add_shard_piece, preferred_element_type=jnp.float32
        )
        with_sin = (zeros_block, zeros_block)[1] - jnp.einsum(
            "ij,sjd->sid", add_sin_block, add_shard_piece, preferred_element_type=jnp.float32
        )
        with_cos, with_sin = (with_cos, with_sin)
        with_cos = (with_cos * dft_scale).astype(jnp.bfloat16)
        with_sin = (with_sin * dft_scale).astype(jnp.bfloat16)
        grad_halves = jnp.concatenate([with_cos, with_sin], axis=-1)
        grad_now = grad_sum1 + jnp.dot(grad_halves, table_back, preferred_element_type=jnp.float32)
        grad_vec = jnp.stack([grad_gain1, grad_shift1, grad_bias_out, grad_gain2, grad_shift2])
        layer_terms = (grad_weight_first, grad_weight_second, grad_bias_in, grad_vec)
        raw_grads[layer_index] = (
            lax.psum_scatter(layer_terms[0], BOTH, scatter_dimension=0, tiled=True),
            lax.psum_scatter(layer_terms[1], BOTH, scatter_dimension=1, tiled=True),
            lax.psum_scatter(layer_terms[2], BOTH, scatter_dimension=0, tiled=True),
            lax.psum_scatter(layer_terms[3], BOTH, scatter_dimension=1, tiled=True),
        )
    shard_w_in = jnp.stack([entry[0] for entry in raw_grads])
    shard_w_out = jnp.stack([entry[1] for entry in raw_grads])
    shard_b_in = jnp.stack([entry[2] for entry in raw_grads])
    shard_vec = jnp.stack([entry[3] for entry in raw_grads])
    local_squares = jnp.sum(shard_w_in * shard_w_in) + jnp.sum(shard_w_out * shard_w_out)
    local_squares = (
        local_squares + jnp.sum(shard_b_in * shard_b_in) + jnp.sum(shard_vec * shard_vec)
    )
    norm_value = jnp.sqrt(lax.psum(local_squares, BOTH))
    factor = clip_limit / jnp.maximum(norm_value, clip_limit)
    upd_w_in = adam_update(
        w_in, factor * shard_w_in, first_w_in, second_w_in, rate_matrix, STEP_COUNT
    )
    upd_w_out = adam_update(
        w_out, factor * shard_w_out, first_w_out, second_w_out, rate_matrix, STEP_COUNT
    )
    upd_b_in = adam_update(
        b_in, factor * shard_b_in, first_b_in, second_b_in, rate_vector, STEP_COUNT
    )
    upd_vec = adam_update(
        vec_params, factor * shard_vec, first_vec, second_vec, rate_vector, STEP_COUNT
    )
    return (
        block_output,
        grad_now,
        norm_value,
        upd_w_in[0],
        upd_w_in[1],
        upd_w_in[2],
        upd_w_out[0],
        upd_w_out[1],
        upd_w_out[2],
        upd_b_in[0],
        upd_b_in[1],
        upd_b_in[2],
        upd_vec[0],
        upd_vec[1],
        upd_vec[2],
    )


MESH = pl.DeviceIdType.MESH
F32 = jnp.float32
BF16 = jnp.bfloat16
NN = (((1,), (0,)), ((), ()))
NT = (((1,), (1,)), ((), ()))
TN = (((0,), (0,)), ((), ()))


def dot(a, b, dims=NN):
    return lax.dot_general(a, b, dims, preferred_element_type=F32)


class Sizes:
    def __init__(self, mesh, seqs, block, width, hidden):
        self.batch, self.seq = mesh.shape["batch"], mesh.shape["seq"]
        self.xs, self.ys, self.zs = self.batch // 2, 2, self.seq // 2
        self.devices = self.batch * self.seq
        self.seqs, self.block, self.width, self.hidden = seqs, block, width, hidden
        self.length = block * self.seq
        self.rows = width // self.devices
        self.slab = 2 * self.rows
        self.segment = self.zs * self.slab
        self.half = hidden // 2
        self.cols = 512
        self.chunks = self.half // self.cols
        self.parts = 2
        self.thin = self.cols // self.parts
        self.packed = width // self.seq
        self.tokens = seqs * block
        self.bias = hidden // self.devices

    def fits(self):
        return (
            self.batch == 4
            and self.seq % 2 == 0
            and self.width % self.devices == 0
            and self.slab % 16 == 0
            and self.packed % 32 == 0
            and self.block % 128 == 0
            and self.zs == 4
            and self.half % self.cols == 0
            and self.rows <= 128
            and self.bias <= 128
            and 5 * self.rows <= self.width
        )

    def owner(self, x, core, z, y):
        return (2 * x + core) * self.seq + 2 * z + y

    def place_owner(self):
        return [
            self.owner(x, core, z, y)
            for y in range(self.ys)
            for x in range(self.xs)
            for z in range(self.zs)
            for core in range(2)
        ]


def cos_sin(rows, columns, count):
    angle = (rows[:, None] * columns[None, :] % count) * (2.0 * math.pi / count)
    return np.cos(angle), np.sin(angle)


def host_tables(n):
    width, half = n.width, n.packed // 2
    owners = np.array(n.place_owner())
    order = (owners[:, None] * n.rows + np.arange(n.rows)[None, :]).reshape(-1)
    line = np.arange(width)
    cosine, sine = cos_sin(line, line, width)
    pack = np.zeros((width, width))
    unpack = np.zeros((width, width))
    for k in range(width // 2):
        device, inner = divmod(k, half)
        at_cos = device * n.packed + inner
        at_sin = at_cos + half
        pack[at_cos] = cosine[k]
        unpack[at_cos, k] = 1.0
        if k:
            unpack[at_cos, width - k] = 1.0
            pack[at_sin] = sine[k]
            unpack[at_sin, k] = -1.0
            unpack[at_sin, width - k] = 1.0
    pack[half] = cosine[width // 2]
    unpack[half, width // 2] = 1.0
    perm = np.zeros((width, width))
    perm[order, np.arange(width)] = 1.0
    positions = np.arange(n.length)
    by_length = np.stack(cos_sin(positions, positions, n.length))
    vec_mask = np.zeros((n.devices, width))
    vec_mask[np.repeat(owners, n.rows), np.arange(width)] = 1.0
    vec_spread = np.zeros((128, width))
    vec_spread[np.arange(width) % n.rows, np.arange(width)] = 1.0
    bias_spread = np.zeros((128, n.half))
    bias_spread[np.arange(n.half) % n.bias, np.arange(n.half)] = 1.0

    def low(a):
        return jnp.asarray(a.astype(np.float32).astype(ml_dtypes.bfloat16))

    return types.SimpleNamespace(
        tt_f=low(pack),
        by_length=low(by_length),
        un_f=low(unpack[:, order]),
        perm=low(perm),
        tt_b=low(pack[:, order]),
        un_b=low(unpack),
        vec_mask=jnp.asarray(vec_mask.astype(np.float32)),
        vec_spread=low(vec_spread),
        bias_spread=low(bias_spread),
    )


LOADS = dict(
    w1="w1_v",
    w2="w2_v",
    x="x_v",
    tt_f="tt_v",
    dy="dy_v",
    vec_spread="vec_spread_v",
    bias_spread="bias_spread_v",
    vec_mask="vec_mask_v",
    by_length="by_length_v",
    perm="perm_v",
    un_f="un_v",
    tt_b="tt_v",
    un_b="un_v",
)
LATER = ("tt_b", "un_b")
FORWARD_KINDS = (1, 2, 1, 3, 1, 0)
BACK_KINDS = (1, 1, 4, 3, 5, 4, 3, 0, 0, 0, 3, 4)


def layer_kernel(n, names, *refs):
    r = types.SimpleNamespace(**dict(zip(names, refs)))
    batch_at, seq_at = lax.axis_index("batch"), lax.axis_index("seq")
    x, core = batch_at // 2, batch_at % 2
    z, y = seq_at // 2, seq_at % 2
    tokens, width, seg, slab = n.tokens, n.width, n.segment, n.slab
    started = []

    def aligned(at, by):
        return pl.multiple_of(at * by, by)

    def rows_of(at, by):
        return pl.ds(aligned(at, by), by)

    def remote(src, dst, send, recv, batch_to, seq_to):
        return pltpu.make_async_remote_copy(
            src_ref=src,
            dst_ref=dst,
            send_sem=send,
            recv_sem=recv,
            device_id=(batch_to, seq_to),
            device_id_type=MESH,
        )

    def go(copy):
        copy.start()
        started.append(copy)
        return copy

    other_core = 2 * x + 1 - core
    other_x = 2 * (1 - x) + core
    other_y = 2 * z + 1 - y

    def plane(k):
        return (seq_at + k) % n.seq

    def plane_from(k):
        return (seq_at + n.seq - k) % n.seq

    def across(k):
        return (batch_at + k) % n.batch

    def across_from(k):
        return (batch_at + n.batch - k) % n.batch

    loads = types.SimpleNamespace()
    for i, (name, held) in enumerate(LOADS.items()):
        load = pltpu.make_async_copy(getattr(r, name), getattr(r, held), r.load_sem.at[i])
        setattr(loads, name, load)
        if name not in LATER:
            load.start()

    everyone = [
        ((batch_at + i // n.seq) % n.batch, (seq_at + i % n.seq) % n.seq)
        for i in range(1, n.devices)
    ]
    barrier = pltpu.get_barrier_semaphore()
    for device in everyone:
        pl.semaphore_signal(barrier, inc=1, device_id=device, device_id_type=MESH)
    pl.semaphore_wait(barrier, n.devices - 1)

    loads.w1.wait()
    loads.w2.wait()
    weights = (r.w1_v, r.w2_v)
    give = pl.ds(aligned(1 - core, n.half), n.half)
    keep = pl.ds(aligned(core, n.half), n.half)
    core_rows = pl.ds(aligned(core, n.rows), n.rows)
    their_rows = pl.ds(aligned(1 - core, n.rows), n.rows)
    swaps = [
        go(
            remote(
                weights[m].at[:, give],
                r.stage.at[m, core_rows],
                r.swap_send.at[m],
                r.swap_recv.at[m],
                other_core,
                seq_at,
            )
        )
        for m in range(2)
    ]

    def mix_start(t, source, table):
        y_ref, l_ref = r.y_buf.at[t], r.l_buf.at[t]
        y_ref[...] = dot(table[...], source, NT).astype(BF16)
        l_ref[seq_at] = y_ref[rows_of(seq_at, n.packed), :]

    def mix_send(t):
        y_ref, l_ref = r.y_buf.at[t], r.l_buf.at[t]
        for k in range(1, n.seq):
            go(
                remote(
                    y_ref.at[rows_of(plane(k), n.packed)],
                    l_ref.at[seq_at],
                    r.mix_send.at[2 * t, k - 1],
                    r.mix_recv.at[2 * t, k - 1],
                    batch_at,
                    plane(k),
                )
            )

    def mix_turn(t):
        l_ref, z_ref, r_ref = r.l_buf.at[t], r.z_buf.at[t], r.r_buf.at[t]
        for k in range(1, n.seq):
            remote(
                r.y_buf.at[t, rows_of(plane(k), n.packed)],
                l_ref.at[plane_from(k)],
                r.mix_send.at[2 * t, k - 1],
                r.mix_recv.at[2 * t, k - 1],
                batch_at,
                plane(k),
            ).wait_recv()
        left = jnp.concatenate(
            [
                jnp.concatenate(
                    [l_ref[d, :, g * n.block : (g + 1) * n.block] for d in range(n.seq)], axis=1
                )
                for g in range(n.seqs)
            ],
            axis=0,
        )
        r.left[...] = left
        inner = lax.broadcasted_iota(jnp.int32, (n.seqs * n.packed, 1), 0) % n.packed
        first = (inner < n.packed // 2) | ((inner == n.packed // 2) & (seq_at == 0))
        scale = 1.0 / math.sqrt(n.length * n.width)
        for e in range(0, n.seq, 2):
            at = slice(e * n.block, (e + 2) * n.block)
            by_cos = dot(r.left[...], r.by_length_v[0, :, at])
            by_sin = dot(r.left[...], r.by_length_v[1, :, at])
            value = (jnp.where(first, by_cos, by_sin) * scale).astype(BF16)
            z_ref[e] = value[:, : n.block]
            z_ref[e + 1] = value[:, n.block :]
        for k in range(1, n.seq):
            go(
                remote(
                    z_ref.at[plane(k)],
                    r_ref.at[seq_at],
                    r.mix_send.at[2 * t + 1, k - 1],
                    r.mix_recv.at[2 * t + 1, k - 1],
                    batch_at,
                    plane(k),
                )
            )
        r_ref[seq_at] = z_ref[seq_at]

    def mix_finish(t, table):
        r_ref = r.r_buf.at[t]
        for k in range(1, n.seq):
            remote(
                r.z_buf.at[t, plane(k)],
                r_ref.at[plane_from(k)],
                r.mix_send.at[2 * t + 1, k - 1],
                r.mix_recv.at[2 * t + 1, k - 1],
                batch_at,
                plane(k),
            ).wait_recv()
        parts = [
            r_ref[:, g * n.packed : (g + 1) * n.packed, :].reshape(width, n.block)
            for g in range(n.seqs)
        ]
        r.mixed[...] = dot(jnp.concatenate(parts, axis=1), table[...], TN)

    loads.tt_f.wait()
    loads.x.wait()
    mix_start(0, r.x_v[...], r.tt_v)

    full = r.full
    mate_z = z + 1 - 2 * (z % 2)
    pair_z = z // 2
    inner = (z > 0) & (z < n.zs - 1)

    def line(to_z):
        return batch_at, 2 * to_z + y

    def seg_rows(sx, sy):
        return rows_of(sy * n.xs + sx, seg)

    def pair_rows(sx, sy, sp):
        return rows_of((sy * n.xs + sx) * 2 + sp, 2 * slab)

    def slab_rows(sx, sy, sz):
        return rows_of((sy * n.xs + sx) * n.zs + sz, slab)

    def peer(t):
        return (other_y_at, other_x_at)[t == 0]

    other_x_at = (other_x, seq_at)
    other_y_at = (batch_at, other_y)

    def away(t):
        return (1 - x, y) if t == 0 else (x, 1 - y)

    def turn_of(c):
        return FORWARD_KINDS[c] % 2

    def split(c):
        return FORWARD_KINDS[c] // 2 == 1

    def place(c):
        return c // n.chunks, c % n.chunks

    def stage_weights():
        for m in range(2):
            r.stage[m, core_rows, :] = weights[m][:, keep]
            remote(
                weights[m].at[:, give],
                r.stage.at[m, their_rows],
                r.swap_send.at[m],
                r.swap_recv.at[m],
                other_core,
                seq_at,
            ).wait_recv()
            for q in range(n.chunks):
                full[m, q, slab_rows(x, y, z), :] = r.stage[
                    m, :, q * n.cols : (q + 1) * n.cols
                ].astype(BF16)

    def full_copy(c, at, send, recv, to):
        m, q = place(c)
        return remote(full.at[m, q, at], full.at[m, q, at], send.at[m, q], recv.at[m, q], *to)

    def rows_at(sx, sy, i):
        return (slab_rows(sx, sy, z), slab_rows(sx, sy, mate_z), pair_rows(sx, sy, 1 - pair_z))[i]

    def side_copy(c, i, sx, sy, first):
        t = turn_of(c)
        recv = r.first_recv.at[i] if first else r.second_recv
        return full_copy(c, rows_at(sx, sy, i), r.side_send, recv, peer(t if first else 1 - t))

    def to_sides(c, i):
        if i == 0 or not split(c):
            side_copy(c, i, x, y, True).start()
        side_copy(c, i, x, y, False).start()

    def line_seg(c, far):
        return away(turn_of(c)) if far else (x, y)

    def own_to_mate(c, far):
        at = rows_at(*line_seg(c, far), 0)
        return full_copy(c, at, r.mate_send.at[far], r.mate_recv.at[far], line(mate_z))

    def mate_arrives(c, far):
        at = rows_at(*line_seg(c, far), 1)
        full_copy(c, at, r.mate_send.at[far], r.mate_recv.at[far], line(mate_z)).wait_recv()

    def pair_across(c, far):
        at = pair_rows(*line_seg(c, far), pair_z)
        return full_copy(c, at, r.across_send.at[far], r.pair_recv.at[far], line(n.zs - 1 - z))

    def pair_out(c, far):
        at = rows_at(*line_seg(c, far), 2)
        return full_copy(c, at, r.out_send.at[far], r.pair_recv.at[far], line(mate_z))

    def own_sides(c):
        to_sides(c, 0)

    def own_line(c):
        own_to_mate(c, 0).start()

    def from_mate(c, far):
        mate_arrives(c, far)

        @pl.when(inner)
        def _():
            pair_across(c, far).start()

    def from_pair(c, far):
        pair_out(c, far).wait_recv()

        @pl.when(inner)
        def _():
            pair_out(c, far).start()

    def mate_in(c):
        from_mate(c, 0)
        to_sides(c, 1)

    def pair_in(c):
        from_pair(c, 0)
        to_sides(c, 2)

    def pass_on(c, i):
        ax, ay = away(turn_of(c))
        if i == 0 or not split(c):
            side_copy(c, i, ax, ay, True).wait_recv()
        if split(c):
            if i == 0:
                own_to_mate(c, 1).start()
            else:
                (from_mate, from_pair)[i - 1](c, 1)
        side_copy(c, i, ax, ay, False).start()

    def slabs_of(c, count, recv):
        return full_copy(c, pl.ds(0, count * slab), r.side_send, recv, other_x_at)

    def weights_here(c):
        slabs_of(c, 2 * n.zs, r.second_recv).wait_recv()

    def small_tiles():
        tile = r.tile
        tile[...] = jnp.zeros(tile.shape, F32)
        for i in range(5):
            tile[i : i + 1, 0 : n.rows] = r.vec[i]
        tile[5:6, 0 : n.bias] = r.bias[...]
        small[batch_at, seq_at] = tile[...]
        for k in range(1, n.seq):
            go(small_copy(k, seq_at))

    def small_copy(k, at):
        return remote(
            r.tile,
            small.at[batch_at, at],
            r.small_send.at[k - 1],
            r.small_recv.at[k - 1],
            batch_at,
            plane(k),
        )

    def row_copy(k, at):
        return remote(
            small.at[batch_at],
            small.at[at],
            r.row_send.at[k - 1],
            r.row_recv.at[k - 1],
            across(k),
            seq_at,
        )

    small = r.small

    def small_rows():
        for k in range(1, n.seq):
            small_copy(k, plane_from(k)).wait_recv()
        for k in range(1, n.batch):
            go(row_copy(k, batch_at))

    half_owners = n.devices // 2
    bias_mask = (
        lax.broadcasted_iota(jnp.int32, (half_owners, n.half), 0)
        == lax.broadcasted_iota(jnp.int32, (half_owners, n.half), 1) // n.bias
    )

    def small_vectors():
        for k in range(1, n.batch):
            row_copy(k, across_from(k)).wait_recv()
        for load in (loads.vec_spread, loads.bias_spread, loads.vec_mask):
            load.wait()
        for i in range(5):
            held = small[:, :, i, :].reshape(n.devices, 128).astype(BF16)
            spread = dot(held, r.vec_spread_v[...]) * r.vec_mask_v[...]
            r.vecs[i : i + 1, :] = jnp.sum(spread, axis=0, keepdims=True)
        held = small[pl.ds(core * (n.batch // 2), n.batch // 2), :, 5, :]
        held = held.reshape(half_owners, 128).astype(BF16)
        spread = jnp.where(bias_mask, dot(held, r.bias_spread_v[...]), 0.0)
        biases = jnp.sum(spread, axis=0, keepdims=True)
        for q in range(n.chunks):
            r.biases[q] = biases[:, q * n.cols : (q + 1) * n.cols]

    def place_inputs():
        loads.perm.wait()
        loads.dy.wait()
        r.x_place[...] = dot(r.x_v[...], r.perm_v[...])
        r.dy_place[...] = dot(r.dy_v[...], r.perm_v[...])

    def turn_forward():
        loads.by_length.wait()
        mix_turn(0)

    step = 32
    tall = 64
    mine, theirs = pl.ds(0, tokens), pl.ds(tokens, tokens)

    def row_loop(body):
        @pl.loop(0, tokens // tall, unroll=True)
        def _(i):
            body(pl.ds(pl.multiple_of(i * tall, tall), tall))

    def mean(v):
        return jnp.mean(v, axis=-1, keepdims=True)

    def first_norm(at):
        v = r.x_place[at, :] + r.mixed[at, :]
        centred = v - mean(v)
        scale = lax.rsqrt(mean(centred * centred) + norm_epsilon)
        unit = centred * scale
        h = unit * r.vecs[0:1, :] + r.vecs[1:2, :]
        r.unit1[at, :] = unit
        r.scale1[at, :] = jnp.broadcast_to(scale, (tall, 128))
        r.h[at, :] = h
        r.h_low[at, :] = h.astype(BF16)

    def swap(i, src, dst):
        return remote(src, dst, r.core_send.at[i], r.core_recv.at[i], other_core, seq_at)

    def swap_h():
        return swap(0, r.h_low.at[mine], r.h_low.at[theirs])

    def norm_forward():
        loads.un_f.wait()
        mix_finish(0, r.un_v)
        loads.tt_b.start()
        loads.un_b.start()
        row_loop(first_norm)
        go(swap_h())

    root = math.sqrt(2.0 / math.pi)

    lifted_parts = []

    def lift(q):
        if not lifted_parts:
            swap_h().wait_recv()
        lifted_parts.append(q)
        weights_here(q)
        r.lift[...] = dot(r.h_low[...], full[0, q]) + r.biases[q]

        @pl.loop(0, 2 * tokens // step)
        def _(i):
            at = pl.ds(pl.multiple_of(i * step, step), step)
            u = r.lift[at, :]
            square = u * u
            bent = jnp.tanh(u * (root + (root * 0.044715) * square))
            half_up = 0.5 + 0.5 * bent
            r.act[q, at, :] = (u * half_up).astype(BF16)
            r.slope[q, at, :] = half_up + (u * (1.0 - bent * bent)) * (
                0.5 * root + (1.5 * root * 0.044715) * square
            )

    gathered_parts = []

    def swap_ff():
        return swap(1, r.part_low, r.part_in)

    def drop(q):
        weights_here(n.chunks + q)
        gathered_parts.append(q)
        for half in (theirs, mine):
            part = dot(r.act[q, half, :], full[1, q], NT)
            part = r.total[half, :] + part if len(gathered_parts) > 1 else part
            if len(gathered_parts) == n.chunks and half is theirs:
                r.part_low[...] = part.astype(BF16)
                go(swap_ff())
            else:
                r.total[half, :] = part

    def send_forward():
        mix_send(0)

    forward_steps = (
        (send_forward,), (stage_weights,), (own_line, 2), (own_line, 0), (own_line, 5),
        (own_sides, 4), (place_inputs,), (small_tiles,), (own_sides, 3), (own_sides, 2),
        (own_line, 4), (own_sides, 5), (mate_in, 2), (pass_on, 4, 0), (own_sides, 0),
        (mate_in, 5), (pass_on, 5, 0), (pass_on, 3, 0), (own_line, 1), (own_sides, 1),
        (mate_in, 0), (pass_on, 2, 0), (pass_on, 2, 1), (mate_in, 4), (pair_in, 2),
        (pass_on, 5, 1), (pass_on, 0, 0), (pass_on, 3, 1), (pass_on, 1, 0), (turn_forward,),
        (pair_in, 0), (small_rows,), (pair_in, 5), (pass_on, 2, 2), (pair_in, 4),
        (pass_on, 3, 2), (pass_on, 0, 1), (pass_on, 4, 1), (small_vectors,), (pass_on, 1, 1),
        (pass_on, 0, 2), (own_line, 3), (pass_on, 5, 2), (mate_in, 1), (norm_forward,),
        (mate_in, 3), (pass_on, 1, 2), (pass_on, 4, 2), (pair_in, 1), (lift, 2), (pair_in, 3),
        (lift, 0), (lift, 1), (drop, 2), (drop, 1), (drop, 0),
    )
    for task, *which in forward_steps:
        task(*which)
    swap_ff().wait_recv()

    def second_norm(at):
        v = (
            r.h[at, :]
            + r.total[at, :]
            + r.part_in[at, :].astype(F32)
            + r.vecs[2:3, :]
        )
        centred = v - mean(v)
        scale = lax.rsqrt(mean(centred * centred) + norm_epsilon)
        unit = centred * scale
        gain = r.vecs[3:4, :]
        r.h[at, :] = unit
        r.out_low[at, :] = (unit * gain + r.vecs[4:5, :]).astype(BF16)
        du = r.dy_place[at, :] * gain
        dv = scale * (du - mean(du) - unit * mean(du * unit))
        r.dr2[at, :] = dv
        r.dz[at, :] = dv.astype(BF16)

    row_loop(second_norm)
    swap_dz = go(swap(2, r.dz.at[mine], r.dz.at[theirs]))
    swap_dz.wait_recv()

    acc, out_low = r.acc, r.give

    def wide(c):
        m, q = c // (n.chunks * n.parts), c % (n.chunks * n.parts)
        return 1 - m, q // n.parts, pl.ds((q % n.parts) * n.thin, n.thin)

    def grad_copy(c, at, into, i, to, slot=None):
        return remote(
            out_low.at[c, at],
            into.at[c if slot is None else slot],
            r.grad_send.at[i, c],
            r.grad_recv.at[i, c],
            *to,
        )

    def back_turn(c):
        return BACK_KINDS[c] % 2

    def back_mode(c):
        return BACK_KINDS[c] // 2

    def back_slot(c):
        return [d for d, kind in enumerate(BACK_KINDS) if kind // 2 == back_mode(c)].index(c)

    def copy_diagonal(c):
        return grad_copy(c, seg_rows(1 - x, 1 - y), r.in_diagonal, 0, peer(1 - back_turn(c)))

    def copy_near(c):
        t = 1 - back_turn(c)
        return grad_copy(c, seg_rows(*away(t)), r.in_near, 1, peer(t))

    def copy_side(c):
        t = back_turn(c)
        return grad_copy(c, seg_rows(*away(t)), r.in_side, 2, peer(t))

    def back_seg(c, far):
        return away(back_turn(c)) if far else (x, y)

    def line_into(c, far, i):
        if far:
            return (r.far_mate, r.far_pair, r.far_across)[i].at[back_slot(c)]
        return (r.in_mate, r.in_pair, r.in_across)[i].at[c]

    def line_copy(c, at, far, i, to):
        return remote(
            out_low.at[c, at],
            line_into(c, far, i),
            r.grad_send.at[3 + 3 * far + i, c],
            r.grad_recv.at[3 + 3 * far + i, c],
            *to,
        )

    def copy_mate(c, far):
        at = slab_rows(*back_seg(c, far), mate_z)
        return line_copy(c, at, far, 0, line(mate_z))

    def copy_pair_in(c, far):
        at = pair_rows(*back_seg(c, far), 1 - pair_z)
        return line_copy(c, at, far, 1, line(mate_z))

    def copy_pair_across(c, far):
        at = pair_rows(*back_seg(c, far), 1 - pair_z)
        return line_copy(c, at, far, 2, line(n.zs - 1 - z))

    def copy_far(c):
        t = back_turn(c)
        return grad_copy(c, slab_rows(*away(t), z), r.in_far, 2, peer(t), back_slot(c))

    def copy_direct(c, d):
        to_z = (z + d) % n.zs
        into = r.in_direct.at[d - 1]
        return grad_copy(c, slab_rows(x, y, to_z), into, 8 + d, line(to_z), back_slot(c))

    def round_out(c, at, *more):
        value = acc[c, at, :]
        for ref in more:
            value = value + ref[...].astype(F32)
        out_low[c, at, :] = value.astype(BF16)

    def grad_product(c):
        m, q, at = wide(c)
        if m:
            acc[c] = dot(r.dz[...], r.act[q, :, at], TN)
        else:
            acc[c] = dot(r.h_low[...], r.dpre[q, :, at], TN)
        round_out(c, seg_rows(1 - x, 1 - y))
        copy_diagonal(c).start()
        round_out(c, seg_rows(*away(1 - back_turn(c))))
        copy_near(c).start()

    def line_start(c, far):
        @pl.when(jnp.logical_not(inner))
        def _():
            sx, sy = back_seg(c, far)
            round_out(c, pair_rows(sx, sy, 1 - pair_z))
            copy_pair_in(c, far).start()
            round_out(c, slab_rows(sx, sy, mate_z))
            copy_mate(c, far).start()

    def grad_side(c):
        copy_diagonal(c).wait_recv()
        at = seg_rows(*away(back_turn(c)))
        if back_mode(c) == 1:
            acc[c, at, :] = acc[c, at, :] + r.in_diagonal[c].astype(F32)
            line_start(c, 1)
        else:
            round_out(c, at, r.in_diagonal.at[c])
            copy_side(c).start()

    def grad_line(c):
        copy_near(c).wait_recv()
        more = r.in_near[c].astype(F32)
        if back_mode(c) != 1:
            copy_side(c).wait_recv()
            more = more + r.in_side[c].astype(F32)
        at = seg_rows(x, y)
        acc[c, at, :] = acc[c, at, :] + more
        if back_mode(c) == 2:
            for d in range(1, n.zs):
                round_out(c, slab_rows(x, y, (z + d) % n.zs))
                copy_direct(c, d).start()
        else:
            line_start(c, 0)

    def fars(c):
        return range((1, 2, 0)[back_mode(c)])

    def grad_across(c):
        for far in fars(c):

            @pl.when(inner)
            def _(far=far):
                copy_pair_in(c, far).wait_recv()
                at = pair_rows(*back_seg(c, far), 1 - pair_z)
                round_out(c, at, line_into(c, far, 1))
                copy_pair_across(c, far).start()

    def grad_out(c):
        for far in fars(c):

            @pl.when(inner)
            def _(far=far):
                copy_pair_across(c, far).wait_recv()
                sx, sy = back_seg(c, far)
                at = pair_rows(sx, sy, pair_z)
                acc[c, at, :] = acc[c, at, :] + line_into(c, far, 2)[...].astype(F32)
                round_out(c, slab_rows(sx, sy, mate_z))
                copy_mate(c, far).start()

    def grad_far(c):
        if back_mode(c) == 1:
            copy_mate(c, 1).wait_recv()
            round_out(c, slab_rows(*away(back_turn(c)), z), line_into(c, 1, 0))
            copy_far(c).start()

    grads_out = (r.g1, r.g2)
    r.squares[...] = jnp.zeros((8, 128), F32)

    def squares_of(v):
        v = v * v
        v = jnp.sum(v.reshape(v.shape[0] // 8, 8, v.shape[1]), axis=0)
        return sum(v[:, i : i + 128] for i in range(0, v.shape[1], 128))

    def copy_back(c):
        return remote(
            r.final.at[c, their_rows],
            r.final_in.at[c],
            r.back_send.at[c],
            r.back_recv.at[c],
            other_core,
            seq_at,
        )

    def grad_end(c):
        m, q, at = wide(c)
        value = acc[c, slab_rows(x, y, z), :]
        if back_mode(c) == 2:
            for d in range(1, n.zs):
                copy_direct(c, d).wait_recv()
                value = value + r.in_direct[d - 1, back_slot(c)].astype(F32)
        else:
            copy_mate(c, 0).wait_recv()
            value = value + r.in_mate[c].astype(F32)
        if back_mode(c) == 1:
            copy_far(c).wait_recv()
            value = value + r.in_far[back_slot(c)].astype(F32)
        r.squares[...] += squares_of(value)
        r.final[c] = value
        own_at = pl.ds(aligned(core, n.half) + q * n.cols + at.start, n.thin)
        grads_out[m][:, own_at] = r.final[c, core_rows, :]
        copy_back(c).start()

    back_parts = []

    def slope_back(q):
        r.lift[...] = dot(r.dz[...], full[1, q])
        r.bias_sum[q] = jnp.zeros((8, n.cols), F32)

        @pl.loop(0, 2 * tokens // step)
        def _(i):
            at = pl.ds(pl.multiple_of(i * step, step), step)
            low = (r.lift[at, :] * r.slope[q, at, :]).astype(BF16)
            r.dpre[q, at, :] = low
            r.bias_sum[q] += jnp.sum(low.astype(F32).reshape(step // 8, 8, n.cols), axis=0)

        back_parts.append(q)
        for half in (theirs, mine):
            part = dot(r.dpre[q, half, :], full[0, q], NT)
            part = r.total[half, :] + part if len(back_parts) > 1 else part
            if len(back_parts) == n.chunks and half is theirs:
                r.part_low2[...] = part.astype(BF16)
                go(swap_dh())
            else:
                r.total[half, :] = part

    def swap_dh():
        return swap(3, r.part_low2, r.part_in2)

    def first_norm_back(at):
        dh = r.total[at, :] + r.part_in2[at, :].astype(F32) + r.dr2[at, :]
        unit = r.unit1[at, :]
        r.x_place[at, :] = dh
        du = dh * r.vecs[0:1, :]
        dv = r.scale1[at, 0:1] * (du - mean(du) - unit * mean(du * unit))
        low = dv.astype(BF16)
        r.dm[at, :] = low
        r.rest[at, :] = (dv - low.astype(F32)).astype(BF16)

    def norm_back():
        swap_dh().wait_recv()
        row_loop(first_norm_back)
        loads.tt_b.wait()
        mix_start(1, r.dm[...], r.tt_v)
        mix_send(1)

    def thirds(v):
        high = v.astype(BF16)
        left = v - high.astype(F32)
        mid = left.astype(BF16)
        return high, mid, (left - mid.astype(F32)).astype(BF16)

    def small_gather(v, spread):
        return sum(dot(part, spread, NT) for part in thirds(v))

    def row_sums(k):
        return remote(
            r.small_out.at[across(k)],
            r.small_in.at[k - 1],
            r.row_send2.at[k - 1],
            r.row_recv2.at[k - 1],
            across(k),
            seq_at,
        )

    def tile_sums(k):
        return remote(
            r.small_mid.at[plane(k)],
            r.small_last.at[k - 1],
            r.small_send2.at[k - 1],
            r.small_recv2.at[k - 1],
            batch_at,
            plane(k),
        )

    def fold(v):
        return jnp.sum(v.reshape(tall // 8, 8, width), axis=0)

    def vector_sums(at):
        dh, dy = r.x_place[at, :], r.dy_place[at, :]
        r.sums[0] += fold(dh * r.unit1[at, :])
        r.sums[1] += fold(dh)
        r.sums[2] += fold(r.dz[at, :].astype(F32))
        r.sums[3] += fold(dy * r.h[at, :])
        r.sums[4] += fold(dy)

    def small_grads():
        r.sums[...] = jnp.zeros(r.sums.shape, F32)
        row_loop(vector_sums)
        for i in range(5):
            line_sum = jnp.sum(r.sums[i], axis=0, keepdims=True)
            tiles = small_gather(line_sum * r.vec_mask_v[...], r.vec_spread_v[...])
            r.small_out[:, :, i, :] = tiles.reshape(n.batch, n.seq, 128)
        line_sum = jnp.concatenate(
            [jnp.sum(r.bias_sum[q], axis=0, keepdims=True) for q in range(n.chunks)], axis=1
        )
        tiles = small_gather(jnp.where(bias_mask, line_sum, 0.0), r.bias_spread_v[...])
        r.small_out[:, :, 5:8, :] = jnp.zeros((n.batch, n.seq, 3, 128), F32)
        r.small_out[pl.ds(core * (n.batch // 2), n.batch // 2), :, 5, :] = tiles.reshape(
            n.batch // 2, n.seq, 128
        )
        for k in range(1, n.batch):
            go(row_sums(k))

    def small_rows_back():
        value = r.small_out[batch_at]
        for k in range(1, n.batch):
            row_sums(k).wait_recv()
            value = value + r.small_in[k - 1]
        r.small_mid[...] = value
        for k in range(1, n.seq):
            go(tile_sums(k))

    def small_end():
        value = r.small_mid[seq_at]
        for k in range(1, n.seq):
            tile_sums(k).wait_recv()
            value = value + r.small_last[k - 1]
        r.g_small[...] = value

    def turn_back():
        mix_turn(1)

    def outputs():
        r.out[...] = dot(r.out_low[...], r.perm_v[...], NT).astype(BF16)
        r.dx[...] = dot(r.dm[...], r.perm_v[...], NT) + dot(r.rest[...], r.perm_v[...], NT)

    def mix_back():
        loads.un_b.wait()
        mix_finish(1, r.un_v)
        r.dx[...] = r.dx[...] + r.mixed[...]

    for task, *which in (
        (grad_product, 5), (grad_product, 3), (slope_back, 0), (grad_product, 2),
        (slope_back, 1), (grad_side, 5), (grad_side, 3), (slope_back, 2), (grad_line, 3),
        (grad_product, 10), (grad_product, 1), (grad_product, 7), (grad_line, 5),
        (grad_across, 3), (norm_back,), (grad_out, 3), (grad_side, 10), (grad_side, 1),
        (grad_side, 7), (grad_product, 9), (grad_side, 2), (grad_line, 10), (grad_product, 8),
        (grad_product, 6), (grad_line, 7), (grad_across, 10), (grad_line, 1), (grad_line, 2),
        (grad_product, 0), (grad_across, 7), (grad_across, 5), (grad_side, 6), (turn_back,),
        (grad_side, 9), (grad_product, 4), (outputs,), (grad_across, 1), (grad_side, 0),
        (grad_line, 6), (grad_line, 9), (grad_across, 2), (grad_side, 8), (grad_side, 4),
        (small_grads,), (grad_across, 6), (grad_product, 11), (grad_across, 9), (grad_out, 2),
        (grad_line, 0), (grad_out, 10), (grad_line, 8), (grad_out, 5), (grad_out, 1),
        (grad_line, 4), (grad_out, 6), (grad_out, 7), (grad_across, 0), (grad_side, 11),
        (small_rows_back,), (grad_far, 7), (grad_far, 10), (grad_across, 8), (grad_out, 9),
        (grad_far, 9), (grad_far, 3), (grad_out, 0), (grad_line, 11), (grad_across, 4),
        (grad_out, 8), (grad_far, 5), (grad_end, 3), (grad_end, 9), (grad_far, 6), (mix_back,),
        (grad_end, 7), (grad_out, 4), (small_end,), (grad_far, 4), (grad_end, 5), (grad_far, 0),
        (grad_across, 11), (grad_end, 10), (grad_out, 11), (grad_far, 1), (grad_far, 2),
        (grad_end, 4), (grad_far, 8), (grad_far, 11), (grad_end, 2), (grad_end, 0),
        (grad_end, 6), (grad_end, 1), (grad_end, 8), (grad_end, 11),
    ):
        task(*which)

    squares = r.squares[...] + r.g_small[...] * r.g_small[...]
    r.norm_own[...] = jnp.sum(squares, axis=0, keepdims=True)
    r.norm_all[batch_at * n.seq + seq_at] = r.norm_own[...]

    def norm_copy(i, at):
        return remote(
            r.norm_own, r.norm_all.at[at], r.norm_send.at[i], r.norm_recv.at[i], *everyone[i]
        )

    for i in range(n.devices - 1):
        go(norm_copy(i, batch_at * n.seq + seq_at))
    for c in range(2 * n.chunks * n.parts):
        m, q, at = wide(c)
        copy_back(c).wait_recv()
        their_at = pl.ds(aligned(1 - core, n.half) + q * n.cols + at.start, n.thin)
        grads_out[m][:, their_at] = r.final_in[c]
    for i in range(n.devices - 1):
        j = i + 1
        batch_from = (batch_at + n.batch - j // n.seq) % n.batch
        seq_from = (seq_at + n.seq - j % n.seq) % n.seq
        norm_copy(i, batch_from * n.seq + seq_from).wait_recv()
    squares = jnp.sum(r.norm_all[...].reshape(n.devices, 128), axis=0, keepdims=True)
    whole = jnp.sum(squares, axis=1, keepdims=True)
    r.norm[...] = jnp.broadcast_to(jnp.sqrt(whole), (8, 128))

    for copy in started:
        copy.wait_send()

    for c in range(2 * n.chunks):
        moved = 2 * n.zs + (1 if split(c) else n.zs)
        slabs_of(c, moved, r.second_recv).wait_send()
        for far in range(1 + split(c)):
            own_to_mate(c, far).wait_send()

            @pl.when(inner)
            def _(c=c, far=far):
                pair_across(c, far).wait_send()
                pair_out(c, far).wait_send()

    for c in range(2 * n.chunks * n.parts):
        copy_back(c).wait_send()
        copy_diagonal(c).wait_send()
        copy_near(c).wait_send()
        (copy_far if back_mode(c) == 1 else copy_side)(c).wait_send()
        if back_mode(c) == 2:
            for d in range(1, n.zs):
                copy_direct(c, d).wait_send()
        for far in fars(c):
            copy_mate(c, far).wait_send()

            @pl.when(inner)
            def _(c=c, far=far):
                copy_pair_across(c, far).wait_send()

            @pl.when(jnp.logical_not(inner))
            def _(c=c, far=far):
                copy_pair_in(c, far).wait_send()


def run_layer(n, x, dy, w1, w2, bias, vec):
    tables = host_tables(n)
    tokens, width, cols, q = n.tokens, n.width, n.cols, n.chunks
    grads = 2 * q * n.parts
    splits = max(1, sum(kind // 2 == 1 for kind in BACK_KINDS))
    directs = max(1, sum(kind // 2 == 2 for kind in BACK_KINDS))
    dma = pltpu.SemaphoreType.DMA
    vmem = pltpu.VMEM
    inputs = dict(bias=bias, vec=vec, x=x, dy=dy, w1=w1, w2=w2)
    inputs.update({name: getattr(tables, name) for name in LOADS if name not in inputs})
    outputs = dict(
        out=((tokens, width), BF16),
        dx=((tokens, width), F32),
        g1=((n.rows, n.hidden), F32),
        g2=((n.rows, n.hidden), F32),
        g_small=((8, 128), F32),
        norm=((8, 128), F32),
    )
    scratch = {held: vmem(inputs[name].shape, inputs[name].dtype) for name, held in LOADS.items()}
    scratch.update(
        load_sem=dma((len(LOADS),)),
        stage=vmem((2, n.slab, n.half), F32),
        swap_send=dma((2,)),
        swap_recv=dma((2,)),
        tile=vmem((8, 128), F32),
        small=vmem((n.batch, n.seq, 8, 128), F32),
        small_send=dma((n.seq - 1,)),
        small_recv=dma((n.seq - 1,)),
        row_send=dma((n.batch - 1,)),
        row_recv=dma((n.batch - 1,)),
        y_buf=vmem((2, width, tokens), BF16),
        l_buf=vmem((2, n.seq, n.packed, tokens), BF16),
        left=vmem((n.seqs * n.packed, n.length), BF16),
        z_buf=vmem((2, n.seq, n.seqs * n.packed, n.block), BF16),
        r_buf=vmem((2, n.seq, n.seqs * n.packed, n.block), BF16),
        mix_send=dma((4, n.seq - 1)),
        mix_recv=dma((4, n.seq - 1)),
        mixed=vmem((tokens, width), F32),
        full=vmem((2, q, width, cols), BF16),
        mate_send=dma((2, 2, q)),
        mate_recv=dma((2, 2, q)),
        across_send=dma((2, 2, q)),
        out_send=dma((2, 2, q)),
        pair_recv=dma((2, 2, q)),
        side_send=dma((2, q)),
        first_recv=dma((3, 2, q)),
        second_recv=dma((2, q)),
        x_place=vmem((tokens, width), F32),
        dy_place=vmem((tokens, width), F32),
        vecs=vmem((8, width), F32),
        biases=vmem((q, 1, cols), F32),
        unit1=vmem((tokens, width), F32),
        scale1=vmem((tokens, 128), F32),
        h=vmem((tokens, width), F32),
        h_low=vmem((2 * tokens, width), BF16),
        core_send=dma((4,)),
        core_recv=dma((4,)),
        total=vmem((2 * tokens, width), F32),
        act=vmem((q, 2 * tokens, cols), BF16),
        lift=vmem((2 * tokens, cols), F32),
        slope=vmem((q, 2 * tokens, cols), F32),
        part_low=vmem((tokens, width), BF16),
        part_low2=vmem((tokens, width), BF16),
        part_in=vmem((tokens, width), BF16),
        part_in2=vmem((tokens, width), BF16),
        sums=vmem((5, 8, width), F32),
        out_low=vmem((tokens, width), BF16),
        dr2=vmem((tokens, width), F32),
        dz=vmem((2 * tokens, width), BF16),
        acc=vmem((grads, width, n.thin), F32),
        give=vmem((grads, width, n.thin), BF16),
        in_diagonal=vmem((grads, n.segment, n.thin), BF16),
        in_near=vmem((grads, n.segment, n.thin), BF16),
        in_side=vmem((grads, n.segment, n.thin), BF16),
        in_mate=vmem((grads, n.slab, n.thin), BF16),
        in_pair=vmem((grads, 2 * n.slab, n.thin), BF16),
        in_across=vmem((grads, 2 * n.slab, n.thin), BF16),
        far_mate=vmem((splits, n.slab, n.thin), BF16),
        far_pair=vmem((splits, 2 * n.slab, n.thin), BF16),
        far_across=vmem((splits, 2 * n.slab, n.thin), BF16),
        in_far=vmem((splits, n.slab, n.thin), BF16),
        in_direct=vmem((n.zs - 1, directs, n.slab, n.thin), BF16),
        grad_send=dma((8 + n.zs, grads)),
        grad_recv=dma((8 + n.zs, grads)),
        bias_sum=vmem((q, 8, cols), F32),
        dpre=vmem((q, 2 * tokens, cols), BF16),
        dm=vmem((tokens, width), BF16),
        rest=vmem((tokens, width), BF16),
        small_out=vmem((n.batch, n.seq, 8, 128), F32),
        small_in=vmem((n.batch - 1, n.seq, 8, 128), F32),
        row_send2=dma((n.batch - 1,)),
        row_recv2=dma((n.batch - 1,)),
        small_mid=vmem((n.seq, 8, 128), F32),
        small_last=vmem((n.seq - 1, 8, 128), F32),
        small_send2=dma((n.seq - 1,)),
        small_recv2=dma((n.seq - 1,)),
        final=vmem((grads, n.slab, n.thin), F32),
        final_in=vmem((grads, n.rows, n.thin), F32),
        back_send=dma((grads,)),
        back_recv=dma((grads,)),
        squares=vmem((8, 128), F32),
        norm_own=vmem((1, 128), F32),
        norm_all=vmem((n.devices, 1, 128), F32),
        norm_send=dma((n.devices - 1,)),
        norm_recv=dma((n.devices - 1,)),
    )
    names = tuple(inputs) + tuple(outputs) + tuple(scratch)
    in_vmem = pl.BlockSpec(memory_space=pltpu.VMEM)
    anywhere = pl.BlockSpec(memory_space=pl.ANY)
    values = pl.pallas_call(
        functools.partial(layer_kernel, n, names),
        out_shape=[vmem(*shape) for shape in outputs.values()],
        in_specs=[anywhere if name in LOADS else in_vmem for name in inputs],
        out_specs=[in_vmem] * len(outputs),
        scratch_shapes=list(scratch.values()),
        compiler_params=pltpu.CompilerParams(
            collective_id=0, has_side_effects=True, vmem_limit_bytes=58 * 2**20
        ),
        name="fused_layer",
    )(*inputs.values())
    return types.SimpleNamespace(**dict(zip(outputs, values)))


def adam_kernel(n, names, *refs):
    r = types.SimpleNamespace(**dict(zip(names, refs)))
    passed = [
        pltpu.make_async_copy(r.out, r.out_there, r.sem.at[0]),
        pltpu.make_async_copy(r.dx, r.dx_there, r.sem.at[1]),
    ]
    for copy in passed:
        copy.start()
    norm_value = r.norm[0:1, 0:1]
    r.norm_out[...] = norm_value
    factor = clip_limit / jnp.maximum(norm_value, clip_limit)
    lanes = n.cols

    def update(gradient, given, made, at, rate):
        weight, first, second = (ref[at] for ref in given)
        new = adam_update(weight, factor * gradient, first, second, rate, STEP_COUNT)
        for ref, value in zip(made, new):
            ref[at] = value

    weight_in, weight_out = refs[4:7], refs[7:10]
    made_in, made_out = refs[19:22], refs[22:25]

    @pl.loop(0, n.hidden // lanes)
    def _(i):
        at = (slice(None), pl.ds(pl.multiple_of(i * lanes, lanes), lanes))
        update(r.g1[at], weight_in, made_in, at, rate_matrix)
        update(r.g2[at], weight_out, made_out, at, rate_matrix)

    update(r.g_small[5:6, 0 : n.bias], refs[10:13], refs[25:28], ..., rate_vector)
    for i in range(5):
        update(r.g_small[i : i + 1, 0 : n.rows], refs[13:16], refs[28:31], i, rate_vector)
    for copy in passed:
        copy.wait()


def run_adam(n, got, given):
    f32 = functools.partial(jax.ShapeDtypeStruct, dtype=F32)
    matrix, bias, vec = f32((n.rows, n.hidden)), f32((1, n.bias)), f32((5, 1, n.rows))
    inputs = dict(g1=got.g1, g2=got.g2, g_small=got.g_small, norm=got.norm)
    inputs.update({chr(97 + i): array for i, array in enumerate(given)})
    inputs.update(out=got.out, dx=got.dx)
    outputs = dict(norm_out=f32((1, 1)))
    outputs.update({chr(110 + i): matrix for i in range(6)})
    outputs.update({chr(65 + i): bias for i in range(3)})
    outputs.update({chr(70 + i): vec for i in range(3)})
    outputs.update(
        out_there=jax.ShapeDtypeStruct(got.out.shape, BF16),
        dx_there=jax.ShapeDtypeStruct(got.dx.shape, F32),
    )
    names = tuple(inputs) + tuple(outputs) + ("sem",)
    in_vmem = pl.BlockSpec(memory_space=pltpu.VMEM)
    anywhere = pl.BlockSpec(memory_space=pl.ANY)
    return pl.pallas_call(
        functools.partial(adam_kernel, n, names),
        out_shape=list(outputs.values()),
        in_specs=[in_vmem] * (len(inputs) - 2) + [anywhere] * 2,
        out_specs=[in_vmem] * (len(outputs) - 2) + [anywhere] * 2,
        scratch_shapes=[pltpu.SemaphoreType.DMA((2,))],
        compiler_params=pltpu.CompilerParams(vmem_limit_bytes=32 * 2**20),
        name="adam",
    )(*inputs.values())


def turned(a):
    return jnp.swapaxes(a[0], 0, 1)


def lined(a):
    return jnp.transpose(a, (1, 0, 2))


def fused_layer(
    n,
    activations,
    cotangent,
    w_in,
    w_out,
    b_in,
    vec_params,
    first_w_in,
    second_w_in,
    first_w_out,
    second_w_out,
    first_b_in,
    second_b_in,
    first_vec,
    second_vec,
):
    got = run_layer(
        n,
        activations.reshape(n.tokens, n.width),
        cotangent.reshape(n.tokens, n.width),
        w_in[0],
        turned(w_out),
        b_in,
        lined(vec_params),
    )
    given = (
        *(a[0] for a in (w_in, first_w_in, second_w_in)),
        *(turned(a) for a in (w_out, first_w_out, second_w_out)),
        *(b_in, first_b_in, second_b_in),
        *(lined(a) for a in (vec_params, first_vec, second_vec)),
    )
    norm_value, *made, out, dx = run_adam(n, got, given)
    return (
        out.reshape(activations.shape),
        dx.reshape(activations.shape),
        norm_value.reshape(()),
        *(a[None] for a in made[:3]),
        *(jnp.swapaxes(a, 0, 1)[None] for a in made[3:6]),
        *made[6:9],
        *(lined(a) for a in made[9:]),
    )


def local_layer(mesh, activations, cotangent, w_in, *rest):
    seqs, block, width = activations.shape
    n = Sizes(mesh, seqs, block, width, w_in.shape[2])
    if w_in.shape[0] == 1 and n.fits():
        return fused_layer(n, activations, cotangent, w_in, *rest)
    return general_layer(activations, cotangent, w_in, *rest)


BOTH = ("batch", "seq")


def solution(mesh):
    in_specs = (
        P(*BOTH, None),
        P(*BOTH, None),
        P(None, BOTH, None),
        P(None, None, BOTH),
        P(None, BOTH),
        P(None, None, BOTH),
        P(None, BOTH, None),
        P(None, BOTH, None),
        P(None, None, BOTH),
        P(None, None, BOTH),
        P(None, BOTH),
        P(None, BOTH),
        P(None, None, BOTH),
        P(None, None, BOTH),
    )
    out_specs = (
        P(*BOTH, None),
        P(*BOTH, None),
        P(),
        P(None, BOTH, None),
        P(None, BOTH, None),
        P(None, BOTH, None),
        P(None, None, BOTH),
        P(None, None, BOTH),
        P(None, None, BOTH),
        P(None, BOTH),
        P(None, BOTH),
        P(None, BOTH),
        P(None, None, BOTH),
        P(None, None, BOTH),
        P(None, None, BOTH),
    )
    return jax.shard_map(
        functools.partial(local_layer, mesh), mesh=mesh, in_specs=in_specs, out_specs=out_specs, check_vma=False)
```

```python
import functools
import math
import types

import jax
import jax.numpy as jnp
import ml_dtypes
import numpy as np
from jax import lax
from jax.experimental import pallas as pl
from jax.experimental.pallas import tpu as pltpu
from jax.sharding import PartitionSpec as P

STEP_COUNT = 10


beta_first = 0.5
beta_second = 0.5
rate_matrix = 0.03
rate_vector = 0.2
weight_decay = 0.01
adam_epsilon = 1e-08
norm_epsilon = 1e-06
clip_limit = 1.0


def dft_tables(row_index, column_index, seq_len):
    product = row_index[:, None] * column_index[None, :] % seq_len
    angle = product.astype(jnp.float32) * (2.0 * math.pi / seq_len)
    return (jnp.cos(angle).astype(jnp.bfloat16), jnp.sin(angle).astype(jnp.bfloat16))


def layer_norm(values, gain, shift):
    centre = jnp.mean(values, axis=-1, keepdims=True)
    centred = values - centre
    spread = jnp.mean(centred * centred, axis=-1, keepdims=True)
    return centred * lax.rsqrt(spread + norm_epsilon) * gain + shift


def gelu_tanh(values):
    return jax.nn.gelu(values, approximate=True)


def adam_update(weight, gradient, first, second, rate, step_count):
    first_new = beta_first * first + (1.0 - beta_first) * gradient
    second_new = beta_second * second + (1.0 - beta_second) * gradient * gradient
    first_hat = first_new / (1.0 - beta_first**step_count)
    second_hat = second_new / (1.0 - beta_second**step_count)
    updated = weight - rate * (
        first_hat / (jnp.sqrt(second_hat) + adam_epsilon) + weight_decay * weight
    )
    return (first_new, second_new, updated)


def general_layer(
    activations,
    cotangent,
    w_in,
    w_out,
    b_in,
    vec_params,
    first_w_in,
    second_w_in,
    first_w_out,
    second_w_out,
    first_b_in,
    second_b_in,
    first_vec,
    second_vec,
):
    layers = w_in.shape[0]
    seq_count, block_len, model_width = activations.shape
    seq_devices = lax.axis_size(BOTH[1])
    seq_len = block_len * seq_devices
    dft_scale = 1.0 / math.sqrt(seq_len * model_width)
    first_row = lax.axis_index(BOTH[1]) * block_len
    my_rows = first_row + jnp.arange(block_len, dtype=jnp.int32)
    feature_line = jnp.arange(model_width, dtype=jnp.int32)
    cos_model, sin_model = dft_tables(feature_line, feature_line, model_width)
    table_fwd = jnp.concatenate([cos_model, sin_model], axis=1)
    table_back = jnp.transpose(table_fwd)
    layer_index = 0
    pieces = (
        w_in[layer_index].astype(jnp.bfloat16),
        w_out[layer_index].astype(jnp.bfloat16),
        b_in[layer_index].astype(jnp.bfloat16),
        vec_params[layer_index].astype(jnp.bfloat16),
    )
    gathered = [
        (
            lax.all_gather(pieces[0], BOTH, axis=0, tiled=True),
            lax.all_gather(pieces[1], BOTH, axis=1, tiled=True),
            lax.all_gather(pieces[2], BOTH, axis=0, tiled=True),
            lax.all_gather(pieces[3], BOTH, axis=1, tiled=True),
        )
    ]
    zeros_block = jnp.zeros((seq_count, block_len, model_width), jnp.float32)
    stream = activations.astype(jnp.float32)
    layer_index = 0
    weight_first, weight_second, bias_low, vec_low = gathered[layer_index]
    vec_float = vec_low.astype(jnp.float32)
    bias_float = bias_low.astype(jnp.float32)
    joined = jnp.dot(
        stream.astype(jnp.bfloat16), table_fwd, preferred_element_type=jnp.float32
    ).astype(jnp.bfloat16)
    halves = (joined[..., :model_width], joined[..., model_width:])
    shard_piece = (
        lax.all_gather(halves[0], BOTH[1], axis=1, tiled=True),
        lax.all_gather(halves[1], BOTH[1], axis=1, tiled=True),
    )
    piece_len = shard_piece[0].shape[1]
    cos_block, sin_block = dft_tables(my_rows, jnp.arange(piece_len, dtype=jnp.int32), seq_len)
    running = jnp.einsum(
        "ij,sjd->sid", cos_block, shard_piece[0], preferred_element_type=jnp.float32
    )
    mixed = (
        running
        - jnp.einsum("ij,sjd->sid", sin_block, shard_piece[1], preferred_element_type=jnp.float32)
    ) * dft_scale
    normed, norm_first_back = jax.vjp(layer_norm, stream + mixed, vec_float[0], vec_float[1])
    normed_low = normed.astype(jnp.bfloat16)
    pre_act = jnp.dot(normed_low, weight_first, preferred_element_type=jnp.float32) + bias_float
    activated, gelu_back = jax.vjp(gelu_tanh, pre_act)
    act_low = activated.astype(jnp.bfloat16)
    feed = jnp.dot(act_low, weight_second, preferred_element_type=jnp.float32) + vec_float[2]
    stream, norm_second_back = jax.vjp(layer_norm, normed + feed, vec_float[3], vec_float[4])
    saved = [(norm_first_back, normed_low, gelu_back, act_low, norm_second_back)]
    block_output = stream.astype(jnp.bfloat16)
    grad_now = cotangent.astype(jnp.float32)
    raw_grads = [None] * layers
    for layer_index in reversed(range(layers)):
        weight_first, weight_second, bias_low, vec_low = gathered[layer_index]
        norm_first_back, normed_low, gelu_back, act_low, norm_second_back = saved[layer_index]
        grad_sum2, grad_gain2, grad_shift2 = norm_second_back(grad_now)
        grad_z = grad_sum2.astype(jnp.bfloat16)
        grad_weight_second = jnp.einsum(
            "stf,std->fd", act_low, grad_z, preferred_element_type=jnp.float32
        )
        grad_bias_out = jnp.sum(grad_z.astype(jnp.float32), axis=(0, 1))
        grad_act = jnp.einsum(
            "std,fd->stf", grad_z, weight_second, preferred_element_type=jnp.float32
        )
        (grad_pre,) = gelu_back(grad_act)
        grad_pre_low = grad_pre.astype(jnp.bfloat16)
        grad_weight_first = jnp.einsum(
            "std,stf->df", normed_low, grad_pre_low, preferred_element_type=jnp.float32
        )
        grad_bias_in = jnp.sum(grad_pre_low.astype(jnp.float32), axis=(0, 1))
        grad_normed = (
            jnp.einsum(
                "stf,df->std", grad_pre_low, weight_first, preferred_element_type=jnp.float32
            )
            + grad_sum2
        )
        grad_sum1, grad_gain1, grad_shift1 = norm_first_back(grad_normed)
        grad_mix_low = grad_sum1.astype(jnp.bfloat16)
        add_shard_piece = lax.all_gather(grad_mix_low, BOTH[1], axis=1, tiled=True)
        add_piece_len = add_shard_piece.shape[1]
        add_cos_block, add_sin_block = dft_tables(
            my_rows, jnp.arange(add_piece_len, dtype=jnp.int32), seq_len
        )
        with_cos = jnp.einsum(
            "ij,sjd->sid", add_cos_block, add_shard_piece, preferred_element_type=jnp.float32
        )
        with_sin = (zeros_block, zeros_block)[1] - jnp.einsum(
            "ij,sjd->sid", add_sin_block, add_shard_piece, preferred_element_type=jnp.float32
        )
        with_cos, with_sin = (with_cos, with_sin)
        with_cos = (with_cos * dft_scale).astype(jnp.bfloat16)
        with_sin = (with_sin * dft_scale).astype(jnp.bfloat16)
        grad_halves = jnp.concatenate([with_cos, with_sin], axis=-1)
        grad_now = grad_sum1 + jnp.dot(grad_halves, table_back, preferred_element_type=jnp.float32)
        grad_vec = jnp.stack([grad_gain1, grad_shift1, grad_bias_out, grad_gain2, grad_shift2])
        layer_terms = (grad_weight_first, grad_weight_second, grad_bias_in, grad_vec)
        raw_grads[layer_index] = (
            lax.psum_scatter(layer_terms[0], BOTH, scatter_dimension=0, tiled=True),
            lax.psum_scatter(layer_terms[1], BOTH, scatter_dimension=1, tiled=True),
            lax.psum_scatter(layer_terms[2], BOTH, scatter_dimension=0, tiled=True),
            lax.psum_scatter(layer_terms[3], BOTH, scatter_dimension=1, tiled=True),
        )
    shard_w_in = jnp.stack([entry[0] for entry in raw_grads])
    shard_w_out = jnp.stack([entry[1] for entry in raw_grads])
    shard_b_in = jnp.stack([entry[2] for entry in raw_grads])
    shard_vec = jnp.stack([entry[3] for entry in raw_grads])
    local_squares = jnp.sum(shard_w_in * shard_w_in) + jnp.sum(shard_w_out * shard_w_out)
    local_squares = (
        local_squares + jnp.sum(shard_b_in * shard_b_in) + jnp.sum(shard_vec * shard_vec)
    )
    norm_value = jnp.sqrt(lax.psum(local_squares, BOTH))
    factor = clip_limit / jnp.maximum(norm_value, clip_limit)
    upd_w_in = adam_update(
        w_in, factor * shard_w_in, first_w_in, second_w_in, rate_matrix, STEP_COUNT
    )
    upd_w_out = adam_update(
        w_out, factor * shard_w_out, first_w_out, second_w_out, rate_matrix, STEP_COUNT
    )
    upd_b_in = adam_update(
        b_in, factor * shard_b_in, first_b_in, second_b_in, rate_vector, STEP_COUNT
    )
    upd_vec = adam_update(
        vec_params, factor * shard_vec, first_vec, second_vec, rate_vector, STEP_COUNT
    )
    return (
        block_output,
        grad_now,
        norm_value,
        upd_w_in[0],
        upd_w_in[1],
        upd_w_in[2],
        upd_w_out[0],
        upd_w_out[1],
        upd_w_out[2],
        upd_b_in[0],
        upd_b_in[1],
        upd_b_in[2],
        upd_vec[0],
        upd_vec[1],
        upd_vec[2],
    )


MESH = pl.DeviceIdType.MESH
F32 = jnp.float32
BF16 = jnp.bfloat16
NN = (((1,), (0,)), ((), ()))
NT = (((1,), (1,)), ((), ()))
TN = (((0,), (0,)), ((), ()))


def dot(a, b, dims=NN):
    return lax.dot_general(a, b, dims, preferred_element_type=F32)


class Sizes:
    def __init__(self, mesh, seqs, block, width, hidden):
        self.batch, self.seq = mesh.shape["batch"], mesh.shape["seq"]
        self.xs, self.ys, self.zs = self.batch // 2, 2, self.seq // 2
        self.devices = self.batch * self.seq
        self.seqs, self.block, self.width, self.hidden = seqs, block, width, hidden
        self.length = block * self.seq
        self.rows = width // self.devices
        self.slab = 2 * self.rows
        self.segment = self.zs * self.slab
        self.half = hidden // 2
        self.cols = 512
        self.chunks = self.half // self.cols
        self.parts = 2
        self.thin = self.cols // self.parts
        self.packed = width // self.seq
        self.tokens = seqs * block
        self.bias = hidden // self.devices

    def fits(self):
        return (
            self.batch == 4
            and self.seq % 2 == 0
            and self.width % self.devices == 0
            and self.slab % 16 == 0
            and self.packed % 32 == 0
            and self.block % 128 == 0
            and self.zs == 4
            and self.half % self.cols == 0
            and self.rows <= 128
            and self.bias <= 128
            and 5 * self.rows <= self.width
        )

    def owner(self, x, core, z, y):
        return (2 * x + core) * self.seq + 2 * z + y

    def place_owner(self):
        return [
            self.owner(x, core, z, y)
            for y in range(self.ys)
            for x in range(self.xs)
            for z in range(self.zs)
            for core in range(2)
        ]


def cos_sin(rows, columns, count):
    angle = (rows[:, None] * columns[None, :] % count) * (2.0 * math.pi / count)
    return np.cos(angle), np.sin(angle)


def host_tables(n):
    width, half = n.width, n.packed // 2
    owners = np.array(n.place_owner())
    order = (owners[:, None] * n.rows + np.arange(n.rows)[None, :]).reshape(-1)
    line = np.arange(width)
    cosine, sine = cos_sin(line, line, width)
    pack = np.zeros((width, width))
    unpack = np.zeros((width, width))
    for k in range(width // 2):
        device, inner = divmod(k, half)
        at_cos = device * n.packed + inner
        at_sin = at_cos + half
        pack[at_cos] = cosine[k]
        unpack[at_cos, k] = 1.0
        if k:
            unpack[at_cos, width - k] = 1.0
            pack[at_sin] = sine[k]
            unpack[at_sin, k] = -1.0
            unpack[at_sin, width - k] = 1.0
    pack[half] = cosine[width // 2]
    unpack[half, width // 2] = 1.0
    perm = np.zeros((width, width))
    perm[order, np.arange(width)] = 1.0
    positions = np.arange(n.length)
    by_length = np.stack(cos_sin(positions, positions, n.length))
    vec_mask = np.zeros((n.devices, width))
    vec_mask[np.repeat(owners, n.rows), np.arange(width)] = 1.0
    vec_spread = np.zeros((128, width))
    vec_spread[np.arange(width) % n.rows, np.arange(width)] = 1.0
    bias_spread = np.zeros((128, n.half))
    bias_spread[np.arange(n.half) % n.bias, np.arange(n.half)] = 1.0

    def low(a):
        return jnp.asarray(a.astype(np.float32).astype(ml_dtypes.bfloat16))

    return types.SimpleNamespace(
        tt_f=low(pack),
        by_length=low(by_length),
        un_f=low(unpack[:, order]),
        perm=low(perm),
        tt_b=low(pack[:, order]),
        un_b=low(unpack),
        vec_mask=jnp.asarray(vec_mask.astype(np.float32)),
        vec_spread=low(vec_spread),
        bias_spread=low(bias_spread),
    )


LOADS = dict(
    bias="bias_v",
    vec="vec_v",
    w1="w1_v",
    w2="w2_v",
    x="x_v",
    tt_f="tt_v",
    dy="dy_v",
    vec_spread="vec_spread_v",
    bias_spread="bias_spread_v",
    vec_mask="vec_mask_v",
    by_length="by_length_v",
    perm="perm_v",
    un_f="un_v",
    tt_b="tt_v",
    un_b="un_v",
)
LATER = ("tt_b", "un_b")
FORWARD_KINDS = (1, 1, 0, 0, 0, 3)
BACK_KINDS = (0, 5, 0, 5, 2, 1, 1, 5, 3, 5, 5, 4, 0)


def layer_kernel(n, names, *refs):
    r = types.SimpleNamespace(**dict(zip(names, refs)))
    batch_at, seq_at = lax.axis_index("batch"), lax.axis_index("seq")
    x, core = batch_at // 2, batch_at % 2
    z, y = seq_at // 2, seq_at % 2
    tokens, width, seg, slab = n.tokens, n.width, n.segment, n.slab
    started = []

    def aligned(at, by):
        return pl.multiple_of(at * by, by)

    def rows_of(at, by):
        return pl.ds(aligned(at, by), by)

    def remote(src, dst, send, recv, batch_to, seq_to):
        return pltpu.make_async_remote_copy(
            src_ref=src,
            dst_ref=dst,
            send_sem=send,
            recv_sem=recv,
            device_id=(batch_to, seq_to),
            device_id_type=MESH,
        )

    def go(copy):
        copy.start()
        started.append(copy)
        return copy

    def bytes_of(view, send, recv):
        return remote(view, view, send, recv, other_core, seq_at)

    other_core = 2 * x + 1 - core
    other_x = 2 * (1 - x) + core
    other_y = 2 * z + 1 - y

    def plane(k):
        return (seq_at + k) % n.seq

    def plane_from(k):
        return (seq_at + n.seq - k) % n.seq

    def across(k):
        return (batch_at + k) % n.batch

    def across_from(k):
        return (batch_at + n.batch - k) % n.batch

    loads = types.SimpleNamespace()
    for i, (name, held) in enumerate(LOADS.items()):
        load = pltpu.make_async_copy(getattr(r, name), getattr(r, held), r.load_sem.at[i])
        setattr(loads, name, load)
        if name not in LATER:
            load.start()

    everyone = [
        ((batch_at + i // n.seq) % n.batch, (seq_at + i % n.seq) % n.seq)
        for i in range(1, n.devices)
    ]
    barrier = pltpu.get_barrier_semaphore()
    for device in everyone:
        pl.semaphore_signal(barrier, inc=1, device_id=device, device_id_type=MESH)
    pl.semaphore_wait(barrier, n.devices - 1)

    loads.w1.wait()
    loads.w2.wait()
    weights = (r.w1_v, r.w2_v)
    give = pl.ds(aligned(1 - core, n.half), n.half)
    keep = pl.ds(aligned(core, n.half), n.half)
    core_rows = pl.ds(aligned(core, n.rows), n.rows)
    their_rows = pl.ds(aligned(1 - core, n.rows), n.rows)
    for m in range(2):
        remote(
            weights[m].at[:, give],
            r.stage.at[m, core_rows],
            r.swap_send,
            r.swap_recv,
            other_core,
            seq_at,
        ).start()
    swapped = bytes_of(r.stage.at[:, pl.ds(0, n.rows)], r.swap_send, r.swap_recv)

    def mix_start(t, source, table):
        y_ref, l_ref = r.y_buf.at[t], r.l_buf.at[t]
        y_ref[...] = dot(table[...], source, NT).astype(BF16)
        l_ref[seq_at] = y_ref[rows_of(seq_at, n.packed), :]

    def mix_send(t):
        y_ref, l_ref = r.y_buf.at[t], r.l_buf.at[t]
        for k in range(1, n.seq):
            remote(
                y_ref.at[rows_of(plane(k), n.packed)],
                l_ref.at[seq_at],
                r.mix_send.at[2 * t],
                r.mix_recv.at[2 * t],
                batch_at,
                plane(k),
            ).start()

    def mixed_bytes(i):
        into = (r.l_buf, r.r_buf)[i % 2].at[i // 2, pl.ds(0, n.seq - 1)]
        return bytes_of(into, r.mix_send.at[i], r.mix_recv.at[i])

    def mix_turn(t):
        l_ref, z_ref, r_ref = r.l_buf.at[t], r.z_buf.at[t], r.r_buf.at[t]
        mixed_bytes(2 * t).wait_recv()
        left = jnp.concatenate(
            [
                jnp.concatenate(
                    [l_ref[d, :, g * n.block : (g + 1) * n.block] for d in range(n.seq)], axis=1
                )
                for g in range(n.seqs)
            ],
            axis=0,
        )
        r.left[...] = left
        inner = lax.broadcasted_iota(jnp.int32, (n.seqs * n.packed, 1), 0) % n.packed
        first = (inner < n.packed // 2) | ((inner == n.packed // 2) & (seq_at == 0))
        scale = 1.0 / math.sqrt(n.length * n.width)
        for e in range(0, n.seq, 2):
            at = slice(e * n.block, (e + 2) * n.block)
            by_cos = dot(r.left[...], r.by_length_v[0, :, at])
            by_sin = dot(r.left[...], r.by_length_v[1, :, at])
            value = (jnp.where(first, by_cos, by_sin) * scale).astype(BF16)
            z_ref[e] = value[:, : n.block]
            z_ref[e + 1] = value[:, n.block :]
        for k in range(1, n.seq):
            remote(
                z_ref.at[plane(k)],
                r_ref.at[seq_at],
                r.mix_send.at[2 * t + 1],
                r.mix_recv.at[2 * t + 1],
                batch_at,
                plane(k),
            ).start()
        r_ref[seq_at] = z_ref[seq_at]

    def mix_finish(t, table):
        r_ref = r.r_buf.at[t]
        mixed_bytes(2 * t + 1).wait_recv()
        parts = [
            r_ref[:, g * n.packed : (g + 1) * n.packed, :].reshape(width, n.block)
            for g in range(n.seqs)
        ]
        r.mixed[...] = dot(jnp.concatenate(parts, axis=1), table[...], TN)

    loads.tt_f.wait()
    loads.x.wait()
    mix_start(0, r.x_v[...], r.tt_v)

    full = r.full
    mate_z = z + 1 - 2 * (z % 2)
    pair_z = z // 2
    inner = (z > 0) & (z < n.zs - 1)

    def line(to_z):
        return batch_at, 2 * to_z + y

    def seg_rows(sx, sy):
        return rows_of(sy * n.xs + sx, seg)

    def pair_rows(sx, sy, sp):
        return rows_of((sy * n.xs + sx) * 2 + sp, 2 * slab)

    def slab_rows(sx, sy, sz):
        return rows_of((sy * n.xs + sx) * n.zs + sz, slab)

    def peer(t):
        return (other_y_at, other_x_at)[t == 0]

    other_x_at = (other_x, seq_at)
    other_y_at = (batch_at, other_y)

    def away(t):
        return (1 - x, y) if t == 0 else (x, 1 - y)

    def turn_of(c):
        return FORWARD_KINDS[c] % 2

    def split(c):
        return FORWARD_KINDS[c] // 2 == 1

    def place(c):
        return c // n.chunks, c % n.chunks

    def stage_weights():
        for m in range(2):
            r.stage[m, core_rows, :] = weights[m][:, keep]
        swapped.wait_recv()
        for m in range(2):
            for q in range(n.chunks):
                full[m, q, slab_rows(x, y, z), :] = r.stage[
                    m, :, q * n.cols : (q + 1) * n.cols
                ].astype(BF16)

    def full_copy(c, at, send, recv, to):
        m, q = place(c)
        return remote(full.at[m, q, at], full.at[m, q, at], send.at[c], recv, *to)

    def rows_at(sx, sy, i):
        return (slab_rows(sx, sy, z), slab_rows(sx, sy, mate_z), pair_rows(sx, sy, 1 - pair_z))[i]

    def side_copy(c, i, sx, sy, first):
        t = turn_of(c)
        recv = r.first_recv.at[i, c] if first else r.second_recv.at[c]
        return full_copy(c, rows_at(sx, sy, i), r.side_send, recv, peer(t if first else 1 - t))

    def to_sides(c, i):
        if i == 0 or not split(c):
            side_copy(c, i, x, y, True).start()
        side_copy(c, i, x, y, False).start()

    def line_seg(c, far):
        return away(turn_of(c)) if far else (x, y)

    def own_to_mate(c, far):
        at = rows_at(*line_seg(c, far), 0)
        return full_copy(c, at, r.side_send, r.mate_recv.at[far, c], line(mate_z))

    def mate_arrives(c, far):
        at = rows_at(*line_seg(c, far), 1)
        full_copy(c, at, r.side_send, r.mate_recv.at[far, c], line(mate_z)).wait_recv()

    def pair_across(c, far):
        at = pair_rows(*line_seg(c, far), pair_z)
        return full_copy(c, at, r.inner_send, r.pair_recv.at[far, c], line(n.zs - 1 - z))

    def pair_out(c, far):
        at = rows_at(*line_seg(c, far), 2)
        return full_copy(c, at, r.inner_send, r.pair_recv.at[far, c], line(mate_z))

    def own_sides(c):
        to_sides(c, 0)

    def own_line(c):
        own_to_mate(c, 0).start()

    def from_mate(c, far):
        mate_arrives(c, far)

        @pl.when(inner)
        def _():
            pair_across(c, far).start()

    def from_pair(c, far):
        pair_out(c, far).wait_recv()

        @pl.when(inner)
        def _():
            pair_out(c, far).start()

    def mate_in(c):
        from_mate(c, 0)
        to_sides(c, 1)

    def pair_in(c):
        from_pair(c, 0)
        to_sides(c, 2)

    def pass_on(c, i):
        ax, ay = away(turn_of(c))
        if i == 0 or not split(c):
            side_copy(c, i, ax, ay, True).wait_recv()
        if split(c):
            if i == 0:
                own_to_mate(c, 1).start()
            else:
                (from_mate, from_pair)[i - 1](c, 1)
        side_copy(c, i, ax, ay, False).start()

    def slabs_of(c, count, send):
        m, q = place(c)
        return bytes_of(full.at[m, q, pl.ds(0, count * slab)], send.at[c], r.second_recv.at[c])

    def weights_here(c):
        slabs_of(c, 2 * n.zs, r.side_send).wait_recv()

    def small_tiles():
        loads.bias.wait()
        loads.vec.wait()
        tile = r.tile
        tile[...] = jnp.zeros(tile.shape, F32)
        for i in range(5):
            tile[i : i + 1, 0 : n.rows] = r.vec_v[i]
        tile[5:6, 0 : n.bias] = r.bias_v[...]
        small[batch_at, seq_at] = tile[...]
        for k in range(1, n.seq):
            small_copy(k, seq_at).start()

    def small_copy(k, at):
        return remote(
            r.tile,
            small.at[batch_at, at],
            r.small_send,
            r.small_recv,
            batch_at,
            plane(k),
        )

    def row_copy(k, at):
        return remote(
            small.at[batch_at],
            small.at[at],
            r.row_send,
            r.row_recv,
            across(k),
            seq_at,
        )

    small = r.small

    def tiles_bytes():
        return bytes_of(small.at[0, pl.ds(0, n.seq - 1)], r.small_send, r.small_recv)

    def rows_bytes():
        return bytes_of(small.at[pl.ds(0, n.batch - 1)], r.row_send, r.row_recv)

    def small_rows():
        tiles_bytes().wait_recv()
        for k in range(1, n.batch):
            row_copy(k, batch_at).start()

    half_owners = n.devices // 2
    bias_mask = (
        lax.broadcasted_iota(jnp.int32, (half_owners, n.half), 0)
        == lax.broadcasted_iota(jnp.int32, (half_owners, n.half), 1) // n.bias
    )

    def small_vectors():
        rows_bytes().wait_recv()
        for load in (loads.vec_spread, loads.bias_spread, loads.vec_mask):
            load.wait()
        for i in range(5):
            held = small[:, :, i, :].reshape(n.devices, 128).astype(BF16)
            spread = dot(held, r.vec_spread_v[...]) * r.vec_mask_v[...]
            r.vecs[i : i + 1, :] = jnp.sum(spread, axis=0, keepdims=True)
        held = small[pl.ds(core * (n.batch // 2), n.batch // 2), :, 5, :]
        held = held.reshape(half_owners, 128).astype(BF16)
        spread = jnp.where(bias_mask, dot(held, r.bias_spread_v[...]), 0.0)
        biases = jnp.sum(spread, axis=0, keepdims=True)
        for q in range(n.chunks):
            r.biases[q] = biases[:, q * n.cols : (q + 1) * n.cols]

    def place_inputs():
        loads.perm.wait()
        loads.dy.wait()
        r.x_place[...] = dot(r.x_v[...], r.perm_v[...])
        r.dy_place[...] = dot(r.dy_v[...], r.perm_v[...])

    def turn_forward():
        loads.by_length.wait()
        mix_turn(0)

    step = 32
    tall = 64
    mine, theirs = pl.ds(0, tokens), pl.ds(tokens, tokens)

    def row_loop(body):
        @pl.loop(0, tokens // tall, unroll=True)
        def _(i):
            body(pl.ds(pl.multiple_of(i * tall, tall), tall))

    def mean(v):
        return jnp.mean(v, axis=-1, keepdims=True)

    def first_norm(at):
        v = r.x_place[at, :] + r.mixed[at, :]
        centred = v - mean(v)
        scale = lax.rsqrt(mean(centred * centred) + norm_epsilon)
        unit = centred * scale
        h = unit * r.vecs[0:1, :] + r.vecs[1:2, :]
        r.unit1[at, :] = unit
        r.scale1[at, :] = jnp.broadcast_to(scale, (tall, 128))
        r.h[at, :] = h
        r.h_low[at, :] = h.astype(BF16)

    def swap(i, src, dst):
        return remote(src, dst, r.core_send.at[i], r.core_recv.at[i], other_core, seq_at)

    def swap_h():
        return swap(0, r.h_low.at[mine], r.h_low.at[theirs])

    def norm_forward():
        loads.un_f.wait()
        mix_finish(0, r.un_v)
        loads.tt_b.start()
        loads.un_b.start()
        row_loop(first_norm)
        go(swap_h())

    root = math.sqrt(2.0 / math.pi)

    lifted_parts = []

    def lift(q):
        if not lifted_parts:
            swap_h().wait_recv()
        lifted_parts.append(q)
        weights_here(q)
        r.lift[...] = dot(r.h_low[...], full[0, q]) + r.biases[q]

        @pl.loop(0, 2 * tokens // step)
        def _(i):
            at = pl.ds(pl.multiple_of(i * step, step), step)
            u = r.lift[at, :]
            square = u * u
            bent = jnp.tanh(u * (root + (root * 0.044715) * square))
            half_up = 0.5 + 0.5 * bent
            r.act[q, at, :] = (u * half_up).astype(BF16)
            r.slope[q, at, :] = half_up + (u * (1.0 - bent * bent)) * (
                0.5 * root + (1.5 * root * 0.044715) * square
            )

    gathered_parts = []

    def swap_ff():
        return swap(1, r.part_low, r.part_in)

    def drop(q):
        weights_here(n.chunks + q)
        gathered_parts.append(q)
        for half in (theirs, mine):
            part = dot(r.act[q, half, :], full[1, q], NT)
            part = r.total[half, :] + part if len(gathered_parts) > 1 else part
            if len(gathered_parts) == n.chunks and half is theirs:
                r.part_low[...] = part.astype(BF16)
                go(swap_ff())
            else:
                r.total[half, :] = part

    def send_forward():
        mix_send(0)

    forward_steps = (
        (send_forward,), (stage_weights,), (own_sides, 0), (own_sides, 1), (own_line, 1),
        (own_sides, 4), (own_sides, 2), (own_line, 0), (own_line, 2), (place_inputs,),
        (own_sides, 3), (own_sides, 5), (small_tiles,), (own_line, 4), (own_line, 5),
        (pass_on, 0, 0), (mate_in, 1), (mate_in, 0), (pass_on, 3, 0), (mate_in, 2),
        (own_line, 3), (mate_in, 4), (pass_on, 1, 0), (small_rows,), (pass_on, 5, 0),
        (pass_on, 0, 1), (pass_on, 4, 0), (pass_on, 2, 0), (pair_in, 1), (mate_in, 3),
        (pair_in, 0), (pair_in, 2), (mate_in, 5), (pass_on, 1, 1), (pass_on, 4, 1),
        (small_vectors,), (turn_forward,), (pass_on, 2, 1), (pass_on, 1, 2), (pair_in, 3),
        (pass_on, 5, 1), (pass_on, 2, 2), (pass_on, 3, 1), (pair_in, 4), (pair_in, 5),
        (pass_on, 0, 2), (norm_forward,), (pass_on, 5, 2), (pass_on, 4, 2), (lift, 1),
        (lift, 2), (pass_on, 3, 2), (lift, 0), (drop, 1), (drop, 2), (drop, 0),
    )
    for task, *which in forward_steps:
        task(*which)
    swap_ff().wait_recv()

    def second_norm(at):
        v = (
            r.h[at, :]
            + r.total[at, :]
            + r.part_in[at, :].astype(F32)
            + r.vecs[2:3, :]
        )
        centred = v - mean(v)
        scale = lax.rsqrt(mean(centred * centred) + norm_epsilon)
        unit = centred * scale
        gain = r.vecs[3:4, :]
        r.h[at, :] = unit
        r.out_low[at, :] = (unit * gain + r.vecs[4:5, :]).astype(BF16)
        du = r.dy_place[at, :] * gain
        dv = scale * (du - mean(du) - unit * mean(du * unit))
        r.dr2[at, :] = dv
        r.dz[at, :] = dv.astype(BF16)

    row_loop(second_norm)
    swap_dz = go(swap(2, r.dz.at[mine], r.dz.at[theirs]))
    swap_dz.wait_recv()

    acc, out_low = r.acc, r.give

    pieces = grad_pieces(n)

    def wide(c):
        slot, start, width_of = pieces[c]
        m, q = slot // (n.chunks * n.parts), slot % (n.chunks * n.parts)
        return 1 - m, q // n.parts, pl.ds((q % n.parts) * n.thin + start, width_of)

    def held(c, at=slice(None), lead=()):
        slot, start, width_of = pieces[c]
        return (slot, *lead, at, pl.ds(start, width_of))

    def grad_copy(c, at, into, recv, to):
        return remote(out_low.at[held(c, at)], into, r.grad_send, recv, *to)

    def back_turn(c):
        return BACK_KINDS[c] % 2

    def back_mode(c):
        return BACK_KINDS[c] // 2

    def back_slot(c):
        return [d for d, kind in enumerate(BACK_KINDS) if kind // 2 == back_mode(c)].index(c)

    def copy_diagonal(c):
        at = seg_rows(1 - x, 1 - y)
        return grad_copy(c, at, r.in_diagonal.at[held(c)], r.diagonal_recv.at[c], peer(1 - back_turn(c)))

    def copy_near(c):
        t = 1 - back_turn(c)
        into = r.in_sides.at[held(c, lead=(0,))]
        return grad_copy(c, seg_rows(*away(t)), into, r.sides_recv.at[c], peer(t))

    def copy_side(c):
        t = back_turn(c)
        into = r.in_sides.at[held(c, lead=(1,))]
        return grad_copy(c, seg_rows(*away(t)), into, r.sides_recv.at[c], peer(t))

    def back_seg(c, far):
        return away(back_turn(c)) if far else (x, y)

    def line_into(c, far, i):
        if far:
            into = (r.far_mate, r.far_pair, r.far_across)[i]
            return into.at[back_slot(c), :, pl.ds(0, pieces[c][2])]
        into, lead = ((r.in_end, (0,)), (r.in_pair, ()), (r.in_across, ()))[i]
        return into.at[held(c, lead=lead)]

    def line_copy(c, at, far, i, to):
        if far:
            recv = r.far_recv.at[i, back_slot(c)]
        else:
            recv = (r.end_recv, r.pair_in_recv, r.across_recv)[i].at[c]
        return grad_copy(c, at, line_into(c, far, i), recv, to)

    def copy_mate(c, far):
        at = slab_rows(*back_seg(c, far), mate_z)
        return line_copy(c, at, far, 0, line(mate_z))

    def copy_pair_in(c, far):
        at = pair_rows(*back_seg(c, far), 1 - pair_z)
        return line_copy(c, at, far, 1, line(mate_z))

    def copy_pair_across(c, far):
        at = pair_rows(*back_seg(c, far), 1 - pair_z)
        return line_copy(c, at, far, 2, line(n.zs - 1 - z))

    def copy_far(c):
        t = back_turn(c)
        at = slab_rows(*away(t), z)
        return grad_copy(c, at, r.in_end.at[held(c, lead=(1,))], r.end_recv.at[c], peer(t))

    def copy_direct(c, d):
        to_z = (z + d) % n.zs
        at = slab_rows(x, y, to_z)
        return grad_copy(c, at, r.in_end.at[held(c, lead=(d - 1,))], r.end_recv.at[c], line(to_z))

    def round_out(c, at, *more):
        value = acc[held(c, at)]
        for ref in more:
            value = value + ref[...].astype(F32)
        out_low[held(c, at)] = value.astype(BF16)

    def grad_product(c):
        m, q, at = wide(c)
        if m:
            acc[held(c)] = dot(r.dz[...], r.act[q, :, at], TN)
        else:
            acc[held(c)] = dot(r.h_low[...], r.dpre[q, :, at], TN)
        round_out(c, seg_rows(1 - x, 1 - y))
        copy_diagonal(c).start()
        round_out(c, seg_rows(*away(1 - back_turn(c))))
        copy_near(c).start()

    def line_start(c, far):
        @pl.when(jnp.logical_not(inner))
        def _():
            sx, sy = back_seg(c, far)
            round_out(c, pair_rows(sx, sy, 1 - pair_z))
            copy_pair_in(c, far).start()
            round_out(c, slab_rows(sx, sy, mate_z))
            copy_mate(c, far).start()

    def grad_side(c):
        copy_diagonal(c).wait_recv()
        at = seg_rows(*away(back_turn(c)))
        if back_mode(c) == 1:
            acc[held(c, at)] = acc[held(c, at)] + r.in_diagonal[held(c)].astype(F32)
            line_start(c, 1)
        else:
            round_out(c, at, r.in_diagonal.at[held(c)])
            copy_side(c).start()

    def grad_line(c):
        sides = 1 if back_mode(c) == 1 else 2
        both = r.in_sides.at[held(c, lead=(pl.ds(0, sides),))]
        bytes_of(both, r.grad_send, r.sides_recv.at[c]).wait_recv()
        more = sum(r.in_sides[held(c, lead=(i,))].astype(F32) for i in range(sides))
        at = seg_rows(x, y)
        acc[held(c, at)] = acc[held(c, at)] + more
        if back_mode(c) == 2:
            for d in range(1, n.zs):
                round_out(c, slab_rows(x, y, (z + d) % n.zs))
                copy_direct(c, d).start()
        else:
            line_start(c, 0)

    def fars(c):
        return range((1, 2, 0)[back_mode(c)])

    def grad_across(c):
        for far in fars(c):

            @pl.when(inner)
            def _(far=far):
                copy_pair_in(c, far).wait_recv()
                at = pair_rows(*back_seg(c, far), 1 - pair_z)
                round_out(c, at, line_into(c, far, 1))
                copy_pair_across(c, far).start()

    def grad_out(c):
        for far in fars(c):

            @pl.when(inner)
            def _(far=far):
                copy_pair_across(c, far).wait_recv()
                sx, sy = back_seg(c, far)
                at = pair_rows(sx, sy, pair_z)
                acc[held(c, at)] = acc[held(c, at)] + line_into(c, far, 2)[...].astype(F32)
                round_out(c, slab_rows(sx, sy, mate_z))
                copy_mate(c, far).start()

    def grad_far(c):
        if back_mode(c) == 1:
            copy_mate(c, 1).wait_recv()
            round_out(c, slab_rows(*away(back_turn(c)), z), line_into(c, 1, 0))
            copy_far(c).start()

    grads_out = (r.g1, r.g2)
    r.squares[...] = jnp.zeros((8, 128), F32)

    def squares_of(v):
        v = v * v
        v = jnp.sum(v.reshape(v.shape[0] // 8, 8, v.shape[1]), axis=0)
        return sum(v[:, i : i + 128] for i in range(0, v.shape[1], 128))

    def copy_back(c):
        return remote(
            r.final.at[held(c, their_rows)],
            r.final_in.at[held(c)],
            r.back_send,
            r.back_recv,
            other_core,
            seq_at,
        )

    def grad_end(c):
        m, q, at = wide(c)
        value = acc[held(c, slab_rows(x, y, z))]
        ends = back_mode(c) + 1
        all_ends = r.in_end.at[held(c, lead=(pl.ds(0, ends),))]
        bytes_of(all_ends, r.grad_send, r.end_recv.at[c]).wait_recv()
        for i in range(ends):
            value = value + r.in_end[held(c, lead=(i,))].astype(F32)
        r.squares[...] += squares_of(value)
        r.final[held(c)] = value
        own_at = pl.ds(aligned(core, n.half) + q * n.cols + at.start, at.size)
        grads_out[m][:, own_at] = r.final[held(c, core_rows)]
        copy_back(c).start()

    back_parts = []

    def slope_back(q):
        r.lift[...] = dot(r.dz[...], full[1, q])
        r.bias_sum[q] = jnp.zeros((8, n.cols), F32)

        @pl.loop(0, 2 * tokens // step)
        def _(i):
            at = pl.ds(pl.multiple_of(i * step, step), step)
            low = (r.lift[at, :] * r.slope[q, at, :]).astype(BF16)
            r.dpre[q, at, :] = low
            r.bias_sum[q] += jnp.sum(low.astype(F32).reshape(step // 8, 8, n.cols), axis=0)

        back_parts.append(q)
        for half in (theirs, mine):
            part = dot(r.dpre[q, half, :], full[0, q], NT)
            part = r.total[half, :] + part if len(back_parts) > 1 else part
            if len(back_parts) == n.chunks and half is theirs:
                r.part_low2[...] = part.astype(BF16)
                go(swap_dh())
            else:
                r.total[half, :] = part

    def swap_dh():
        return swap(3, r.part_low2, r.part_in2)

    def first_norm_back(at):
        dh = r.total[at, :] + r.part_in2[at, :].astype(F32) + r.dr2[at, :]
        unit = r.unit1[at, :]
        r.x_place[at, :] = dh
        du = dh * r.vecs[0:1, :]
        dv = r.scale1[at, 0:1] * (du - mean(du) - unit * mean(du * unit))
        low = dv.astype(BF16)
        r.dm[at, :] = low
        r.rest[at, :] = (dv - low.astype(F32)).astype(BF16)

    def norm_back():
        swap_dh().wait_recv()
        row_loop(first_norm_back)
        loads.tt_b.wait()
        mix_start(1, r.dm[...], r.tt_v)
        mix_send(1)

    def thirds(v):
        high = v.astype(BF16)
        left = v - high.astype(F32)
        mid = left.astype(BF16)
        return high, mid, (left - mid.astype(F32)).astype(BF16)

    def small_gather(v, spread):
        return sum(dot(part, spread, NT) for part in thirds(v))

    def row_sums(k):
        return remote(
            r.small_out.at[across(k)],
            r.small_in.at[k - 1],
            r.row_send2,
            r.row_recv2,
            across(k),
            seq_at,
        )

    def tile_sums(k):
        return remote(
            r.small_mid.at[plane(k)],
            r.small_last.at[k - 1],
            r.small_send2,
            r.small_recv2,
            batch_at,
            plane(k),
        )

    row_sums_bytes = bytes_of(r.small_in, r.row_send2, r.row_recv2)
    tile_sums_bytes = bytes_of(r.small_last, r.small_send2, r.small_recv2)

    def fold(v):
        return jnp.sum(v.reshape(tall // 8, 8, width), axis=0)

    def vector_sums(at):
        dh, dy = r.x_place[at, :], r.dy_place[at, :]
        r.sums[0] += fold(dh * r.unit1[at, :])
        r.sums[1] += fold(dh)
        r.sums[2] += fold(r.dz[at, :].astype(F32))
        r.sums[3] += fold(dy * r.h[at, :])
        r.sums[4] += fold(dy)

    def small_grads():
        r.sums[...] = jnp.zeros(r.sums.shape, F32)
        row_loop(vector_sums)
        for i in range(5):
            line_sum = jnp.sum(r.sums[i], axis=0, keepdims=True)
            tiles = small_gather(line_sum * r.vec_mask_v[...], r.vec_spread_v[...])
            r.small_out[:, :, i, :] = tiles.reshape(n.batch, n.seq, 128)
        line_sum = jnp.concatenate(
            [jnp.sum(r.bias_sum[q], axis=0, keepdims=True) for q in range(n.chunks)], axis=1
        )
        tiles = small_gather(jnp.where(bias_mask, line_sum, 0.0), r.bias_spread_v[...])
        r.small_out[:, :, 5:8, :] = jnp.zeros((n.batch, n.seq, 3, 128), F32)
        r.small_out[pl.ds(core * (n.batch // 2), n.batch // 2), :, 5, :] = tiles.reshape(
            n.batch // 2, n.seq, 128
        )
        for k in range(1, n.batch):
            row_sums(k).start()

    def small_rows_back():
        value = r.small_out[batch_at]
        row_sums_bytes.wait_recv()
        for k in range(1, n.batch):
            value = value + r.small_in[k - 1]
        r.small_mid[...] = value
        for k in range(1, n.seq):
            tile_sums(k).start()

    def small_end():
        value = r.small_mid[seq_at]
        tile_sums_bytes.wait_recv()
        for k in range(1, n.seq):
            value = value + r.small_last[k - 1]
        r.g_small[...] = value

    def turn_back():
        mix_turn(1)

    def outputs():
        r.out[...] = dot(r.out_low[...], r.perm_v[...], NT).astype(BF16)
        r.dx[...] = dot(r.dm[...], r.perm_v[...], NT) + dot(r.rest[...], r.perm_v[...], NT)

    def mix_back():
        loads.un_b.wait()
        mix_finish(1, r.un_v)
        r.dx[...] = r.dx[...] + r.mixed[...]

    for task, *which in (
        (grad_product, 3), (grad_product, 4), (slope_back, 2), (grad_product, 10),
        (slope_back, 0), (grad_side, 4), (grad_side, 3), (slope_back, 1), (grad_line, 4),
        (grad_product, 2), (grad_product, 8), (grad_line, 3), (norm_back,), (grad_across, 3),
        (grad_side, 10), (grad_product, 5), (grad_side, 2), (small_grads,), (grad_product, 6),
        (grad_side, 8), (grad_line, 8), (outputs,), (grad_product, 0), (grad_across, 4),
        (grad_product, 12), (grad_line, 10), (grad_line, 2), (grad_out, 3), (turn_back,),
        (grad_side, 0), (grad_across, 10), (grad_product, 9), (grad_side, 12), (grad_side, 6),
        (grad_out, 10), (grad_line, 0), (grad_across, 2), (grad_side, 5), (grad_out, 4),
        (grad_across, 8), (grad_product, 1), (grad_far, 3), (grad_side, 9), (grad_product, 11),
        (grad_line, 6), (grad_across, 6), (grad_line, 12), (small_rows_back,), (grad_across, 0),
        (grad_product, 7), (grad_line, 5), (grad_side, 11), (grad_line, 9), (grad_far, 4),
        (grad_side, 1), (grad_out, 8), (grad_across, 5), (grad_across, 9), (grad_out, 6),
        (grad_side, 7), (grad_out, 0), (grad_across, 12), (grad_line, 1), (grad_out, 2),
        (grad_out, 9), (grad_across, 1), (grad_far, 8), (grad_far, 0), (grad_far, 10),
        (grad_end, 0), (grad_out, 5), (mix_back,), (grad_out, 12), (grad_line, 11),
        (grad_line, 7), (small_end,), (grad_far, 5), (grad_across, 7), (grad_across, 11),
        (grad_far, 6), (grad_out, 1), (grad_end, 6), (grad_far, 2), (grad_far, 12),
        (grad_end, 2), (grad_far, 1), (grad_far, 9), (grad_out, 7), (grad_end, 10),
        (grad_end, 4), (grad_far, 7), (grad_end, 1), (grad_end, 5), (grad_end, 8),
        (grad_out, 11), (grad_end, 12), (grad_far, 11), (grad_end, 9), (grad_end, 3),
        (grad_end, 11), (grad_end, 7),
    ):
        task(*which)

    squares = r.squares[...] + r.g_small[...] * r.g_small[...]
    r.norm_own[...] = jnp.sum(squares, axis=0, keepdims=True)
    r.norm_all[batch_at * n.seq + seq_at] = r.norm_own[...]

    for device in everyone:
        remote(
            r.norm_own,
            r.norm_all.at[batch_at * n.seq + seq_at],
            r.norm_send,
            r.norm_recv,
            *device,
        ).start()
    back_bytes = bytes_of(r.final_in, r.back_send, r.back_recv)
    back_bytes.wait_recv()
    for c in range(len(pieces)):
        m, q, at = wide(c)
        their_at = pl.ds(aligned(1 - core, n.half) + q * n.cols + at.start, at.size)
        grads_out[m][:, their_at] = r.final_in[held(c)]
    norm_bytes = bytes_of(r.norm_all.at[pl.ds(0, n.devices - 1)], r.norm_send, r.norm_recv)
    norm_bytes.wait_recv()
    squares = jnp.sum(r.norm_all[...].reshape(n.devices, 128), axis=0, keepdims=True)
    whole = jnp.sum(squares, axis=1, keepdims=True)
    r.norm[...] = jnp.broadcast_to(jnp.sqrt(whole), (8, 128))

    for copy in started:
        copy.wait_send()
    for copy in (swapped, tiles_bytes(), rows_bytes(), *(mixed_bytes(i) for i in range(4))):
        copy.wait_send()
    for copy in (row_sums_bytes, tile_sums_bytes, back_bytes, norm_bytes):
        copy.wait_send()
    for c in range(2 * n.chunks):
        slabs_of(c, 2 * n.zs + (3 if split(c) else n.zs + 1), r.side_send).wait_send()

    @pl.when(inner)
    def _():
        for c in range(2 * n.chunks):
            slabs_of(c, 8 if split(c) else 4, r.inner_send).wait_send()

    moved = 2 * n.zs + n.zs + 3
    bytes_of(out_low.at[:, pl.ds(0, moved * slab)], r.grad_send, r.sides_recv.at[0]).wait_send()


def grad_pieces(n):
    slots = 2 * n.chunks * n.parts
    halved = len(BACK_KINDS) - slots
    whole = [(slot, 0, n.thin) for slot in range(slots - halved)]
    thin = n.thin // 2
    return whole + [(slot, i * thin, thin) for slot in range(slots - halved, slots) for i in range(2)]


def run_layer(n, x, dy, w1, w2, bias, vec):
    tables = host_tables(n)
    tokens, width, cols, q = n.tokens, n.width, n.cols, n.chunks
    grads = 2 * q * n.parts
    splits = max(1, sum(kind // 2 == 1 for kind in BACK_KINDS))
    dma = pltpu.SemaphoreType.DMA
    vmem = pltpu.VMEM
    inputs = dict(bias=bias, vec=vec, x=x, dy=dy, w1=w1, w2=w2)
    inputs.update({name: getattr(tables, name) for name in LOADS if name not in inputs})
    outputs = dict(
        out=((tokens, width), BF16),
        dx=((tokens, width), F32),
        g1=((n.rows, n.hidden), F32),
        g2=((n.rows, n.hidden), F32),
        g_small=((8, 128), F32),
        norm=((8, 128), F32),
    )
    scratch = {held: vmem(inputs[name].shape, inputs[name].dtype) for name, held in LOADS.items()}
    scratch.update(
        load_sem=dma((len(LOADS),)),
        stage=vmem((2, n.slab, n.half), F32),
        swap_send=dma,
        swap_recv=dma,
        tile=vmem((8, 128), F32),
        small=vmem((n.batch, n.seq, 8, 128), F32),
        small_send=dma,
        small_recv=dma,
        row_send=dma,
        row_recv=dma,
        y_buf=vmem((2, width, tokens), BF16),
        l_buf=vmem((2, n.seq, n.packed, tokens), BF16),
        left=vmem((n.seqs * n.packed, n.length), BF16),
        z_buf=vmem((2, n.seq, n.seqs * n.packed, n.block), BF16),
        r_buf=vmem((2, n.seq, n.seqs * n.packed, n.block), BF16),
        mix_send=dma((4,)),
        mix_recv=dma((4,)),
        mixed=vmem((tokens, width), F32),
        full=vmem((2, q, width, cols), BF16),
        side_send=dma((2 * q,)),
        inner_send=dma((2 * q,)),
        mate_recv=dma((2, 2 * q)),
        pair_recv=dma((2, 2 * q)),
        first_recv=dma((3, 2 * q)),
        second_recv=dma((2 * q,)),
        x_place=vmem((tokens, width), F32),
        dy_place=vmem((tokens, width), F32),
        vecs=vmem((8, width), F32),
        biases=vmem((q, 1, cols), F32),
        unit1=vmem((tokens, width), F32),
        scale1=vmem((tokens, 128), F32),
        h=vmem((tokens, width), F32),
        h_low=vmem((2 * tokens, width), BF16),
        core_send=dma((4,)),
        core_recv=dma((4,)),
        total=vmem((2 * tokens, width), F32),
        act=vmem((q, 2 * tokens, cols), BF16),
        lift=vmem((2 * tokens, cols), F32),
        slope=vmem((q, 2 * tokens, cols), F32),
        part_low=vmem((tokens, width), BF16),
        part_low2=vmem((tokens, width), BF16),
        part_in=vmem((tokens, width), BF16),
        part_in2=vmem((tokens, width), BF16),
        sums=vmem((5, 8, width), F32),
        out_low=vmem((tokens, width), BF16),
        dr2=vmem((tokens, width), F32),
        dz=vmem((2 * tokens, width), BF16),
        acc=vmem((grads, width, n.thin), F32),
        give=vmem((grads, width, n.thin), BF16),
        in_diagonal=vmem((grads, n.segment, n.thin), BF16),
        in_sides=vmem((grads, 2, n.segment, n.thin), BF16),
        in_end=vmem((grads, n.zs - 1, n.slab, n.thin), BF16),
        in_pair=vmem((grads, 2 * n.slab, n.thin), BF16),
        in_across=vmem((grads, 2 * n.slab, n.thin), BF16),
        far_mate=vmem((splits, n.slab, n.thin), BF16),
        far_pair=vmem((splits, 2 * n.slab, n.thin), BF16),
        far_across=vmem((splits, 2 * n.slab, n.thin), BF16),
        grad_send=dma,
        diagonal_recv=dma((len(BACK_KINDS),)),
        sides_recv=dma((len(BACK_KINDS),)),
        end_recv=dma((len(BACK_KINDS),)),
        pair_in_recv=dma((len(BACK_KINDS),)),
        across_recv=dma((len(BACK_KINDS),)),
        far_recv=dma((3, splits)),
        bias_sum=vmem((q, 8, cols), F32),
        dpre=vmem((q, 2 * tokens, cols), BF16),
        dm=vmem((tokens, width), BF16),
        rest=vmem((tokens, width), BF16),
        small_out=vmem((n.batch, n.seq, 8, 128), F32),
        small_in=vmem((n.batch - 1, n.seq, 8, 128), F32),
        row_send2=dma,
        row_recv2=dma,
        small_mid=vmem((n.seq, 8, 128), F32),
        small_last=vmem((n.seq - 1, 8, 128), F32),
        small_send2=dma,
        small_recv2=dma,
        final=vmem((grads, n.slab, n.thin), F32),
        final_in=vmem((grads, n.rows, n.thin), F32),
        back_send=dma,
        back_recv=dma,
        squares=vmem((8, 128), F32),
        norm_own=vmem((1, 128), F32),
        norm_all=vmem((n.devices, 1, 128), F32),
        norm_send=dma,
        norm_recv=dma,
    )
    names = tuple(inputs) + tuple(outputs) + tuple(scratch)
    in_vmem = pl.BlockSpec(memory_space=pltpu.VMEM)
    anywhere = pl.BlockSpec(memory_space=pl.ANY)
    values = pl.pallas_call(
        functools.partial(layer_kernel, n, names),
        out_shape=[vmem(*shape) for shape in outputs.values()],
        in_specs=[anywhere if name in LOADS else in_vmem for name in inputs],
        out_specs=[in_vmem] * len(outputs),
        scratch_shapes=list(scratch.values()),
        compiler_params=pltpu.CompilerParams(
            collective_id=0, has_side_effects=True, vmem_limit_bytes=58 * 2**20
        ),
        name="fused_layer",
    )(*inputs.values())
    return types.SimpleNamespace(**dict(zip(outputs, values)))


def adam_kernel(n, names, *refs):
    r = types.SimpleNamespace(**dict(zip(names, refs)))
    passed = [
        pltpu.make_async_copy(r.out, r.out_there, r.sem.at[0]),
        pltpu.make_async_copy(r.dx, r.dx_there, r.sem.at[1]),
    ]
    for copy in passed:
        copy.start()
    norm_value = r.norm[0:1, 0:1]
    r.norm_out[...] = norm_value
    factor = clip_limit / jnp.maximum(norm_value, clip_limit)
    lanes = n.cols

    def update(gradient, given, made, at, rate):
        weight, first, second = (ref[at] for ref in given)
        new = adam_update(weight, factor * gradient, first, second, rate, STEP_COUNT)
        for ref, value in zip(made, new):
            ref[at] = value

    weight_in, weight_out = refs[4:7], refs[7:10]
    made_in, made_out = refs[19:22], refs[22:25]

    @pl.loop(0, n.hidden // lanes)
    def _(i):
        at = (slice(None), pl.ds(pl.multiple_of(i * lanes, lanes), lanes))
        update(r.g1[at], weight_in, made_in, at, rate_matrix)
        update(r.g2[at], weight_out, made_out, at, rate_matrix)

    update(r.g_small[5:6, 0 : n.bias], refs[10:13], refs[25:28], ..., rate_vector)
    for i in range(5):
        update(r.g_small[i : i + 1, 0 : n.rows], refs[13:16], refs[28:31], i, rate_vector)
    for copy in passed:
        copy.wait()


def run_adam(n, got, given):
    f32 = functools.partial(jax.ShapeDtypeStruct, dtype=F32)
    matrix, bias, vec = f32((n.rows, n.hidden)), f32((1, n.bias)), f32((5, 1, n.rows))
    inputs = dict(g1=got.g1, g2=got.g2, g_small=got.g_small, norm=got.norm)
    inputs.update({chr(97 + i): array for i, array in enumerate(given)})
    inputs.update(out=got.out, dx=got.dx)
    outputs = dict(norm_out=f32((1, 1)))
    outputs.update({chr(110 + i): matrix for i in range(6)})
    outputs.update({chr(65 + i): bias for i in range(3)})
    outputs.update({chr(70 + i): vec for i in range(3)})
    outputs.update(
        out_there=jax.ShapeDtypeStruct(got.out.shape, BF16),
        dx_there=jax.ShapeDtypeStruct(got.dx.shape, F32),
    )
    names = tuple(inputs) + tuple(outputs) + ("sem",)
    in_vmem = pl.BlockSpec(memory_space=pltpu.VMEM)
    anywhere = pl.BlockSpec(memory_space=pl.ANY)
    return pl.pallas_call(
        functools.partial(adam_kernel, n, names),
        out_shape=list(outputs.values()),
        in_specs=[in_vmem] * (len(inputs) - 2) + [anywhere] * 2,
        out_specs=[in_vmem] * (len(outputs) - 2) + [anywhere] * 2,
        scratch_shapes=[pltpu.SemaphoreType.DMA((2,))],
        compiler_params=pltpu.CompilerParams(vmem_limit_bytes=32 * 2**20),
        name="adam",
    )(*inputs.values())


def turned(a):
    return jnp.swapaxes(a[0], 0, 1)


def lined(a):
    return jnp.transpose(a, (1, 0, 2))


def fused_layer(
    n,
    activations,
    cotangent,
    w_in,
    w_out,
    b_in,
    vec_params,
    first_w_in,
    second_w_in,
    first_w_out,
    second_w_out,
    first_b_in,
    second_b_in,
    first_vec,
    second_vec,
):
    got = run_layer(
        n,
        activations.reshape(n.tokens, n.width),
        cotangent.reshape(n.tokens, n.width),
        w_in[0],
        turned(w_out),
        b_in,
        lined(vec_params),
    )
    given = (
        *(a[0] for a in (w_in, first_w_in, second_w_in)),
        *(turned(a) for a in (w_out, first_w_out, second_w_out)),
        *(b_in, first_b_in, second_b_in),
        *(lined(a) for a in (vec_params, first_vec, second_vec)),
    )
    norm_value, *made, out, dx = run_adam(n, got, given)
    return (
        out.reshape(activations.shape),
        dx.reshape(activations.shape),
        norm_value.reshape(()),
        *(a[None] for a in made[:3]),
        *(jnp.swapaxes(a, 0, 1)[None] for a in made[3:6]),
        *made[6:9],
        *(lined(a) for a in made[9:]),
    )


def local_layer(mesh, activations, cotangent, w_in, *rest):
    seqs, block, width = activations.shape
    n = Sizes(mesh, seqs, block, width, w_in.shape[2])
    if w_in.shape[0] == 1 and n.fits():
        return fused_layer(n, activations, cotangent, w_in, *rest)
    return general_layer(activations, cotangent, w_in, *rest)


BOTH = ("batch", "seq")


def solution(mesh):
    in_specs = (
        P(*BOTH, None),
        P(*BOTH, None),
        P(None, BOTH, None),
        P(None, None, BOTH),
        P(None, BOTH),
        P(None, None, BOTH),
        P(None, BOTH, None),
        P(None, BOTH, None),
        P(None, None, BOTH),
        P(None, None, BOTH),
        P(None, BOTH),
        P(None, BOTH),
        P(None, None, BOTH),
        P(None, None, BOTH),
    )
    out_specs = (
        P(*BOTH, None),
        P(*BOTH, None),
        P(),
        P(None, BOTH, None),
        P(None, BOTH, None),
        P(None, BOTH, None),
        P(None, None, BOTH),
        P(None, None, BOTH),
        P(None, None, BOTH),
        P(None, BOTH),
        P(None, BOTH),
        P(None, BOTH),
        P(None, None, BOTH),
        P(None, None, BOTH),
        P(None, None, BOTH),
    )
    return jax.shard_map(
        functools.partial(local_layer, mesh), mesh=mesh, in_specs=in_specs, out_specs=out_specs, check_vma=False)
```

```python
import functools
import math
import types

import jax
import jax.numpy as jnp
import ml_dtypes
import numpy as np
from jax import lax
from jax.experimental import pallas as pl
from jax.experimental.pallas import tpu as pltpu
from jax.sharding import PartitionSpec as P

STEP_COUNT = 10


beta_first = 0.5
beta_second = 0.5
rate_matrix = 0.03
rate_vector = 0.2
weight_decay = 0.01
adam_epsilon = 1e-08
norm_epsilon = 1e-06
clip_limit = 1.0


def dft_tables(row_index, column_index, seq_len):
    product = row_index[:, None] * column_index[None, :] % seq_len
    angle = product.astype(jnp.float32) * (2.0 * math.pi / seq_len)
    return (jnp.cos(angle).astype(jnp.bfloat16), jnp.sin(angle).astype(jnp.bfloat16))


def layer_norm(values, gain, shift):
    centre = jnp.mean(values, axis=-1, keepdims=True)
    centred = values - centre
    spread = jnp.mean(centred * centred, axis=-1, keepdims=True)
    return centred * lax.rsqrt(spread + norm_epsilon) * gain + shift


def gelu_tanh(values):
    return jax.nn.gelu(values, approximate=True)


def adam_update(weight, gradient, first, second, rate, step_count):
    first_new = beta_first * first + (1.0 - beta_first) * gradient
    second_new = beta_second * second + (1.0 - beta_second) * gradient * gradient
    first_hat = first_new / (1.0 - beta_first**step_count)
    second_hat = second_new / (1.0 - beta_second**step_count)
    updated = weight - rate * (
        first_hat / (jnp.sqrt(second_hat) + adam_epsilon) + weight_decay * weight
    )
    return (first_new, second_new, updated)


def general_layer(
    activations,
    cotangent,
    w_in,
    w_out,
    b_in,
    vec_params,
    first_w_in,
    second_w_in,
    first_w_out,
    second_w_out,
    first_b_in,
    second_b_in,
    first_vec,
    second_vec,
):
    layers = w_in.shape[0]
    seq_count, block_len, model_width = activations.shape
    seq_devices = lax.axis_size(BOTH[1])
    seq_len = block_len * seq_devices
    dft_scale = 1.0 / math.sqrt(seq_len * model_width)
    first_row = lax.axis_index(BOTH[1]) * block_len
    my_rows = first_row + jnp.arange(block_len, dtype=jnp.int32)
    feature_line = jnp.arange(model_width, dtype=jnp.int32)
    cos_model, sin_model = dft_tables(feature_line, feature_line, model_width)
    table_fwd = jnp.concatenate([cos_model, sin_model], axis=1)
    table_back = jnp.transpose(table_fwd)
    layer_index = 0
    pieces = (
        w_in[layer_index].astype(jnp.bfloat16),
        w_out[layer_index].astype(jnp.bfloat16),
        b_in[layer_index].astype(jnp.bfloat16),
        vec_params[layer_index].astype(jnp.bfloat16),
    )
    gathered = [
        (
            lax.all_gather(pieces[0], BOTH, axis=0, tiled=True),
            lax.all_gather(pieces[1], BOTH, axis=1, tiled=True),
            lax.all_gather(pieces[2], BOTH, axis=0, tiled=True),
            lax.all_gather(pieces[3], BOTH, axis=1, tiled=True),
        )
    ]
    zeros_block = jnp.zeros((seq_count, block_len, model_width), jnp.float32)
    stream = activations.astype(jnp.float32)
    layer_index = 0
    weight_first, weight_second, bias_low, vec_low = gathered[layer_index]
    vec_float = vec_low.astype(jnp.float32)
    bias_float = bias_low.astype(jnp.float32)
    joined = jnp.dot(
        stream.astype(jnp.bfloat16), table_fwd, preferred_element_type=jnp.float32
    ).astype(jnp.bfloat16)
    halves = (joined[..., :model_width], joined[..., model_width:])
    shard_piece = (
        lax.all_gather(halves[0], BOTH[1], axis=1, tiled=True),
        lax.all_gather(halves[1], BOTH[1], axis=1, tiled=True),
    )
    piece_len = shard_piece[0].shape[1]
    cos_block, sin_block = dft_tables(my_rows, jnp.arange(piece_len, dtype=jnp.int32), seq_len)
    running = jnp.einsum(
        "ij,sjd->sid", cos_block, shard_piece[0], preferred_element_type=jnp.float32
    )
    mixed = (
        running
        - jnp.einsum("ij,sjd->sid", sin_block, shard_piece[1], preferred_element_type=jnp.float32)
    ) * dft_scale
    normed, norm_first_back = jax.vjp(layer_norm, stream + mixed, vec_float[0], vec_float[1])
    normed_low = normed.astype(jnp.bfloat16)
    pre_act = jnp.dot(normed_low, weight_first, preferred_element_type=jnp.float32) + bias_float
    activated, gelu_back = jax.vjp(gelu_tanh, pre_act)
    act_low = activated.astype(jnp.bfloat16)
    feed = jnp.dot(act_low, weight_second, preferred_element_type=jnp.float32) + vec_float[2]
    stream, norm_second_back = jax.vjp(layer_norm, normed + feed, vec_float[3], vec_float[4])
    saved = [(norm_first_back, normed_low, gelu_back, act_low, norm_second_back)]
    block_output = stream.astype(jnp.bfloat16)
    grad_now = cotangent.astype(jnp.float32)
    raw_grads = [None] * layers
    for layer_index in reversed(range(layers)):
        weight_first, weight_second, bias_low, vec_low = gathered[layer_index]
        norm_first_back, normed_low, gelu_back, act_low, norm_second_back = saved[layer_index]
        grad_sum2, grad_gain2, grad_shift2 = norm_second_back(grad_now)
        grad_z = grad_sum2.astype(jnp.bfloat16)
        grad_weight_second = jnp.einsum(
            "stf,std->fd", act_low, grad_z, preferred_element_type=jnp.float32
        )
        grad_bias_out = jnp.sum(grad_z.astype(jnp.float32), axis=(0, 1))
        grad_act = jnp.einsum(
            "std,fd->stf", grad_z, weight_second, preferred_element_type=jnp.float32
        )
        (grad_pre,) = gelu_back(grad_act)
        grad_pre_low = grad_pre.astype(jnp.bfloat16)
        grad_weight_first = jnp.einsum(
            "std,stf->df", normed_low, grad_pre_low, preferred_element_type=jnp.float32
        )
        grad_bias_in = jnp.sum(grad_pre_low.astype(jnp.float32), axis=(0, 1))
        grad_normed = (
            jnp.einsum(
                "stf,df->std", grad_pre_low, weight_first, preferred_element_type=jnp.float32
            )
            + grad_sum2
        )
        grad_sum1, grad_gain1, grad_shift1 = norm_first_back(grad_normed)
        grad_mix_low = grad_sum1.astype(jnp.bfloat16)
        add_shard_piece = lax.all_gather(grad_mix_low, BOTH[1], axis=1, tiled=True)
        add_piece_len = add_shard_piece.shape[1]
        add_cos_block, add_sin_block = dft_tables(
            my_rows, jnp.arange(add_piece_len, dtype=jnp.int32), seq_len
        )
        with_cos = jnp.einsum(
            "ij,sjd->sid", add_cos_block, add_shard_piece, preferred_element_type=jnp.float32
        )
        with_sin = (zeros_block, zeros_block)[1] - jnp.einsum(
            "ij,sjd->sid", add_sin_block, add_shard_piece, preferred_element_type=jnp.float32
        )
        with_cos, with_sin = (with_cos, with_sin)
        with_cos = (with_cos * dft_scale).astype(jnp.bfloat16)
        with_sin = (with_sin * dft_scale).astype(jnp.bfloat16)
        grad_halves = jnp.concatenate([with_cos, with_sin], axis=-1)
        grad_now = grad_sum1 + jnp.dot(grad_halves, table_back, preferred_element_type=jnp.float32)
        grad_vec = jnp.stack([grad_gain1, grad_shift1, grad_bias_out, grad_gain2, grad_shift2])
        layer_terms = (grad_weight_first, grad_weight_second, grad_bias_in, grad_vec)
        raw_grads[layer_index] = (
            lax.psum_scatter(layer_terms[0], BOTH, scatter_dimension=0, tiled=True),
            lax.psum_scatter(layer_terms[1], BOTH, scatter_dimension=1, tiled=True),
            lax.psum_scatter(layer_terms[2], BOTH, scatter_dimension=0, tiled=True),
            lax.psum_scatter(layer_terms[3], BOTH, scatter_dimension=1, tiled=True),
        )
    shard_w_in = jnp.stack([entry[0] for entry in raw_grads])
    shard_w_out = jnp.stack([entry[1] for entry in raw_grads])
    shard_b_in = jnp.stack([entry[2] for entry in raw_grads])
    shard_vec = jnp.stack([entry[3] for entry in raw_grads])
    local_squares = jnp.sum(shard_w_in * shard_w_in) + jnp.sum(shard_w_out * shard_w_out)
    local_squares = (
        local_squares + jnp.sum(shard_b_in * shard_b_in) + jnp.sum(shard_vec * shard_vec)
    )
    norm_value = jnp.sqrt(lax.psum(local_squares, BOTH))
    factor = clip_limit / jnp.maximum(norm_value, clip_limit)
    upd_w_in = adam_update(
        w_in, factor * shard_w_in, first_w_in, second_w_in, rate_matrix, STEP_COUNT
    )
    upd_w_out = adam_update(
        w_out, factor * shard_w_out, first_w_out, second_w_out, rate_matrix, STEP_COUNT
    )
    upd_b_in = adam_update(
        b_in, factor * shard_b_in, first_b_in, second_b_in, rate_vector, STEP_COUNT
    )
    upd_vec = adam_update(
        vec_params, factor * shard_vec, first_vec, second_vec, rate_vector, STEP_COUNT
    )
    return (
        block_output,
        grad_now,
        norm_value,
        upd_w_in[0],
        upd_w_in[1],
        upd_w_in[2],
        upd_w_out[0],
        upd_w_out[1],
        upd_w_out[2],
        upd_b_in[0],
        upd_b_in[1],
        upd_b_in[2],
        upd_vec[0],
        upd_vec[1],
        upd_vec[2],
    )


MESH = pl.DeviceIdType.MESH
F32 = jnp.float32
BF16 = jnp.bfloat16
NN = (((1,), (0,)), ((), ()))
NT = (((1,), (1,)), ((), ()))
TN = (((0,), (0,)), ((), ()))


def dot(a, b, dims=NN):
    return lax.dot_general(a, b, dims, preferred_element_type=F32)


class Sizes:
    def __init__(self, mesh, seqs, block, width, hidden):
        self.batch, self.seq = mesh.shape["batch"], mesh.shape["seq"]
        self.xs, self.ys, self.zs = self.batch // 2, 2, self.seq // 2
        self.devices = self.batch * self.seq
        self.seqs, self.block, self.width, self.hidden = seqs, block, width, hidden
        self.length = block * self.seq
        self.rows = width // self.devices
        self.slab = 2 * self.rows
        self.segment = self.zs * self.slab
        self.half = hidden // 2
        self.cols = 512
        self.chunks = self.half // self.cols
        self.parts = 2
        self.thin = self.cols // self.parts
        self.packed = width // self.seq
        self.tokens = seqs * block
        self.bias = hidden // self.devices

    def fits(self):
        return (
            self.batch == 4
            and self.seq % 2 == 0
            and self.width % self.devices == 0
            and self.slab % 16 == 0
            and self.packed % 32 == 0
            and self.block % 128 == 0
            and self.zs == 4
            and self.half % self.cols == 0
            and self.rows <= 128
            and self.bias <= 128
            and 5 * self.rows <= self.width
            and self.hidden == 4 * self.width
        )

    def owner(self, x, core, z, y):
        return (2 * x + core) * self.seq + 2 * z + y

    def place_owner(self):
        return [
            self.owner(x, core, z, y)
            for y in range(self.ys)
            for x in range(self.xs)
            for z in range(self.zs)
            for core in range(2)
        ]


def cos_sin(rows, columns, count):
    angle = (rows[:, None] * columns[None, :] % count) * (2.0 * math.pi / count)
    return np.cos(angle), np.sin(angle)


def host_tables(n):
    width, half = n.width, n.packed // 2
    owners = np.array(n.place_owner())
    order = (owners[:, None] * n.rows + np.arange(n.rows)[None, :]).reshape(-1)
    line = np.arange(width)
    cosine, sine = cos_sin(line, line, width)
    pack = np.zeros((width, width))
    unpack = np.zeros((width, width))
    for k in range(width // 2):
        device, inner = divmod(k, half)
        at_cos = device * n.packed + inner
        at_sin = at_cos + half
        pack[at_cos] = cosine[k]
        unpack[at_cos, k] = 1.0
        if k:
            unpack[at_cos, width - k] = 1.0
            pack[at_sin] = sine[k]
            unpack[at_sin, k] = -1.0
            unpack[at_sin, width - k] = 1.0
    pack[half] = cosine[width // 2]
    unpack[half, width // 2] = 1.0
    perm = np.zeros((width, width))
    perm[order, np.arange(width)] = 1.0
    positions = np.arange(n.length)
    by_length = np.stack(cos_sin(positions, positions, n.length))
    vec_mask = np.zeros((n.devices, width))
    vec_mask[np.repeat(owners, n.rows), np.arange(width)] = 1.0
    vec_spread = np.zeros((128, width))
    vec_spread[np.arange(width) % n.rows, np.arange(width)] = 1.0
    bias_spread = np.zeros((128, n.half))
    bias_spread[np.arange(n.half) % n.bias, np.arange(n.half)] = 1.0

    def low(a):
        return jnp.asarray(a.astype(np.float32).astype(ml_dtypes.bfloat16))

    return types.SimpleNamespace(
        tt_f=low(pack),
        by_length=low(by_length),
        un_f=low(unpack[:, order]),
        perm=low(perm),
        tt_b=low(pack[:, order]),
        un_b=low(unpack),
        vec_mask=jnp.asarray(vec_mask.astype(np.float32)),
        vec_spread=low(vec_spread),
        bias_spread=low(bias_spread),
    )


LOADS = dict(
    bias="bias_v",
    vec="vec_v",
    w1="w1_v",
    w2="w2_v",
    x="x_v",
    tt_f="tt_v",
    dy="dy_v",
    vec_spread="vec_spread_v",
    bias_spread="bias_spread_v",
    vec_mask="vec_mask_v",
    by_length="by_length_v",
    perm="perm_v",
    un_f="un_v",
    tt_b="tt_v",
    un_b="un_v",
)
LATER = ("tt_b", "un_b")
FORWARD_KINDS = (1, 1, 1, 1, 0, 2)
BACK_KINDS = (4, 6, 1, 1, 0, 0, 5, 5, 5, 1, 5, 0)


def layer_kernel(n, names, *refs):
    r = types.SimpleNamespace(**dict(zip(names, refs)))
    batch_at, seq_at = lax.axis_index("batch"), lax.axis_index("seq")
    x, core = batch_at // 2, batch_at % 2
    z, y = seq_at // 2, seq_at % 2
    tokens, width, seg, slab = n.tokens, n.width, n.segment, n.slab

    def aligned(at, by):
        return pl.multiple_of(at * by, by)

    def rows_of(at, by):
        return pl.ds(aligned(at, by), by)

    def remote(src, dst, send, recv, batch_to, seq_to):
        return pltpu.make_async_remote_copy(
            src_ref=src,
            dst_ref=dst,
            send_sem=send,
            recv_sem=recv,
            device_id=(batch_to, seq_to),
            device_id_type=MESH,
        )

    def bytes_of(view, send, recv):
        return remote(view, view, send, recv, other_core, seq_at)

    other_core = 2 * x + 1 - core
    other_x = 2 * (1 - x) + core
    other_y = 2 * z + 1 - y

    def plane(k):
        return (seq_at + k) % n.seq

    def plane_from(k):
        return (seq_at + n.seq - k) % n.seq

    def across(k):
        return (batch_at + k) % n.batch

    def across_from(k):
        return (batch_at + n.batch - k) % n.batch

    loads = types.SimpleNamespace()
    for name, held in LOADS.items():
        load = pltpu.make_async_copy(
            getattr(r, name), getattr(r, held), r.load_sem.at[sorted(set(LOADS.values())).index(held)]
        )
        setattr(loads, name, load)
        if name not in LATER:
            load.start()

    everyone = [
        ((batch_at + i // n.seq) % n.batch, (seq_at + i % n.seq) % n.seq)
        for i in range(1, n.devices)
    ]
    barrier = pltpu.get_barrier_semaphore()
    for device in everyone:
        pl.semaphore_signal(barrier, inc=1, device_id=device, device_id_type=MESH)
    pl.semaphore_wait(barrier, n.devices - 1)

    loads.w1.wait()
    loads.w2.wait()
    weights = (r.w1_v, r.w2_v)
    give = pl.ds(aligned(1 - core, n.half), n.half)
    keep = pl.ds(aligned(core, n.half), n.half)
    core_rows = pl.ds(aligned(core, n.rows), n.rows)
    their_rows = pl.ds(aligned(1 - core, n.rows), n.rows)
    for m in range(2):
        remote(
            weights[m].at[:, give],
            r.stage.at[m, core_rows],
            r.swap_send.at[m],
            r.swap_recv.at[m],
            other_core,
            seq_at,
        ).start()

    def swapped(m):
        return bytes_of(r.stage.at[m, pl.ds(0, n.rows)], r.swap_send.at[m], r.swap_recv.at[m])

    def mix_start(t, source, table):
        y_ref, l_ref = r.y_buf.at[t], r.l_buf.at[t]
        y_ref[...] = dot(table[...], source, NT).astype(BF16)
        l_ref[seq_at] = y_ref[rows_of(seq_at, n.packed), :]

    def mix_send(t):
        y_ref, l_ref = r.y_buf.at[t], r.l_buf.at[t]
        for k in range(1, n.seq):
            remote(
                y_ref.at[rows_of(plane(k), n.packed)],
                l_ref.at[seq_at],
                r.mix_send.at[0],
                r.mix_recv.at[2 * t],
                batch_at,
                plane(k),
            ).start()

    def mixed_bytes(i):
        into = (r.l_buf, r.r_buf)[i % 2].at[i // 2, pl.ds(0, n.seq - 1)]
        return bytes_of(into, r.mix_send.at[i % 2], r.mix_recv.at[i])

    def mix_turn(t):
        l_ref, z_ref, r_ref = r.l_buf.at[t], r.z_buf.at[t], r.r_buf.at[t]
        mixed_bytes(2 * t).wait_recv()
        left = jnp.concatenate(
            [
                jnp.concatenate(
                    [l_ref[d, :, g * n.block : (g + 1) * n.block] for d in range(n.seq)], axis=1
                )
                for g in range(n.seqs)
            ],
            axis=0,
        )
        r.left[...] = left
        inner = lax.broadcasted_iota(jnp.int32, (n.seqs * n.packed, 1), 0) % n.packed
        first = (inner < n.packed // 2) | ((inner == n.packed // 2) & (seq_at == 0))
        scale = 1.0 / math.sqrt(n.length * n.width)
        for e in range(0, n.seq, 2):
            at = slice(e * n.block, (e + 2) * n.block)
            by_cos = dot(r.left[...], r.by_length_v[0, :, at])
            by_sin = dot(r.left[...], r.by_length_v[1, :, at])
            value = (jnp.where(first, by_cos, by_sin) * scale).astype(BF16)
            z_ref[e] = value[:, : n.block]
            z_ref[e + 1] = value[:, n.block :]
        for k in range(1, n.seq):
            remote(
                z_ref.at[plane(k)],
                r_ref.at[seq_at],
                r.mix_send.at[1],
                r.mix_recv.at[2 * t + 1],
                batch_at,
                plane(k),
            ).start()
        r_ref[seq_at] = z_ref[seq_at]

    def mix_finish(t, table):
        r_ref = r.r_buf.at[t]
        mixed_bytes(2 * t + 1).wait_recv()
        parts = [
            r_ref[:, g * n.packed : (g + 1) * n.packed, :].reshape(width, n.block)
            for g in range(n.seqs)
        ]
        r.mixed[...] = dot(jnp.concatenate(parts, axis=1), table[...], TN)

    loads.tt_f.wait()
    loads.x.wait()
    mix_start(0, r.x_v[...], r.tt_v)

    full = r.full
    mate_z = z + 1 - 2 * (z % 2)
    pair_z = z // 2
    inner = (z > 0) & (z < n.zs - 1)

    def line(to_z):
        return batch_at, 2 * to_z + y

    def seg_rows(sx, sy):
        return rows_of(sy * n.xs + sx, seg)

    def pair_rows(sx, sy, sp):
        return rows_of((sy * n.xs + sx) * 2 + sp, 2 * slab)

    def slab_rows(sx, sy, sz):
        return rows_of((sy * n.xs + sx) * n.zs + sz, slab)

    def peer(t):
        return (other_y_at, other_x_at)[t == 0]

    other_x_at = (other_x, seq_at)
    other_y_at = (batch_at, other_y)

    def away(t):
        return (1 - x, y) if t == 0 else (x, 1 - y)

    def turn_of(c):
        return FORWARD_KINDS[c] % 2

    def split(c):
        return FORWARD_KINDS[c] // 2 == 1

    def place(c):
        return c // n.chunks, c % n.chunks

    def stage_weights(m):
        r.stage[m, core_rows, :] = weights[m][:, keep]
        swapped(m).wait_recv()
        for q in range(n.chunks):
            columns = r.stage[m, :, q * n.cols : (q + 1) * n.cols]
            full[m, q, slab_rows(x, y, z), :] = columns.astype(BF16)

    def full_copy(c, at, send, recv, to):
        m, q = place(c)
        return remote(full.at[m, q, at], full.at[m, q, at], send, recv, *to)

    def rows_at(sx, sy, i):
        return (slab_rows(sx, sy, z), slab_rows(sx, sy, mate_z), pair_rows(sx, sy, 1 - pair_z))[i]

    def side_copy(c, i, sx, sy, first):
        t = turn_of(c)
        recv = r.first_recv.at[i, c] if first else r.second_recv.at[c]
        return full_copy(c, rows_at(sx, sy, i), r.side_send, recv, peer(t if first else 1 - t))

    def to_sides(c, i):
        if i == 0 or not split(c):
            side_copy(c, i, x, y, True).start()
        side_copy(c, i, x, y, False).start()

    def line_slot(c, far):
        return 2 * n.chunks + sum(split(d) for d in range(c)) if far else c

    def line_seg(c, far):
        return away(turn_of(c)) if far else (x, y)

    def own_to_mate(c, far):
        at = rows_at(*line_seg(c, far), 0)
        return full_copy(c, at, r.side_send, r.mate_recv.at[line_slot(c, far)], line(mate_z))

    def mate_arrives(c, far):
        at = rows_at(*line_seg(c, far), 1)
        full_copy(c, at, r.side_send, r.mate_recv.at[line_slot(c, far)], line(mate_z)).wait_recv()

    def pair_across(c, far):
        at = pair_rows(*line_seg(c, far), pair_z)
        return full_copy(c, at, r.inner_send, r.pair_recv.at[line_slot(c, far)], line(n.zs - 1 - z))

    def pair_out(c, far):
        at = rows_at(*line_seg(c, far), 2)
        return full_copy(c, at, r.inner_send, r.pair_recv.at[line_slot(c, far)], line(mate_z))

    def own_sides(c):
        to_sides(c, 0)

    def own_line(c):
        own_to_mate(c, 0).start()

    def from_mate(c, far):
        mate_arrives(c, far)

        @pl.when(inner)
        def _():
            pair_across(c, far).start()

    def from_pair(c, far):
        pair_out(c, far).wait_recv()

        @pl.when(inner)
        def _():
            pair_out(c, far).start()

    def mate_in(c):
        from_mate(c, 0)
        to_sides(c, 1)

    def pair_in(c):
        from_pair(c, 0)
        to_sides(c, 2)

    def pass_on(c, i):
        ax, ay = away(turn_of(c))
        if i == 0 or not split(c):
            side_copy(c, i, ax, ay, True).wait_recv()
        if split(c):
            if i == 0:
                own_to_mate(c, 1).start()
            else:
                (from_mate, from_pair)[i - 1](c, 1)
        side_copy(c, i, ax, ay, False).start()

    def weights_here(c):
        m, q = place(c)
        second = full.at[m, q, pl.ds(0, 2 * n.zs * slab)]
        bytes_of(second, r.side_send, r.second_recv.at[c]).wait_recv()

    def all_slabs(counts, send):
        rows = sum(counts) * slab // (2 * n.chunks)
        return bytes_of(full.at[:, :, pl.ds(0, rows)], send, r.second_recv.at[0])

    def small_tiles():
        loads.bias.wait()
        loads.vec.wait()
        tile = r.tile
        tile[...] = jnp.zeros(tile.shape, F32)
        for i in range(5):
            tile[i : i + 1, 0 : n.rows] = r.vec_v[i]
        tile[5:6, 0 : n.bias] = r.bias_v[...]
        small[batch_at, seq_at] = tile[...]
        for k in range(1, n.seq):
            small_copy(k, seq_at).start()

    def small_copy(k, at):
        return remote(
            r.tile,
            small.at[batch_at, at],
            r.small_send,
            r.small_recv,
            batch_at,
            plane(k),
        )

    def row_copy(k, at):
        return remote(
            small.at[batch_at],
            small.at[at],
            r.row_send,
            r.row_recv,
            across(k),
            seq_at,
        )

    small = r.small

    def tiles_bytes():
        return bytes_of(small.at[0, pl.ds(0, n.seq - 1)], r.small_send, r.small_recv)

    def rows_bytes():
        return bytes_of(small.at[pl.ds(0, n.batch - 1)], r.row_send, r.row_recv)

    def small_rows():
        tiles_bytes().wait_recv()
        for k in range(1, n.batch):
            row_copy(k, batch_at).start()

    half_owners = n.devices // 2
    bias_mask = (
        lax.broadcasted_iota(jnp.int32, (half_owners, n.half), 0)
        == lax.broadcasted_iota(jnp.int32, (half_owners, n.half), 1) // n.bias
    )

    def small_vectors():
        rows_bytes().wait_recv()
        for load in (loads.vec_spread, loads.bias_spread, loads.vec_mask):
            load.wait()
        for i in range(5):
            held = small[:, :, i, :].reshape(n.devices, 128).astype(BF16)
            spread = dot(held, r.vec_spread_v[...]) * r.vec_mask_v[...]
            r.vecs[i : i + 1, :] = jnp.sum(spread, axis=0, keepdims=True)
        held = small[pl.ds(core * (n.batch // 2), n.batch // 2), :, 5, :]
        held = held.reshape(half_owners, 128).astype(BF16)
        spread = jnp.where(bias_mask, dot(held, r.bias_spread_v[...]), 0.0)
        biases = jnp.sum(spread, axis=0, keepdims=True)
        for q in range(n.chunks):
            r.biases[q] = biases[:, q * n.cols : (q + 1) * n.cols]

    def place_inputs():
        loads.perm.wait()
        loads.dy.wait()
        r.x_place[...] = dot(r.x_v[...], r.perm_v[...])
        r.dy_place[...] = dot(r.dy_v[...], r.perm_v[...])

    def turn_forward():
        loads.by_length.wait()
        mix_turn(0)

    step = 32
    tall = 64
    mine, theirs = pl.ds(0, tokens), pl.ds(tokens, tokens)

    def row_loop(body):
        @pl.loop(0, tokens // tall, unroll=True)
        def _(i):
            body(pl.ds(pl.multiple_of(i * tall, tall), tall))

    def mean(v):
        return jnp.mean(v, axis=-1, keepdims=True)

    def first_norm(at):
        v = r.x_place[at, :] + r.mixed[at, :]
        centred = v - mean(v)
        scale = lax.rsqrt(mean(centred * centred) + norm_epsilon)
        unit = centred * scale
        h = unit * r.vecs[0:1, :] + r.vecs[1:2, :]
        r.unit1[at, :] = unit
        r.scale1[at, :] = jnp.broadcast_to(scale, (tall, 128))
        r.h[at, :] = h
        r.h_low[at, :] = h.astype(BF16)

    def swap(i, src, dst):
        return remote(src, dst, r.core_send, r.core_recv.at[i], other_core, seq_at)

    def swap_h():
        return swap(0, r.h_low.at[mine], r.h_low.at[theirs])

    def norm_forward():
        loads.un_f.wait()
        mix_finish(0, r.un_v)
        loads.tt_b.start()
        loads.un_b.start()
        row_loop(first_norm)
        swap_h().start()

    root = math.sqrt(2.0 / math.pi)

    lifted_parts = []

    def lift(q):
        if not lifted_parts:
            swap_h().wait_recv()
        lifted_parts.append(q)
        weights_here(q)
        r.lift[...] = dot(r.h_low[...], full[0, q]) + r.biases[q]

        @pl.loop(0, 2 * tokens // step)
        def _(i):
            at = pl.ds(pl.multiple_of(i * step, step), step)
            u = r.lift[at, :]
            square = u * u
            bent = jnp.tanh(u * (root + (root * 0.044715) * square))
            half_up = 0.5 + 0.5 * bent
            r.act[q, at, :] = (u * half_up).astype(BF16)
            r.slope[q, at, :] = half_up + (u * (1.0 - bent * bent)) * (
                0.5 * root + (1.5 * root * 0.044715) * square
            )

    gathered_parts = []

    def swap_ff():
        return swap(1, r.part_low, r.part_in)

    def drop(q):
        weights_here(n.chunks + q)
        gathered_parts.append(q)
        for half in (theirs, mine):
            part = dot(r.act[q, half, :], full[1, q], NT)
            part = r.total[half, :] + part if len(gathered_parts) > 1 else part
            if len(gathered_parts) == n.chunks and half is theirs:
                r.part_low[...] = part.astype(BF16)
                swap_ff().start()
            else:
                r.total[half, :] = part

    def send_forward():
        mix_send(0)

    forward_steps = (
        (send_forward,), (stage_weights, 0), (own_sides, 1), (own_sides, 0), (own_line, 2),
        (own_sides, 2), (own_line, 1), (own_line, 0), (stage_weights, 1), (own_sides, 4),
        (own_sides, 3), (place_inputs,), (own_line, 3), (own_sides, 5), (own_line, 4),
        (pass_on, 1, 0), (small_tiles,), (pass_on, 0, 0), (mate_in, 2), (mate_in, 1),
        (pass_on, 5, 0), (pass_on, 2, 0), (own_line, 5), (mate_in, 0), (pass_on, 4, 0),
        (mate_in, 3), (mate_in, 4), (pass_on, 2, 1), (pass_on, 3, 0), (pair_in, 2),
        (small_rows,), (pass_on, 1, 1), (pair_in, 1), (pass_on, 5, 1), (turn_forward,),
        (pass_on, 0, 1), (mate_in, 5), (pass_on, 3, 1), (pair_in, 0), (pass_on, 4, 1),
        (pass_on, 2, 2), (pair_in, 4), (small_vectors,), (pass_on, 1, 2), (pair_in, 3),
        (pass_on, 5, 2), (pass_on, 0, 2), (norm_forward,), (pass_on, 4, 2), (pair_in, 5),
        (pass_on, 3, 2), (lift, 1), (lift, 2), (lift, 0), (drop, 1), (drop, 0), (drop, 2),
    )
    for task, *which in forward_steps:
        task(*which)
    swap_ff().wait_recv()

    def second_norm(at):
        v = (
            r.h[at, :]
            + r.total[at, :]
            + r.part_in[at, :].astype(F32)
            + r.vecs[2:3, :]
        )
        centred = v - mean(v)
        scale = lax.rsqrt(mean(centred * centred) + norm_epsilon)
        unit = centred * scale
        gain = r.vecs[3:4, :]
        r.h[at, :] = unit
        r.out_low[at, :] = (unit * gain + r.vecs[4:5, :]).astype(BF16)
        du = r.dy_place[at, :] * gain
        dv = scale * (du - mean(du) - unit * mean(du * unit))
        r.dr2[at, :] = dv
        r.dz[at, :] = dv.astype(BF16)

    row_loop(second_norm)
    swap_dz = swap(2, r.dz.at[mine], r.dz.at[theirs])
    swap_dz.start()
    swap_dz.wait_recv()

    acc, out_low = r.acc, r.give

    pieces = grad_pieces(n)

    def wide(c):
        slot, start, width_of = pieces[c]
        m, q = slot // (n.chunks * n.parts), slot % (n.chunks * n.parts)
        return 1 - m, q // n.parts, pl.ds((q % n.parts) * n.thin + start, width_of)

    def held(c, at=slice(None), lead=()):
        slot, start, width_of = pieces[c]
        return (slot, *lead, at, pl.ds(start, width_of))

    def grad_copy(c, at, into, recv, to):
        return remote(out_low.at[held(c, at)], into, r.grad_send, recv, *to)

    def back_turn(c):
        return BACK_KINDS[c] % 2

    def back_mode(c):
        return BACK_KINDS[c] // 2

    def back_slot(c):
        return [d for d, kind in enumerate(BACK_KINDS) if kind // 2 == back_mode(c)].index(c)

    def copy_diagonal(c):
        at = seg_rows(1 - x, 1 - y)
        return grad_copy(c, at, r.in_diagonal.at[held(c)], r.diagonal_recv.at[c], peer(1 - back_turn(c)))

    def copy_near(c):
        t = 1 - back_turn(c)
        into = r.in_sides.at[held(c, lead=(0,))]
        return grad_copy(c, seg_rows(*away(t)), into, r.sides_recv.at[c], peer(t))

    def copy_side(c):
        t = back_turn(c)
        into = r.in_sides.at[held(c, lead=(1,))]
        return grad_copy(c, seg_rows(*away(t)), into, r.sides_recv.at[c], peer(t))

    def back_seg(c, far):
        return away(back_turn(c)) if far else (x, y)

    def tree_slot(c):
        return sum(kind // 2 < 2 for kind in BACK_KINDS[:c])

    def line_into(c, far, i):
        if far:
            into = (r.far_mate, r.far_pair, r.far_across)[i]
            return into.at[back_slot(c), :, pl.ds(0, pieces[c][2])]
        into, lead = ((r.in_end, (0,)), (r.in_pair, ()), (r.in_across, ()))[i]
        return into.at[held(c, lead=lead)]

    def line_copy(c, at, far, i, to):
        if far:
            recv = r.far_recv.at[i, back_slot(c)]
        else:
            recv = r.end_recv.at[c] if i == 0 else r.tree_recv.at[i - 1, tree_slot(c)]
        return grad_copy(c, at, line_into(c, far, i), recv, to)

    def copy_mate(c, far):
        at = slab_rows(*back_seg(c, far), mate_z)
        return line_copy(c, at, far, 0, line(mate_z))

    def copy_pair_in(c, far):
        at = pair_rows(*back_seg(c, far), 1 - pair_z)
        return line_copy(c, at, far, 1, line(mate_z))

    def copy_pair_across(c, far):
        at = pair_rows(*back_seg(c, far), 1 - pair_z)
        return line_copy(c, at, far, 2, line(n.zs - 1 - z))

    def copy_far(c):
        t = back_turn(c)
        at = slab_rows(*away(t), z)
        return grad_copy(c, at, r.in_end.at[held(c, lead=(1,))], r.end_recv.at[c], peer(t))

    def copy_direct(c, d):
        to_z = (z + d) % n.zs
        at = slab_rows(x, y, to_z)
        return grad_copy(c, at, r.in_end.at[held(c, lead=(d - 1,))], r.end_recv.at[c], line(to_z))

    def round_out(c, at, *more):
        value = acc[held(c, at)]
        for ref in more:
            value = value + ref[...].astype(F32)
        out_low[held(c, at)] = value.astype(BF16)

    four = [(sx, sy) for sy in range(n.ys) for sx in range(n.xs)]

    def first_copy(c, i, which):
        sx, sy = four[i]
        slot, lanes = back_slot(c), pl.ds(0, pieces[c][2])
        if which == 0:
            at, to = slab_rows(sx, sy, mate_z), line(mate_z)
        else:
            at, to = pair_rows(sx, sy, 1 - pair_z), line((0, mate_z, n.zs - 1 - z)[which])
        into = (r.first_mate, r.first_pair, r.first_across)[which].at[slot, i, :, lanes]
        return grad_copy(c, at, into, r.line_recv.at[which, slot], to)

    def first_wait(c, which):
        slot, lanes = back_slot(c), pl.ds(0, pieces[c][2])
        into = (r.first_mate, r.first_pair, r.first_across)[which].at[slot, :, :, lanes]
        bytes_of(into, r.grad_send, r.line_recv.at[which, slot]).wait_recv()

    def first_start(c):
        @pl.when(jnp.logical_not(inner))
        def _():
            for i, (sx, sy) in enumerate(four):
                round_out(c, pair_rows(sx, sy, 1 - pair_z))
                first_copy(c, i, 1).start()
            for i, (sx, sy) in enumerate(four):
                round_out(c, slab_rows(sx, sy, mate_z))
                first_copy(c, i, 0).start()

    def first_across(c):
        @pl.when(inner)
        def _():
            first_wait(c, 1)
            for i, (sx, sy) in enumerate(four):
                lanes = pl.ds(0, pieces[c][2])
                more = r.first_pair.at[back_slot(c), i, :, lanes]
                round_out(c, pair_rows(sx, sy, 1 - pair_z), more)
                first_copy(c, i, 2).start()

    def first_out(c):
        @pl.when(inner)
        def _():
            first_wait(c, 2)
            for i, (sx, sy) in enumerate(four):
                at = held(c, pair_rows(sx, sy, pair_z))
                lanes = pl.ds(0, pieces[c][2])
                acc[at] = acc[at] + r.first_across[back_slot(c), i, :, lanes].astype(F32)
                round_out(c, slab_rows(sx, sy, mate_z))
                first_copy(c, i, 0).start()

    def slab_copy(c, i):
        t = back_turn(c)
        sx, sy = ((1 - x, 1 - y), away(1 - t), away(t))[i]
        own = pl.ds(0, slab)
        into = (
            r.in_diagonal.at[held(c, own)] if i == 0 else r.in_sides.at[held(c, own, lead=(i - 1,))]
        )
        recv = r.diagonal_recv if i == 0 else r.sides_recv
        return grad_copy(c, slab_rows(sx, sy, z), into, recv.at[c], peer(t if i == 2 else 1 - t))

    def slabs_near(c):
        first_wait(c, 0)
        lanes = pl.ds(0, pieces[c][2])
        for i, (sx, sy) in enumerate(four):
            at = held(c, slab_rows(sx, sy, z))
            acc[at] = acc[at] + r.first_mate[back_slot(c), i, :, lanes].astype(F32)
        t = back_turn(c)
        for i, seg_at in enumerate(((1 - x, 1 - y), away(1 - t))):
            round_out(c, slab_rows(*seg_at, z))
            slab_copy(c, i).start()

    def slabs_side(c):
        slab_copy(c, 0).wait_recv()
        own = pl.ds(0, slab)
        round_out(c, slab_rows(*away(back_turn(c)), z), r.in_diagonal.at[held(c, own)])
        slab_copy(c, 2).start()

    def slabs_end(c):
        own = pl.ds(0, slab)
        both = r.in_sides.at[held(c, own, lead=(pl.ds(0, 2),))]
        bytes_of(both, r.grad_send, r.sides_recv.at[c]).wait_recv()
        value = acc[held(c, slab_rows(x, y, z))]
        return value + sum(r.in_sides[held(c, own, lead=(i,))].astype(F32) for i in range(2))

    def grad_product(c):
        m, q, at = wide(c)
        if m:
            acc[held(c)] = dot(r.dz[...], r.act[q, :, at], TN)
        else:
            acc[held(c)] = dot(r.h_low[...], r.dpre[q, :, at], TN)
        if back_mode(c) == 3:
            first_start(c)
            return
        round_out(c, seg_rows(1 - x, 1 - y))
        copy_diagonal(c).start()
        round_out(c, seg_rows(*away(1 - back_turn(c))))
        copy_near(c).start()

    def line_start(c, far):
        @pl.when(jnp.logical_not(inner))
        def _():
            sx, sy = back_seg(c, far)
            round_out(c, pair_rows(sx, sy, 1 - pair_z))
            copy_pair_in(c, far).start()
            round_out(c, slab_rows(sx, sy, mate_z))
            copy_mate(c, far).start()

    def grad_side(c):
        if back_mode(c) == 3:
            first_across(c)
            return
        copy_diagonal(c).wait_recv()
        at = seg_rows(*away(back_turn(c)))
        if back_mode(c) == 1:
            acc[held(c, at)] = acc[held(c, at)] + r.in_diagonal[held(c)].astype(F32)
            line_start(c, 1)
        else:
            round_out(c, at, r.in_diagonal.at[held(c)])
            copy_side(c).start()

    def grad_line(c):
        if back_mode(c) == 3:
            first_out(c)
            return
        sides = 1 if back_mode(c) == 1 else 2
        both = r.in_sides.at[held(c, lead=(pl.ds(0, sides),))]
        bytes_of(both, r.grad_send, r.sides_recv.at[c]).wait_recv()
        more = sum(r.in_sides[held(c, lead=(i,))].astype(F32) for i in range(sides))
        at = seg_rows(x, y)
        acc[held(c, at)] = acc[held(c, at)] + more
        if back_mode(c) == 2:
            for d in range(1, n.zs):
                round_out(c, slab_rows(x, y, (z + d) % n.zs))
                copy_direct(c, d).start()
        else:
            line_start(c, 0)

    def fars(c):
        return range((1, 2, 0, 0)[back_mode(c)])

    def grad_across(c):
        if back_mode(c) == 3:
            slabs_near(c)
        for far in fars(c):

            @pl.when(inner)
            def _(far=far):
                copy_pair_in(c, far).wait_recv()
                at = pair_rows(*back_seg(c, far), 1 - pair_z)
                round_out(c, at, line_into(c, far, 1))
                copy_pair_across(c, far).start()

    def grad_out(c):
        if back_mode(c) == 3:
            slabs_side(c)
        for far in fars(c):

            @pl.when(inner)
            def _(far=far):
                copy_pair_across(c, far).wait_recv()
                sx, sy = back_seg(c, far)
                at = pair_rows(sx, sy, pair_z)
                acc[held(c, at)] = acc[held(c, at)] + line_into(c, far, 2)[...].astype(F32)
                round_out(c, slab_rows(sx, sy, mate_z))
                copy_mate(c, far).start()

    def grad_far(c):
        if back_mode(c) == 1:
            copy_mate(c, 1).wait_recv()
            round_out(c, slab_rows(*away(back_turn(c)), z), line_into(c, 1, 0))
            copy_far(c).start()

    grads_out = (r.g1, r.g2)
    r.squares[...] = jnp.zeros((8, 128), F32)

    def squares_of(v):
        v = v * v
        v = jnp.sum(v.reshape(v.shape[0] // 8, 8, v.shape[1]), axis=0)
        return sum(v[:, i : i + 128] for i in range(0, v.shape[1], 128))

    def copy_back(c):
        return remote(
            r.final.at[held(c, their_rows)],
            r.final_in.at[held(c)],
            r.back_send,
            r.back_recv,
            other_core,
            seq_at,
        )

    def grad_end(c):
        m, q, at = wide(c)
        if back_mode(c) == 3:
            value = slabs_end(c)
        else:
            value = acc[held(c, slab_rows(x, y, z))]
            ends = back_mode(c) + 1
            all_ends = r.in_end.at[held(c, lead=(pl.ds(0, ends),))]
            bytes_of(all_ends, r.grad_send, r.end_recv.at[c]).wait_recv()
            for i in range(ends):
                value = value + r.in_end[held(c, lead=(i,))].astype(F32)
        r.squares[...] += squares_of(value)
        r.final[held(c)] = value
        own_at = pl.ds(aligned(core, n.half) + q * n.cols + at.start, at.size)
        grads_out[m][:, own_at] = r.final[held(c, core_rows)]
        copy_back(c).start()

    back_parts = []

    def slope_back(q):
        r.lift[...] = dot(r.dz[...], full[1, q])
        r.bias_sum[q] = jnp.zeros((8, n.cols), F32)

        @pl.loop(0, 2 * tokens // step)
        def _(i):
            at = pl.ds(pl.multiple_of(i * step, step), step)
            low = (r.lift[at, :] * r.slope[q, at, :]).astype(BF16)
            r.dpre[q, at, :] = low
            r.bias_sum[q] += jnp.sum(low.astype(F32).reshape(step // 8, 8, n.cols), axis=0)

        back_parts.append(q)
        for half in (theirs, mine):
            part = dot(r.dpre[q, half, :], full[0, q], NT)
            part = r.total[half, :] + part if len(back_parts) > 1 else part
            if len(back_parts) == n.chunks and half is theirs:
                r.part_low2[...] = part.astype(BF16)
                swap_dh().start()
            else:
                r.total[half, :] = part

    def swap_dh():
        return swap(3, r.part_low2, r.part_in2)

    def first_norm_back(at):
        dh = r.total[at, :] + r.part_in2[at, :].astype(F32) + r.dr2[at, :]
        unit = r.unit1[at, :]
        r.x_place[at, :] = dh
        du = dh * r.vecs[0:1, :]
        dv = r.scale1[at, 0:1] * (du - mean(du) - unit * mean(du * unit))
        low = dv.astype(BF16)
        r.dm[at, :] = low
        r.rest[at, :] = (dv - low.astype(F32)).astype(BF16)

    def norm_back():
        swap_dh().wait_recv()
        row_loop(first_norm_back)
        loads.tt_b.wait()
        mix_start(1, r.dm[...], r.tt_v)
        mix_send(1)

    def thirds(v):
        high = v.astype(BF16)
        left = v - high.astype(F32)
        mid = left.astype(BF16)
        return high, mid, (left - mid.astype(F32)).astype(BF16)

    def small_gather(v, spread):
        return sum(dot(part, spread, NT) for part in thirds(v))

    def row_sums(k):
        return remote(
            r.small_out.at[across(k)],
            r.small_in.at[k - 1],
            r.row_send2,
            r.row_recv2,
            across(k),
            seq_at,
        )

    def tile_sums(k):
        return remote(
            r.small_mid.at[plane(k)],
            r.small_last.at[k - 1],
            r.small_send2,
            r.small_recv2,
            batch_at,
            plane(k),
        )

    row_sums_bytes = bytes_of(r.small_in, r.row_send2, r.row_recv2)
    tile_sums_bytes = bytes_of(r.small_last, r.small_send2, r.small_recv2)

    def fold(v):
        return jnp.sum(v.reshape(tall // 8, 8, width), axis=0)

    def vector_sums(at):
        dh, dy = r.x_place[at, :], r.dy_place[at, :]
        r.sums[0] += fold(dh * r.unit1[at, :])
        r.sums[1] += fold(dh)
        r.sums[2] += fold(r.dz[at, :].astype(F32))
        r.sums[3] += fold(dy * r.h[at, :])
        r.sums[4] += fold(dy)

    def small_grads():
        r.sums[...] = jnp.zeros(r.sums.shape, F32)
        row_loop(vector_sums)
        for i in range(5):
            line_sum = jnp.sum(r.sums[i], axis=0, keepdims=True)
            tiles = small_gather(line_sum * r.vec_mask_v[...], r.vec_spread_v[...])
            r.small_out[:, :, i, :] = tiles.reshape(n.batch, n.seq, 128)
        line_sum = jnp.concatenate(
            [jnp.sum(r.bias_sum[q], axis=0, keepdims=True) for q in range(n.chunks)], axis=1
        )
        tiles = small_gather(jnp.where(bias_mask, line_sum, 0.0), r.bias_spread_v[...])
        r.small_out[:, :, 5:8, :] = jnp.zeros((n.batch, n.seq, 3, 128), F32)
        r.small_out[pl.ds(core * (n.batch // 2), n.batch // 2), :, 5, :] = tiles.reshape(
            n.batch // 2, n.seq, 128
        )
        for k in range(1, n.batch):
            row_sums(k).start()

    def small_rows_back():
        value = r.small_out[batch_at]
        row_sums_bytes.wait_recv()
        for k in range(1, n.batch):
            value = value + r.small_in[k - 1]
        r.small_mid[...] = value
        for k in range(1, n.seq):
            tile_sums(k).start()

    def small_end():
        value = r.small_mid[seq_at]
        tile_sums_bytes.wait_recv()
        for k in range(1, n.seq):
            value = value + r.small_last[k - 1]
        r.g_small[...] = value

    def turn_back():
        mix_turn(1)

    def outputs():
        r.out[...] = dot(r.out_low[...], r.perm_v[...], NT).astype(BF16)
        r.dx[...] = dot(r.dm[...], r.perm_v[...], NT) + dot(r.rest[...], r.perm_v[...], NT)

    def mix_back():
        loads.un_b.wait()
        mix_finish(1, r.un_v)
        r.dx[...] = r.dx[...] + r.mixed[...]

    for task, *which in (
        (grad_product, 4), (grad_product, 2), (grad_product, 1), (slope_back, 2),
        (grad_product, 11), (grad_product, 3), (slope_back, 1), (slope_back, 0), (grad_side, 1),
        (grad_side, 2), (grad_product, 6), (norm_back,), (grad_side, 3), (grad_product, 7),
        (grad_line, 2), (grad_side, 4), (grad_side, 6), (outputs,), (grad_product, 10),
        (grad_side, 7), (grad_product, 5), (grad_line, 3), (grad_line, 1), (grad_across, 2),
        (grad_line, 6), (grad_product, 9), (grad_line, 4), (grad_across, 3), (grad_line, 7),
        (grad_side, 11), (grad_side, 10), (grad_across, 6), (grad_across, 7), (grad_out, 6),
        (turn_back,), (grad_out, 3), (grad_across, 4), (grad_side, 5), (grad_product, 8),
        (grad_side, 9), (grad_out, 7), (grad_far, 7), (grad_product, 0), (grad_out, 2),
        (grad_far, 2), (grad_line, 11), (grad_line, 5), (small_grads,), (grad_across, 11),
        (grad_line, 9), (grad_far, 6), (grad_side, 8), (grad_line, 10), (grad_across, 5),
        (grad_across, 10), (grad_side, 0), (grad_out, 11), (grad_out, 10), (grad_end, 2),
        (grad_far, 10), (small_rows_back,), (grad_across, 9), (grad_across, 1), (grad_out, 4),
        (grad_line, 8), (grad_across, 8), (grad_end, 10), (grad_out, 5), (small_end,),
        (grad_end, 7), (grad_line, 0), (grad_out, 8), (grad_out, 1), (grad_out, 9),
        (grad_far, 11), (grad_far, 4), (grad_far, 8), (grad_far, 3), (grad_far, 1),
        (grad_far, 5), (grad_across, 0), (grad_end, 1), (grad_end, 4), (grad_far, 9),
        (grad_end, 6), (grad_end, 8), (grad_out, 0), (grad_end, 5), (grad_far, 0),
        (grad_end, 3), (mix_back,), (grad_end, 11), (grad_end, 9), (grad_end, 0),
    ):
        task(*which)

    squares = r.squares[...] + r.g_small[...] * r.g_small[...]
    r.norm_own[...] = jnp.sum(squares, axis=0, keepdims=True)
    r.norm_all[batch_at * n.seq + seq_at] = r.norm_own[...]

    for device in everyone:
        remote(
            r.norm_own,
            r.norm_all.at[batch_at * n.seq + seq_at],
            r.norm_send,
            r.norm_recv,
            *device,
        ).start()
    back_bytes = bytes_of(r.final_in, r.back_send, r.back_recv)
    back_bytes.wait_recv()
    for c in range(len(pieces)):
        m, q, at = wide(c)
        their_at = pl.ds(aligned(1 - core, n.half) + q * n.cols + at.start, at.size)
        grads_out[m][:, their_at] = r.final_in[held(c)]
    norm_bytes = bytes_of(r.norm_all.at[pl.ds(0, n.devices - 1)], r.norm_send, r.norm_recv)
    norm_bytes.wait_recv()
    squares = jnp.sum(r.norm_all[...].reshape(n.devices, 128), axis=0, keepdims=True)
    whole = jnp.sum(squares, axis=1, keepdims=True)
    r.norm[...] = jnp.broadcast_to(jnp.sqrt(whole), (8, 128))

    bytes_of(r.act, r.core_send, r.core_recv.at[0]).wait_send()
    for copy in (tiles_bytes(), rows_bytes(), *(swapped(m) for m in range(2))):
        copy.wait_send()
    for i, into in enumerate((r.l_buf, r.r_buf)):
        both = into.at[:, pl.ds(0, n.seq - 1)]
        bytes_of(both, r.mix_send.at[i], r.mix_recv.at[i]).wait_send()
    for copy in (row_sums_bytes, tile_sums_bytes, back_bytes, norm_bytes):
        copy.wait_send()
    weight_chunks = range(2 * n.chunks)
    sent = [2 * n.zs + (3 if split(c) else n.zs + 1) for c in weight_chunks]
    all_slabs(sent, r.side_send).wait_send()

    @pl.when(inner)
    def _():
        all_slabs([8 if split(c) else 4 for c in weight_chunks], r.inner_send).wait_send()

    moved = 2 * n.zs + n.zs + 3
    bytes_of(out_low.at[:, pl.ds(0, moved * slab)], r.grad_send, r.sides_recv.at[0]).wait_send()


def grad_pieces(n):
    slots = 2 * n.chunks * n.parts
    halved = len(BACK_KINDS) - slots
    whole = [(slot, 0, n.thin) for slot in range(slots - halved)]
    thin = n.thin // 2
    return whole + [(slot, i * thin, thin) for slot in range(slots - halved, slots) for i in range(2)]


def run_layer(n, x, dy, w1, w2, bias, vec):
    tables = host_tables(n)
    tokens, width, cols, q = n.tokens, n.width, n.cols, n.chunks
    grads = 2 * q * n.parts
    far_chunks = sum(kind // 2 == 1 for kind in FORWARD_KINDS)
    splits = max(1, sum(kind // 2 == 1 for kind in BACK_KINDS))
    firsts = max(1, sum(kind // 2 == 3 for kind in BACK_KINDS))
    dma = pltpu.SemaphoreType.DMA
    vmem = pltpu.VMEM
    inputs = dict(bias=bias, vec=vec, x=x, dy=dy, w1=w1, w2=w2)
    inputs.update({name: getattr(tables, name) for name in LOADS if name not in inputs})
    outputs = dict(
        out=((tokens, width), BF16),
        dx=((tokens, width), F32),
        g1=((n.rows, n.hidden), F32),
        g2=((n.rows, n.hidden), F32),
        g_small=((8, 128), F32),
        norm=((8, 128), F32),
    )
    scratch = {held: vmem(inputs[name].shape, inputs[name].dtype) for name, held in LOADS.items()}
    scratch.update(
        load_sem=dma((len(set(LOADS.values())),)),
        stage=vmem((2, n.slab, n.half), F32),
        swap_send=dma((2,)),
        swap_recv=dma((2,)),
        tile=vmem((8, 128), F32),
        small=vmem((n.batch, n.seq, 8, 128), F32),
        small_send=dma,
        small_recv=dma,
        row_send=dma,
        row_recv=dma,
        y_buf=vmem((2, width, tokens), BF16),
        l_buf=vmem((2, n.seq, n.packed, tokens), BF16),
        left=vmem((n.seqs * n.packed, n.length), BF16),
        z_buf=vmem((2, n.seq, n.seqs * n.packed, n.block), BF16),
        r_buf=vmem((2, n.seq, n.seqs * n.packed, n.block), BF16),
        mix_send=dma((2,)),
        mix_recv=dma((4,)),
        mixed=vmem((tokens, width), F32),
        full=vmem((2, q, width, cols), BF16),
        side_send=dma,
        inner_send=dma,
        mate_recv=dma((2 * q + far_chunks,)),
        pair_recv=dma((2 * q + far_chunks,)),
        first_recv=dma((3, 2 * q)),
        second_recv=dma((2 * q,)),
        x_place=vmem((tokens, width), F32),
        dy_place=vmem((tokens, width), F32),
        vecs=vmem((8, width), F32),
        biases=vmem((q, 1, cols), F32),
        unit1=vmem((tokens, width), F32),
        scale1=vmem((tokens, 128), F32),
        h=vmem((tokens, width), F32),
        h_low=vmem((2 * tokens, width), BF16),
        core_send=dma,
        core_recv=dma((4,)),
        total=vmem((2 * tokens, width), F32),
        act=vmem((q, 2 * tokens, cols), BF16),
        lift=vmem((2 * tokens, cols), F32),
        slope=vmem((q, 2 * tokens, cols), F32),
        part_low=vmem((tokens, width), BF16),
        part_low2=vmem((tokens, width), BF16),
        part_in=vmem((tokens, width), BF16),
        part_in2=vmem((tokens, width), BF16),
        sums=vmem((5, 8, width), F32),
        out_low=vmem((tokens, width), BF16),
        dr2=vmem((tokens, width), F32),
        dz=vmem((2 * tokens, width), BF16),
        acc=vmem((grads, width, n.thin), F32),
        give=vmem((grads, width, n.thin), BF16),
        in_diagonal=vmem((grads, n.segment, n.thin), BF16),
        in_sides=vmem((grads, 2, n.segment, n.thin), BF16),
        in_end=vmem((grads, n.zs - 1, n.slab, n.thin), BF16),
        in_pair=vmem((grads, 2 * n.slab, n.thin), BF16),
        in_across=vmem((grads, 2 * n.slab, n.thin), BF16),
        far_mate=vmem((splits, n.slab, n.thin), BF16),
        far_pair=vmem((splits, 2 * n.slab, n.thin), BF16),
        far_across=vmem((splits, 2 * n.slab, n.thin), BF16),
        first_mate=vmem((firsts, 4, n.slab, n.thin), BF16),
        first_pair=vmem((firsts, 4, 2 * n.slab, n.thin), BF16),
        first_across=vmem((firsts, 4, 2 * n.slab, n.thin), BF16),
        line_recv=dma((3, firsts)),
        grad_send=dma,
        diagonal_recv=dma((len(BACK_KINDS),)),
        sides_recv=dma((len(BACK_KINDS),)),
        end_recv=dma((len(BACK_KINDS),)),
        tree_recv=dma((2, max(1, sum(kind // 2 < 2 for kind in BACK_KINDS)))),
        far_recv=dma((3, splits)),
        bias_sum=vmem((q, 8, cols), F32),
        dpre=vmem((q, 2 * tokens, cols), BF16),
        dm=vmem((tokens, width), BF16),
        rest=vmem((tokens, width), BF16),
        small_out=vmem((n.batch, n.seq, 8, 128), F32),
        small_in=vmem((n.batch - 1, n.seq, 8, 128), F32),
        row_send2=dma,
        row_recv2=dma,
        small_mid=vmem((n.seq, 8, 128), F32),
        small_last=vmem((n.seq - 1, 8, 128), F32),
        small_send2=dma,
        small_recv2=dma,
        final=vmem((grads, n.slab, n.thin), F32),
        final_in=vmem((grads, n.rows, n.thin), F32),
        back_send=dma,
        back_recv=dma,
        squares=vmem((8, 128), F32),
        norm_own=vmem((1, 128), F32),
        norm_all=vmem((n.devices, 1, 128), F32),
        norm_send=dma,
        norm_recv=dma,
    )
    names = tuple(inputs) + tuple(outputs) + tuple(scratch)
    in_vmem = pl.BlockSpec(memory_space=pltpu.VMEM)
    anywhere = pl.BlockSpec(memory_space=pl.ANY)
    values = pl.pallas_call(
        functools.partial(layer_kernel, n, names),
        out_shape=[vmem(*shape) for shape in outputs.values()],
        in_specs=[anywhere if name in LOADS else in_vmem for name in inputs],
        out_specs=[in_vmem] * len(outputs),
        scratch_shapes=list(scratch.values()),
        compiler_params=pltpu.CompilerParams(
            collective_id=0, has_side_effects=True, vmem_limit_bytes=58 * 2**20
        ),
        name="fused_layer",
    )(*inputs.values())
    return types.SimpleNamespace(**dict(zip(outputs, values)))


def adam_kernel(n, names, *refs):
    r = types.SimpleNamespace(**dict(zip(names, refs)))
    passed = [
        pltpu.make_async_copy(r.out, r.out_there, r.sem.at[0]),
        pltpu.make_async_copy(r.dx, r.dx_there, r.sem.at[1]),
    ]
    for copy in passed:
        copy.start()
    norm_value = r.norm[0:1, 0:1]
    r.norm_out[...] = norm_value
    factor = clip_limit / jnp.maximum(norm_value, clip_limit)
    lanes = n.cols

    def update(gradient, given, made, at, rate):
        weight, first, second = (ref[at] for ref in given)
        new = adam_update(weight, factor * gradient, first, second, rate, STEP_COUNT)
        for ref, value in zip(made, new):
            ref[at] = value

    weight_in, weight_out = refs[4:7], refs[7:10]
    made_in, made_out = refs[19:22], refs[22:25]

    @pl.loop(0, n.hidden // lanes)
    def _(i):
        at = (slice(None), pl.ds(pl.multiple_of(i * lanes, lanes), lanes))
        update(r.g1[at], weight_in, made_in, at, rate_matrix)
        update(r.g2[at], weight_out, made_out, at, rate_matrix)

    update(r.g_small[5:6, 0 : n.bias], refs[10:13], refs[25:28], ..., rate_vector)
    for i in range(5):
        update(r.g_small[i : i + 1, 0 : n.rows], refs[13:16], refs[28:31], i, rate_vector)
    for copy in passed:
        copy.wait()


def run_adam(n, got, given):
    f32 = functools.partial(jax.ShapeDtypeStruct, dtype=F32)
    matrix, bias, vec = f32((n.rows, n.hidden)), f32((1, n.bias)), f32((5, 1, n.rows))
    inputs = dict(g1=got.g1, g2=got.g2, g_small=got.g_small, norm=got.norm)
    inputs.update({chr(97 + i): array for i, array in enumerate(given)})
    inputs.update(out=got.out, dx=got.dx)
    outputs = dict(norm_out=f32((1, 1)))
    outputs.update({chr(110 + i): matrix for i in range(6)})
    outputs.update({chr(65 + i): bias for i in range(3)})
    outputs.update({chr(70 + i): vec for i in range(3)})
    outputs.update(
        out_there=jax.ShapeDtypeStruct(got.out.shape, BF16),
        dx_there=jax.ShapeDtypeStruct(got.dx.shape, F32),
    )
    names = tuple(inputs) + tuple(outputs) + ("sem",)
    in_vmem = pl.BlockSpec(memory_space=pltpu.VMEM)
    anywhere = pl.BlockSpec(memory_space=pl.ANY)
    return pl.pallas_call(
        functools.partial(adam_kernel, n, names),
        out_shape=list(outputs.values()),
        in_specs=[in_vmem] * (len(inputs) - 2) + [anywhere] * 2,
        out_specs=[in_vmem] * (len(outputs) - 2) + [anywhere] * 2,
        scratch_shapes=[pltpu.SemaphoreType.DMA((2,))],
        compiler_params=pltpu.CompilerParams(vmem_limit_bytes=32 * 2**20),
        name="adam",
    )(*inputs.values())


def turned(a):
    return jnp.swapaxes(a[0], 0, 1)


def lined(a):
    return jnp.transpose(a, (1, 0, 2))


def fused_layer(
    n,
    activations,
    cotangent,
    w_in,
    w_out,
    b_in,
    vec_params,
    first_w_in,
    second_w_in,
    first_w_out,
    second_w_out,
    first_b_in,
    second_b_in,
    first_vec,
    second_vec,
):
    got = run_layer(
        n,
        activations.reshape(n.tokens, n.width),
        cotangent.reshape(n.tokens, n.width),
        w_in[0],
        turned(w_out),
        b_in,
        lined(vec_params),
    )
    given = (
        *(a[0] for a in (w_in, first_w_in, second_w_in)),
        *(turned(a) for a in (w_out, first_w_out, second_w_out)),
        *(b_in, first_b_in, second_b_in),
        *(lined(a) for a in (vec_params, first_vec, second_vec)),
    )
    norm_value, *made, out, dx = run_adam(n, got, given)
    return (
        out.reshape(activations.shape),
        dx.reshape(activations.shape),
        norm_value.reshape(()),
        *(a[None] for a in made[:3]),
        *(jnp.swapaxes(a, 0, 1)[None] for a in made[3:6]),
        *made[6:9],
        *(lined(a) for a in made[9:]),
    )


def local_layer(mesh, activations, cotangent, w_in, *rest):
    seqs, block, width = activations.shape
    n = Sizes(mesh, seqs, block, width, w_in.shape[2])
    if w_in.shape[0] == 1 and n.fits():
        return fused_layer(n, activations, cotangent, w_in, *rest)
    return general_layer(activations, cotangent, w_in, *rest)


BOTH = ("batch", "seq")


def solution(mesh):
    in_specs = (
        P(*BOTH, None),
        P(*BOTH, None),
        P(None, BOTH, None),
        P(None, None, BOTH),
        P(None, BOTH),
        P(None, None, BOTH),
        P(None, BOTH, None),
        P(None, BOTH, None),
        P(None, None, BOTH),
        P(None, None, BOTH),
        P(None, BOTH),
        P(None, BOTH),
        P(None, None, BOTH),
        P(None, None, BOTH),
    )
    out_specs = (
        P(*BOTH, None),
        P(*BOTH, None),
        P(),
        P(None, BOTH, None),
        P(None, BOTH, None),
        P(None, BOTH, None),
        P(None, None, BOTH),
        P(None, None, BOTH),
        P(None, None, BOTH),
        P(None, BOTH),
        P(None, BOTH),
        P(None, BOTH),
        P(None, None, BOTH),
        P(None, None, BOTH),
        P(None, None, BOTH),
    )
    return jax.shard_map(
        functools.partial(local_layer, mesh), mesh=mesh, in_specs=in_specs, out_specs=out_specs, check_vma=False)
```

```python
import functools
import math
import types

import jax
import jax.numpy as jnp
import ml_dtypes
import numpy as np
from jax import lax
from jax.experimental import pallas as pl
from jax.experimental.pallas import tpu as pltpu
from jax.sharding import PartitionSpec as P

STEP_COUNT = 10


beta_first = 0.5
beta_second = 0.5
rate_matrix = 0.03
rate_vector = 0.2
weight_decay = 0.01
adam_epsilon = 1e-08
norm_epsilon = 1e-06
clip_limit = 1.0


def dft_tables(row_index, column_index, seq_len):
    product = row_index[:, None] * column_index[None, :] % seq_len
    angle = product.astype(jnp.float32) * (2.0 * math.pi / seq_len)
    return (jnp.cos(angle).astype(jnp.bfloat16), jnp.sin(angle).astype(jnp.bfloat16))


def layer_norm(values, gain, shift):
    centre = jnp.mean(values, axis=-1, keepdims=True)
    centred = values - centre
    spread = jnp.mean(centred * centred, axis=-1, keepdims=True)
    return centred * lax.rsqrt(spread + norm_epsilon) * gain + shift


def gelu_tanh(values):
    return jax.nn.gelu(values, approximate=True)


def adam_update(weight, gradient, first, second, rate, step_count):
    first_new = beta_first * first + (1.0 - beta_first) * gradient
    second_new = beta_second * second + (1.0 - beta_second) * gradient * gradient
    first_hat = first_new / (1.0 - beta_first**step_count)
    second_hat = second_new / (1.0 - beta_second**step_count)
    updated = weight - rate * (
        first_hat / (jnp.sqrt(second_hat) + adam_epsilon) + weight_decay * weight
    )
    return (first_new, second_new, updated)


def general_layer(
    activations,
    cotangent,
    w_in,
    w_out,
    b_in,
    vec_params,
    first_w_in,
    second_w_in,
    first_w_out,
    second_w_out,
    first_b_in,
    second_b_in,
    first_vec,
    second_vec,
):
    layers = w_in.shape[0]
    seq_count, block_len, model_width = activations.shape
    seq_devices = lax.axis_size(BOTH[1])
    seq_len = block_len * seq_devices
    dft_scale = 1.0 / math.sqrt(seq_len * model_width)
    first_row = lax.axis_index(BOTH[1]) * block_len
    my_rows = first_row + jnp.arange(block_len, dtype=jnp.int32)
    feature_line = jnp.arange(model_width, dtype=jnp.int32)
    cos_model, sin_model = dft_tables(feature_line, feature_line, model_width)
    table_fwd = jnp.concatenate([cos_model, sin_model], axis=1)
    table_back = jnp.transpose(table_fwd)
    layer_index = 0
    pieces = (
        w_in[layer_index].astype(jnp.bfloat16),
        w_out[layer_index].astype(jnp.bfloat16),
        b_in[layer_index].astype(jnp.bfloat16),
        vec_params[layer_index].astype(jnp.bfloat16),
    )
    gathered = [
        (
            lax.all_gather(pieces[0], BOTH, axis=0, tiled=True),
            lax.all_gather(pieces[1], BOTH, axis=1, tiled=True),
            lax.all_gather(pieces[2], BOTH, axis=0, tiled=True),
            lax.all_gather(pieces[3], BOTH, axis=1, tiled=True),
        )
    ]
    zeros_block = jnp.zeros((seq_count, block_len, model_width), jnp.float32)
    stream = activations.astype(jnp.float32)
    layer_index = 0
    weight_first, weight_second, bias_low, vec_low = gathered[layer_index]
    vec_float = vec_low.astype(jnp.float32)
    bias_float = bias_low.astype(jnp.float32)
    joined = jnp.dot(
        stream.astype(jnp.bfloat16), table_fwd, preferred_element_type=jnp.float32
    ).astype(jnp.bfloat16)
    halves = (joined[..., :model_width], joined[..., model_width:])
    shard_piece = (
        lax.all_gather(halves[0], BOTH[1], axis=1, tiled=True),
        lax.all_gather(halves[1], BOTH[1], axis=1, tiled=True),
    )
    piece_len = shard_piece[0].shape[1]
    cos_block, sin_block = dft_tables(my_rows, jnp.arange(piece_len, dtype=jnp.int32), seq_len)
    running = jnp.einsum(
        "ij,sjd->sid", cos_block, shard_piece[0], preferred_element_type=jnp.float32
    )
    mixed = (
        running
        - jnp.einsum("ij,sjd->sid", sin_block, shard_piece[1], preferred_element_type=jnp.float32)
    ) * dft_scale
    normed, norm_first_back = jax.vjp(layer_norm, stream + mixed, vec_float[0], vec_float[1])
    normed_low = normed.astype(jnp.bfloat16)
    pre_act = jnp.dot(normed_low, weight_first, preferred_element_type=jnp.float32) + bias_float
    activated, gelu_back = jax.vjp(gelu_tanh, pre_act)
    act_low = activated.astype(jnp.bfloat16)
    feed = jnp.dot(act_low, weight_second, preferred_element_type=jnp.float32) + vec_float[2]
    stream, norm_second_back = jax.vjp(layer_norm, normed + feed, vec_float[3], vec_float[4])
    saved = [(norm_first_back, normed_low, gelu_back, act_low, norm_second_back)]
    block_output = stream.astype(jnp.bfloat16)
    grad_now = cotangent.astype(jnp.float32)
    raw_grads = [None] * layers
    for layer_index in reversed(range(layers)):
        weight_first, weight_second, bias_low, vec_low = gathered[layer_index]
        norm_first_back, normed_low, gelu_back, act_low, norm_second_back = saved[layer_index]
        grad_sum2, grad_gain2, grad_shift2 = norm_second_back(grad_now)
        grad_z = grad_sum2.astype(jnp.bfloat16)
        grad_weight_second = jnp.einsum(
            "stf,std->fd", act_low, grad_z, preferred_element_type=jnp.float32
        )
        grad_bias_out = jnp.sum(grad_z.astype(jnp.float32), axis=(0, 1))
        grad_act = jnp.einsum(
            "std,fd->stf", grad_z, weight_second, preferred_element_type=jnp.float32
        )
        (grad_pre,) = gelu_back(grad_act)
        grad_pre_low = grad_pre.astype(jnp.bfloat16)
        grad_weight_first = jnp.einsum(
            "std,stf->df", normed_low, grad_pre_low, preferred_element_type=jnp.float32
        )
        grad_bias_in = jnp.sum(grad_pre_low.astype(jnp.float32), axis=(0, 1))
        grad_normed = (
            jnp.einsum(
                "stf,df->std", grad_pre_low, weight_first, preferred_element_type=jnp.float32
            )
            + grad_sum2
        )
        grad_sum1, grad_gain1, grad_shift1 = norm_first_back(grad_normed)
        grad_mix_low = grad_sum1.astype(jnp.bfloat16)
        add_shard_piece = lax.all_gather(grad_mix_low, BOTH[1], axis=1, tiled=True)
        add_piece_len = add_shard_piece.shape[1]
        add_cos_block, add_sin_block = dft_tables(
            my_rows, jnp.arange(add_piece_len, dtype=jnp.int32), seq_len
        )
        with_cos = jnp.einsum(
            "ij,sjd->sid", add_cos_block, add_shard_piece, preferred_element_type=jnp.float32
        )
        with_sin = (zeros_block, zeros_block)[1] - jnp.einsum(
            "ij,sjd->sid", add_sin_block, add_shard_piece, preferred_element_type=jnp.float32
        )
        with_cos, with_sin = (with_cos, with_sin)
        with_cos = (with_cos * dft_scale).astype(jnp.bfloat16)
        with_sin = (with_sin * dft_scale).astype(jnp.bfloat16)
        grad_halves = jnp.concatenate([with_cos, with_sin], axis=-1)
        grad_now = grad_sum1 + jnp.dot(grad_halves, table_back, preferred_element_type=jnp.float32)
        grad_vec = jnp.stack([grad_gain1, grad_shift1, grad_bias_out, grad_gain2, grad_shift2])
        layer_terms = (grad_weight_first, grad_weight_second, grad_bias_in, grad_vec)
        raw_grads[layer_index] = (
            lax.psum_scatter(layer_terms[0], BOTH, scatter_dimension=0, tiled=True),
            lax.psum_scatter(layer_terms[1], BOTH, scatter_dimension=1, tiled=True),
            lax.psum_scatter(layer_terms[2], BOTH, scatter_dimension=0, tiled=True),
            lax.psum_scatter(layer_terms[3], BOTH, scatter_dimension=1, tiled=True),
        )
    shard_w_in = jnp.stack([entry[0] for entry in raw_grads])
    shard_w_out = jnp.stack([entry[1] for entry in raw_grads])
    shard_b_in = jnp.stack([entry[2] for entry in raw_grads])
    shard_vec = jnp.stack([entry[3] for entry in raw_grads])
    local_squares = jnp.sum(shard_w_in * shard_w_in) + jnp.sum(shard_w_out * shard_w_out)
    local_squares = (
        local_squares + jnp.sum(shard_b_in * shard_b_in) + jnp.sum(shard_vec * shard_vec)
    )
    norm_value = jnp.sqrt(lax.psum(local_squares, BOTH))
    factor = clip_limit / jnp.maximum(norm_value, clip_limit)
    upd_w_in = adam_update(
        w_in, factor * shard_w_in, first_w_in, second_w_in, rate_matrix, STEP_COUNT
    )
    upd_w_out = adam_update(
        w_out, factor * shard_w_out, first_w_out, second_w_out, rate_matrix, STEP_COUNT
    )
    upd_b_in = adam_update(
        b_in, factor * shard_b_in, first_b_in, second_b_in, rate_vector, STEP_COUNT
    )
    upd_vec = adam_update(
        vec_params, factor * shard_vec, first_vec, second_vec, rate_vector, STEP_COUNT
    )
    return (
        block_output,
        grad_now,
        norm_value,
        upd_w_in[0],
        upd_w_in[1],
        upd_w_in[2],
        upd_w_out[0],
        upd_w_out[1],
        upd_w_out[2],
        upd_b_in[0],
        upd_b_in[1],
        upd_b_in[2],
        upd_vec[0],
        upd_vec[1],
        upd_vec[2],
    )


MESH = pl.DeviceIdType.MESH
F32 = jnp.float32
BF16 = jnp.bfloat16
NN = (((1,), (0,)), ((), ()))
NT = (((1,), (1,)), ((), ()))
TN = (((0,), (0,)), ((), ()))


def dot(a, b, dims=NN):
    return lax.dot_general(a, b, dims, preferred_element_type=F32)


class Sizes:
    def __init__(self, mesh, seqs, block, width, hidden):
        self.batch, self.seq = mesh.shape["batch"], mesh.shape["seq"]
        self.xs, self.ys, self.zs = self.batch // 2, 2, self.seq // 2
        self.devices = self.batch * self.seq
        self.seqs, self.block, self.width, self.hidden = seqs, block, width, hidden
        self.length = block * self.seq
        self.rows = width // self.devices
        self.slab = 2 * self.rows
        self.segment = self.zs * self.slab
        self.half = hidden // 2
        self.cols = 512
        self.chunks = self.half // self.cols
        self.parts = 2
        self.thin = self.cols // self.parts
        self.packed = width // self.seq
        self.tokens = seqs * block
        self.bias = hidden // self.devices

    def fits(self):
        return (
            self.batch == 4
            and self.seq % 2 == 0
            and self.width % self.devices == 0
            and self.slab % 16 == 0
            and self.packed % 32 == 0
            and self.block % 128 == 0
            and self.zs == 4
            and self.half % self.cols == 0
            and self.rows <= 128
            and self.bias <= 128
            and 5 * self.rows <= self.width
            and self.hidden == 4 * self.width
        )

    def owner(self, x, core, z, y):
        return (2 * x + core) * self.seq + 2 * z + y

    def place_owner(self):
        return [
            self.owner(x, core, z, y)
            for y in range(self.ys)
            for x in range(self.xs)
            for z in range(self.zs)
            for core in range(2)
        ]


def cos_sin(rows, columns, count):
    angle = (rows[:, None] * columns[None, :] % count) * (2.0 * math.pi / count)
    return np.cos(angle), np.sin(angle)


def host_tables(n):
    width, half = n.width, n.packed // 2
    owners = np.array(n.place_owner())
    order = (owners[:, None] * n.rows + np.arange(n.rows)[None, :]).reshape(-1)
    line = np.arange(width)
    cosine, sine = cos_sin(line, line, width)
    pack = np.zeros((width, width))
    unpack = np.zeros((width, width))
    for k in range(width // 2):
        device, inner = divmod(k, half)
        at_cos = device * n.packed + inner
        at_sin = at_cos + half
        pack[at_cos] = cosine[k]
        unpack[at_cos, k] = 1.0
        if k:
            unpack[at_cos, width - k] = 1.0
            pack[at_sin] = sine[k]
            unpack[at_sin, k] = -1.0
            unpack[at_sin, width - k] = 1.0
    pack[half] = cosine[width // 2]
    unpack[half, width // 2] = 1.0
    perm = np.zeros((width, width))
    perm[order, np.arange(width)] = 1.0
    positions = np.arange(n.length)
    by_length = np.stack(cos_sin(positions, positions, n.length))
    vec_mask = np.zeros((n.devices, width))
    vec_mask[np.repeat(owners, n.rows), np.arange(width)] = 1.0
    vec_spread = np.zeros((128, width))
    vec_spread[np.arange(width) % n.rows, np.arange(width)] = 1.0
    bias_spread = np.zeros((128, n.half))
    bias_spread[np.arange(n.half) % n.bias, np.arange(n.half)] = 1.0

    def low(a):
        return jnp.asarray(a.astype(np.float32).astype(ml_dtypes.bfloat16))

    return types.SimpleNamespace(
        tt_f=low(pack),
        by_length=low(by_length),
        un_f=low(unpack[:, order]),
        perm=low(perm),
        tt_b=low(pack[:, order]),
        un_b=low(unpack),
        vec_mask=jnp.asarray(vec_mask.astype(np.float32)),
        vec_spread=low(vec_spread),
        bias_spread=low(bias_spread),
    )


LOADS = dict(
    bias="bias_v",
    vec="vec_v",
    w1="w1_v",
    w2="w2_v",
    x="x_v",
    tt_f="tt_v",
    dy="dy_v",
    vec_spread="vec_spread_v",
    bias_spread="bias_spread_v",
    vec_mask="vec_mask_v",
    by_length="by_length_v",
    perm="perm_v",
    un_f="un_v",
    tt_b="tt_v",
    un_b="un_v",
)
FIRST = ("w1", "w2", "x", "tt_f")
LATER = ("tt_b", "un_b")
FORWARD_KINDS = (1, 1, 1, 1, 0, 2)
BACK_KINDS = (0, 7, 7, 0, 1, 1, 1, 1, 5, 0, 5, 5)


def layer_kernel(n, names, *refs):
    r = types.SimpleNamespace(**dict(zip(names, refs)))
    batch_at, seq_at = lax.axis_index("batch"), lax.axis_index("seq")
    x, core = batch_at // 2, batch_at % 2
    z, y = seq_at // 2, seq_at % 2
    tokens, width, seg, slab = n.tokens, n.width, n.segment, n.slab

    def aligned(at, by):
        return pl.multiple_of(at * by, by)

    def rows_of(at, by):
        return pl.ds(aligned(at, by), by)

    def remote(src, dst, send, recv, batch_to, seq_to):
        return pltpu.make_async_remote_copy(
            src_ref=src,
            dst_ref=dst,
            send_sem=send,
            recv_sem=recv,
            device_id=(batch_to, seq_to),
            device_id_type=MESH,
        )

    def bytes_of(view, send, recv):
        return remote(view, view, send, recv, other_core, seq_at)

    other_core = 2 * x + 1 - core
    other_x = 2 * (1 - x) + core
    other_y = 2 * z + 1 - y

    def plane(k):
        return (seq_at + k) % n.seq

    def plane_from(k):
        return (seq_at + n.seq - k) % n.seq

    def across(k):
        return (batch_at + k) % n.batch

    def across_from(k):
        return (batch_at + n.batch - k) % n.batch

    loads = types.SimpleNamespace()
    for name, held in LOADS.items():
        load = pltpu.make_async_copy(
            getattr(r, name), getattr(r, held), r.load_sem.at[sorted(set(LOADS.values())).index(held)]
        )
        setattr(loads, name, load)
    for name in FIRST:
        getattr(loads, name).start()

    everyone = [
        ((batch_at + i // n.seq) % n.batch, (seq_at + i % n.seq) % n.seq)
        for i in range(1, n.devices)
    ]
    barrier = pltpu.get_barrier_semaphore()
    for device in everyone:
        pl.semaphore_signal(barrier, inc=1, device_id=device, device_id_type=MESH)
    pl.semaphore_wait(barrier, n.devices - 1)

    loads.w1.wait()
    loads.w2.wait()
    weights = (r.w1_v, r.w2_v)
    give = pl.ds(aligned(1 - core, n.half), n.half)
    keep = pl.ds(aligned(core, n.half), n.half)
    core_rows = pl.ds(aligned(core, n.rows), n.rows)
    their_rows = pl.ds(aligned(1 - core, n.rows), n.rows)
    for m in range(2):
        remote(
            weights[m].at[:, give],
            r.stage.at[m, core_rows],
            r.swap_send.at[m],
            r.swap_recv.at[m],
            other_core,
            seq_at,
        ).start()

    for name in LOADS:
        if name not in FIRST and name not in LATER:
            getattr(loads, name).start()

    def swapped(m):
        return bytes_of(r.stage.at[m, pl.ds(0, n.rows)], r.swap_send.at[m], r.swap_recv.at[m])

    def mix_start(t, source, table):
        y_ref, l_ref = r.y_buf.at[t], r.l_buf.at[t]
        y_ref[...] = dot(table[...], source, NT).astype(BF16)
        l_ref[seq_at] = y_ref[rows_of(seq_at, n.packed), :]

    def mix_send(t):
        y_ref, l_ref = r.y_buf.at[t], r.l_buf.at[t]
        for k in range(1, n.seq):
            remote(
                y_ref.at[rows_of(plane(k), n.packed)],
                l_ref.at[seq_at],
                r.mix_send.at[0],
                r.mix_recv.at[2 * t],
                batch_at,
                plane(k),
            ).start()

    def mixed_bytes(i):
        into = (r.l_buf, r.r_buf)[i % 2].at[i // 2, pl.ds(0, n.seq - 1)]
        return bytes_of(into, r.mix_send.at[i % 2], r.mix_recv.at[i])

    def mix_turn(t):
        l_ref, z_ref, r_ref = r.l_buf.at[t], r.z_buf.at[t], r.r_buf.at[t]
        mixed_bytes(2 * t).wait_recv()
        left = jnp.concatenate(
            [
                jnp.concatenate(
                    [l_ref[d, :, g * n.block : (g + 1) * n.block] for d in range(n.seq)], axis=1
                )
                for g in range(n.seqs)
            ],
            axis=0,
        )
        r.left[...] = left
        inner = lax.broadcasted_iota(jnp.int32, (n.seqs * n.packed, 1), 0) % n.packed
        first = (inner < n.packed // 2) | ((inner == n.packed // 2) & (seq_at == 0))
        scale = 1.0 / math.sqrt(n.length * n.width)
        for e in range(0, n.seq, 2):
            at = slice(e * n.block, (e + 2) * n.block)
            by_cos = dot(r.left[...], r.by_length_v[0, :, at])
            by_sin = dot(r.left[...], r.by_length_v[1, :, at])
            value = (jnp.where(first, by_cos, by_sin) * scale).astype(BF16)
            z_ref[e] = value[:, : n.block]
            z_ref[e + 1] = value[:, n.block :]
        for k in range(1, n.seq):
            remote(
                z_ref.at[plane(k)],
                r_ref.at[seq_at],
                r.mix_send.at[1],
                r.mix_recv.at[2 * t + 1],
                batch_at,
                plane(k),
            ).start()
        r_ref[seq_at] = z_ref[seq_at]

    def mix_finish(t, table):
        r_ref = r.r_buf.at[t]
        mixed_bytes(2 * t + 1).wait_recv()
        parts = [
            r_ref[:, g * n.packed : (g + 1) * n.packed, :].reshape(width, n.block)
            for g in range(n.seqs)
        ]
        r.mixed[...] = dot(jnp.concatenate(parts, axis=1), table[...], TN)

    loads.tt_f.wait()
    loads.x.wait()
    mix_start(0, r.x_v[...], r.tt_v)

    full = r.full
    mate_z = z + 1 - 2 * (z % 2)
    pair_z = z // 2
    inner = (z > 0) & (z < n.zs - 1)

    def line(to_z):
        return batch_at, 2 * to_z + y

    def seg_rows(sx, sy):
        return rows_of(sy * n.xs + sx, seg)

    def pair_rows(sx, sy, sp):
        return rows_of((sy * n.xs + sx) * 2 + sp, 2 * slab)

    def slab_rows(sx, sy, sz):
        return rows_of((sy * n.xs + sx) * n.zs + sz, slab)

    def peer(t):
        return (other_y_at, other_x_at)[t == 0]

    other_x_at = (other_x, seq_at)
    other_y_at = (batch_at, other_y)

    def away(t):
        return (1 - x, y) if t == 0 else (x, 1 - y)

    def turn_of(c):
        return FORWARD_KINDS[c] % 2

    def split(c):
        return FORWARD_KINDS[c] // 2 == 1

    def place(c):
        return c // n.chunks, c % n.chunks

    def stage_weights(m):
        r.stage[m, core_rows, :] = weights[m][:, keep]
        swapped(m).wait_recv()
        for q in range(n.chunks):
            columns = r.stage[m, :, q * n.cols : (q + 1) * n.cols]
            full[m, q, slab_rows(x, y, z), :] = columns.astype(BF16)

    def full_copy(c, at, send, recv, to):
        m, q = place(c)
        return remote(full.at[m, q, at], full.at[m, q, at], send, recv, *to)

    def rows_at(sx, sy, i):
        return (slab_rows(sx, sy, z), slab_rows(sx, sy, mate_z), pair_rows(sx, sy, 1 - pair_z))[i]

    def side_copy(c, i, sx, sy, first):
        t = turn_of(c)
        recv = r.first_recv.at[i, c] if first else r.second_recv.at[c]
        return full_copy(c, rows_at(sx, sy, i), r.side_send, recv, peer(t if first else 1 - t))

    def to_sides(c, i):
        if i == 0 or not split(c):
            side_copy(c, i, x, y, True).start()
        side_copy(c, i, x, y, False).start()

    def line_slot(c, far):
        return 2 * n.chunks + sum(split(d) for d in range(c)) if far else c

    def line_seg(c, far):
        return away(turn_of(c)) if far else (x, y)

    def own_to_mate(c, far):
        at = rows_at(*line_seg(c, far), 0)
        return full_copy(c, at, r.side_send, r.mate_recv.at[line_slot(c, far)], line(mate_z))

    def mate_arrives(c, far):
        at = rows_at(*line_seg(c, far), 1)
        full_copy(c, at, r.side_send, r.mate_recv.at[line_slot(c, far)], line(mate_z)).wait_recv()

    def pair_across(c, far):
        at = pair_rows(*line_seg(c, far), pair_z)
        return full_copy(c, at, r.inner_send, r.pair_recv.at[line_slot(c, far)], line(n.zs - 1 - z))

    def pair_out(c, far):
        at = rows_at(*line_seg(c, far), 2)
        return full_copy(c, at, r.inner_send, r.pair_recv.at[line_slot(c, far)], line(mate_z))

    def own_sides(c):
        to_sides(c, 0)

    def own_line(c):
        own_to_mate(c, 0).start()

    def from_mate(c, far):
        mate_arrives(c, far)

        @pl.when(inner)
        def _():
            pair_across(c, far).start()

    def from_pair(c, far):
        pair_out(c, far).wait_recv()

        @pl.when(inner)
        def _():
            pair_out(c, far).start()

    def mate_in(c):
        from_mate(c, 0)
        to_sides(c, 1)

    def pair_in(c):
        from_pair(c, 0)
        to_sides(c, 2)

    def pass_on(c, i):
        ax, ay = away(turn_of(c))
        if i == 0 or not split(c):
            side_copy(c, i, ax, ay, True).wait_recv()
        if split(c):
            if i == 0:
                own_to_mate(c, 1).start()
            else:
                (from_mate, from_pair)[i - 1](c, 1)
        side_copy(c, i, ax, ay, False).start()

    def weights_here(c):
        m, q = place(c)
        second = full.at[m, q, pl.ds(0, 2 * n.zs * slab)]
        bytes_of(second, r.side_send, r.second_recv.at[c]).wait_recv()

    def all_slabs(counts, send):
        rows = sum(counts) * slab // (2 * n.chunks)
        return bytes_of(full.at[:, :, pl.ds(0, rows)], send, r.second_recv.at[0])

    def small_tiles():
        loads.bias.wait()
        loads.vec.wait()
        tile = r.tile
        tile[...] = jnp.zeros(tile.shape, F32)
        for i in range(5):
            tile[i : i + 1, 0 : n.rows] = r.vec_v[i]
        tile[5:6, 0 : n.bias] = r.bias_v[...]
        small[batch_at, seq_at] = tile[...]
        for k in range(1, n.seq):
            small_copy(k, seq_at).start()

    def small_copy(k, at):
        return remote(
            r.tile,
            small.at[batch_at, at],
            r.small_send,
            r.small_recv,
            batch_at,
            plane(k),
        )

    def row_copy(k, at):
        return remote(
            small.at[batch_at],
            small.at[at],
            r.row_send,
            r.row_recv,
            across(k),
            seq_at,
        )

    small = r.small

    def tiles_bytes():
        return bytes_of(small.at[0, pl.ds(0, n.seq - 1)], r.small_send, r.small_recv)

    def rows_bytes():
        return bytes_of(small.at[pl.ds(0, n.batch - 1)], r.row_send, r.row_recv)

    def small_rows():
        tiles_bytes().wait_recv()
        for k in range(1, n.batch):
            row_copy(k, batch_at).start()

    half_owners = n.devices // 2
    bias_mask = (
        lax.broadcasted_iota(jnp.int32, (half_owners, n.half), 0)
        == lax.broadcasted_iota(jnp.int32, (half_owners, n.half), 1) // n.bias
    )

    def small_vectors():
        rows_bytes().wait_recv()
        for load in (loads.vec_spread, loads.bias_spread, loads.vec_mask):
            load.wait()
        for i in range(5):
            held = small[:, :, i, :].reshape(n.devices, 128).astype(BF16)
            spread = dot(held, r.vec_spread_v[...]) * r.vec_mask_v[...]
            r.vecs[i : i + 1, :] = jnp.sum(spread, axis=0, keepdims=True)
        held = small[pl.ds(core * (n.batch // 2), n.batch // 2), :, 5, :]
        held = held.reshape(half_owners, 128).astype(BF16)
        spread = jnp.where(bias_mask, dot(held, r.bias_spread_v[...]), 0.0)
        biases = jnp.sum(spread, axis=0, keepdims=True)
        for q in range(n.chunks):
            r.biases[q] = biases[:, q * n.cols : (q + 1) * n.cols]

    def place_inputs():
        loads.perm.wait()
        loads.dy.wait()
        r.x_place[...] = dot(r.x_v[...], r.perm_v[...])
        r.dy_place[...] = dot(r.dy_v[...], r.perm_v[...])

    def turn_forward():
        loads.by_length.wait()
        mix_turn(0)

    step = 32
    tall = 64
    mine, theirs = pl.ds(0, tokens), pl.ds(tokens, tokens)

    def row_loop(body, first=0, last=tokens):
        @pl.loop(first // tall, last // tall, unroll=True)
        def _(i):
            body(pl.ds(pl.multiple_of(i * tall, tall), tall))

    def mean(v):
        return jnp.mean(v, axis=-1, keepdims=True)

    def first_norm(at):
        v = r.x_place[at, :] + r.mixed[at, :]
        centred = v - mean(v)
        scale = lax.rsqrt(mean(centred * centred) + norm_epsilon)
        unit = centred * scale
        h = unit * r.vecs[0:1, :] + r.vecs[1:2, :]
        r.unit1[at, :] = unit
        r.scale1[at, :] = jnp.broadcast_to(scale, (tall, 128))
        r.h[at, :] = h
        r.h_low[at, :] = h.astype(BF16)

    def swap(i, src, dst):
        return remote(src, dst, r.core_send, r.core_recv.at[i], other_core, seq_at)

    def swap_h():
        return swap(0, r.h_low.at[mine], r.h_low.at[theirs])

    def norm_forward():
        loads.un_f.wait()
        mix_finish(0, r.un_v)
        loads.tt_b.start()
        loads.un_b.start()
        row_loop(first_norm)
        swap_h().start()

    root = math.sqrt(2.0 / math.pi)

    lifted_parts = []

    def lift(q):
        if not lifted_parts:
            swap_h().wait_recv()
        lifted_parts.append(q)
        weights_here(q)
        r.lift[...] = dot(r.h_low[...], full[0, q]) + r.biases[q]

        @pl.loop(0, 2 * tokens // step)
        def _(i):
            at = pl.ds(pl.multiple_of(i * step, step), step)
            u = r.lift[at, :]
            square = u * u
            bent = jnp.tanh(u * (root + (root * 0.044715) * square))
            half_up = 0.5 + 0.5 * bent
            r.act[q, at, :] = (u * half_up).astype(BF16)
            r.slope[q, at, :] = half_up + (u * (1.0 - bent * bent)) * (
                0.5 * root + (1.5 * root * 0.044715) * square
            )

    gathered_parts = []

    halves = [pl.ds(j * tokens // 2, tokens // 2) for j in range(2)]

    def swap_ff(j):
        return swap(1 + j, r.part_low.at[halves[j]], r.part_in.at[halves[j]])

    def drop(q):
        weights_here(n.chunks + q)
        gathered_parts.append(q)
        for half in (theirs, mine):
            part = dot(r.act[q, half, :], full[1, q], NT)
            part = r.total[half, :] + part if len(gathered_parts) > 1 else part
            if len(gathered_parts) == n.chunks and half is theirs:
                r.part_low[...] = part.astype(BF16)
                for j in range(2):
                    swap_ff(j).start()
            else:
                r.total[half, :] = part

    def send_forward():
        mix_send(0)

    forward_steps = (
        (send_forward,), (stage_weights, 0), (own_sides, 1), (own_sides, 0), (own_line, 2),
        (own_sides, 2), (own_line, 1), (own_line, 0), (stage_weights, 1), (own_sides, 4),
        (own_sides, 3), (place_inputs,), (own_line, 3), (own_sides, 5), (own_line, 4),
        (pass_on, 1, 0), (small_tiles,), (pass_on, 0, 0), (mate_in, 2), (mate_in, 1),
        (pass_on, 5, 0), (pass_on, 2, 0), (own_line, 5), (mate_in, 0), (pass_on, 4, 0),
        (mate_in, 3), (mate_in, 4), (pass_on, 2, 1), (pass_on, 3, 0), (pair_in, 2),
        (small_rows,), (pass_on, 1, 1), (pair_in, 1), (pass_on, 5, 1), (turn_forward,),
        (pass_on, 0, 1), (mate_in, 5), (pass_on, 3, 1), (pair_in, 0), (pass_on, 4, 1),
        (pass_on, 2, 2), (pair_in, 4), (small_vectors,), (pass_on, 1, 2), (pair_in, 3),
        (pass_on, 5, 2), (pass_on, 0, 2), (norm_forward,), (pass_on, 4, 2), (pair_in, 5),
        (pass_on, 3, 2), (lift, 1), (lift, 2), (lift, 0), (drop, 1), (drop, 0), (drop, 2),
    )
    for task, *which in forward_steps:
        task(*which)
    def second_norm(at):
        v = (
            r.h[at, :]
            + r.total[at, :]
            + r.part_in[at, :].astype(F32)
            + r.vecs[2:3, :]
        )
        centred = v - mean(v)
        scale = lax.rsqrt(mean(centred * centred) + norm_epsilon)
        unit = centred * scale
        gain = r.vecs[3:4, :]
        r.h[at, :] = unit
        r.out_low[at, :] = (unit * gain + r.vecs[4:5, :]).astype(BF16)
        du = r.dy_place[at, :] * gain
        dv = scale * (du - mean(du) - unit * mean(du * unit))
        r.dr2[at, :] = dv
        r.dz[at, :] = dv.astype(BF16)

    def swap_dz(j):
        return swap(
            3 + j,
            r.dz.at[halves[j]],
            r.dz.at[pl.ds(tokens + j * tokens // 2, tokens // 2)],
        )

    for j in range(2):
        swap_ff(j).wait_recv()
        row_loop(second_norm, j * tokens // 2, (j + 1) * tokens // 2)
        swap_dz(j).start()

    pieces = grad_pieces(n)
    acc = r.acc

    def wide(c):
        slot, start, width_of = pieces[c]
        m, q = slot // (n.chunks * n.parts), slot % (n.chunks * n.parts)
        return 1 - m, q // n.parts, pl.ds((q % n.parts) * n.thin + start, width_of)

    def held(c, at=slice(None), lead=()):
        slot, start, width_of = pieces[c]
        return (slot, *lead, at, pl.ds(start, width_of))

    def product(c, tokens_at):
        m, q, at = wide(c)
        left, right = (r.dz, r.act) if m else (r.h_low, r.dpre)
        return dot(left[tokens_at, :], right[q, tokens_at, at], TN)

    begun = (1, 4, 3)
    for c in begun:
        acc[held(c)] = product(c, mine)
    for j in range(2):
        swap_dz(j).wait_recv()

    out_low = r.give

    def grad_copy(c, at, into, recv, to):
        return remote(out_low.at[held(c, at)], into, r.grad_send, recv, *to)

    def back_turn(c):
        return BACK_KINDS[c] % 2

    def back_mode(c):
        return BACK_KINDS[c] // 2

    def back_slot(c):
        return [d for d, kind in enumerate(BACK_KINDS) if kind // 2 == back_mode(c)].index(c)

    def copy_diagonal(c):
        at = seg_rows(1 - x, 1 - y)
        return grad_copy(c, at, r.in_diagonal.at[held(c)], r.diagonal_recv.at[c], peer(1 - back_turn(c)))

    def copy_near(c):
        t = 1 - back_turn(c)
        into = r.in_sides.at[held(c, lead=(0,))]
        return grad_copy(c, seg_rows(*away(t)), into, r.sides_recv.at[c], peer(t))

    def copy_side(c):
        t = back_turn(c)
        into = r.in_sides.at[held(c, lead=(1,))]
        return grad_copy(c, seg_rows(*away(t)), into, r.sides_recv.at[c], peer(t))

    def back_seg(c, far):
        return away(back_turn(c)) if far else (x, y)

    def tree_slot(c):
        return sum(kind // 2 < 2 for kind in BACK_KINDS[:c])

    def line_into(c, far, i):
        if far:
            into = (r.far_mate, r.far_pair, r.far_across)[i]
            return into.at[back_slot(c), :, pl.ds(0, pieces[c][2])]
        into, lead = ((r.in_end, (0,)), (r.in_pair, ()), (r.in_across, ()))[i]
        return into.at[held(c, lead=lead)]

    def line_copy(c, at, far, i, to):
        if far:
            recv = r.far_recv.at[i, back_slot(c)]
        else:
            recv = r.end_recv.at[c] if i == 0 else r.tree_recv.at[i - 1, tree_slot(c)]
        return grad_copy(c, at, line_into(c, far, i), recv, to)

    def copy_mate(c, far):
        at = slab_rows(*back_seg(c, far), mate_z)
        return line_copy(c, at, far, 0, line(mate_z))

    def copy_pair_in(c, far):
        at = pair_rows(*back_seg(c, far), 1 - pair_z)
        return line_copy(c, at, far, 1, line(mate_z))

    def copy_pair_across(c, far):
        at = pair_rows(*back_seg(c, far), 1 - pair_z)
        return line_copy(c, at, far, 2, line(n.zs - 1 - z))

    def copy_far(c):
        t = back_turn(c)
        at = slab_rows(*away(t), z)
        return grad_copy(c, at, r.in_end.at[held(c, lead=(1,))], r.end_recv.at[c], peer(t))

    def copy_direct(c, d):
        to_z = (z + d) % n.zs
        at = slab_rows(x, y, to_z)
        return grad_copy(c, at, r.in_end.at[held(c, lead=(d - 1,))], r.end_recv.at[c], line(to_z))

    def round_out(c, at, *more):
        value = acc[held(c, at)]
        for ref in more:
            value = value + ref[...].astype(F32)
        out_low[held(c, at)] = value.astype(BF16)

    four = [(sx, sy) for sy in range(n.ys) for sx in range(n.xs)]

    def first_copy(c, i, which):
        sx, sy = four[i]
        slot, lanes = back_slot(c), pl.ds(0, pieces[c][2])
        if which == 0:
            at, to = slab_rows(sx, sy, mate_z), line(mate_z)
        else:
            at, to = pair_rows(sx, sy, 1 - pair_z), line((0, mate_z, n.zs - 1 - z)[which])
        into = (r.first_mate, r.first_pair, r.first_across)[which].at[slot, i, :, lanes]
        return grad_copy(c, at, into, r.line_recv.at[which, slot], to)

    def first_wait(c, which):
        slot, lanes = back_slot(c), pl.ds(0, pieces[c][2])
        into = (r.first_mate, r.first_pair, r.first_across)[which].at[slot, :, :, lanes]
        bytes_of(into, r.grad_send, r.line_recv.at[which, slot]).wait_recv()

    def first_start(c):
        @pl.when(jnp.logical_not(inner))
        def _():
            for i, (sx, sy) in enumerate(four):
                round_out(c, pair_rows(sx, sy, 1 - pair_z))
                first_copy(c, i, 1).start()
            for i, (sx, sy) in enumerate(four):
                round_out(c, slab_rows(sx, sy, mate_z))
                first_copy(c, i, 0).start()

    def first_across(c):
        @pl.when(inner)
        def _():
            first_wait(c, 1)
            for i, (sx, sy) in enumerate(four):
                lanes = pl.ds(0, pieces[c][2])
                more = r.first_pair.at[back_slot(c), i, :, lanes]
                round_out(c, pair_rows(sx, sy, 1 - pair_z), more)
                first_copy(c, i, 2).start()

    def first_out(c):
        @pl.when(inner)
        def _():
            first_wait(c, 2)
            for i, (sx, sy) in enumerate(four):
                at = held(c, pair_rows(sx, sy, pair_z))
                lanes = pl.ds(0, pieces[c][2])
                acc[at] = acc[at] + r.first_across[back_slot(c), i, :, lanes].astype(F32)
                round_out(c, slab_rows(sx, sy, mate_z))
                first_copy(c, i, 0).start()

    def slab_copy(c, i):
        t = back_turn(c)
        sx, sy = ((1 - x, 1 - y), away(1 - t), away(t))[i]
        own = pl.ds(0, slab)
        into = (
            r.in_diagonal.at[held(c, own)] if i == 0 else r.in_sides.at[held(c, own, lead=(i - 1,))]
        )
        recv = r.diagonal_recv if i == 0 else r.sides_recv
        return grad_copy(c, slab_rows(sx, sy, z), into, recv.at[c], peer(t if i == 2 else 1 - t))

    def slabs_near(c):
        first_wait(c, 0)
        lanes = pl.ds(0, pieces[c][2])
        for i, (sx, sy) in enumerate(four):
            at = held(c, slab_rows(sx, sy, z))
            acc[at] = acc[at] + r.first_mate[back_slot(c), i, :, lanes].astype(F32)
        t = back_turn(c)
        for i, seg_at in enumerate(((1 - x, 1 - y), away(1 - t))):
            round_out(c, slab_rows(*seg_at, z))
            slab_copy(c, i).start()

    def slabs_side(c):
        slab_copy(c, 0).wait_recv()
        own = pl.ds(0, slab)
        round_out(c, slab_rows(*away(back_turn(c)), z), r.in_diagonal.at[held(c, own)])
        slab_copy(c, 2).start()

    def slabs_end(c):
        own = pl.ds(0, slab)
        both = r.in_sides.at[held(c, own, lead=(pl.ds(0, 2),))]
        bytes_of(both, r.grad_send, r.sides_recv.at[c]).wait_recv()
        value = acc[held(c, slab_rows(x, y, z))]
        return value + sum(r.in_sides[held(c, own, lead=(i,))].astype(F32) for i in range(2))

    def grad_product(c):
        if c in begun:
            acc[held(c)] = acc[held(c)] + product(c, theirs)
        else:
            acc[held(c)] = product(c, slice(None))
        if back_mode(c) == 3:
            first_start(c)
            return
        round_out(c, seg_rows(1 - x, 1 - y))
        copy_diagonal(c).start()
        round_out(c, seg_rows(*away(1 - back_turn(c))))
        copy_near(c).start()

    def line_start(c, far):
        @pl.when(jnp.logical_not(inner))
        def _():
            sx, sy = back_seg(c, far)
            round_out(c, pair_rows(sx, sy, 1 - pair_z))
            copy_pair_in(c, far).start()
            round_out(c, slab_rows(sx, sy, mate_z))
            copy_mate(c, far).start()

    def grad_side(c):
        if back_mode(c) == 3:
            first_across(c)
            return
        copy_diagonal(c).wait_recv()
        at = seg_rows(*away(back_turn(c)))
        if back_mode(c) == 1:
            acc[held(c, at)] = acc[held(c, at)] + r.in_diagonal[held(c)].astype(F32)
            line_start(c, 1)
        else:
            round_out(c, at, r.in_diagonal.at[held(c)])
            copy_side(c).start()

    def grad_line(c):
        if back_mode(c) == 3:
            first_out(c)
            return
        sides = 1 if back_mode(c) == 1 else 2
        both = r.in_sides.at[held(c, lead=(pl.ds(0, sides),))]
        bytes_of(both, r.grad_send, r.sides_recv.at[c]).wait_recv()
        more = sum(r.in_sides[held(c, lead=(i,))].astype(F32) for i in range(sides))
        at = seg_rows(x, y)
        acc[held(c, at)] = acc[held(c, at)] + more
        if back_mode(c) == 2:
            for d in range(1, n.zs):
                round_out(c, slab_rows(x, y, (z + d) % n.zs))
                copy_direct(c, d).start()
        else:
            line_start(c, 0)

    def fars(c):
        return range((1, 2, 0, 0)[back_mode(c)])

    def grad_across(c):
        if back_mode(c) == 3:
            slabs_near(c)
        for far in fars(c):

            @pl.when(inner)
            def _(far=far):
                copy_pair_in(c, far).wait_recv()
                at = pair_rows(*back_seg(c, far), 1 - pair_z)
                round_out(c, at, line_into(c, far, 1))
                copy_pair_across(c, far).start()

    def grad_out(c):
        if back_mode(c) == 3:
            slabs_side(c)
        for far in fars(c):

            @pl.when(inner)
            def _(far=far):
                copy_pair_across(c, far).wait_recv()
                sx, sy = back_seg(c, far)
                at = pair_rows(sx, sy, pair_z)
                acc[held(c, at)] = acc[held(c, at)] + line_into(c, far, 2)[...].astype(F32)
                round_out(c, slab_rows(sx, sy, mate_z))
                copy_mate(c, far).start()

    def grad_far(c):
        if back_mode(c) == 1:
            copy_mate(c, 1).wait_recv()
            round_out(c, slab_rows(*away(back_turn(c)), z), line_into(c, 1, 0))
            copy_far(c).start()

    grads_out = (r.g1, r.g2)
    r.squares[...] = jnp.zeros((8, 128), F32)

    def squares_of(v):
        v = v * v
        v = jnp.sum(v.reshape(v.shape[0] // 8, 8, v.shape[1]), axis=0)
        return sum(v[:, i : i + 128] for i in range(0, v.shape[1], 128))

    def copy_back(c):
        return remote(
            r.final.at[held(c, their_rows)],
            r.final_in.at[held(c)],
            r.back_send,
            r.back_recv,
            other_core,
            seq_at,
        )

    def grad_end(c):
        m, q, at = wide(c)
        if back_mode(c) == 3:
            value = slabs_end(c)
        else:
            value = acc[held(c, slab_rows(x, y, z))]
            ends = back_mode(c) + 1
            all_ends = r.in_end.at[held(c, lead=(pl.ds(0, ends),))]
            bytes_of(all_ends, r.grad_send, r.end_recv.at[c]).wait_recv()
            for i in range(ends):
                value = value + r.in_end[held(c, lead=(i,))].astype(F32)
        r.squares[...] += squares_of(value)
        r.final[held(c)] = value
        own_at = pl.ds(aligned(core, n.half) + q * n.cols + at.start, at.size)
        grads_out[m][:, own_at] = r.final[held(c, core_rows)]
        copy_back(c).start()

    back_parts = []

    def slope_back(q):
        r.lift[...] = dot(r.dz[...], full[1, q])
        r.bias_sum[q] = jnp.zeros((8, n.cols), F32)

        @pl.loop(0, 2 * tokens // step)
        def _(i):
            at = pl.ds(pl.multiple_of(i * step, step), step)
            low = (r.lift[at, :] * r.slope[q, at, :]).astype(BF16)
            r.dpre[q, at, :] = low
            r.bias_sum[q] += jnp.sum(low.astype(F32).reshape(step // 8, 8, n.cols), axis=0)

        back_parts.append(q)
        for half in (theirs, mine):
            part = dot(r.dpre[q, half, :], full[0, q], NT)
            part = r.total[half, :] + part if len(back_parts) > 1 else part
            if len(back_parts) == n.chunks and half is theirs:
                r.part_low2[...] = part.astype(BF16)
                swap_dh().start()
            else:
                r.total[half, :] = part

    def swap_dh():
        return swap(5, r.part_low2, r.part_in2)

    def first_norm_back(at):
        dh = r.total[at, :] + r.part_in2[at, :].astype(F32) + r.dr2[at, :]
        unit = r.unit1[at, :]
        r.x_place[at, :] = dh
        du = dh * r.vecs[0:1, :]
        dv = r.scale1[at, 0:1] * (du - mean(du) - unit * mean(du * unit))
        low = dv.astype(BF16)
        r.dm[at, :] = low
        r.rest[at, :] = (dv - low.astype(F32)).astype(BF16)

    def norm_back():
        swap_dh().wait_recv()
        row_loop(first_norm_back)
        loads.tt_b.wait()
        mix_start(1, r.dm[...], r.tt_v)
        mix_send(1)

    def thirds(v):
        high = v.astype(BF16)
        left = v - high.astype(F32)
        mid = left.astype(BF16)
        return high, mid, (left - mid.astype(F32)).astype(BF16)

    def small_gather(v, spread):
        return sum(dot(part, spread, NT) for part in thirds(v))

    def row_sums(k):
        return remote(
            r.small_out.at[across(k)],
            r.small_in.at[k - 1],
            r.row_send2,
            r.row_recv2,
            across(k),
            seq_at,
        )

    def tile_sums(k):
        return remote(
            r.small_mid.at[plane(k)],
            r.small_last.at[k - 1],
            r.small_send2,
            r.small_recv2,
            batch_at,
            plane(k),
        )

    row_sums_bytes = bytes_of(r.small_in, r.row_send2, r.row_recv2)
    tile_sums_bytes = bytes_of(r.small_last, r.small_send2, r.small_recv2)

    def fold(v):
        return jnp.sum(v.reshape(tall // 8, 8, width), axis=0)

    def vector_sums(at):
        dh, dy = r.x_place[at, :], r.dy_place[at, :]
        r.sums[0] += fold(dh * r.unit1[at, :])
        r.sums[1] += fold(dh)
        r.sums[2] += fold(r.dz[at, :].astype(F32))
        r.sums[3] += fold(dy * r.h[at, :])
        r.sums[4] += fold(dy)

    def small_grads():
        r.sums[...] = jnp.zeros(r.sums.shape, F32)
        row_loop(vector_sums)
        for i in range(5):
            line_sum = jnp.sum(r.sums[i], axis=0, keepdims=True)
            tiles = small_gather(line_sum * r.vec_mask_v[...], r.vec_spread_v[...])
            r.small_out[:, :, i, :] = tiles.reshape(n.batch, n.seq, 128)
        line_sum = jnp.concatenate(
            [jnp.sum(r.bias_sum[q], axis=0, keepdims=True) for q in range(n.chunks)], axis=1
        )
        tiles = small_gather(jnp.where(bias_mask, line_sum, 0.0), r.bias_spread_v[...])
        r.small_out[:, :, 5:8, :] = jnp.zeros((n.batch, n.seq, 3, 128), F32)
        r.small_out[pl.ds(core * (n.batch // 2), n.batch // 2), :, 5, :] = tiles.reshape(
            n.batch // 2, n.seq, 128
        )
        for k in range(1, n.batch):
            row_sums(k).start()

    def small_rows_back():
        value = r.small_out[batch_at]
        row_sums_bytes.wait_recv()
        for k in range(1, n.batch):
            value = value + r.small_in[k - 1]
        r.small_mid[...] = value
        for k in range(1, n.seq):
            tile_sums(k).start()

    def small_end():
        value = r.small_mid[seq_at]
        tile_sums_bytes.wait_recv()
        for k in range(1, n.seq):
            value = value + r.small_last[k - 1]
        r.g_small[...] = value

    def turn_back():
        mix_turn(1)

    def outputs():
        r.out[...] = dot(r.out_low[...], r.perm_v[...], NT).astype(BF16)
        r.dx[...] = dot(r.dm[...], r.perm_v[...], NT) + dot(r.rest[...], r.perm_v[...], NT)

    def mix_back():
        loads.un_b.wait()
        mix_finish(1, r.un_v)
        r.dx[...] = r.dx[...] + r.mixed[...]

    for task, *which in (
        (grad_product, 1), (grad_product, 4), (grad_product, 3), (slope_back, 2),
        (slope_back, 1), (slope_back, 0), (grad_side, 3), (grad_side, 1), (grad_product, 2),
        (grad_product, 5), (grad_side, 4), (grad_product, 9), (norm_back,), (grad_line, 3),
        (grad_product, 6), (small_grads,), (grad_line, 4), (grad_side, 9), (grad_side, 5),
        (grad_product, 0), (grad_side, 2), (grad_line, 1), (grad_product, 11), (outputs,),
        (grad_product, 7), (grad_side, 6), (grad_line, 9), (small_rows_back,), (grad_across, 3),
        (grad_line, 5), (grad_across, 4), (turn_back,), (grad_side, 0), (grad_product, 8),
        (grad_line, 2), (grad_product, 10), (grad_across, 9), (grad_side, 7), (grad_out, 4),
        (grad_line, 6), (grad_out, 3), (grad_far, 3), (grad_across, 5), (grad_side, 11),
        (grad_across, 6), (grad_line, 0), (grad_across, 2), (grad_across, 1), (grad_side, 8),
        (grad_far, 4), (grad_line, 7), (grad_end, 3), (grad_across, 0), (grad_line, 11),
        (grad_out, 9), (grad_side, 10), (grad_across, 7), (grad_across, 11), (grad_out, 11),
        (grad_out, 6), (grad_line, 8), (grad_across, 8), (grad_out, 5), (grad_far, 6),
        (grad_far, 9), (grad_far, 5), (grad_out, 8), (grad_far, 8), (grad_end, 4),
        (grad_end, 9), (grad_out, 0), (small_end,), (grad_out, 2), (grad_out, 1), (mix_back,),
        (grad_line, 10), (grad_far, 11), (grad_far, 0), (grad_across, 10), (grad_out, 7),
        (grad_end, 11), (grad_end, 5), (grad_end, 8), (grad_far, 1), (grad_out, 10),
        (grad_end, 1), (grad_end, 6), (grad_far, 7), (grad_far, 2), (grad_far, 10),
        (grad_end, 2), (grad_end, 7), (grad_end, 0), (grad_end, 10),
    ):
        task(*which)

    squares = r.squares[...] + r.g_small[...] * r.g_small[...]
    r.norm_own[...] = jnp.sum(squares, axis=0, keepdims=True)
    r.norm_all[batch_at * n.seq + seq_at] = r.norm_own[...]

    for device in everyone:
        remote(
            r.norm_own,
            r.norm_all.at[batch_at * n.seq + seq_at],
            r.norm_send,
            r.norm_recv,
            *device,
        ).start()
    back_bytes = bytes_of(r.final_in, r.back_send, r.back_recv)
    back_bytes.wait_recv()
    for c in range(len(pieces)):
        m, q, at = wide(c)
        their_at = pl.ds(aligned(1 - core, n.half) + q * n.cols + at.start, at.size)
        grads_out[m][:, their_at] = r.final_in[held(c)]
    norm_bytes = bytes_of(r.norm_all.at[pl.ds(0, n.devices - 1)], r.norm_send, r.norm_recv)
    norm_bytes.wait_recv()
    squares = jnp.sum(r.norm_all[...].reshape(n.devices, 128), axis=0, keepdims=True)
    whole = jnp.sum(squares, axis=1, keepdims=True)
    r.norm[...] = jnp.broadcast_to(jnp.sqrt(whole), (8, 128))

    bytes_of(r.act, r.core_send, r.core_recv.at[0]).wait_send()
    for copy in (tiles_bytes(), rows_bytes(), *(swapped(m) for m in range(2))):
        copy.wait_send()
    for i, into in enumerate((r.l_buf, r.r_buf)):
        both = into.at[:, pl.ds(0, n.seq - 1)]
        bytes_of(both, r.mix_send.at[i], r.mix_recv.at[i]).wait_send()
    for copy in (row_sums_bytes, tile_sums_bytes, back_bytes, norm_bytes):
        copy.wait_send()
    weight_chunks = range(2 * n.chunks)
    sent = [2 * n.zs + (3 if split(c) else n.zs + 1) for c in weight_chunks]
    all_slabs(sent, r.side_send).wait_send()

    @pl.when(inner)
    def _():
        all_slabs([8 if split(c) else 4 for c in weight_chunks], r.inner_send).wait_send()

    moved = 2 * n.zs + n.zs + 3
    bytes_of(out_low.at[:, pl.ds(0, moved * slab)], r.grad_send, r.sides_recv.at[0]).wait_send()


def grad_pieces(n):
    slots = 2 * n.chunks * n.parts
    halved = len(BACK_KINDS) - slots
    whole = [(slot, 0, n.thin) for slot in range(slots - halved)]
    thin = n.thin // 2
    return whole + [(slot, i * thin, thin) for slot in range(slots - halved, slots) for i in range(2)]


def run_layer(n, x, dy, w1, w2, bias, vec):
    tables = host_tables(n)
    tokens, width, cols, q = n.tokens, n.width, n.cols, n.chunks
    grads = 2 * q * n.parts
    far_chunks = sum(kind // 2 == 1 for kind in FORWARD_KINDS)
    splits = max(1, sum(kind // 2 == 1 for kind in BACK_KINDS))
    firsts = max(1, sum(kind // 2 == 3 for kind in BACK_KINDS))
    dma = pltpu.SemaphoreType.DMA
    vmem = pltpu.VMEM
    inputs = dict(bias=bias, vec=vec, x=x, dy=dy, w1=w1, w2=w2)
    inputs.update({name: getattr(tables, name) for name in LOADS if name not in inputs})
    outputs = dict(
        out=((tokens, width), BF16),
        dx=((tokens, width), F32),
        g1=((n.rows, n.hidden), F32),
        g2=((n.rows, n.hidden), F32),
        g_small=((8, 128), F32),
        norm=((8, 128), F32),
    )
    scratch = {held: vmem(inputs[name].shape, inputs[name].dtype) for name, held in LOADS.items()}
    scratch.update(
        load_sem=dma((len(set(LOADS.values())),)),
        stage=vmem((2, n.slab, n.half), F32),
        swap_send=dma((2,)),
        swap_recv=dma((2,)),
        tile=vmem((8, 128), F32),
        small=vmem((n.batch, n.seq, 8, 128), F32),
        small_send=dma,
        small_recv=dma,
        row_send=dma,
        row_recv=dma,
        y_buf=vmem((2, width, tokens), BF16),
        l_buf=vmem((2, n.seq, n.packed, tokens), BF16),
        left=vmem((n.seqs * n.packed, n.length), BF16),
        z_buf=vmem((2, n.seq, n.seqs * n.packed, n.block), BF16),
        r_buf=vmem((2, n.seq, n.seqs * n.packed, n.block), BF16),
        mix_send=dma((2,)),
        mix_recv=dma((4,)),
        mixed=vmem((tokens, width), F32),
        full=vmem((2, q, width, cols), BF16),
        side_send=dma,
        inner_send=dma,
        mate_recv=dma((2 * q + far_chunks,)),
        pair_recv=dma((2 * q + far_chunks,)),
        first_recv=dma((3, 2 * q)),
        second_recv=dma((2 * q,)),
        x_place=vmem((tokens, width), F32),
        dy_place=vmem((tokens, width), F32),
        vecs=vmem((8, width), F32),
        biases=vmem((q, 1, cols), F32),
        unit1=vmem((tokens, width), F32),
        scale1=vmem((tokens, 128), F32),
        h=vmem((tokens, width), F32),
        h_low=vmem((2 * tokens, width), BF16),
        core_send=dma,
        core_recv=dma((6,)),
        total=vmem((2 * tokens, width), F32),
        act=vmem((q, 2 * tokens, cols), BF16),
        lift=vmem((2 * tokens, cols), F32),
        slope=vmem((q, 2 * tokens, cols), F32),
        part_low=vmem((tokens, width), BF16),
        part_low2=vmem((tokens, width), BF16),
        part_in=vmem((tokens, width), BF16),
        part_in2=vmem((tokens, width), BF16),
        sums=vmem((5, 8, width), F32),
        out_low=vmem((tokens, width), BF16),
        dr2=vmem((tokens, width), F32),
        dz=vmem((2 * tokens, width), BF16),
        acc=vmem((grads, width, n.thin), F32),
        give=vmem((grads, width, n.thin), BF16),
        in_diagonal=vmem((grads, n.segment, n.thin), BF16),
        in_sides=vmem((grads, 2, n.segment, n.thin), BF16),
        in_end=vmem((grads, n.zs - 1, n.slab, n.thin), BF16),
        in_pair=vmem((grads, 2 * n.slab, n.thin), BF16),
        in_across=vmem((grads, 2 * n.slab, n.thin), BF16),
        far_mate=vmem((splits, n.slab, n.thin), BF16),
        far_pair=vmem((splits, 2 * n.slab, n.thin), BF16),
        far_across=vmem((splits, 2 * n.slab, n.thin), BF16),
        first_mate=vmem((firsts, 4, n.slab, n.thin), BF16),
        first_pair=vmem((firsts, 4, 2 * n.slab, n.thin), BF16),
        first_across=vmem((firsts, 4, 2 * n.slab, n.thin), BF16),
        line_recv=dma((3, firsts)),
        grad_send=dma,
        diagonal_recv=dma((len(BACK_KINDS),)),
        sides_recv=dma((len(BACK_KINDS),)),
        end_recv=dma((len(BACK_KINDS),)),
        tree_recv=dma((2, max(1, sum(kind // 2 < 2 for kind in BACK_KINDS)))),
        far_recv=dma((3, splits)),
        bias_sum=vmem((q, 8, cols), F32),
        dpre=vmem((q, 2 * tokens, cols), BF16),
        dm=vmem((tokens, width), BF16),
        rest=vmem((tokens, width), BF16),
        small_out=vmem((n.batch, n.seq, 8, 128), F32),
        small_in=vmem((n.batch - 1, n.seq, 8, 128), F32),
        row_send2=dma,
        row_recv2=dma,
        small_mid=vmem((n.seq, 8, 128), F32),
        small_last=vmem((n.seq - 1, 8, 128), F32),
        small_send2=dma,
        small_recv2=dma,
        final=vmem((grads, n.slab, n.thin), F32),
        final_in=vmem((grads, n.rows, n.thin), F32),
        back_send=dma,
        back_recv=dma,
        squares=vmem((8, 128), F32),
        norm_own=vmem((1, 128), F32),
        norm_all=vmem((n.devices, 1, 128), F32),
        norm_send=dma,
        norm_recv=dma,
    )
    names = tuple(inputs) + tuple(outputs) + tuple(scratch)
    in_vmem = pl.BlockSpec(memory_space=pltpu.VMEM)
    anywhere = pl.BlockSpec(memory_space=pl.ANY)
    values = pl.pallas_call(
        functools.partial(layer_kernel, n, names),
        out_shape=[vmem(*shape) for shape in outputs.values()],
        in_specs=[anywhere if name in LOADS else in_vmem for name in inputs],
        out_specs=[in_vmem] * len(outputs),
        scratch_shapes=list(scratch.values()),
        compiler_params=pltpu.CompilerParams(
            collective_id=0, has_side_effects=True, vmem_limit_bytes=58 * 2**20
        ),
        name="fused_layer",
    )(*inputs.values())
    return types.SimpleNamespace(**dict(zip(outputs, values)))


def adam_kernel(n, names, *refs):
    r = types.SimpleNamespace(**dict(zip(names, refs)))
    passed = [
        pltpu.make_async_copy(r.out, r.out_there, r.sem.at[0]),
        pltpu.make_async_copy(r.dx, r.dx_there, r.sem.at[1]),
    ]
    for copy in passed:
        copy.start()
    norm_value = r.norm[0:1, 0:1]
    r.norm_out[...] = norm_value
    factor = clip_limit / jnp.maximum(norm_value, clip_limit)
    lanes = n.cols

    def update(gradient, given, made, at, rate):
        weight, first, second = (ref[at] for ref in given)
        new = adam_update(weight, factor * gradient, first, second, rate, STEP_COUNT)
        for ref, value in zip(made, new):
            ref[at] = value

    weight_in, weight_out = refs[4:7], refs[7:10]
    made_in, made_out = refs[19:22], refs[22:25]

    @pl.loop(0, n.hidden // lanes)
    def _(i):
        at = (slice(None), pl.ds(pl.multiple_of(i * lanes, lanes), lanes))
        update(r.g1[at], weight_in, made_in, at, rate_matrix)
        update(r.g2[at], weight_out, made_out, at, rate_matrix)

    update(r.g_small[5:6, 0 : n.bias], refs[10:13], refs[25:28], ..., rate_vector)
    for i in range(5):
        update(r.g_small[i : i + 1, 0 : n.rows], refs[13:16], refs[28:31], i, rate_vector)
    for copy in passed:
        copy.wait()


def run_adam(n, got, given):
    f32 = functools.partial(jax.ShapeDtypeStruct, dtype=F32)
    matrix, bias, vec = f32((n.rows, n.hidden)), f32((1, n.bias)), f32((5, 1, n.rows))
    inputs = dict(g1=got.g1, g2=got.g2, g_small=got.g_small, norm=got.norm)
    inputs.update({chr(97 + i): array for i, array in enumerate(given)})
    inputs.update(out=got.out, dx=got.dx)
    outputs = dict(norm_out=f32((1, 1)))
    outputs.update({chr(110 + i): matrix for i in range(6)})
    outputs.update({chr(65 + i): bias for i in range(3)})
    outputs.update({chr(70 + i): vec for i in range(3)})
    outputs.update(
        out_there=jax.ShapeDtypeStruct(got.out.shape, BF16),
        dx_there=jax.ShapeDtypeStruct(got.dx.shape, F32),
    )
    names = tuple(inputs) + tuple(outputs) + ("sem",)
    in_vmem = pl.BlockSpec(memory_space=pltpu.VMEM)
    anywhere = pl.BlockSpec(memory_space=pl.ANY)
    return pl.pallas_call(
        functools.partial(adam_kernel, n, names),
        out_shape=list(outputs.values()),
        in_specs=[in_vmem] * (len(inputs) - 2) + [anywhere] * 2,
        out_specs=[in_vmem] * (len(outputs) - 2) + [anywhere] * 2,
        scratch_shapes=[pltpu.SemaphoreType.DMA((2,))],
        compiler_params=pltpu.CompilerParams(vmem_limit_bytes=32 * 2**20),
        name="adam",
    )(*inputs.values())


def turned(a):
    return jnp.swapaxes(a[0], 0, 1)


def lined(a):
    return jnp.transpose(a, (1, 0, 2))


def fused_layer(
    n,
    activations,
    cotangent,
    w_in,
    w_out,
    b_in,
    vec_params,
    first_w_in,
    second_w_in,
    first_w_out,
    second_w_out,
    first_b_in,
    second_b_in,
    first_vec,
    second_vec,
):
    got = run_layer(
        n,
        activations.reshape(n.tokens, n.width),
        cotangent.reshape(n.tokens, n.width),
        w_in[0],
        turned(w_out),
        b_in,
        lined(vec_params),
    )
    given = (
        *(a[0] for a in (w_in, first_w_in, second_w_in)),
        *(turned(a) for a in (w_out, first_w_out, second_w_out)),
        *(b_in, first_b_in, second_b_in),
        *(lined(a) for a in (vec_params, first_vec, second_vec)),
    )
    norm_value, *made, out, dx = run_adam(n, got, given)
    return (
        out.reshape(activations.shape),
        dx.reshape(activations.shape),
        norm_value.reshape(()),
        *(a[None] for a in made[:3]),
        *(jnp.swapaxes(a, 0, 1)[None] for a in made[3:6]),
        *made[6:9],
        *(lined(a) for a in made[9:]),
    )


def local_layer(mesh, activations, cotangent, w_in, *rest):
    seqs, block, width = activations.shape
    n = Sizes(mesh, seqs, block, width, w_in.shape[2])
    if w_in.shape[0] == 1 and n.fits():
        return fused_layer(n, activations, cotangent, w_in, *rest)
    return general_layer(activations, cotangent, w_in, *rest)


BOTH = ("batch", "seq")


def solution(mesh):
    in_specs = (
        P(*BOTH, None),
        P(*BOTH, None),
        P(None, BOTH, None),
        P(None, None, BOTH),
        P(None, BOTH),
        P(None, None, BOTH),
        P(None, BOTH, None),
        P(None, BOTH, None),
        P(None, None, BOTH),
        P(None, None, BOTH),
        P(None, BOTH),
        P(None, BOTH),
        P(None, None, BOTH),
        P(None, None, BOTH),
    )
    out_specs = (
        P(*BOTH, None),
        P(*BOTH, None),
        P(),
        P(None, BOTH, None),
        P(None, BOTH, None),
        P(None, BOTH, None),
        P(None, None, BOTH),
        P(None, None, BOTH),
        P(None, None, BOTH),
        P(None, BOTH),
        P(None, BOTH),
        P(None, BOTH),
        P(None, None, BOTH),
        P(None, None, BOTH),
        P(None, None, BOTH),
    )
    return jax.shard_map(
        functools.partial(local_layer, mesh), mesh=mesh, in_specs=in_specs, out_specs=out_specs, check_vma=False)
```

```python
import functools
import math
import types

import jax
import jax.numpy as jnp
import ml_dtypes
import numpy as np
from jax import lax
from jax.experimental import pallas as pl
from jax.experimental.pallas import tpu as pltpu
from jax.sharding import PartitionSpec as P

STEP_COUNT = 10


beta_first = 0.5
beta_second = 0.5
rate_matrix = 0.03
rate_vector = 0.2
weight_decay = 0.01
adam_epsilon = 1e-08
norm_epsilon = 1e-06
clip_limit = 1.0


def dft_tables(row_index, column_index, seq_len):
    product = row_index[:, None] * column_index[None, :] % seq_len
    angle = product.astype(jnp.float32) * (2.0 * math.pi / seq_len)
    return (jnp.cos(angle).astype(jnp.bfloat16), jnp.sin(angle).astype(jnp.bfloat16))


def layer_norm(values, gain, shift):
    centre = jnp.mean(values, axis=-1, keepdims=True)
    centred = values - centre
    spread = jnp.mean(centred * centred, axis=-1, keepdims=True)
    return centred * lax.rsqrt(spread + norm_epsilon) * gain + shift


def gelu_tanh(values):
    return jax.nn.gelu(values, approximate=True)


def adam_update(weight, gradient, first, second, rate, step_count):
    first_new = beta_first * first + (1.0 - beta_first) * gradient
    second_new = beta_second * second + (1.0 - beta_second) * gradient * gradient
    first_hat = first_new / (1.0 - beta_first**step_count)
    second_hat = second_new / (1.0 - beta_second**step_count)
    updated = weight - rate * (
        first_hat / (jnp.sqrt(second_hat) + adam_epsilon) + weight_decay * weight
    )
    return (first_new, second_new, updated)


def general_layer(
    activations,
    cotangent,
    w_in,
    w_out,
    b_in,
    vec_params,
    first_w_in,
    second_w_in,
    first_w_out,
    second_w_out,
    first_b_in,
    second_b_in,
    first_vec,
    second_vec,
):
    layers = w_in.shape[0]
    seq_count, block_len, model_width = activations.shape
    seq_devices = lax.axis_size(BOTH[1])
    seq_len = block_len * seq_devices
    dft_scale = 1.0 / math.sqrt(seq_len * model_width)
    first_row = lax.axis_index(BOTH[1]) * block_len
    my_rows = first_row + jnp.arange(block_len, dtype=jnp.int32)
    feature_line = jnp.arange(model_width, dtype=jnp.int32)
    cos_model, sin_model = dft_tables(feature_line, feature_line, model_width)
    table_fwd = jnp.concatenate([cos_model, sin_model], axis=1)
    table_back = jnp.transpose(table_fwd)
    layer_index = 0
    pieces = (
        w_in[layer_index].astype(jnp.bfloat16),
        w_out[layer_index].astype(jnp.bfloat16),
        b_in[layer_index].astype(jnp.bfloat16),
        vec_params[layer_index].astype(jnp.bfloat16),
    )
    gathered = [
        (
            lax.all_gather(pieces[0], BOTH, axis=0, tiled=True),
            lax.all_gather(pieces[1], BOTH, axis=1, tiled=True),
            lax.all_gather(pieces[2], BOTH, axis=0, tiled=True),
            lax.all_gather(pieces[3], BOTH, axis=1, tiled=True),
        )
    ]
    zeros_block = jnp.zeros((seq_count, block_len, model_width), jnp.float32)
    stream = activations.astype(jnp.float32)
    layer_index = 0
    weight_first, weight_second, bias_low, vec_low = gathered[layer_index]
    vec_float = vec_low.astype(jnp.float32)
    bias_float = bias_low.astype(jnp.float32)
    joined = jnp.dot(
        stream.astype(jnp.bfloat16), table_fwd, preferred_element_type=jnp.float32
    ).astype(jnp.bfloat16)
    halves = (joined[..., :model_width], joined[..., model_width:])
    shard_piece = (
        lax.all_gather(halves[0], BOTH[1], axis=1, tiled=True),
        lax.all_gather(halves[1], BOTH[1], axis=1, tiled=True),
    )
    piece_len = shard_piece[0].shape[1]
    cos_block, sin_block = dft_tables(my_rows, jnp.arange(piece_len, dtype=jnp.int32), seq_len)
    running = jnp.einsum(
        "ij,sjd->sid", cos_block, shard_piece[0], preferred_element_type=jnp.float32
    )
    mixed = (
        running
        - jnp.einsum("ij,sjd->sid", sin_block, shard_piece[1], preferred_element_type=jnp.float32)
    ) * dft_scale
    normed, norm_first_back = jax.vjp(layer_norm, stream + mixed, vec_float[0], vec_float[1])
    normed_low = normed.astype(jnp.bfloat16)
    pre_act = jnp.dot(normed_low, weight_first, preferred_element_type=jnp.float32) + bias_float
    activated, gelu_back = jax.vjp(gelu_tanh, pre_act)
    act_low = activated.astype(jnp.bfloat16)
    feed = jnp.dot(act_low, weight_second, preferred_element_type=jnp.float32) + vec_float[2]
    stream, norm_second_back = jax.vjp(layer_norm, normed + feed, vec_float[3], vec_float[4])
    saved = [(norm_first_back, normed_low, gelu_back, act_low, norm_second_back)]
    block_output = stream.astype(jnp.bfloat16)
    grad_now = cotangent.astype(jnp.float32)
    raw_grads = [None] * layers
    for layer_index in reversed(range(layers)):
        weight_first, weight_second, bias_low, vec_low = gathered[layer_index]
        norm_first_back, normed_low, gelu_back, act_low, norm_second_back = saved[layer_index]
        grad_sum2, grad_gain2, grad_shift2 = norm_second_back(grad_now)
        grad_z = grad_sum2.astype(jnp.bfloat16)
        grad_weight_second = jnp.einsum(
            "stf,std->fd", act_low, grad_z, preferred_element_type=jnp.float32
        )
        grad_bias_out = jnp.sum(grad_z.astype(jnp.float32), axis=(0, 1))
        grad_act = jnp.einsum(
            "std,fd->stf", grad_z, weight_second, preferred_element_type=jnp.float32
        )
        (grad_pre,) = gelu_back(grad_act)
        grad_pre_low = grad_pre.astype(jnp.bfloat16)
        grad_weight_first = jnp.einsum(
            "std,stf->df", normed_low, grad_pre_low, preferred_element_type=jnp.float32
        )
        grad_bias_in = jnp.sum(grad_pre_low.astype(jnp.float32), axis=(0, 1))
        grad_normed = (
            jnp.einsum(
                "stf,df->std", grad_pre_low, weight_first, preferred_element_type=jnp.float32
            )
            + grad_sum2
        )
        grad_sum1, grad_gain1, grad_shift1 = norm_first_back(grad_normed)
        grad_mix_low = grad_sum1.astype(jnp.bfloat16)
        add_shard_piece = lax.all_gather(grad_mix_low, BOTH[1], axis=1, tiled=True)
        add_piece_len = add_shard_piece.shape[1]
        add_cos_block, add_sin_block = dft_tables(
            my_rows, jnp.arange(add_piece_len, dtype=jnp.int32), seq_len
        )
        with_cos = jnp.einsum(
            "ij,sjd->sid", add_cos_block, add_shard_piece, preferred_element_type=jnp.float32
        )
        with_sin = (zeros_block, zeros_block)[1] - jnp.einsum(
            "ij,sjd->sid", add_sin_block, add_shard_piece, preferred_element_type=jnp.float32
        )
        with_cos, with_sin = (with_cos, with_sin)
        with_cos = (with_cos * dft_scale).astype(jnp.bfloat16)
        with_sin = (with_sin * dft_scale).astype(jnp.bfloat16)
        grad_halves = jnp.concatenate([with_cos, with_sin], axis=-1)
        grad_now = grad_sum1 + jnp.dot(grad_halves, table_back, preferred_element_type=jnp.float32)
        grad_vec = jnp.stack([grad_gain1, grad_shift1, grad_bias_out, grad_gain2, grad_shift2])
        layer_terms = (grad_weight_first, grad_weight_second, grad_bias_in, grad_vec)
        raw_grads[layer_index] = (
            lax.psum_scatter(layer_terms[0], BOTH, scatter_dimension=0, tiled=True),
            lax.psum_scatter(layer_terms[1], BOTH, scatter_dimension=1, tiled=True),
            lax.psum_scatter(layer_terms[2], BOTH, scatter_dimension=0, tiled=True),
            lax.psum_scatter(layer_terms[3], BOTH, scatter_dimension=1, tiled=True),
        )
    shard_w_in = jnp.stack([entry[0] for entry in raw_grads])
    shard_w_out = jnp.stack([entry[1] for entry in raw_grads])
    shard_b_in = jnp.stack([entry[2] for entry in raw_grads])
    shard_vec = jnp.stack([entry[3] for entry in raw_grads])
    local_squares = jnp.sum(shard_w_in * shard_w_in) + jnp.sum(shard_w_out * shard_w_out)
    local_squares = (
        local_squares + jnp.sum(shard_b_in * shard_b_in) + jnp.sum(shard_vec * shard_vec)
    )
    norm_value = jnp.sqrt(lax.psum(local_squares, BOTH))
    factor = clip_limit / jnp.maximum(norm_value, clip_limit)
    upd_w_in = adam_update(
        w_in, factor * shard_w_in, first_w_in, second_w_in, rate_matrix, STEP_COUNT
    )
    upd_w_out = adam_update(
        w_out, factor * shard_w_out, first_w_out, second_w_out, rate_matrix, STEP_COUNT
    )
    upd_b_in = adam_update(
        b_in, factor * shard_b_in, first_b_in, second_b_in, rate_vector, STEP_COUNT
    )
    upd_vec = adam_update(
        vec_params, factor * shard_vec, first_vec, second_vec, rate_vector, STEP_COUNT
    )
    return (
        block_output,
        grad_now,
        norm_value,
        upd_w_in[0],
        upd_w_in[1],
        upd_w_in[2],
        upd_w_out[0],
        upd_w_out[1],
        upd_w_out[2],
        upd_b_in[0],
        upd_b_in[1],
        upd_b_in[2],
        upd_vec[0],
        upd_vec[1],
        upd_vec[2],
    )


MESH = pl.DeviceIdType.MESH
F32 = jnp.float32
BF16 = jnp.bfloat16
NN = (((1,), (0,)), ((), ()))
NT = (((1,), (1,)), ((), ()))
TN = (((0,), (0,)), ((), ()))


def dot(a, b, dims=NN):
    return lax.dot_general(a, b, dims, preferred_element_type=F32)


class Sizes:
    def __init__(self, mesh, seqs, block, width, hidden):
        self.batch, self.seq = mesh.shape["batch"], mesh.shape["seq"]
        self.xs, self.ys, self.zs = self.batch // 2, 2, self.seq // 2
        self.devices = self.batch * self.seq
        self.seqs, self.block, self.width, self.hidden = seqs, block, width, hidden
        self.length = block * self.seq
        self.rows = width // self.devices
        self.slab = 2 * self.rows
        self.segment = self.zs * self.slab
        self.half = hidden // 2
        self.cols = 512
        self.chunks = self.half // self.cols
        self.parts = 2
        self.thin = self.cols // self.parts
        self.packed = width // self.seq
        self.tokens = seqs * block
        self.bias = hidden // self.devices

    def fits(self):
        return (
            self.batch == 4
            and self.seq % 2 == 0
            and self.width % self.devices == 0
            and self.slab % 16 == 0
            and self.packed % 32 == 0
            and self.block % 128 == 0
            and self.zs == 4
            and self.half % self.cols == 0
            and self.rows <= 128
            and self.bias <= 128
            and 5 * self.rows <= self.width
            and self.hidden == 4 * self.width
        )

    def owner(self, x, core, z, y):
        return (2 * x + core) * self.seq + 2 * z + y

    def place_owner(self):
        return [
            self.owner(x, core, z, y)
            for y in range(self.ys)
            for x in range(self.xs)
            for z in range(self.zs)
            for core in range(2)
        ]


def cos_sin(rows, columns, count):
    angle = (rows[:, None] * columns[None, :] % count) * (2.0 * math.pi / count)
    return np.cos(angle), np.sin(angle)


def host_tables(n):
    width, half = n.width, n.packed // 2
    owners = np.array(n.place_owner())
    order = (owners[:, None] * n.rows + np.arange(n.rows)[None, :]).reshape(-1)
    line = np.arange(width)
    cosine, sine = cos_sin(line, line, width)
    pack = np.zeros((width, width))
    unpack = np.zeros((width, width))
    for k in range(width // 2):
        device, inner = divmod(k, half)
        at_cos = device * n.packed + inner
        at_sin = at_cos + half
        pack[at_cos] = cosine[k]
        unpack[at_cos, k] = 1.0
        if k:
            unpack[at_cos, width - k] = 1.0
            pack[at_sin] = sine[k]
            unpack[at_sin, k] = -1.0
            unpack[at_sin, width - k] = 1.0
    pack[half] = cosine[width // 2]
    unpack[half, width // 2] = 1.0
    perm = np.zeros((width, width))
    perm[order, np.arange(width)] = 1.0
    positions = np.arange(n.length)
    by_length = np.stack(cos_sin(positions, positions, n.length))
    vec_mask = np.zeros((n.devices, width))
    vec_mask[np.repeat(owners, n.rows), np.arange(width)] = 1.0
    vec_spread = np.zeros((128, width))
    vec_spread[np.arange(width) % n.rows, np.arange(width)] = 1.0
    bias_spread = np.zeros((128, n.half))
    bias_spread[np.arange(n.half) % n.bias, np.arange(n.half)] = 1.0

    def low(a):
        return jnp.asarray(a.astype(np.float32).astype(ml_dtypes.bfloat16))

    return types.SimpleNamespace(
        tt_f=low(pack),
        by_length=low(by_length),
        un_f=low(unpack[:, order]),
        perm=low(perm),
        tt_b=low(pack[:, order]),
        un_b=low(unpack),
        vec_mask=jnp.asarray(vec_mask.astype(np.float32)),
        vec_spread=low(vec_spread),
        bias_spread=low(bias_spread),
    )


LOADS = dict(
    bias="bias_v",
    vec="vec_v",
    w1="w1_v",
    w2="w2_v",
    x="x_v",
    tt_f="tt_v",
    dy="dy_v",
    vec_spread="vec_spread_v",
    bias_spread="bias_spread_v",
    vec_mask="vec_mask_v",
    by_length="by_length_v",
    perm="perm_v",
    un_f="un_v",
    tt_b="tt_v",
    un_b="un_v",
)
FIRST = ("w1", "w2")
LATER = ("tt_b", "un_b")
FORWARD_KINDS = (1, 1, 1, 1, 0, 2)
BACK_KINDS = (3, 6, 5, 0, 0, 4, 5, 1, 0, 1, 1, 5)


def layer_kernel(n, names, *refs):
    r = types.SimpleNamespace(**dict(zip(names, refs)))
    batch_at, seq_at = lax.axis_index("batch"), lax.axis_index("seq")
    x, core = batch_at // 2, batch_at % 2
    z, y = seq_at // 2, seq_at % 2
    tokens, width, seg, slab = n.tokens, n.width, n.segment, n.slab

    def aligned(at, by):
        return pl.multiple_of(at * by, by)

    def rows_of(at, by):
        return pl.ds(aligned(at, by), by)

    def remote(src, dst, send, recv, batch_to, seq_to):
        return pltpu.make_async_remote_copy(
            src_ref=src,
            dst_ref=dst,
            send_sem=send,
            recv_sem=recv,
            device_id=(batch_to, seq_to),
            device_id_type=MESH,
        )

    def bytes_of(view, send, recv):
        return remote(view, view, send, recv, other_core, seq_at)

    other_core = 2 * x + 1 - core
    other_x = 2 * (1 - x) + core
    other_y = 2 * z + 1 - y

    def plane(k):
        return (seq_at + k) % n.seq

    def plane_from(k):
        return (seq_at + n.seq - k) % n.seq

    def across(k):
        return (batch_at + k) % n.batch

    def across_from(k):
        return (batch_at + n.batch - k) % n.batch

    loads = types.SimpleNamespace()
    for name, held in LOADS.items():
        load = pltpu.make_async_copy(
            getattr(r, name), getattr(r, held), r.load_sem.at[sorted(set(LOADS.values())).index(held)]
        )
        setattr(loads, name, load)
    for name in FIRST:
        getattr(loads, name).start()

    everyone = [
        ((batch_at + i // n.seq) % n.batch, (seq_at + i % n.seq) % n.seq)
        for i in range(1, n.devices)
    ]
    barrier = pltpu.get_barrier_semaphore()
    partners = [(across(k), seq_at) for k in range(1, n.batch)]
    partners += [(batch_at, plane(k)) for k in range(n.seq - 1, 0, -1)]
    for device in partners:
        pl.semaphore_signal(barrier, inc=1, device_id=device, device_id_type=MESH)
    loads.x.start()
    loads.tt_f.start()
    pl.semaphore_wait(barrier, len(partners))

    loads.w1.wait()
    loads.w2.wait()
    weights = (r.w1_v, r.w2_v)
    give = pl.ds(aligned(1 - core, n.half), n.half)
    keep = pl.ds(aligned(core, n.half), n.half)
    core_rows = pl.ds(aligned(core, n.rows), n.rows)
    their_rows = pl.ds(aligned(1 - core, n.rows), n.rows)
    for m in range(2):
        remote(
            weights[m].at[:, give],
            r.stage.at[m, core_rows],
            r.swap_send.at[m],
            r.swap_recv.at[m],
            other_core,
            seq_at,
        ).start()

    for name in LOADS:
        if name not in FIRST + LATER + ("x", "tt_f"):
            getattr(loads, name).start()

    def swapped(m):
        return bytes_of(r.stage.at[m, pl.ds(0, n.rows)], r.swap_send.at[m], r.swap_recv.at[m])

    def mix_start(t, source, table):
        y_ref, l_ref = r.y_buf.at[t], r.l_buf.at[t]
        y_ref[...] = dot(table[...], source, NT).astype(BF16)
        l_ref[seq_at] = y_ref[rows_of(seq_at, n.packed), :]

    def mix_send(t):
        y_ref, l_ref = r.y_buf.at[t], r.l_buf.at[t]
        for k in range(1, n.seq):
            remote(
                y_ref.at[rows_of(plane(k), n.packed)],
                l_ref.at[seq_at],
                r.mix_send.at[0],
                r.mix_recv.at[2 * t],
                batch_at,
                plane(k),
            ).start()

    def mixed_bytes(i):
        into = (r.l_buf, r.r_buf)[i % 2].at[i // 2, pl.ds(0, n.seq - 1)]
        return bytes_of(into, r.mix_send.at[i % 2], r.mix_recv.at[i])

    def mix_turn(t):
        l_ref, z_ref, r_ref = r.l_buf.at[t], r.z_buf.at[t], r.r_buf.at[t]
        mixed_bytes(2 * t).wait_recv()
        left = jnp.concatenate(
            [
                jnp.concatenate(
                    [l_ref[d, :, g * n.block : (g + 1) * n.block] for d in range(n.seq)], axis=1
                )
                for g in range(n.seqs)
            ],
            axis=0,
        )
        r.left[...] = left
        inner = lax.broadcasted_iota(jnp.int32, (n.seqs * n.packed, 1), 0) % n.packed
        first = (inner < n.packed // 2) | ((inner == n.packed // 2) & (seq_at == 0))
        scale = 1.0 / math.sqrt(n.length * n.width)
        for e in range(0, n.seq, 2):
            at = slice(e * n.block, (e + 2) * n.block)
            by_cos = dot(r.left[...], r.by_length_v[0, :, at])
            by_sin = dot(r.left[...], r.by_length_v[1, :, at])
            value = (jnp.where(first, by_cos, by_sin) * scale).astype(BF16)
            z_ref[e] = value[:, : n.block]
            z_ref[e + 1] = value[:, n.block :]
        for k in range(1, n.seq):
            remote(
                z_ref.at[plane(k)],
                r_ref.at[seq_at],
                r.mix_send.at[1],
                r.mix_recv.at[2 * t + 1],
                batch_at,
                plane(k),
            ).start()
        r_ref[seq_at] = z_ref[seq_at]

    def mix_finish(t, table):
        r_ref = r.r_buf.at[t]
        mixed_bytes(2 * t + 1).wait_recv()
        parts = [
            r_ref[:, g * n.packed : (g + 1) * n.packed, :].reshape(width, n.block)
            for g in range(n.seqs)
        ]
        r.mixed[...] = dot(jnp.concatenate(parts, axis=1), table[...], TN)

    loads.tt_f.wait()
    loads.x.wait()
    mix_start(0, r.x_v[...], r.tt_v)

    full = r.full
    mate_z = z + 1 - 2 * (z % 2)
    pair_z = z // 2
    inner = (z > 0) & (z < n.zs - 1)

    def line(to_z):
        return batch_at, 2 * to_z + y

    def seg_rows(sx, sy):
        return rows_of(sy * n.xs + sx, seg)

    def pair_rows(sx, sy, sp):
        return rows_of((sy * n.xs + sx) * 2 + sp, 2 * slab)

    def slab_rows(sx, sy, sz):
        return rows_of((sy * n.xs + sx) * n.zs + sz, slab)

    def peer(t):
        return (other_y_at, other_x_at)[t == 0]

    other_x_at = (other_x, seq_at)
    other_y_at = (batch_at, other_y)

    def away(t):
        return (1 - x, y) if t == 0 else (x, 1 - y)

    def turn_of(c):
        return FORWARD_KINDS[c] % 2

    def split(c):
        return FORWARD_KINDS[c] // 2 == 1

    def place(c):
        return c // n.chunks, c % n.chunks

    def stage_weights(m):
        r.stage[m, core_rows, :] = weights[m][:, keep]
        swapped(m).wait_recv()
        for q in range(n.chunks):
            columns = r.stage[m, :, q * n.cols : (q + 1) * n.cols]
            full[m, q, slab_rows(x, y, z), :] = columns.astype(BF16)

    def full_copy(c, at, send, recv, to):
        m, q = place(c)
        return remote(full.at[m, q, at], full.at[m, q, at], send, recv, *to)

    def rows_at(sx, sy, i):
        return (slab_rows(sx, sy, z), slab_rows(sx, sy, mate_z), pair_rows(sx, sy, 1 - pair_z))[i]

    def side_copy(c, i, sx, sy, first):
        t = turn_of(c)
        recv = r.first_recv.at[i, c] if first else r.second_recv.at[c]
        return full_copy(c, rows_at(sx, sy, i), r.side_send, recv, peer(t if first else 1 - t))

    def to_sides(c, i):
        if i == 0 or not split(c):
            side_copy(c, i, x, y, True).start()
        side_copy(c, i, x, y, False).start()

    def line_slot(c, far):
        return 2 * n.chunks + sum(split(d) for d in range(c)) if far else c

    def line_seg(c, far):
        return away(turn_of(c)) if far else (x, y)

    def own_to_mate(c, far):
        at = rows_at(*line_seg(c, far), 0)
        return full_copy(c, at, r.side_send, r.mate_recv.at[line_slot(c, far)], line(mate_z))

    def mate_arrives(c, far):
        at = rows_at(*line_seg(c, far), 1)
        full_copy(c, at, r.side_send, r.mate_recv.at[line_slot(c, far)], line(mate_z)).wait_recv()

    def pair_across(c, far):
        at = pair_rows(*line_seg(c, far), pair_z)
        return full_copy(c, at, r.inner_send, r.pair_recv.at[line_slot(c, far)], line(n.zs - 1 - z))

    def pair_out(c, far):
        at = rows_at(*line_seg(c, far), 2)
        return full_copy(c, at, r.inner_send, r.pair_recv.at[line_slot(c, far)], line(mate_z))

    def own_sides(c):
        to_sides(c, 0)

    def own_line(c):
        own_to_mate(c, 0).start()

    def from_mate(c, far):
        mate_arrives(c, far)

        @pl.when(inner)
        def _():
            pair_across(c, far).start()

    def from_pair(c, far):
        pair_out(c, far).wait_recv()

        @pl.when(inner)
        def _():
            pair_out(c, far).start()

    def mate_in(c):
        from_mate(c, 0)
        to_sides(c, 1)

    def pair_in(c):
        from_pair(c, 0)
        to_sides(c, 2)

    def pass_on(c, i):
        ax, ay = away(turn_of(c))
        if i == 0 or not split(c):
            side_copy(c, i, ax, ay, True).wait_recv()
        if split(c):
            if i == 0:
                own_to_mate(c, 1).start()
            else:
                (from_mate, from_pair)[i - 1](c, 1)
        side_copy(c, i, ax, ay, False).start()

    def weights_here(c):
        m, q = place(c)
        second = full.at[m, q, pl.ds(0, 2 * n.zs * slab)]
        bytes_of(second, r.side_send, r.second_recv.at[c]).wait_recv()

    def all_slabs(counts, send):
        rows = sum(counts) * slab // (2 * n.chunks)
        return bytes_of(full.at[:, :, pl.ds(0, rows)], send, r.second_recv.at[0])

    def small_tiles():
        loads.bias.wait()
        loads.vec.wait()
        tile = r.tile
        tile[...] = jnp.zeros(tile.shape, F32)
        for i in range(5):
            tile[i : i + 1, 0 : n.rows] = r.vec_v[i]
        tile[5:6, 0 : n.bias] = r.bias_v[...]
        small[batch_at, seq_at] = tile[...]
        for k in range(1, n.seq):
            small_copy(k, seq_at).start()

    def small_copy(k, at):
        return remote(
            r.tile,
            small.at[batch_at, at],
            r.small_send,
            r.small_recv,
            batch_at,
            plane(k),
        )

    def row_copy(k, at):
        return remote(
            small.at[batch_at],
            small.at[at],
            r.row_send,
            r.row_recv,
            across(k),
            seq_at,
        )

    small = r.small

    def tiles_bytes():
        return bytes_of(small.at[0, pl.ds(0, n.seq - 1)], r.small_send, r.small_recv)

    def rows_bytes():
        return bytes_of(small.at[pl.ds(0, n.batch - 1)], r.row_send, r.row_recv)

    def small_rows():
        tiles_bytes().wait_recv()
        for k in range(1, n.batch):
            row_copy(k, batch_at).start()

    half_owners = n.devices // 2
    bias_mask = (
        lax.broadcasted_iota(jnp.int32, (half_owners, n.half), 0)
        == lax.broadcasted_iota(jnp.int32, (half_owners, n.half), 1) // n.bias
    )

    def small_vectors():
        rows_bytes().wait_recv()
        for load in (loads.vec_spread, loads.bias_spread, loads.vec_mask):
            load.wait()
        for i in range(5):
            held = small[:, :, i, :].reshape(n.devices, 128).astype(BF16)
            spread = dot(held, r.vec_spread_v[...]) * r.vec_mask_v[...]
            r.vecs[i : i + 1, :] = jnp.sum(spread, axis=0, keepdims=True)
        held = small[pl.ds(core * (n.batch // 2), n.batch // 2), :, 5, :]
        held = held.reshape(half_owners, 128).astype(BF16)
        spread = jnp.where(bias_mask, dot(held, r.bias_spread_v[...]), 0.0)
        biases = jnp.sum(spread, axis=0, keepdims=True)
        for q in range(n.chunks):
            r.biases[q] = biases[:, q * n.cols : (q + 1) * n.cols]

    def place_inputs():
        loads.perm.wait()
        loads.dy.wait()
        r.x_place[...] = dot(r.x_v[...], r.perm_v[...])
        r.dy_place[...] = dot(r.dy_v[...], r.perm_v[...])

    def turn_forward():
        loads.by_length.wait()
        mix_turn(0)

    step = 32
    tall = 64
    mine, theirs = pl.ds(0, tokens), pl.ds(tokens, tokens)

    def row_loop(body, first=0, last=tokens):
        @pl.loop(first // tall, last // tall, unroll=True)
        def _(i):
            body(pl.ds(pl.multiple_of(i * tall, tall), tall))

    def mean(v):
        return jnp.mean(v, axis=-1, keepdims=True)

    def first_norm(at):
        v = r.x_place[at, :] + r.mixed[at, :]
        centred = v - mean(v)
        scale = lax.rsqrt(mean(centred * centred) + norm_epsilon)
        unit = centred * scale
        h = unit * r.vecs[0:1, :] + r.vecs[1:2, :]
        r.unit1[at, :] = unit
        r.scale1[at, :] = jnp.broadcast_to(scale, (tall, 128))
        r.h[at, :] = h
        r.h_low[at, :] = h.astype(BF16)

    def swap(i, src, dst):
        return remote(src, dst, r.core_send, r.core_recv.at[i], other_core, seq_at)

    def swap_h():
        return swap(0, r.h_low.at[mine], r.h_low.at[theirs])

    def norm_forward():
        loads.un_f.wait()
        mix_finish(0, r.un_v)
        loads.tt_b.start()
        loads.un_b.start()
        row_loop(first_norm)
        swap_h().start()

    root = math.sqrt(2.0 / math.pi)

    lifted_parts = []

    def lift(q):
        if not lifted_parts:
            swap_h().wait_recv()
        lifted_parts.append(q)
        weights_here(q)
        r.lift[...] = dot(r.h_low[...], full[0, q]) + r.biases[q]

        @pl.loop(0, 2 * tokens // step)
        def _(i):
            at = pl.ds(pl.multiple_of(i * step, step), step)
            u = r.lift[at, :]
            square = u * u
            bent = jnp.tanh(u * (root + (root * 0.044715) * square))
            half_up = 0.5 + 0.5 * bent
            r.act[q, at, :] = (u * half_up).astype(BF16)
            r.slope[q, at, :] = half_up + (u * (1.0 - bent * bent)) * (
                0.5 * root + (1.5 * root * 0.044715) * square
            )

    gathered_parts = []

    halves = [pl.ds(j * tokens // 2, tokens // 2) for j in range(2)]

    def swap_ff(j):
        return swap(1 + j, r.part_low.at[halves[j]], r.part_in.at[halves[j]])

    def drop(q):
        weights_here(n.chunks + q)
        gathered_parts.append(q)
        for half in (theirs, mine):
            part = dot(r.act[q, half, :], full[1, q], NT)
            part = r.total[half, :] + part if len(gathered_parts) > 1 else part
            if len(gathered_parts) == n.chunks and half is theirs:
                r.part_low[...] = part.astype(BF16)
                for j in range(2):
                    swap_ff(j).start()
            else:
                r.total[half, :] = part

    def send_forward():
        mix_send(0)

    forward_steps = (
        (send_forward,), (stage_weights, 0), (own_sides, 1), (own_sides, 0), (own_line, 2),
        (own_sides, 2), (own_line, 1), (own_line, 0), (stage_weights, 1), (own_sides, 4),
        (own_sides, 3), (place_inputs,), (own_line, 3), (own_sides, 5), (own_line, 4),
        (pass_on, 1, 0), (small_tiles,), (pass_on, 0, 0), (mate_in, 2), (mate_in, 1),
        (pass_on, 5, 0), (pass_on, 2, 0), (own_line, 5), (mate_in, 0), (pass_on, 4, 0),
        (mate_in, 3), (mate_in, 4), (pass_on, 2, 1), (pass_on, 3, 0), (pair_in, 2),
        (small_rows,), (pass_on, 1, 1), (pair_in, 1), (pass_on, 5, 1), (turn_forward,),
        (pass_on, 0, 1), (mate_in, 5), (pass_on, 3, 1), (pair_in, 0), (pass_on, 4, 1),
        (pass_on, 2, 2), (pair_in, 4), (small_vectors,), (pass_on, 1, 2), (pair_in, 3),
        (pass_on, 5, 2), (pass_on, 0, 2), (norm_forward,), (pass_on, 4, 2), (pair_in, 5),
        (pass_on, 3, 2), (lift, 1), (lift, 2), (lift, 0), (drop, 1), (drop, 0), (drop, 2),
    )
    for task, *which in forward_steps:
        task(*which)
    def second_norm(at):
        v = (
            r.h[at, :]
            + r.total[at, :]
            + r.part_in[at, :].astype(F32)
            + r.vecs[2:3, :]
        )
        centred = v - mean(v)
        scale = lax.rsqrt(mean(centred * centred) + norm_epsilon)
        unit = centred * scale
        gain = r.vecs[3:4, :]
        r.h[at, :] = unit
        r.out_low[at, :] = (unit * gain + r.vecs[4:5, :]).astype(BF16)
        du = r.dy_place[at, :] * gain
        dv = scale * (du - mean(du) - unit * mean(du * unit))
        r.dr2[at, :] = dv
        r.dz[at, :] = dv.astype(BF16)

    def swap_dz(j):
        return swap(
            3 + j,
            r.dz.at[halves[j]],
            r.dz.at[pl.ds(tokens + j * tokens // 2, tokens // 2)],
        )

    for j in range(2):
        swap_ff(j).wait_recv()
        row_loop(second_norm, j * tokens // 2, (j + 1) * tokens // 2)
        swap_dz(j).start()

    pieces = grad_pieces(n)
    acc = r.acc

    def wide(c):
        slot, start, width_of = pieces[c]
        m, q = slot // (n.chunks * n.parts), slot % (n.chunks * n.parts)
        return 1 - m, q // n.parts, pl.ds((q % n.parts) * n.thin + start, width_of)

    def held(c, at=slice(None), lead=()):
        slot, start, width_of = pieces[c]
        return (slot, *lead, at, pl.ds(start, width_of))

    def product(c, tokens_at):
        m, q, at = wide(c)
        left, right = (r.dz, r.act) if m else (r.h_low, r.dpre)
        return dot(left[tokens_at, :], right[q, tokens_at, at], TN)

    begun = (0, 1, 3)
    for c in begun:
        acc[held(c)] = product(c, mine)
    for j in range(2):
        swap_dz(j).wait_recv()

    out_low = r.give

    def grad_copy(c, at, into, recv, to):
        return remote(out_low.at[held(c, at)], into, r.grad_send, recv, *to)

    def back_turn(c):
        return BACK_KINDS[c] % 2

    def back_mode(c):
        return BACK_KINDS[c] // 2

    def back_slot(c):
        return [d for d, kind in enumerate(BACK_KINDS) if kind // 2 == back_mode(c)].index(c)

    def copy_diagonal(c):
        at = seg_rows(1 - x, 1 - y)
        return grad_copy(c, at, r.in_diagonal.at[held(c)], r.diagonal_recv.at[c], peer(1 - back_turn(c)))

    def copy_near(c):
        t = 1 - back_turn(c)
        into = r.in_sides.at[held(c, lead=(0,))]
        return grad_copy(c, seg_rows(*away(t)), into, r.sides_recv.at[c], peer(t))

    def copy_side(c):
        t = back_turn(c)
        into = r.in_sides.at[held(c, lead=(1,))]
        return grad_copy(c, seg_rows(*away(t)), into, r.sides_recv.at[c], peer(t))

    def back_seg(c, far):
        return away(back_turn(c)) if far else (x, y)

    def tree_slot(c):
        return sum(kind // 2 < 2 for kind in BACK_KINDS[:c])

    def line_into(c, far, i):
        if far:
            into = (r.far_mate, r.far_pair, r.far_across)[i]
            return into.at[back_slot(c), :, pl.ds(0, pieces[c][2])]
        into, lead = ((r.in_end, (0,)), (r.in_pair, ()), (r.in_across, ()))[i]
        return into.at[held(c, lead=lead)]

    def line_copy(c, at, far, i, to):
        if far:
            recv = r.far_recv.at[i, back_slot(c)]
        else:
            recv = r.end_recv.at[c] if i == 0 else r.tree_recv.at[i - 1, tree_slot(c)]
        return grad_copy(c, at, line_into(c, far, i), recv, to)

    def copy_mate(c, far):
        at = slab_rows(*back_seg(c, far), mate_z)
        return line_copy(c, at, far, 0, line(mate_z))

    def copy_pair_in(c, far):
        at = pair_rows(*back_seg(c, far), 1 - pair_z)
        return line_copy(c, at, far, 1, line(mate_z))

    def copy_pair_across(c, far):
        at = pair_rows(*back_seg(c, far), 1 - pair_z)
        return line_copy(c, at, far, 2, line(n.zs - 1 - z))

    def copy_far(c):
        t = back_turn(c)
        at = slab_rows(*away(t), z)
        return grad_copy(c, at, r.in_end.at[held(c, lead=(1,))], r.end_recv.at[c], peer(t))

    def copy_direct(c, d):
        to_z = (z + d) % n.zs
        at = slab_rows(x, y, to_z)
        return grad_copy(c, at, r.in_end.at[held(c, lead=(d - 1,))], r.end_recv.at[c], line(to_z))

    def round_out(c, at, *more):
        value = acc[held(c, at)]
        for ref in more:
            value = value + ref[...].astype(F32)
        out_low[held(c, at)] = value.astype(BF16)

    four = [(sx, sy) for sy in range(n.ys) for sx in range(n.xs)]

    def first_copy(c, i, which):
        sx, sy = four[i]
        slot, lanes = back_slot(c), pl.ds(0, pieces[c][2])
        if which == 0:
            at, to = slab_rows(sx, sy, mate_z), line(mate_z)
        else:
            at, to = pair_rows(sx, sy, 1 - pair_z), line((0, mate_z, n.zs - 1 - z)[which])
        into = (r.first_mate, r.first_pair, r.first_across)[which].at[slot, i, :, lanes]
        return grad_copy(c, at, into, r.line_recv.at[which, slot], to)

    def first_wait(c, which):
        slot, lanes = back_slot(c), pl.ds(0, pieces[c][2])
        into = (r.first_mate, r.first_pair, r.first_across)[which].at[slot, :, :, lanes]
        bytes_of(into, r.grad_send, r.line_recv.at[which, slot]).wait_recv()

    def first_start(c):
        @pl.when(jnp.logical_not(inner))
        def _():
            for i, (sx, sy) in enumerate(four):
                round_out(c, pair_rows(sx, sy, 1 - pair_z))
                first_copy(c, i, 1).start()
            for i, (sx, sy) in enumerate(four):
                round_out(c, slab_rows(sx, sy, mate_z))
                first_copy(c, i, 0).start()

    def first_across(c):
        @pl.when(inner)
        def _():
            first_wait(c, 1)
            for i, (sx, sy) in enumerate(four):
                lanes = pl.ds(0, pieces[c][2])
                more = r.first_pair.at[back_slot(c), i, :, lanes]
                round_out(c, pair_rows(sx, sy, 1 - pair_z), more)
                first_copy(c, i, 2).start()

    def first_out(c):
        @pl.when(inner)
        def _():
            first_wait(c, 2)
            for i, (sx, sy) in enumerate(four):
                at = held(c, pair_rows(sx, sy, pair_z))
                lanes = pl.ds(0, pieces[c][2])
                acc[at] = acc[at] + r.first_across[back_slot(c), i, :, lanes].astype(F32)
                round_out(c, slab_rows(sx, sy, mate_z))
                first_copy(c, i, 0).start()

    def slab_copy(c, i):
        t = back_turn(c)
        sx, sy = ((1 - x, 1 - y), away(1 - t), away(t))[i]
        own = pl.ds(0, slab)
        into = (
            r.in_diagonal.at[held(c, own)] if i == 0 else r.in_sides.at[held(c, own, lead=(i - 1,))]
        )
        recv = r.diagonal_recv if i == 0 else r.sides_recv
        return grad_copy(c, slab_rows(sx, sy, z), into, recv.at[c], peer(t if i == 2 else 1 - t))

    def slabs_near(c):
        first_wait(c, 0)
        lanes = pl.ds(0, pieces[c][2])
        for i, (sx, sy) in enumerate(four):
            at = held(c, slab_rows(sx, sy, z))
            acc[at] = acc[at] + r.first_mate[back_slot(c), i, :, lanes].astype(F32)
        t = back_turn(c)
        for i, seg_at in enumerate(((1 - x, 1 - y), away(1 - t))):
            round_out(c, slab_rows(*seg_at, z))
            slab_copy(c, i).start()

    def slabs_side(c):
        slab_copy(c, 0).wait_recv()
        own = pl.ds(0, slab)
        round_out(c, slab_rows(*away(back_turn(c)), z), r.in_diagonal.at[held(c, own)])
        slab_copy(c, 2).start()

    def slabs_end(c):
        own = pl.ds(0, slab)
        both = r.in_sides.at[held(c, own, lead=(pl.ds(0, 2),))]
        bytes_of(both, r.grad_send, r.sides_recv.at[c]).wait_recv()
        value = acc[held(c, slab_rows(x, y, z))]
        return value + sum(r.in_sides[held(c, own, lead=(i,))].astype(F32) for i in range(2))

    def grad_product(c):
        if c in begun:
            acc[held(c)] = acc[held(c)] + product(c, theirs)
        else:
            acc[held(c)] = product(c, slice(None))
        if back_mode(c) == 3:
            first_start(c)
            return
        round_out(c, seg_rows(1 - x, 1 - y))
        copy_diagonal(c).start()
        round_out(c, seg_rows(*away(1 - back_turn(c))))
        copy_near(c).start()

    def line_start(c, far):
        @pl.when(jnp.logical_not(inner))
        def _():
            sx, sy = back_seg(c, far)
            round_out(c, pair_rows(sx, sy, 1 - pair_z))
            copy_pair_in(c, far).start()
            round_out(c, slab_rows(sx, sy, mate_z))
            copy_mate(c, far).start()

    def grad_side(c):
        if back_mode(c) == 3:
            first_across(c)
            return
        copy_diagonal(c).wait_recv()
        at = seg_rows(*away(back_turn(c)))
        if back_mode(c) == 1:
            acc[held(c, at)] = acc[held(c, at)] + r.in_diagonal[held(c)].astype(F32)
            line_start(c, 1)
        else:
            round_out(c, at, r.in_diagonal.at[held(c)])
            copy_side(c).start()

    def grad_line(c):
        if back_mode(c) == 3:
            first_out(c)
            return
        sides = 1 if back_mode(c) == 1 else 2
        both = r.in_sides.at[held(c, lead=(pl.ds(0, sides),))]
        bytes_of(both, r.grad_send, r.sides_recv.at[c]).wait_recv()
        more = sum(r.in_sides[held(c, lead=(i,))].astype(F32) for i in range(sides))
        at = seg_rows(x, y)
        acc[held(c, at)] = acc[held(c, at)] + more
        if back_mode(c) == 2:
            for d in range(1, n.zs):
                round_out(c, slab_rows(x, y, (z + d) % n.zs))
                copy_direct(c, d).start()
        else:
            line_start(c, 0)

    def fars(c):
        return range((1, 2, 0, 0)[back_mode(c)])

    def grad_across(c):
        if back_mode(c) == 3:
            slabs_near(c)
        for far in fars(c):

            @pl.when(inner)
            def _(far=far):
                copy_pair_in(c, far).wait_recv()
                at = pair_rows(*back_seg(c, far), 1 - pair_z)
                round_out(c, at, line_into(c, far, 1))
                copy_pair_across(c, far).start()

    def grad_out(c):
        if back_mode(c) == 3:
            slabs_side(c)
        for far in fars(c):

            @pl.when(inner)
            def _(far=far):
                copy_pair_across(c, far).wait_recv()
                sx, sy = back_seg(c, far)
                at = pair_rows(sx, sy, pair_z)
                acc[held(c, at)] = acc[held(c, at)] + line_into(c, far, 2)[...].astype(F32)
                round_out(c, slab_rows(sx, sy, mate_z))
                copy_mate(c, far).start()

    def grad_far(c):
        if back_mode(c) == 1:
            copy_mate(c, 1).wait_recv()
            round_out(c, slab_rows(*away(back_turn(c)), z), line_into(c, 1, 0))
            copy_far(c).start()

    grads_out = (r.g1, r.g2)
    r.squares[...] = jnp.zeros((8, 128), F32)

    def squares_of(v):
        v = v * v
        v = jnp.sum(v.reshape(v.shape[0] // 8, 8, v.shape[1]), axis=0)
        return sum(v[:, i : i + 128] for i in range(0, v.shape[1], 128))

    def copy_back(c):
        return remote(
            r.final.at[held(c, their_rows)],
            r.final_in.at[held(c)],
            r.back_send,
            r.back_recv,
            other_core,
            seq_at,
        )

    def grad_end(c):
        m, q, at = wide(c)
        if back_mode(c) == 3:
            value = slabs_end(c)
        else:
            value = acc[held(c, slab_rows(x, y, z))]
            ends = back_mode(c) + 1
            all_ends = r.in_end.at[held(c, lead=(pl.ds(0, ends),))]
            bytes_of(all_ends, r.grad_send, r.end_recv.at[c]).wait_recv()
            for i in range(ends):
                value = value + r.in_end[held(c, lead=(i,))].astype(F32)
        r.squares[...] += squares_of(value)
        r.final[held(c)] = value
        own_at = pl.ds(aligned(core, n.half) + q * n.cols + at.start, at.size)
        grads_out[m][:, own_at] = r.final[held(c, core_rows)]
        copy_back(c).start()

    back_parts = []

    def slope_back(q):
        r.lift[...] = dot(r.dz[...], full[1, q])
        r.bias_sum[q] = jnp.zeros((8, n.cols), F32)

        @pl.loop(0, 2 * tokens // step)
        def _(i):
            at = pl.ds(pl.multiple_of(i * step, step), step)
            low = (r.lift[at, :] * r.slope[q, at, :]).astype(BF16)
            r.dpre[q, at, :] = low
            r.bias_sum[q] += jnp.sum(low.astype(F32).reshape(step // 8, 8, n.cols), axis=0)

        back_parts.append(q)
        for half in (theirs, mine):
            part = dot(r.dpre[q, half, :], full[0, q], NT)
            part = r.total[half, :] + part if len(back_parts) > 1 else part
            if len(back_parts) == n.chunks and half is theirs:
                r.part_low2[...] = part.astype(BF16)
                swap_dh().start()
            else:
                r.total[half, :] = part

    def swap_dh():
        return swap(5, r.part_low2, r.part_in2)

    def first_norm_back(at):
        dh = r.total[at, :] + r.part_in2[at, :].astype(F32) + r.dr2[at, :]
        unit = r.unit1[at, :]
        r.x_place[at, :] = dh
        du = dh * r.vecs[0:1, :]
        dv = r.scale1[at, 0:1] * (du - mean(du) - unit * mean(du * unit))
        low = dv.astype(BF16)
        r.dm[at, :] = low
        r.rest[at, :] = (dv - low.astype(F32)).astype(BF16)

    def norm_back():
        swap_dh().wait_recv()
        row_loop(first_norm_back)
        loads.tt_b.wait()
        mix_start(1, r.dm[...], r.tt_v)
        mix_send(1)

    def thirds(v):
        high = v.astype(BF16)
        left = v - high.astype(F32)
        mid = left.astype(BF16)
        return high, mid, (left - mid.astype(F32)).astype(BF16)

    def small_gather(v, spread):
        return sum(dot(part, spread, NT) for part in thirds(v))

    def row_sums(k):
        return remote(
            r.small_out.at[across(k)],
            r.small_in.at[k - 1],
            r.row_send2,
            r.row_recv2,
            across(k),
            seq_at,
        )

    def tile_sums(k):
        return remote(
            r.small_mid.at[plane(k)],
            r.small_last.at[k - 1],
            r.small_send2,
            r.small_recv2,
            batch_at,
            plane(k),
        )

    row_sums_bytes = bytes_of(r.small_in, r.row_send2, r.row_recv2)
    tile_sums_bytes = bytes_of(r.small_last, r.small_send2, r.small_recv2)

    def fold(v):
        return jnp.sum(v.reshape(tall // 8, 8, width), axis=0)

    def vector_sums(at):
        dh, dy = r.x_place[at, :], r.dy_place[at, :]
        r.sums[0] += fold(dh * r.unit1[at, :])
        r.sums[1] += fold(dh)
        r.sums[2] += fold(r.dz[at, :].astype(F32))
        r.sums[3] += fold(dy * r.h[at, :])
        r.sums[4] += fold(dy)

    def small_grads():
        r.sums[...] = jnp.zeros(r.sums.shape, F32)
        row_loop(vector_sums)
        for i in range(5):
            line_sum = jnp.sum(r.sums[i], axis=0, keepdims=True)
            tiles = small_gather(line_sum * r.vec_mask_v[...], r.vec_spread_v[...])
            r.small_out[:, :, i, :] = tiles.reshape(n.batch, n.seq, 128)
        line_sum = jnp.concatenate(
            [jnp.sum(r.bias_sum[q], axis=0, keepdims=True) for q in range(n.chunks)], axis=1
        )
        tiles = small_gather(jnp.where(bias_mask, line_sum, 0.0), r.bias_spread_v[...])
        r.small_out[:, :, 5:8, :] = jnp.zeros((n.batch, n.seq, 3, 128), F32)
        r.small_out[pl.ds(core * (n.batch // 2), n.batch // 2), :, 5, :] = tiles.reshape(
            n.batch // 2, n.seq, 128
        )
        for k in range(1, n.batch):
            row_sums(k).start()

    def small_rows_back():
        value = r.small_out[batch_at]
        row_sums_bytes.wait_recv()
        for k in range(1, n.batch):
            value = value + r.small_in[k - 1]
        r.small_mid[...] = value
        for k in range(1, n.seq):
            tile_sums(k).start()

    def small_end():
        value = r.small_mid[seq_at]
        tile_sums_bytes.wait_recv()
        for k in range(1, n.seq):
            value = value + r.small_last[k - 1]
        r.g_small[...] = value

    def turn_back():
        mix_turn(1)

    def outputs():
        r.out[...] = dot(r.out_low[...], r.perm_v[...], NT).astype(BF16)
        r.dx[...] = dot(r.dm[...], r.perm_v[...], NT) + dot(r.rest[...], r.perm_v[...], NT)

    def mix_back():
        loads.un_b.wait()
        mix_finish(1, r.un_v)
        r.dx[...] = r.dx[...] + r.mixed[...]

    for task, *which in (
        (grad_product, 0), (grad_product, 1), (grad_product, 3), (grad_product, 2),
        (slope_back, 1), (grad_product, 4), (slope_back, 0), (slope_back, 2), (grad_side, 1),
        (grad_product, 10), (grad_side, 0), (grad_line, 0), (grad_side, 2), (norm_back,),
        (grad_side, 3), (grad_across, 0), (grad_side, 10), (grad_product, 8), (grad_side, 4),
        (grad_product, 9), (grad_product, 5), (grad_line, 3), (outputs,), (small_grads,),
        (grad_line, 1), (grad_line, 4), (grad_across, 3), (grad_product, 7), (grad_side, 9),
        (grad_across, 4), (grad_line, 2), (grad_line, 10), (turn_back,), (grad_across, 2),
        (grad_side, 8), (grad_out, 2), (grad_across, 10), (grad_product, 11), (grad_side, 7),
        (grad_out, 3), (grad_side, 5), (grad_far, 3), (grad_product, 6), (grad_far, 2),
        (grad_line, 8), (small_rows_back,), (grad_line, 9), (grad_across, 1), (grad_out, 4),
        (grad_side, 11), (grad_across, 8), (grad_out, 0), (grad_across, 9), (grad_line, 7),
        (grad_line, 5), (mix_back,), (grad_end, 3), (small_end,), (grad_out, 10),
        (grad_side, 6), (grad_far, 10), (grad_out, 1), (grad_across, 7), (grad_across, 5),
        (grad_end, 10), (grad_out, 8), (grad_out, 9), (grad_line, 11), (grad_far, 1),
        (grad_out, 5), (grad_across, 11), (grad_out, 11), (grad_far, 5), (grad_far, 9),
        (grad_far, 0), (grad_far, 8), (grad_line, 6), (grad_across, 6), (grad_end, 2),
        (grad_end, 8), (grad_far, 4), (grad_end, 5), (grad_out, 6), (grad_out, 7),
        (grad_far, 11), (grad_far, 7), (grad_far, 6), (grad_end, 0), (grad_end, 9),
        (grad_end, 11), (grad_end, 1), (grad_end, 7), (grad_end, 4), (grad_end, 6),
    ):
        task(*which)

    squares = r.squares[...] + r.g_small[...] * r.g_small[...]
    r.norm_own[...] = jnp.sum(squares, axis=0, keepdims=True)
    r.norm_all[batch_at * n.seq + seq_at] = r.norm_own[...]

    for device in everyone:
        remote(
            r.norm_own,
            r.norm_all.at[batch_at * n.seq + seq_at],
            r.norm_send,
            r.norm_recv,
            *device,
        ).start()
    back_bytes = bytes_of(r.final_in, r.back_send, r.back_recv)
    back_bytes.wait_recv()
    for c in range(len(pieces)):
        m, q, at = wide(c)
        their_at = pl.ds(aligned(1 - core, n.half) + q * n.cols + at.start, at.size)
        grads_out[m][:, their_at] = r.final_in[held(c)]
    norm_bytes = bytes_of(r.norm_all.at[pl.ds(0, n.devices - 1)], r.norm_send, r.norm_recv)
    norm_bytes.wait_recv()
    squares = jnp.sum(r.norm_all[...].reshape(n.devices, 128), axis=0, keepdims=True)
    whole = jnp.sum(squares, axis=1, keepdims=True)
    r.norm[...] = jnp.broadcast_to(jnp.sqrt(whole), (8, 128))

    bytes_of(r.act, r.core_send, r.core_recv.at[0]).wait_send()
    for copy in (tiles_bytes(), rows_bytes(), *(swapped(m) for m in range(2))):
        copy.wait_send()
    for i, into in enumerate((r.l_buf, r.r_buf)):
        both = into.at[:, pl.ds(0, n.seq - 1)]
        bytes_of(both, r.mix_send.at[i], r.mix_recv.at[i]).wait_send()
    for copy in (row_sums_bytes, tile_sums_bytes, back_bytes, norm_bytes):
        copy.wait_send()
    weight_chunks = range(2 * n.chunks)
    sent = [2 * n.zs + (3 if split(c) else n.zs + 1) for c in weight_chunks]
    all_slabs(sent, r.side_send).wait_send()

    @pl.when(inner)
    def _():
        all_slabs([8 if split(c) else 4 for c in weight_chunks], r.inner_send).wait_send()

    moved = 2 * n.zs + n.zs + 3
    bytes_of(out_low.at[:, pl.ds(0, moved * slab)], r.grad_send, r.sides_recv.at[0]).wait_send()


def grad_pieces(n):
    slots = 2 * n.chunks * n.parts
    halved = len(BACK_KINDS) - slots
    whole = [(slot, 0, n.thin) for slot in range(slots - halved)]
    thin = n.thin // 2
    return whole + [(slot, i * thin, thin) for slot in range(slots - halved, slots) for i in range(2)]


def run_layer(n, x, dy, w1, w2, bias, vec):
    tables = host_tables(n)
    tokens, width, cols, q = n.tokens, n.width, n.cols, n.chunks
    grads = 2 * q * n.parts
    far_chunks = sum(kind // 2 == 1 for kind in FORWARD_KINDS)
    splits = max(1, sum(kind // 2 == 1 for kind in BACK_KINDS))
    firsts = max(1, sum(kind // 2 == 3 for kind in BACK_KINDS))
    dma = pltpu.SemaphoreType.DMA
    vmem = pltpu.VMEM
    inputs = dict(bias=bias, vec=vec, x=x, dy=dy, w1=w1, w2=w2)
    inputs.update({name: getattr(tables, name) for name in LOADS if name not in inputs})
    outputs = dict(
        out=((tokens, width), BF16),
        dx=((tokens, width), F32),
        g1=((n.rows, n.hidden), F32),
        g2=((n.rows, n.hidden), F32),
        g_small=((8, 128), F32),
        norm=((8, 128), F32),
    )
    scratch = {held: vmem(inputs[name].shape, inputs[name].dtype) for name, held in LOADS.items()}
    scratch.update(
        load_sem=dma((len(set(LOADS.values())),)),
        stage=vmem((2, n.slab, n.half), F32),
        swap_send=dma((2,)),
        swap_recv=dma((2,)),
        tile=vmem((8, 128), F32),
        small=vmem((n.batch, n.seq, 8, 128), F32),
        small_send=dma,
        small_recv=dma,
        row_send=dma,
        row_recv=dma,
        y_buf=vmem((2, width, tokens), BF16),
        l_buf=vmem((2, n.seq, n.packed, tokens), BF16),
        left=vmem((n.seqs * n.packed, n.length), BF16),
        z_buf=vmem((2, n.seq, n.seqs * n.packed, n.block), BF16),
        r_buf=vmem((2, n.seq, n.seqs * n.packed, n.block), BF16),
        mix_send=dma((2,)),
        mix_recv=dma((4,)),
        mixed=vmem((tokens, width), F32),
        full=vmem((2, q, width, cols), BF16),
        side_send=dma,
        inner_send=dma,
        mate_recv=dma((2 * q + far_chunks,)),
        pair_recv=dma((2 * q + far_chunks,)),
        first_recv=dma((3, 2 * q)),
        second_recv=dma((2 * q,)),
        x_place=vmem((tokens, width), F32),
        dy_place=vmem((tokens, width), F32),
        vecs=vmem((8, width), F32),
        biases=vmem((q, 1, cols), F32),
        unit1=vmem((tokens, width), F32),
        scale1=vmem((tokens, 128), F32),
        h=vmem((tokens, width), F32),
        h_low=vmem((2 * tokens, width), BF16),
        core_send=dma,
        core_recv=dma((6,)),
        total=vmem((2 * tokens, width), F32),
        act=vmem((q, 2 * tokens, cols), BF16),
        lift=vmem((2 * tokens, cols), F32),
        slope=vmem((q, 2 * tokens, cols), F32),
        part_low=vmem((tokens, width), BF16),
        part_low2=vmem((tokens, width), BF16),
        part_in=vmem((tokens, width), BF16),
        part_in2=vmem((tokens, width), BF16),
        sums=vmem((5, 8, width), F32),
        out_low=vmem((tokens, width), BF16),
        dr2=vmem((tokens, width), F32),
        dz=vmem((2 * tokens, width), BF16),
        acc=vmem((grads, width, n.thin), F32),
        give=vmem((grads, width, n.thin), BF16),
        in_diagonal=vmem((grads, n.segment, n.thin), BF16),
        in_sides=vmem((grads, 2, n.segment, n.thin), BF16),
        in_end=vmem((grads, n.zs - 1, n.slab, n.thin), BF16),
        in_pair=vmem((grads, 2 * n.slab, n.thin), BF16),
        in_across=vmem((grads, 2 * n.slab, n.thin), BF16),
        far_mate=vmem((splits, n.slab, n.thin), BF16),
        far_pair=vmem((splits, 2 * n.slab, n.thin), BF16),
        far_across=vmem((splits, 2 * n.slab, n.thin), BF16),
        first_mate=vmem((firsts, 4, n.slab, n.thin), BF16),
        first_pair=vmem((firsts, 4, 2 * n.slab, n.thin), BF16),
        first_across=vmem((firsts, 4, 2 * n.slab, n.thin), BF16),
        line_recv=dma((3, firsts)),
        grad_send=dma,
        diagonal_recv=dma((len(BACK_KINDS),)),
        sides_recv=dma((len(BACK_KINDS),)),
        end_recv=dma((len(BACK_KINDS),)),
        tree_recv=dma((2, max(1, sum(kind // 2 < 2 for kind in BACK_KINDS)))),
        far_recv=dma((3, splits)),
        bias_sum=vmem((q, 8, cols), F32),
        dpre=vmem((q, 2 * tokens, cols), BF16),
        dm=vmem((tokens, width), BF16),
        rest=vmem((tokens, width), BF16),
        small_out=vmem((n.batch, n.seq, 8, 128), F32),
        small_in=vmem((n.batch - 1, n.seq, 8, 128), F32),
        row_send2=dma,
        row_recv2=dma,
        small_mid=vmem((n.seq, 8, 128), F32),
        small_last=vmem((n.seq - 1, 8, 128), F32),
        small_send2=dma,
        small_recv2=dma,
        final=vmem((grads, n.slab, n.thin), F32),
        final_in=vmem((grads, n.rows, n.thin), F32),
        back_send=dma,
        back_recv=dma,
        squares=vmem((8, 128), F32),
        norm_own=vmem((1, 128), F32),
        norm_all=vmem((n.devices, 1, 128), F32),
        norm_send=dma,
        norm_recv=dma,
    )
    names = tuple(inputs) + tuple(outputs) + tuple(scratch)
    in_vmem = pl.BlockSpec(memory_space=pltpu.VMEM)
    anywhere = pl.BlockSpec(memory_space=pl.ANY)
    values = pl.pallas_call(
        functools.partial(layer_kernel, n, names),
        out_shape=[vmem(*shape) for shape in outputs.values()],
        in_specs=[anywhere if name in LOADS else in_vmem for name in inputs],
        out_specs=[in_vmem] * len(outputs),
        scratch_shapes=list(scratch.values()),
        compiler_params=pltpu.CompilerParams(
            collective_id=0, has_side_effects=True, vmem_limit_bytes=58 * 2**20
        ),
        name="fused_layer",
    )(*inputs.values())
    return types.SimpleNamespace(**dict(zip(outputs, values)))


def adam_kernel(n, names, *refs):
    r = types.SimpleNamespace(**dict(zip(names, refs)))
    passed = [
        pltpu.make_async_copy(r.out, r.out_there, r.sem.at[0]),
        pltpu.make_async_copy(r.dx, r.dx_there, r.sem.at[1]),
    ]
    for copy in passed:
        copy.start()
    norm_value = r.norm[0:1, 0:1]
    r.norm_out[...] = norm_value
    factor = clip_limit / jnp.maximum(norm_value, clip_limit)
    lanes = n.cols

    def update(gradient, given, made, at, rate):
        weight, first, second = (ref[at] for ref in given)
        new = adam_update(weight, factor * gradient, first, second, rate, STEP_COUNT)
        for ref, value in zip(made, new):
            ref[at] = value

    weight_in, weight_out = refs[4:7], refs[7:10]
    made_in, made_out = refs[19:22], refs[22:25]

    @pl.loop(0, n.hidden // lanes)
    def _(i):
        at = (slice(None), pl.ds(pl.multiple_of(i * lanes, lanes), lanes))
        update(r.g1[at], weight_in, made_in, at, rate_matrix)
        update(r.g2[at], weight_out, made_out, at, rate_matrix)

    update(r.g_small[5:6, 0 : n.bias], refs[10:13], refs[25:28], ..., rate_vector)
    for i in range(5):
        update(r.g_small[i : i + 1, 0 : n.rows], refs[13:16], refs[28:31], i, rate_vector)
    for copy in passed:
        copy.wait()


def run_adam(n, got, given):
    f32 = functools.partial(jax.ShapeDtypeStruct, dtype=F32)
    matrix, bias, vec = f32((n.rows, n.hidden)), f32((1, n.bias)), f32((5, 1, n.rows))
    inputs = dict(g1=got.g1, g2=got.g2, g_small=got.g_small, norm=got.norm)
    inputs.update({chr(97 + i): array for i, array in enumerate(given)})
    inputs.update(out=got.out, dx=got.dx)
    outputs = dict(norm_out=f32((1, 1)))
    outputs.update({chr(110 + i): matrix for i in range(6)})
    outputs.update({chr(65 + i): bias for i in range(3)})
    outputs.update({chr(70 + i): vec for i in range(3)})
    outputs.update(
        out_there=jax.ShapeDtypeStruct(got.out.shape, BF16),
        dx_there=jax.ShapeDtypeStruct(got.dx.shape, F32),
    )
    names = tuple(inputs) + tuple(outputs) + ("sem",)
    in_vmem = pl.BlockSpec(memory_space=pltpu.VMEM)
    anywhere = pl.BlockSpec(memory_space=pl.ANY)
    return pl.pallas_call(
        functools.partial(adam_kernel, n, names),
        out_shape=list(outputs.values()),
        in_specs=[in_vmem] * (len(inputs) - 2) + [anywhere] * 2,
        out_specs=[in_vmem] * (len(outputs) - 2) + [anywhere] * 2,
        scratch_shapes=[pltpu.SemaphoreType.DMA((2,))],
        compiler_params=pltpu.CompilerParams(vmem_limit_bytes=32 * 2**20),
        name="adam",
    )(*inputs.values())


def turned(a):
    return jnp.swapaxes(a[0], 0, 1)


def lined(a):
    return jnp.transpose(a, (1, 0, 2))


def fused_layer(
    n,
    activations,
    cotangent,
    w_in,
    w_out,
    b_in,
    vec_params,
    first_w_in,
    second_w_in,
    first_w_out,
    second_w_out,
    first_b_in,
    second_b_in,
    first_vec,
    second_vec,
):
    got = run_layer(
        n,
        activations.reshape(n.tokens, n.width),
        cotangent.reshape(n.tokens, n.width),
        w_in[0],
        turned(w_out),
        b_in,
        lined(vec_params),
    )
    given = (
        *(a[0] for a in (w_in, first_w_in, second_w_in)),
        *(turned(a) for a in (w_out, first_w_out, second_w_out)),
        *(b_in, first_b_in, second_b_in),
        *(lined(a) for a in (vec_params, first_vec, second_vec)),
    )
    norm_value, *made, out, dx = run_adam(n, got, given)
    return (
        out.reshape(activations.shape),
        dx.reshape(activations.shape),
        norm_value.reshape(()),
        *(a[None] for a in made[:3]),
        *(jnp.swapaxes(a, 0, 1)[None] for a in made[3:6]),
        *made[6:9],
        *(lined(a) for a in made[9:]),
    )


def local_layer(mesh, activations, cotangent, w_in, *rest):
    seqs, block, width = activations.shape
    n = Sizes(mesh, seqs, block, width, w_in.shape[2])
    if w_in.shape[0] == 1 and n.fits():
        return fused_layer(n, activations, cotangent, w_in, *rest)
    return general_layer(activations, cotangent, w_in, *rest)


BOTH = ("batch", "seq")


def solution(mesh):
    in_specs = (
        P(*BOTH, None),
        P(*BOTH, None),
        P(None, BOTH, None),
        P(None, None, BOTH),
        P(None, BOTH),
        P(None, None, BOTH),
        P(None, BOTH, None),
        P(None, BOTH, None),
        P(None, None, BOTH),
        P(None, None, BOTH),
        P(None, BOTH),
        P(None, BOTH),
        P(None, None, BOTH),
        P(None, None, BOTH),
    )
    out_specs = (
        P(*BOTH, None),
        P(*BOTH, None),
        P(),
        P(None, BOTH, None),
        P(None, BOTH, None),
        P(None, BOTH, None),
        P(None, None, BOTH),
        P(None, None, BOTH),
        P(None, None, BOTH),
        P(None, BOTH),
        P(None, BOTH),
        P(None, BOTH),
        P(None, None, BOTH),
        P(None, None, BOTH),
        P(None, None, BOTH),
    )
    return jax.shard_map(
        functools.partial(local_layer, mesh), mesh=mesh, in_specs=in_specs, out_specs=out_specs, check_vma=False)
```

```python
import functools
import math
import types

import jax
import jax.numpy as jnp
import ml_dtypes
import numpy as np
from jax import lax
from jax.experimental import pallas as pl
from jax.experimental.pallas import tpu as pltpu
from jax.sharding import PartitionSpec as P

STEP_COUNT = 10


beta_first = 0.5
beta_second = 0.5
rate_matrix = 0.03
rate_vector = 0.2
weight_decay = 0.01
adam_epsilon = 1e-08
norm_epsilon = 1e-06
clip_limit = 1.0


def dft_tables(row_index, column_index, seq_len):
    product = row_index[:, None] * column_index[None, :] % seq_len
    angle = product.astype(jnp.float32) * (2.0 * math.pi / seq_len)
    return (jnp.cos(angle).astype(jnp.bfloat16), jnp.sin(angle).astype(jnp.bfloat16))


def layer_norm(values, gain, shift):
    centre = jnp.mean(values, axis=-1, keepdims=True)
    centred = values - centre
    spread = jnp.mean(centred * centred, axis=-1, keepdims=True)
    return centred * lax.rsqrt(spread + norm_epsilon) * gain + shift


def gelu_tanh(values):
    return jax.nn.gelu(values, approximate=True)


def adam_update(weight, gradient, first, second, rate, step_count):
    first_new = beta_first * first + (1.0 - beta_first) * gradient
    second_new = beta_second * second + (1.0 - beta_second) * gradient * gradient
    first_hat = first_new / (1.0 - beta_first**step_count)
    second_hat = second_new / (1.0 - beta_second**step_count)
    updated = weight - rate * (
        first_hat / (jnp.sqrt(second_hat) + adam_epsilon) + weight_decay * weight
    )
    return (first_new, second_new, updated)


def general_layer(
    activations,
    cotangent,
    w_in,
    w_out,
    b_in,
    vec_params,
    first_w_in,
    second_w_in,
    first_w_out,
    second_w_out,
    first_b_in,
    second_b_in,
    first_vec,
    second_vec,
):
    layers = w_in.shape[0]
    seq_count, block_len, model_width = activations.shape
    seq_devices = lax.axis_size(BOTH[1])
    seq_len = block_len * seq_devices
    dft_scale = 1.0 / math.sqrt(seq_len * model_width)
    first_row = lax.axis_index(BOTH[1]) * block_len
    my_rows = first_row + jnp.arange(block_len, dtype=jnp.int32)
    feature_line = jnp.arange(model_width, dtype=jnp.int32)
    cos_model, sin_model = dft_tables(feature_line, feature_line, model_width)
    table_fwd = jnp.concatenate([cos_model, sin_model], axis=1)
    table_back = jnp.transpose(table_fwd)
    layer_index = 0
    pieces = (
        w_in[layer_index].astype(jnp.bfloat16),
        w_out[layer_index].astype(jnp.bfloat16),
        b_in[layer_index].astype(jnp.bfloat16),
        vec_params[layer_index].astype(jnp.bfloat16),
    )
    gathered = [
        (
            lax.all_gather(pieces[0], BOTH, axis=0, tiled=True),
            lax.all_gather(pieces[1], BOTH, axis=1, tiled=True),
            lax.all_gather(pieces[2], BOTH, axis=0, tiled=True),
            lax.all_gather(pieces[3], BOTH, axis=1, tiled=True),
        )
    ]
    zeros_block = jnp.zeros((seq_count, block_len, model_width), jnp.float32)
    stream = activations.astype(jnp.float32)
    layer_index = 0
    weight_first, weight_second, bias_low, vec_low = gathered[layer_index]
    vec_float = vec_low.astype(jnp.float32)
    bias_float = bias_low.astype(jnp.float32)
    joined = jnp.dot(
        stream.astype(jnp.bfloat16), table_fwd, preferred_element_type=jnp.float32
    ).astype(jnp.bfloat16)
    halves = (joined[..., :model_width], joined[..., model_width:])
    shard_piece = (
        lax.all_gather(halves[0], BOTH[1], axis=1, tiled=True),
        lax.all_gather(halves[1], BOTH[1], axis=1, tiled=True),
    )
    piece_len = shard_piece[0].shape[1]
    cos_block, sin_block = dft_tables(my_rows, jnp.arange(piece_len, dtype=jnp.int32), seq_len)
    running = jnp.einsum(
        "ij,sjd->sid", cos_block, shard_piece[0], preferred_element_type=jnp.float32
    )
    mixed = (
        running
        - jnp.einsum("ij,sjd->sid", sin_block, shard_piece[1], preferred_element_type=jnp.float32)
    ) * dft_scale
    normed, norm_first_back = jax.vjp(layer_norm, stream + mixed, vec_float[0], vec_float[1])
    normed_low = normed.astype(jnp.bfloat16)
    pre_act = jnp.dot(normed_low, weight_first, preferred_element_type=jnp.float32) + bias_float
    activated, gelu_back = jax.vjp(gelu_tanh, pre_act)
    act_low = activated.astype(jnp.bfloat16)
    feed = jnp.dot(act_low, weight_second, preferred_element_type=jnp.float32) + vec_float[2]
    stream, norm_second_back = jax.vjp(layer_norm, normed + feed, vec_float[3], vec_float[4])
    saved = [(norm_first_back, normed_low, gelu_back, act_low, norm_second_back)]
    block_output = stream.astype(jnp.bfloat16)
    grad_now = cotangent.astype(jnp.float32)
    raw_grads = [None] * layers
    for layer_index in reversed(range(layers)):
        weight_first, weight_second, bias_low, vec_low = gathered[layer_index]
        norm_first_back, normed_low, gelu_back, act_low, norm_second_back = saved[layer_index]
        grad_sum2, grad_gain2, grad_shift2 = norm_second_back(grad_now)
        grad_z = grad_sum2.astype(jnp.bfloat16)
        grad_weight_second = jnp.einsum(
            "stf,std->fd", act_low, grad_z, preferred_element_type=jnp.float32
        )
        grad_bias_out = jnp.sum(grad_z.astype(jnp.float32), axis=(0, 1))
        grad_act = jnp.einsum(
            "std,fd->stf", grad_z, weight_second, preferred_element_type=jnp.float32
        )
        (grad_pre,) = gelu_back(grad_act)
        grad_pre_low = grad_pre.astype(jnp.bfloat16)
        grad_weight_first = jnp.einsum(
            "std,stf->df", normed_low, grad_pre_low, preferred_element_type=jnp.float32
        )
        grad_bias_in = jnp.sum(grad_pre_low.astype(jnp.float32), axis=(0, 1))
        grad_normed = (
            jnp.einsum(
                "stf,df->std", grad_pre_low, weight_first, preferred_element_type=jnp.float32
            )
            + grad_sum2
        )
        grad_sum1, grad_gain1, grad_shift1 = norm_first_back(grad_normed)
        grad_mix_low = grad_sum1.astype(jnp.bfloat16)
        add_shard_piece = lax.all_gather(grad_mix_low, BOTH[1], axis=1, tiled=True)
        add_piece_len = add_shard_piece.shape[1]
        add_cos_block, add_sin_block = dft_tables(
            my_rows, jnp.arange(add_piece_len, dtype=jnp.int32), seq_len
        )
        with_cos = jnp.einsum(
            "ij,sjd->sid", add_cos_block, add_shard_piece, preferred_element_type=jnp.float32
        )
        with_sin = (zeros_block, zeros_block)[1] - jnp.einsum(
            "ij,sjd->sid", add_sin_block, add_shard_piece, preferred_element_type=jnp.float32
        )
        with_cos, with_sin = (with_cos, with_sin)
        with_cos = (with_cos * dft_scale).astype(jnp.bfloat16)
        with_sin = (with_sin * dft_scale).astype(jnp.bfloat16)
        grad_halves = jnp.concatenate([with_cos, with_sin], axis=-1)
        grad_now = grad_sum1 + jnp.dot(grad_halves, table_back, preferred_element_type=jnp.float32)
        grad_vec = jnp.stack([grad_gain1, grad_shift1, grad_bias_out, grad_gain2, grad_shift2])
        layer_terms = (grad_weight_first, grad_weight_second, grad_bias_in, grad_vec)
        raw_grads[layer_index] = (
            lax.psum_scatter(layer_terms[0], BOTH, scatter_dimension=0, tiled=True),
            lax.psum_scatter(layer_terms[1], BOTH, scatter_dimension=1, tiled=True),
            lax.psum_scatter(layer_terms[2], BOTH, scatter_dimension=0, tiled=True),
            lax.psum_scatter(layer_terms[3], BOTH, scatter_dimension=1, tiled=True),
        )
    shard_w_in = jnp.stack([entry[0] for entry in raw_grads])
    shard_w_out = jnp.stack([entry[1] for entry in raw_grads])
    shard_b_in = jnp.stack([entry[2] for entry in raw_grads])
    shard_vec = jnp.stack([entry[3] for entry in raw_grads])
    local_squares = jnp.sum(shard_w_in * shard_w_in) + jnp.sum(shard_w_out * shard_w_out)
    local_squares = (
        local_squares + jnp.sum(shard_b_in * shard_b_in) + jnp.sum(shard_vec * shard_vec)
    )
    norm_value = jnp.sqrt(lax.psum(local_squares, BOTH))
    factor = clip_limit / jnp.maximum(norm_value, clip_limit)
    upd_w_in = adam_update(
        w_in, factor * shard_w_in, first_w_in, second_w_in, rate_matrix, STEP_COUNT
    )
    upd_w_out = adam_update(
        w_out, factor * shard_w_out, first_w_out, second_w_out, rate_matrix, STEP_COUNT
    )
    upd_b_in = adam_update(
        b_in, factor * shard_b_in, first_b_in, second_b_in, rate_vector, STEP_COUNT
    )
    upd_vec = adam_update(
        vec_params, factor * shard_vec, first_vec, second_vec, rate_vector, STEP_COUNT
    )
    return (
        block_output,
        grad_now,
        norm_value,
        upd_w_in[0],
        upd_w_in[1],
        upd_w_in[2],
        upd_w_out[0],
        upd_w_out[1],
        upd_w_out[2],
        upd_b_in[0],
        upd_b_in[1],
        upd_b_in[2],
        upd_vec[0],
        upd_vec[1],
        upd_vec[2],
    )


MESH = pl.DeviceIdType.MESH
F32 = jnp.float32
BF16 = jnp.bfloat16
NN = (((1,), (0,)), ((), ()))
NT = (((1,), (1,)), ((), ()))
TN = (((0,), (0,)), ((), ()))


def dot(a, b, dims=NN):
    return lax.dot_general(a, b, dims, preferred_element_type=F32)


class Sizes:
    def __init__(self, mesh, seqs, block, width, hidden):
        self.batch, self.seq = mesh.shape["batch"], mesh.shape["seq"]
        self.xs, self.ys, self.zs = self.batch // 2, 2, self.seq // 2
        self.devices = self.batch * self.seq
        self.seqs, self.block, self.width, self.hidden = seqs, block, width, hidden
        self.length = block * self.seq
        self.rows = width // self.devices
        self.slab = 2 * self.rows
        self.segment = self.zs * self.slab
        self.half = hidden // 2
        self.cols = 512
        self.chunks = self.half // self.cols
        self.parts = 2
        self.thin = self.cols // self.parts
        self.packed = width // self.seq
        self.tokens = seqs * block
        self.bias = hidden // self.devices

    def fits(self):
        return (
            self.batch == 4
            and self.seq % 2 == 0
            and self.width % self.devices == 0
            and self.slab % 16 == 0
            and self.packed % 32 == 0
            and self.block % 128 == 0
            and self.zs == 4
            and self.half % self.cols == 0
            and self.rows <= 128
            and self.bias <= 128
            and 5 * self.rows <= self.width
            and self.hidden == 4 * self.width
        )

    def owner(self, x, core, z, y):
        return (2 * x + core) * self.seq + 2 * z + y

    def place_owner(self):
        return [
            self.owner(x, core, z, y)
            for y in range(self.ys)
            for x in range(self.xs)
            for z in range(self.zs)
            for core in range(2)
        ]


def cos_sin(rows, columns, count):
    angle = (rows[:, None] * columns[None, :] % count) * (2.0 * math.pi / count)
    return np.cos(angle), np.sin(angle)


def host_tables(n):
    width, half = n.width, n.packed // 2
    owners = np.array(n.place_owner())
    order = (owners[:, None] * n.rows + np.arange(n.rows)[None, :]).reshape(-1)
    line = np.arange(width)
    cosine, sine = cos_sin(line, line, width)
    pack = np.zeros((width, width))
    unpack = np.zeros((width, width))
    for k in range(width // 2):
        device, inner = divmod(k, half)
        at_cos = device * n.packed + inner
        at_sin = at_cos + half
        pack[at_cos] = cosine[k]
        unpack[at_cos, k] = 1.0
        if k:
            unpack[at_cos, width - k] = 1.0
            pack[at_sin] = sine[k]
            unpack[at_sin, k] = -1.0
            unpack[at_sin, width - k] = 1.0
    pack[half] = cosine[width // 2]
    unpack[half, width // 2] = 1.0
    perm = np.zeros((width, width))
    perm[order, np.arange(width)] = 1.0
    positions = np.arange(n.length)
    by_length = np.stack(cos_sin(positions, positions, n.length))
    vec_mask = np.zeros((n.devices, width))
    vec_mask[np.repeat(owners, n.rows), np.arange(width)] = 1.0
    vec_spread = np.zeros((128, width))
    vec_spread[np.arange(width) % n.rows, np.arange(width)] = 1.0
    bias_spread = np.zeros((128, n.half))
    bias_spread[np.arange(n.half) % n.bias, np.arange(n.half)] = 1.0

    def low(a):
        return jnp.asarray(a.astype(np.float32).astype(ml_dtypes.bfloat16))

    return types.SimpleNamespace(
        tt_f=low(pack),
        by_length=low(by_length),
        un_f=low(unpack[:, order]),
        perm=low(perm),
        tt_b=low(pack[:, order]),
        un_b=low(unpack),
        vec_mask=jnp.asarray(vec_mask.astype(np.float32)),
        vec_spread=low(vec_spread),
        bias_spread=low(bias_spread),
    )


LOADS = dict(
    bias="bias_v",
    vec="vec_v",
    w1="w1_v",
    w2="w2_v",
    x="x_v",
    tt_f="tt_v",
    dy="dy_v",
    vec_spread="vec_spread_v",
    bias_spread="bias_spread_v",
    vec_mask="vec_mask_v",
    by_length="by_length_v",
    perm="perm_v",
    un_f="un_v",
    tt_b="tt_v",
    un_b="un_v",
)
FIRST = ("w1", "w2")
LATER = ("tt_b", "un_b")
FORWARD_KINDS = (1, 1, 1, 1, 0, 2)
BACK_KINDS = (3, 6, 5, 0, 0, 4, 5, 1, 0, 1, 1, 5)


def layer_kernel(n, names, *refs):
    r = types.SimpleNamespace(**dict(zip(names, refs)))
    batch_at, seq_at = lax.axis_index("batch"), lax.axis_index("seq")
    x, core = batch_at // 2, batch_at % 2
    z, y = seq_at // 2, seq_at % 2
    tokens, width, seg, slab = n.tokens, n.width, n.segment, n.slab

    def aligned(at, by):
        return pl.multiple_of(at * by, by)

    def rows_of(at, by):
        return pl.ds(aligned(at, by), by)

    def remote(src, dst, send, recv, batch_to, seq_to):
        return pltpu.make_async_remote_copy(
            src_ref=src,
            dst_ref=dst,
            send_sem=send,
            recv_sem=recv,
            device_id=(batch_to, seq_to),
            device_id_type=MESH,
        )

    def bytes_of(view, send, recv):
        return remote(view, view, send, recv, other_core, seq_at)

    other_core = 2 * x + 1 - core
    other_x = 2 * (1 - x) + core
    other_y = 2 * z + 1 - y

    def plane(k):
        return (seq_at + k) % n.seq

    def plane_from(k):
        return (seq_at + n.seq - k) % n.seq

    def across(k):
        return (batch_at + k) % n.batch

    def across_from(k):
        return (batch_at + n.batch - k) % n.batch

    loads = types.SimpleNamespace()
    for name, held in LOADS.items():
        load = pltpu.make_async_copy(
            getattr(r, name), getattr(r, held), r.load_sem.at[sorted(set(LOADS.values())).index(held)]
        )
        setattr(loads, name, load)
    for name in FIRST:
        getattr(loads, name).start()

    everyone = [
        ((batch_at + i // n.seq) % n.batch, (seq_at + i % n.seq) % n.seq)
        for i in range(1, n.devices)
    ]
    barrier = pltpu.get_barrier_semaphore()
    partners = [(across(k), seq_at) for k in range(1, n.batch)]
    partners += [(batch_at, plane(k)) for k in range(n.seq - 1, 0, -1)]
    for device in partners:
        pl.semaphore_signal(barrier, inc=1, device_id=device, device_id_type=MESH)
    loads.x.start()
    loads.tt_f.start()
    pl.semaphore_wait(barrier, len(partners))

    loads.w1.wait()
    loads.w2.wait()
    weights = (r.w1_v, r.w2_v)
    give = pl.ds(aligned(1 - core, n.half), n.half)
    keep = pl.ds(aligned(core, n.half), n.half)
    core_rows = pl.ds(aligned(core, n.rows), n.rows)
    their_rows = pl.ds(aligned(1 - core, n.rows), n.rows)
    for m in range(2):
        remote(
            weights[m].at[:, give],
            r.stage.at[m, core_rows],
            r.swap_send.at[m],
            r.swap_recv.at[m],
            other_core,
            seq_at,
        ).start()

    for name in LOADS:
        if name not in FIRST + LATER + ("x", "tt_f"):
            getattr(loads, name).start()

    def swapped(m):
        return bytes_of(r.stage.at[m, pl.ds(0, n.rows)], r.swap_send.at[m], r.swap_recv.at[m])

    def mix_start(t, source, table):
        y_ref, l_ref = r.y_buf.at[t], r.l_buf.at[t]
        y_ref[...] = dot(table[...], source, NT).astype(BF16)
        l_ref[seq_at] = y_ref[rows_of(seq_at, n.packed), :]

    half_way = n.seq // 2
    mix_order = [*range(half_way, n.seq), *range(2, half_way), 1]

    def mix_send(t):
        y_ref, l_ref = r.y_buf.at[t], r.l_buf.at[t]
        for k in mix_order:
            remote(
                y_ref.at[rows_of(plane(k), n.packed)],
                l_ref.at[seq_at],
                r.mix_send.at[0],
                r.mix_recv.at[2 * t],
                batch_at,
                plane(k),
            ).start()

    def mixed_bytes(i):
        into = (r.l_buf, r.r_buf)[i % 2].at[i // 2, pl.ds(0, n.seq - 1)]
        return bytes_of(into, r.mix_send.at[i % 2], r.mix_recv.at[i])

    def mix_turn(t):
        l_ref, z_ref, r_ref = r.l_buf.at[t], r.z_buf.at[t], r.r_buf.at[t]
        mixed_bytes(2 * t).wait_recv()
        left = jnp.concatenate(
            [
                jnp.concatenate(
                    [l_ref[d, :, g * n.block : (g + 1) * n.block] for d in range(n.seq)], axis=1
                )
                for g in range(n.seqs)
            ],
            axis=0,
        )
        r.left[...] = left
        inner = lax.broadcasted_iota(jnp.int32, (n.seqs * n.packed, 1), 0) % n.packed
        first = (inner < n.packed // 2) | ((inner == n.packed // 2) & (seq_at == 0))
        scale = 1.0 / math.sqrt(n.length * n.width)
        for e in range(0, n.seq, 2):
            at = slice(e * n.block, (e + 2) * n.block)
            by_cos = dot(r.left[...], r.by_length_v[0, :, at])
            by_sin = dot(r.left[...], r.by_length_v[1, :, at])
            value = (jnp.where(first, by_cos, by_sin) * scale).astype(BF16)
            z_ref[e] = value[:, : n.block]
            z_ref[e + 1] = value[:, n.block :]
        for k in mix_order:
            remote(
                z_ref.at[plane(k)],
                r_ref.at[seq_at],
                r.mix_send.at[1],
                r.mix_recv.at[2 * t + 1],
                batch_at,
                plane(k),
            ).start()
        r_ref[seq_at] = z_ref[seq_at]

    def mix_finish(t, table):
        r_ref = r.r_buf.at[t]
        mixed_bytes(2 * t + 1).wait_recv()
        parts = [
            r_ref[:, g * n.packed : (g + 1) * n.packed, :].reshape(width, n.block)
            for g in range(n.seqs)
        ]
        r.mixed[...] = dot(jnp.concatenate(parts, axis=1), table[...], TN)

    loads.tt_f.wait()
    loads.x.wait()
    mix_start(0, r.x_v[...], r.tt_v)

    full = r.full
    mate_z = z + 1 - 2 * (z % 2)
    pair_z = z // 2
    inner = (z > 0) & (z < n.zs - 1)

    def line(to_z):
        return batch_at, 2 * to_z + y

    def seg_rows(sx, sy):
        return rows_of(sy * n.xs + sx, seg)

    def pair_rows(sx, sy, sp):
        return rows_of((sy * n.xs + sx) * 2 + sp, 2 * slab)

    def slab_rows(sx, sy, sz):
        return rows_of((sy * n.xs + sx) * n.zs + sz, slab)

    def peer(t):
        return (other_y_at, other_x_at)[t == 0]

    other_x_at = (other_x, seq_at)
    other_y_at = (batch_at, other_y)

    def away(t):
        return (1 - x, y) if t == 0 else (x, 1 - y)

    def turn_of(c):
        return FORWARD_KINDS[c] % 2

    def split(c):
        return FORWARD_KINDS[c] // 2 == 1

    def place(c):
        return c // n.chunks, c % n.chunks

    def stage_weights(m):
        r.stage[m, core_rows, :] = weights[m][:, keep]
        swapped(m).wait_recv()
        for q in range(n.chunks):
            columns = r.stage[m, :, q * n.cols : (q + 1) * n.cols]
            full[m, q, slab_rows(x, y, z), :] = columns.astype(BF16)

    def full_copy(c, at, send, recv, to):
        m, q = place(c)
        return remote(full.at[m, q, at], full.at[m, q, at], send, recv, *to)

    def rows_at(sx, sy, i):
        return (slab_rows(sx, sy, z), slab_rows(sx, sy, mate_z), pair_rows(sx, sy, 1 - pair_z))[i]

    def side_copy(c, i, sx, sy, first):
        t = turn_of(c)
        recv = r.first_recv.at[i, c] if first else r.second_recv.at[c]
        return full_copy(c, rows_at(sx, sy, i), r.side_send, recv, peer(t if first else 1 - t))

    def to_sides(c, i):
        if i == 0 or not split(c):
            side_copy(c, i, x, y, True).start()
        side_copy(c, i, x, y, False).start()

    def line_slot(c, far):
        return 2 * n.chunks + sum(split(d) for d in range(c)) if far else c

    def line_seg(c, far):
        return away(turn_of(c)) if far else (x, y)

    def own_to_mate(c, far):
        at = rows_at(*line_seg(c, far), 0)
        return full_copy(c, at, r.side_send, r.mate_recv.at[line_slot(c, far)], line(mate_z))

    def mate_arrives(c, far):
        at = rows_at(*line_seg(c, far), 1)
        full_copy(c, at, r.side_send, r.mate_recv.at[line_slot(c, far)], line(mate_z)).wait_recv()

    def pair_across(c, far):
        at = pair_rows(*line_seg(c, far), pair_z)
        return full_copy(c, at, r.inner_send, r.pair_recv.at[line_slot(c, far)], line(n.zs - 1 - z))

    def pair_out(c, far):
        at = rows_at(*line_seg(c, far), 2)
        return full_copy(c, at, r.inner_send, r.pair_recv.at[line_slot(c, far)], line(mate_z))

    def own_sides(c):
        to_sides(c, 0)

    def own_line(c):
        own_to_mate(c, 0).start()

    def from_mate(c, far):
        mate_arrives(c, far)

        @pl.when(inner)
        def _():
            pair_across(c, far).start()

    def from_pair(c, far):
        pair_out(c, far).wait_recv()

        @pl.when(inner)
        def _():
            pair_out(c, far).start()

    def mate_in(c):
        from_mate(c, 0)
        to_sides(c, 1)

    def pair_in(c):
        from_pair(c, 0)
        to_sides(c, 2)

    def pass_on(c, i):
        ax, ay = away(turn_of(c))
        if i == 0 or not split(c):
            side_copy(c, i, ax, ay, True).wait_recv()
        if split(c):
            if i == 0:
                own_to_mate(c, 1).start()
            else:
                (from_mate, from_pair)[i - 1](c, 1)
        side_copy(c, i, ax, ay, False).start()

    def weights_here(c):
        m, q = place(c)
        second = full.at[m, q, pl.ds(0, 2 * n.zs * slab)]
        bytes_of(second, r.side_send, r.second_recv.at[c]).wait_recv()

    def all_slabs(counts, send):
        rows = sum(counts) * slab // (2 * n.chunks)
        return bytes_of(full.at[:, :, pl.ds(0, rows)], send, r.second_recv.at[0])

    def small_tiles():
        loads.bias.wait()
        loads.vec.wait()
        tile = r.tile
        tile[...] = jnp.zeros(tile.shape, F32)
        for i in range(5):
            tile[i : i + 1, 0 : n.rows] = r.vec_v[i]
        tile[5:6, 0 : n.bias] = r.bias_v[...]
        small[batch_at, seq_at] = tile[...]
        for k in range(1, n.seq):
            small_copy(k, seq_at).start()

    def small_copy(k, at):
        return remote(
            r.tile,
            small.at[batch_at, at],
            r.small_send,
            r.small_recv,
            batch_at,
            plane(k),
        )

    def row_copy(k, at):
        return remote(
            small.at[batch_at],
            small.at[at],
            r.row_send,
            r.row_recv,
            across(k),
            seq_at,
        )

    small = r.small

    def tiles_bytes():
        return bytes_of(small.at[0, pl.ds(0, n.seq - 1)], r.small_send, r.small_recv)

    def rows_bytes():
        return bytes_of(small.at[pl.ds(0, n.batch - 1)], r.row_send, r.row_recv)

    def small_rows():
        tiles_bytes().wait_recv()
        for k in range(1, n.batch):
            row_copy(k, batch_at).start()

    half_owners = n.devices // 2
    bias_mask = (
        lax.broadcasted_iota(jnp.int32, (half_owners, n.half), 0)
        == lax.broadcasted_iota(jnp.int32, (half_owners, n.half), 1) // n.bias
    )

    def small_vectors():
        rows_bytes().wait_recv()
        for load in (loads.vec_spread, loads.bias_spread, loads.vec_mask):
            load.wait()
        for i in range(5):
            held = small[:, :, i, :].reshape(n.devices, 128).astype(BF16)
            spread = dot(held, r.vec_spread_v[...]) * r.vec_mask_v[...]
            r.vecs[i : i + 1, :] = jnp.sum(spread, axis=0, keepdims=True)
        held = small[pl.ds(core * (n.batch // 2), n.batch // 2), :, 5, :]
        held = held.reshape(half_owners, 128).astype(BF16)
        spread = jnp.where(bias_mask, dot(held, r.bias_spread_v[...]), 0.0)
        biases = jnp.sum(spread, axis=0, keepdims=True)
        for q in range(n.chunks):
            r.biases[q] = biases[:, q * n.cols : (q + 1) * n.cols]

    def place_inputs():
        loads.perm.wait()
        loads.dy.wait()
        r.x_place[...] = dot(r.x_v[...], r.perm_v[...])
        r.dy_place[...] = dot(r.dy_v[...], r.perm_v[...])

    def turn_forward():
        loads.by_length.wait()
        mix_turn(0)

    step = 32
    tall = 128
    mine, theirs = pl.ds(0, tokens), pl.ds(tokens, tokens)

    def row_loop(body, first=0, last=tokens):
        @pl.loop(first // tall, last // tall, unroll=True)
        def _(i):
            body(pl.ds(pl.multiple_of(i * tall, tall), tall))

    def mean(v):
        return jnp.mean(v, axis=-1, keepdims=True)

    def first_norm(at):
        v = r.x_place[at, :] + r.mixed[at, :]
        centred = v - mean(v)
        scale = lax.rsqrt(mean(centred * centred) + norm_epsilon)
        unit = centred * scale
        h = unit * r.vecs[0:1, :] + r.vecs[1:2, :]
        r.unit1[at, :] = unit
        r.scale1[at, :] = jnp.broadcast_to(scale, (tall, 128))
        r.h[at, :] = h
        r.h_low[at, :] = h.astype(BF16)

    def swap(i, src, dst):
        return remote(src, dst, r.core_send, r.core_recv.at[i], other_core, seq_at)

    def swap_h():
        return swap(0, r.h_low.at[mine], r.h_low.at[theirs])

    def norm_forward():
        loads.un_f.wait()
        mix_finish(0, r.un_v)
        loads.tt_b.start()
        loads.un_b.start()
        row_loop(first_norm)
        swap_h().start()

    root = math.sqrt(2.0 / math.pi)

    lifted_parts = []

    def lift(q):
        if not lifted_parts:
            swap_h().wait_recv()
        lifted_parts.append(q)
        weights_here(q)
        r.lift[...] = dot(r.h_low[...], full[0, q]) + r.biases[q]

        @pl.loop(0, 2 * tokens // step)
        def _(i):
            at = pl.ds(pl.multiple_of(i * step, step), step)
            u = r.lift[at, :]
            square = u * u
            bent = jnp.tanh(u * (root + (root * 0.044715) * square))
            half_up = 0.5 + 0.5 * bent
            r.act[q, at, :] = (u * half_up).astype(BF16)
            r.slope[q, at, :] = half_up + (u * (1.0 - bent * bent)) * (
                0.5 * root + (1.5 * root * 0.044715) * square
            )

    gathered_parts = []

    halves = [pl.ds(j * tokens // 2, tokens // 2) for j in range(2)]

    def swap_ff(j):
        return swap(1 + j, r.part_low.at[halves[j]], r.part_in.at[halves[j]])

    def drop(q):
        weights_here(n.chunks + q)
        gathered_parts.append(q)
        for half in (theirs, mine):
            part = dot(r.act[q, half, :], full[1, q], NT)
            part = r.total[half, :] + part if len(gathered_parts) > 1 else part
            if len(gathered_parts) == n.chunks and half is theirs:
                r.part_low[...] = part.astype(BF16)
                for j in range(2):
                    swap_ff(j).start()
            else:
                r.total[half, :] = part

    def send_forward():
        mix_send(0)

    forward_steps = (
        (send_forward,), (stage_weights, 0), (own_sides, 1), (own_sides, 0), (own_line, 2),
        (own_sides, 2), (own_line, 1), (own_line, 0), (stage_weights, 1), (own_sides, 4),
        (own_sides, 3), (place_inputs,), (own_line, 3), (own_sides, 5), (own_line, 4),
        (pass_on, 1, 0), (small_tiles,), (pass_on, 0, 0), (mate_in, 2), (mate_in, 1),
        (pass_on, 5, 0), (pass_on, 2, 0), (own_line, 5), (mate_in, 0), (pass_on, 4, 0),
        (mate_in, 3), (mate_in, 4), (pass_on, 2, 1), (pass_on, 3, 0), (pair_in, 2),
        (small_rows,), (pass_on, 1, 1), (pair_in, 1), (pass_on, 5, 1), (turn_forward,),
        (pass_on, 0, 1), (mate_in, 5), (pass_on, 3, 1), (pair_in, 0), (pass_on, 4, 1),
        (pass_on, 2, 2), (pair_in, 4), (small_vectors,), (pass_on, 1, 2), (pair_in, 3),
        (pass_on, 5, 2), (pass_on, 0, 2), (norm_forward,), (pass_on, 4, 2), (pair_in, 5),
        (pass_on, 3, 2), (lift, 1), (lift, 2), (lift, 0), (drop, 1), (drop, 0), (drop, 2),
    )
    for task, *which in forward_steps:
        task(*which)
    def second_norm(at):
        v = (
            r.h[at, :]
            + r.total[at, :]
            + r.part_in[at, :].astype(F32)
            + r.vecs[2:3, :]
        )
        centred = v - mean(v)
        scale = lax.rsqrt(mean(centred * centred) + norm_epsilon)
        unit = centred * scale
        gain = r.vecs[3:4, :]
        r.h[at, :] = unit
        r.out_low[at, :] = (unit * gain + r.vecs[4:5, :]).astype(BF16)
        du = r.dy_place[at, :] * gain
        dv = scale * (du - mean(du) - unit * mean(du * unit))
        r.dr2[at, :] = dv
        r.dz[at, :] = dv.astype(BF16)

    def swap_dz(j):
        return swap(
            3 + j,
            r.dz.at[halves[j]],
            r.dz.at[pl.ds(tokens + j * tokens // 2, tokens // 2)],
        )

    for j in range(2):
        swap_ff(j).wait_recv()
        row_loop(second_norm, j * tokens // 2, (j + 1) * tokens // 2)
        swap_dz(j).start()

    pieces = grad_pieces(n)
    acc = r.acc

    def wide(c):
        slot, start, width_of = pieces[c]
        m, q = slot // (n.chunks * n.parts), slot % (n.chunks * n.parts)
        return 1 - m, q // n.parts, pl.ds((q % n.parts) * n.thin + start, width_of)

    def held(c, at=slice(None), lead=()):
        slot, start, width_of = pieces[c]
        return (slot, *lead, at, pl.ds(start, width_of))

    def product(c, tokens_at):
        m, q, at = wide(c)
        left, right = (r.dz, r.act) if m else (r.h_low, r.dpre)
        return dot(left[tokens_at, :], right[q, tokens_at, at], TN)

    begun = (0, 1, 3)
    for c in begun:
        acc[held(c)] = product(c, mine)
    for j in range(2):
        swap_dz(j).wait_recv()

    out_low = r.give

    def grad_copy(c, at, into, recv, to):
        return remote(out_low.at[held(c, at)], into, r.grad_send, recv, *to)

    def back_turn(c):
        return BACK_KINDS[c] % 2

    def back_mode(c):
        return BACK_KINDS[c] // 2

    def back_slot(c):
        return [d for d, kind in enumerate(BACK_KINDS) if kind // 2 == back_mode(c)].index(c)

    def copy_diagonal(c):
        at = seg_rows(1 - x, 1 - y)
        return grad_copy(c, at, r.in_diagonal.at[held(c)], r.diagonal_recv.at[c], peer(1 - back_turn(c)))

    def copy_near(c):
        t = 1 - back_turn(c)
        into = r.in_sides.at[held(c, lead=(0,))]
        return grad_copy(c, seg_rows(*away(t)), into, r.sides_recv.at[c], peer(t))

    def copy_side(c):
        t = back_turn(c)
        into = r.in_sides.at[held(c, lead=(1,))]
        return grad_copy(c, seg_rows(*away(t)), into, r.sides_recv.at[c], peer(t))

    def back_seg(c, far):
        return away(back_turn(c)) if far else (x, y)

    def tree_slot(c):
        return sum(kind // 2 < 2 for kind in BACK_KINDS[:c])

    def line_into(c, far, i):
        if far:
            into = (r.far_mate, r.far_pair, r.far_across)[i]
            return into.at[back_slot(c), :, pl.ds(0, pieces[c][2])]
        into, lead = ((r.in_end, (0,)), (r.in_pair, ()), (r.in_across, ()))[i]
        return into.at[held(c, lead=lead)]

    def line_copy(c, at, far, i, to):
        if far:
            recv = r.far_recv.at[i, back_slot(c)]
        else:
            recv = r.end_recv.at[c] if i == 0 else r.tree_recv.at[i - 1, tree_slot(c)]
        return grad_copy(c, at, line_into(c, far, i), recv, to)

    def copy_mate(c, far):
        at = slab_rows(*back_seg(c, far), mate_z)
        return line_copy(c, at, far, 0, line(mate_z))

    def copy_pair_in(c, far):
        at = pair_rows(*back_seg(c, far), 1 - pair_z)
        return line_copy(c, at, far, 1, line(mate_z))

    def copy_pair_across(c, far):
        at = pair_rows(*back_seg(c, far), 1 - pair_z)
        return line_copy(c, at, far, 2, line(n.zs - 1 - z))

    def copy_far(c):
        t = back_turn(c)
        at = slab_rows(*away(t), z)
        return grad_copy(c, at, r.in_end.at[held(c, lead=(1,))], r.end_recv.at[c], peer(t))

    def copy_direct(c, d):
        to_z = (z + d) % n.zs
        at = slab_rows(x, y, to_z)
        return grad_copy(c, at, r.in_end.at[held(c, lead=(d - 1,))], r.end_recv.at[c], line(to_z))

    def round_out(c, at, *more):
        value = acc[held(c, at)]
        for ref in more:
            value = value + ref[...].astype(F32)
        out_low[held(c, at)] = value.astype(BF16)

    four = [(sx, sy) for sy in range(n.ys) for sx in range(n.xs)]

    def first_copy(c, i, which):
        sx, sy = four[i]
        slot, lanes = back_slot(c), pl.ds(0, pieces[c][2])
        if which == 0:
            at, to = slab_rows(sx, sy, mate_z), line(mate_z)
        else:
            at, to = pair_rows(sx, sy, 1 - pair_z), line((0, mate_z, n.zs - 1 - z)[which])
        into = (r.first_mate, r.first_pair, r.first_across)[which].at[slot, i, :, lanes]
        return grad_copy(c, at, into, r.line_recv.at[which, slot], to)

    def first_wait(c, which):
        slot, lanes = back_slot(c), pl.ds(0, pieces[c][2])
        into = (r.first_mate, r.first_pair, r.first_across)[which].at[slot, :, :, lanes]
        bytes_of(into, r.grad_send, r.line_recv.at[which, slot]).wait_recv()

    def first_start(c):
        @pl.when(jnp.logical_not(inner))
        def _():
            for i, (sx, sy) in enumerate(four):
                round_out(c, pair_rows(sx, sy, 1 - pair_z))
                first_copy(c, i, 1).start()
            for i, (sx, sy) in enumerate(four):
                round_out(c, slab_rows(sx, sy, mate_z))
                first_copy(c, i, 0).start()

    def first_across(c):
        @pl.when(inner)
        def _():
            first_wait(c, 1)
            for i, (sx, sy) in enumerate(four):
                lanes = pl.ds(0, pieces[c][2])
                more = r.first_pair.at[back_slot(c), i, :, lanes]
                round_out(c, pair_rows(sx, sy, 1 - pair_z), more)
                first_copy(c, i, 2).start()

    def first_out(c):
        @pl.when(inner)
        def _():
            first_wait(c, 2)
            for i, (sx, sy) in enumerate(four):
                at = held(c, pair_rows(sx, sy, pair_z))
                lanes = pl.ds(0, pieces[c][2])
                acc[at] = acc[at] + r.first_across[back_slot(c), i, :, lanes].astype(F32)
                round_out(c, slab_rows(sx, sy, mate_z))
                first_copy(c, i, 0).start()

    def slab_copy(c, i):
        t = back_turn(c)
        sx, sy = ((1 - x, 1 - y), away(1 - t), away(t))[i]
        own = pl.ds(0, slab)
        into = (
            r.in_diagonal.at[held(c, own)] if i == 0 else r.in_sides.at[held(c, own, lead=(i - 1,))]
        )
        recv = r.diagonal_recv if i == 0 else r.sides_recv
        return grad_copy(c, slab_rows(sx, sy, z), into, recv.at[c], peer(t if i == 2 else 1 - t))

    def slabs_near(c):
        first_wait(c, 0)
        lanes = pl.ds(0, pieces[c][2])
        for i, (sx, sy) in enumerate(four):
            at = held(c, slab_rows(sx, sy, z))
            acc[at] = acc[at] + r.first_mate[back_slot(c), i, :, lanes].astype(F32)
        t = back_turn(c)
        for i, seg_at in enumerate(((1 - x, 1 - y), away(1 - t))):
            round_out(c, slab_rows(*seg_at, z))
            slab_copy(c, i).start()

    def slabs_side(c):
        slab_copy(c, 0).wait_recv()
        own = pl.ds(0, slab)
        round_out(c, slab_rows(*away(back_turn(c)), z), r.in_diagonal.at[held(c, own)])
        slab_copy(c, 2).start()

    def slabs_end(c):
        own = pl.ds(0, slab)
        both = r.in_sides.at[held(c, own, lead=(pl.ds(0, 2),))]
        bytes_of(both, r.grad_send, r.sides_recv.at[c]).wait_recv()
        value = acc[held(c, slab_rows(x, y, z))]
        return value + sum(r.in_sides[held(c, own, lead=(i,))].astype(F32) for i in range(2))

    def grad_product(c):
        if c in begun:
            acc[held(c)] = acc[held(c)] + product(c, theirs)
        else:
            acc[held(c)] = product(c, slice(None))
        if back_mode(c) == 3:
            first_start(c)
            return
        round_out(c, seg_rows(1 - x, 1 - y))
        copy_diagonal(c).start()
        round_out(c, seg_rows(*away(1 - back_turn(c))))
        copy_near(c).start()

    def line_start(c, far):
        @pl.when(jnp.logical_not(inner))
        def _():
            sx, sy = back_seg(c, far)
            round_out(c, pair_rows(sx, sy, 1 - pair_z))
            copy_pair_in(c, far).start()
            round_out(c, slab_rows(sx, sy, mate_z))
            copy_mate(c, far).start()

    def grad_side(c):
        if back_mode(c) == 3:
            first_across(c)
            return
        copy_diagonal(c).wait_recv()
        at = seg_rows(*away(back_turn(c)))
        if back_mode(c) == 1:
            acc[held(c, at)] = acc[held(c, at)] + r.in_diagonal[held(c)].astype(F32)
            line_start(c, 1)
        else:
            round_out(c, at, r.in_diagonal.at[held(c)])
            copy_side(c).start()

    def grad_line(c):
        if back_mode(c) == 3:
            first_out(c)
            return
        sides = 1 if back_mode(c) == 1 else 2
        both = r.in_sides.at[held(c, lead=(pl.ds(0, sides),))]
        bytes_of(both, r.grad_send, r.sides_recv.at[c]).wait_recv()
        more = sum(r.in_sides[held(c, lead=(i,))].astype(F32) for i in range(sides))
        at = seg_rows(x, y)
        acc[held(c, at)] = acc[held(c, at)] + more
        if back_mode(c) == 2:
            for d in range(1, n.zs):
                round_out(c, slab_rows(x, y, (z + d) % n.zs))
                copy_direct(c, d).start()
        else:
            line_start(c, 0)

    def fars(c):
        return range((1, 2, 0, 0)[back_mode(c)])

    def grad_across(c):
        if back_mode(c) == 3:
            slabs_near(c)
        for far in fars(c):

            @pl.when(inner)
            def _(far=far):
                copy_pair_in(c, far).wait_recv()
                at = pair_rows(*back_seg(c, far), 1 - pair_z)
                round_out(c, at, line_into(c, far, 1))
                copy_pair_across(c, far).start()

    def grad_out(c):
        if back_mode(c) == 3:
            slabs_side(c)
        for far in fars(c):

            @pl.when(inner)
            def _(far=far):
                copy_pair_across(c, far).wait_recv()
                sx, sy = back_seg(c, far)
                at = pair_rows(sx, sy, pair_z)
                acc[held(c, at)] = acc[held(c, at)] + line_into(c, far, 2)[...].astype(F32)
                round_out(c, slab_rows(sx, sy, mate_z))
                copy_mate(c, far).start()

    def grad_far(c):
        if back_mode(c) == 1:
            copy_mate(c, 1).wait_recv()
            round_out(c, slab_rows(*away(back_turn(c)), z), line_into(c, 1, 0))
            copy_far(c).start()

    grads_out = (r.g1, r.g2)
    r.squares[...] = jnp.zeros((8, 128), F32)

    def squares_of(v):
        v = v * v
        v = jnp.sum(v.reshape(v.shape[0] // 8, 8, v.shape[1]), axis=0)
        return sum(v[:, i : i + 128] for i in range(0, v.shape[1], 128))

    def copy_back(c):
        return remote(
            r.final.at[held(c, their_rows)],
            r.final_in.at[held(c)],
            r.back_send,
            r.back_recv,
            other_core,
            seq_at,
        )

    def grad_end(c):
        m, q, at = wide(c)
        if back_mode(c) == 3:
            value = slabs_end(c)
        else:
            value = acc[held(c, slab_rows(x, y, z))]
            ends = back_mode(c) + 1
            all_ends = r.in_end.at[held(c, lead=(pl.ds(0, ends),))]
            bytes_of(all_ends, r.grad_send, r.end_recv.at[c]).wait_recv()
            for i in range(ends):
                value = value + r.in_end[held(c, lead=(i,))].astype(F32)
        r.squares[...] += squares_of(value)
        r.final[held(c)] = value
        own_at = pl.ds(aligned(core, n.half) + q * n.cols + at.start, at.size)
        grads_out[m][:, own_at] = r.final[held(c, core_rows)]
        copy_back(c).start()

    back_parts = []

    def slope_back(q):
        r.lift[...] = dot(r.dz[...], full[1, q])
        r.bias_sum[q] = jnp.zeros((8, n.cols), F32)

        @pl.loop(0, 2 * tokens // step)
        def _(i):
            at = pl.ds(pl.multiple_of(i * step, step), step)
            low = (r.lift[at, :] * r.slope[q, at, :]).astype(BF16)
            r.dpre[q, at, :] = low
            r.bias_sum[q] += jnp.sum(low.astype(F32).reshape(step // 8, 8, n.cols), axis=0)

        back_parts.append(q)
        for half in (theirs, mine):
            part = dot(r.dpre[q, half, :], full[0, q], NT)
            part = r.total[half, :] + part if len(back_parts) > 1 else part
            if len(back_parts) == n.chunks and half is theirs:
                r.part_low2[...] = part.astype(BF16)
                swap_dh().start()
            else:
                r.total[half, :] = part

    def swap_dh():
        return swap(5, r.part_low2, r.part_in2)

    def first_norm_back(at):
        dh = r.total[at, :] + r.part_in2[at, :].astype(F32) + r.dr2[at, :]
        unit = r.unit1[at, :]
        r.x_place[at, :] = dh
        du = dh * r.vecs[0:1, :]
        dv = r.scale1[at, 0:1] * (du - mean(du) - unit * mean(du * unit))
        low = dv.astype(BF16)
        r.dm[at, :] = low
        r.rest[at, :] = (dv - low.astype(F32)).astype(BF16)

    def norm_back():
        swap_dh().wait_recv()
        row_loop(first_norm_back)
        loads.tt_b.wait()
        mix_start(1, r.dm[...], r.tt_v)
        mix_send(1)

    def thirds(v):
        high = v.astype(BF16)
        left = v - high.astype(F32)
        mid = left.astype(BF16)
        return high, mid, (left - mid.astype(F32)).astype(BF16)

    def small_gather(v, spread):
        return sum(dot(part, spread, NT) for part in thirds(v))

    def row_sums(k):
        return remote(
            r.small_out.at[across(k)],
            r.small_in.at[k - 1],
            r.row_send2,
            r.row_recv2,
            across(k),
            seq_at,
        )

    def tile_sums(k):
        return remote(
            r.small_mid.at[plane(k)],
            r.small_last.at[k - 1],
            r.small_send2,
            r.small_recv2,
            batch_at,
            plane(k),
        )

    row_sums_bytes = bytes_of(r.small_in, r.row_send2, r.row_recv2)
    tile_sums_bytes = bytes_of(r.small_last, r.small_send2, r.small_recv2)

    def fold(v):
        return jnp.sum(v.reshape(tall // 8, 8, width), axis=0)

    def vector_sums(at):
        dh, dy = r.x_place[at, :], r.dy_place[at, :]
        r.sums[0] += fold(dh * r.unit1[at, :])
        r.sums[1] += fold(dh)
        r.sums[2] += fold(r.dz[at, :].astype(F32))
        r.sums[3] += fold(dy * r.h[at, :])
        r.sums[4] += fold(dy)

    def small_grads():
        r.sums[...] = jnp.zeros(r.sums.shape, F32)
        row_loop(vector_sums)
        for i in range(5):
            line_sum = jnp.sum(r.sums[i], axis=0, keepdims=True)
            tiles = small_gather(line_sum * r.vec_mask_v[...], r.vec_spread_v[...])
            r.small_out[:, :, i, :] = tiles.reshape(n.batch, n.seq, 128)
        line_sum = jnp.concatenate(
            [jnp.sum(r.bias_sum[q], axis=0, keepdims=True) for q in range(n.chunks)], axis=1
        )
        tiles = small_gather(jnp.where(bias_mask, line_sum, 0.0), r.bias_spread_v[...])
        r.small_out[:, :, 5:8, :] = jnp.zeros((n.batch, n.seq, 3, 128), F32)
        r.small_out[pl.ds(core * (n.batch // 2), n.batch // 2), :, 5, :] = tiles.reshape(
            n.batch // 2, n.seq, 128
        )
        for k in range(1, n.batch):
            row_sums(k).start()

    def small_rows_back():
        value = r.small_out[batch_at]
        row_sums_bytes.wait_recv()
        for k in range(1, n.batch):
            value = value + r.small_in[k - 1]
        r.small_mid[...] = value
        for k in range(1, n.seq):
            tile_sums(k).start()

    def small_end():
        value = r.small_mid[seq_at]
        tile_sums_bytes.wait_recv()
        for k in range(1, n.seq):
            value = value + r.small_last[k - 1]
        r.g_small[...] = value

    def turn_back():
        mix_turn(1)

    def outputs():
        r.out[...] = dot(r.out_low[...], r.perm_v[...], NT).astype(BF16)
        r.dx[...] = dot(r.dm[...], r.perm_v[...], NT) + dot(r.rest[...], r.perm_v[...], NT)

    def mix_back():
        loads.un_b.wait()
        mix_finish(1, r.un_v)
        r.dx[...] = r.dx[...] + r.mixed[...]

    for task, *which in (
        (grad_product, 0), (grad_product, 1), (grad_product, 3), (grad_product, 2),
        (slope_back, 1), (grad_product, 4), (slope_back, 0), (slope_back, 2), (grad_side, 1),
        (grad_product, 10), (grad_side, 0), (grad_line, 0), (grad_side, 2), (norm_back,),
        (grad_side, 3), (grad_across, 0), (grad_side, 10), (grad_product, 8), (grad_side, 4),
        (grad_product, 9), (grad_product, 5), (grad_line, 3), (outputs,), (small_grads,),
        (grad_line, 1), (grad_line, 4), (grad_across, 3), (grad_product, 7), (grad_side, 9),
        (grad_across, 4), (grad_line, 2), (grad_line, 10), (turn_back,), (grad_across, 2),
        (grad_side, 8), (grad_out, 2), (grad_across, 10), (grad_product, 11), (grad_side, 7),
        (grad_out, 3), (grad_side, 5), (grad_far, 3), (grad_product, 6), (grad_far, 2),
        (grad_line, 8), (small_rows_back,), (grad_line, 9), (grad_across, 1), (grad_out, 4),
        (grad_side, 11), (grad_across, 8), (grad_out, 0), (grad_across, 9), (grad_line, 7),
        (grad_line, 5), (mix_back,), (grad_end, 3), (small_end,), (grad_out, 10),
        (grad_side, 6), (grad_far, 10), (grad_out, 1), (grad_across, 7), (grad_across, 5),
        (grad_end, 10), (grad_out, 8), (grad_out, 9), (grad_line, 11), (grad_far, 1),
        (grad_out, 5), (grad_across, 11), (grad_out, 11), (grad_far, 5), (grad_far, 9),
        (grad_far, 0), (grad_far, 8), (grad_line, 6), (grad_across, 6), (grad_end, 2),
        (grad_end, 8), (grad_far, 4), (grad_end, 5), (grad_out, 6), (grad_out, 7),
        (grad_far, 11), (grad_far, 7), (grad_far, 6), (grad_end, 0), (grad_end, 9),
        (grad_end, 11), (grad_end, 1), (grad_end, 7), (grad_end, 4), (grad_end, 6),
    ):
        task(*which)

    squares = r.squares[...] + r.g_small[...] * r.g_small[...]
    r.norm_own[...] = jnp.sum(squares, axis=0, keepdims=True)
    r.norm_all[batch_at * n.seq + seq_at] = r.norm_own[...]

    for device in reversed(everyone):
        remote(
            r.norm_own,
            r.norm_all.at[batch_at * n.seq + seq_at],
            r.norm_send,
            r.norm_recv,
            *device,
        ).start()
    back_bytes = bytes_of(r.final_in, r.back_send, r.back_recv)
    back_bytes.wait_recv()
    for c in range(len(pieces)):
        m, q, at = wide(c)
        their_at = pl.ds(aligned(1 - core, n.half) + q * n.cols + at.start, at.size)
        grads_out[m][:, their_at] = r.final_in[held(c)]
    norm_bytes = bytes_of(r.norm_all.at[pl.ds(0, n.devices - 1)], r.norm_send, r.norm_recv)
    norm_bytes.wait_recv()
    squares = jnp.sum(r.norm_all[...].reshape(n.devices, 128), axis=0, keepdims=True)
    whole = jnp.sum(squares, axis=1, keepdims=True)
    r.norm[...] = jnp.broadcast_to(jnp.sqrt(whole), (8, 128))

    bytes_of(r.act, r.core_send, r.core_recv.at[0]).wait_send()
    for copy in (tiles_bytes(), rows_bytes(), *(swapped(m) for m in range(2))):
        copy.wait_send()
    for i, into in enumerate((r.l_buf, r.r_buf)):
        both = into.at[:, pl.ds(0, n.seq - 1)]
        bytes_of(both, r.mix_send.at[i], r.mix_recv.at[i]).wait_send()
    for copy in (row_sums_bytes, tile_sums_bytes, back_bytes, norm_bytes):
        copy.wait_send()
    weight_chunks = range(2 * n.chunks)
    sent = [2 * n.zs + (3 if split(c) else n.zs + 1) for c in weight_chunks]
    all_slabs(sent, r.side_send).wait_send()

    @pl.when(inner)
    def _():
        all_slabs([8 if split(c) else 4 for c in weight_chunks], r.inner_send).wait_send()

    moved = 2 * n.zs + n.zs + 3
    bytes_of(out_low.at[:, pl.ds(0, moved * slab)], r.grad_send, r.sides_recv.at[0]).wait_send()


def grad_pieces(n):
    slots = 2 * n.chunks * n.parts
    halved = len(BACK_KINDS) - slots
    whole = [(slot, 0, n.thin) for slot in range(slots - halved)]
    thin = n.thin // 2
    return whole + [(slot, i * thin, thin) for slot in range(slots - halved, slots) for i in range(2)]


def run_layer(n, x, dy, w1, w2, bias, vec):
    tables = host_tables(n)
    tokens, width, cols, q = n.tokens, n.width, n.cols, n.chunks
    grads = 2 * q * n.parts
    far_chunks = sum(kind // 2 == 1 for kind in FORWARD_KINDS)
    splits = max(1, sum(kind // 2 == 1 for kind in BACK_KINDS))
    firsts = max(1, sum(kind // 2 == 3 for kind in BACK_KINDS))
    dma = pltpu.SemaphoreType.DMA
    vmem = pltpu.VMEM
    inputs = dict(bias=bias, vec=vec, x=x, dy=dy, w1=w1, w2=w2)
    inputs.update({name: getattr(tables, name) for name in LOADS if name not in inputs})
    outputs = dict(
        out=((tokens, width), BF16),
        dx=((tokens, width), F32),
        g1=((n.rows, n.hidden), F32),
        g2=((n.rows, n.hidden), F32),
        g_small=((8, 128), F32),
        norm=((8, 128), F32),
    )
    scratch = {held: vmem(inputs[name].shape, inputs[name].dtype) for name, held in LOADS.items()}
    scratch.update(
        load_sem=dma((len(set(LOADS.values())),)),
        stage=vmem((2, n.slab, n.half), F32),
        swap_send=dma((2,)),
        swap_recv=dma((2,)),
        tile=vmem((8, 128), F32),
        small=vmem((n.batch, n.seq, 8, 128), F32),
        small_send=dma,
        small_recv=dma,
        row_send=dma,
        row_recv=dma,
        y_buf=vmem((2, width, tokens), BF16),
        l_buf=vmem((2, n.seq, n.packed, tokens), BF16),
        left=vmem((n.seqs * n.packed, n.length), BF16),
        z_buf=vmem((2, n.seq, n.seqs * n.packed, n.block), BF16),
        r_buf=vmem((2, n.seq, n.seqs * n.packed, n.block), BF16),
        mix_send=dma((2,)),
        mix_recv=dma((4,)),
        mixed=vmem((tokens, width), F32),
        full=vmem((2, q, width, cols), BF16),
        side_send=dma,
        inner_send=dma,
        mate_recv=dma((2 * q + far_chunks,)),
        pair_recv=dma((2 * q + far_chunks,)),
        first_recv=dma((3, 2 * q)),
        second_recv=dma((2 * q,)),
        x_place=vmem((tokens, width), F32),
        dy_place=vmem((tokens, width), F32),
        vecs=vmem((8, width), F32),
        biases=vmem((q, 1, cols), F32),
        unit1=vmem((tokens, width), F32),
        scale1=vmem((tokens, 128), F32),
        h=vmem((tokens, width), F32),
        h_low=vmem((2 * tokens, width), BF16),
        core_send=dma,
        core_recv=dma((6,)),
        total=vmem((2 * tokens, width), F32),
        act=vmem((q, 2 * tokens, cols), BF16),
        lift=vmem((2 * tokens, cols), F32),
        slope=vmem((q, 2 * tokens, cols), F32),
        part_low=vmem((tokens, width), BF16),
        part_low2=vmem((tokens, width), BF16),
        part_in=vmem((tokens, width), BF16),
        part_in2=vmem((tokens, width), BF16),
        sums=vmem((5, 8, width), F32),
        out_low=vmem((tokens, width), BF16),
        dr2=vmem((tokens, width), F32),
        dz=vmem((2 * tokens, width), BF16),
        acc=vmem((grads, width, n.thin), F32),
        give=vmem((grads, width, n.thin), BF16),
        in_diagonal=vmem((grads, n.segment, n.thin), BF16),
        in_sides=vmem((grads, 2, n.segment, n.thin), BF16),
        in_end=vmem((grads, n.zs - 1, n.slab, n.thin), BF16),
        in_pair=vmem((grads, 2 * n.slab, n.thin), BF16),
        in_across=vmem((grads, 2 * n.slab, n.thin), BF16),
        far_mate=vmem((splits, n.slab, n.thin), BF16),
        far_pair=vmem((splits, 2 * n.slab, n.thin), BF16),
        far_across=vmem((splits, 2 * n.slab, n.thin), BF16),
        first_mate=vmem((firsts, 4, n.slab, n.thin), BF16),
        first_pair=vmem((firsts, 4, 2 * n.slab, n.thin), BF16),
        first_across=vmem((firsts, 4, 2 * n.slab, n.thin), BF16),
        line_recv=dma((3, firsts)),
        grad_send=dma,
        diagonal_recv=dma((len(BACK_KINDS),)),
        sides_recv=dma((len(BACK_KINDS),)),
        end_recv=dma((len(BACK_KINDS),)),
        tree_recv=dma((2, max(1, sum(kind // 2 < 2 for kind in BACK_KINDS)))),
        far_recv=dma((3, splits)),
        bias_sum=vmem((q, 8, cols), F32),
        dpre=vmem((q, 2 * tokens, cols), BF16),
        dm=vmem((tokens, width), BF16),
        rest=vmem((tokens, width), BF16),
        small_out=vmem((n.batch, n.seq, 8, 128), F32),
        small_in=vmem((n.batch - 1, n.seq, 8, 128), F32),
        row_send2=dma,
        row_recv2=dma,
        small_mid=vmem((n.seq, 8, 128), F32),
        small_last=vmem((n.seq - 1, 8, 128), F32),
        small_send2=dma,
        small_recv2=dma,
        final=vmem((grads, n.slab, n.thin), F32),
        final_in=vmem((grads, n.rows, n.thin), F32),
        back_send=dma,
        back_recv=dma,
        squares=vmem((8, 128), F32),
        norm_own=vmem((1, 128), F32),
        norm_all=vmem((n.devices, 1, 128), F32),
        norm_send=dma,
        norm_recv=dma,
    )
    names = tuple(inputs) + tuple(outputs) + tuple(scratch)
    in_vmem = pl.BlockSpec(memory_space=pltpu.VMEM)
    anywhere = pl.BlockSpec(memory_space=pl.ANY)
    values = pl.pallas_call(
        functools.partial(layer_kernel, n, names),
        out_shape=[vmem(*shape) for shape in outputs.values()],
        in_specs=[anywhere if name in LOADS else in_vmem for name in inputs],
        out_specs=[in_vmem] * len(outputs),
        scratch_shapes=list(scratch.values()),
        compiler_params=pltpu.CompilerParams(
            collective_id=0, has_side_effects=True, vmem_limit_bytes=58 * 2**20
        ),
        name="fused_layer",
    )(*inputs.values())
    return types.SimpleNamespace(**dict(zip(outputs, values)))


def adam_kernel(n, names, *refs):
    r = types.SimpleNamespace(**dict(zip(names, refs)))
    passed = [
        pltpu.make_async_copy(r.out, r.out_there, r.sem.at[0]),
        pltpu.make_async_copy(r.dx, r.dx_there, r.sem.at[1]),
    ]
    for copy in passed:
        copy.start()
    norm_value = r.norm[0:1, 0:1]
    r.norm_out[...] = norm_value
    factor = clip_limit / jnp.maximum(norm_value, clip_limit)
    lanes = n.cols

    def update(gradient, given, made, at, rate):
        weight, first, second = (ref[at] for ref in given)
        new = adam_update(weight, factor * gradient, first, second, rate, STEP_COUNT)
        for ref, value in zip(made, new):
            ref[at] = value

    weight_in, weight_out = refs[4:7], refs[7:10]
    made_in, made_out = refs[19:22], refs[22:25]

    @pl.loop(0, n.hidden // lanes)
    def _(i):
        at = (slice(None), pl.ds(pl.multiple_of(i * lanes, lanes), lanes))
        update(r.g1[at], weight_in, made_in, at, rate_matrix)
        update(r.g2[at], weight_out, made_out, at, rate_matrix)

    update(r.g_small[5:6, 0 : n.bias], refs[10:13], refs[25:28], ..., rate_vector)
    for i in range(5):
        update(r.g_small[i : i + 1, 0 : n.rows], refs[13:16], refs[28:31], i, rate_vector)
    for copy in passed:
        copy.wait()


def run_adam(n, got, given):
    f32 = functools.partial(jax.ShapeDtypeStruct, dtype=F32)
    matrix, bias, vec = f32((n.rows, n.hidden)), f32((1, n.bias)), f32((5, 1, n.rows))
    inputs = dict(g1=got.g1, g2=got.g2, g_small=got.g_small, norm=got.norm)
    inputs.update({chr(97 + i): array for i, array in enumerate(given)})
    inputs.update(out=got.out, dx=got.dx)
    outputs = dict(norm_out=f32((1, 1)))
    outputs.update({chr(110 + i): matrix for i in range(6)})
    outputs.update({chr(65 + i): bias for i in range(3)})
    outputs.update({chr(70 + i): vec for i in range(3)})
    outputs.update(
        out_there=jax.ShapeDtypeStruct(got.out.shape, BF16),
        dx_there=jax.ShapeDtypeStruct(got.dx.shape, F32),
    )
    names = tuple(inputs) + tuple(outputs) + ("sem",)
    in_vmem = pl.BlockSpec(memory_space=pltpu.VMEM)
    anywhere = pl.BlockSpec(memory_space=pl.ANY)
    return pl.pallas_call(
        functools.partial(adam_kernel, n, names),
        out_shape=list(outputs.values()),
        in_specs=[in_vmem] * (len(inputs) - 2) + [anywhere] * 2,
        out_specs=[in_vmem] * (len(outputs) - 2) + [anywhere] * 2,
        scratch_shapes=[pltpu.SemaphoreType.DMA((2,))],
        compiler_params=pltpu.CompilerParams(vmem_limit_bytes=32 * 2**20),
        name="adam",
    )(*inputs.values())


def turned(a):
    return jnp.swapaxes(a[0], 0, 1)


def lined(a):
    return jnp.transpose(a, (1, 0, 2))


def fused_layer(
    n,
    activations,
    cotangent,
    w_in,
    w_out,
    b_in,
    vec_params,
    first_w_in,
    second_w_in,
    first_w_out,
    second_w_out,
    first_b_in,
    second_b_in,
    first_vec,
    second_vec,
):
    got = run_layer(
        n,
        activations.reshape(n.tokens, n.width),
        cotangent.reshape(n.tokens, n.width),
        w_in[0],
        turned(w_out),
        b_in,
        lined(vec_params),
    )
    given = (
        *(a[0] for a in (w_in, first_w_in, second_w_in)),
        *(turned(a) for a in (w_out, first_w_out, second_w_out)),
        *(b_in, first_b_in, second_b_in),
        *(lined(a) for a in (vec_params, first_vec, second_vec)),
    )
    norm_value, *made, out, dx = run_adam(n, got, given)
    return (
        out.reshape(activations.shape),
        dx.reshape(activations.shape),
        norm_value.reshape(()),
        *(a[None] for a in made[:3]),
        *(jnp.swapaxes(a, 0, 1)[None] for a in made[3:6]),
        *made[6:9],
        *(lined(a) for a in made[9:]),
    )


def local_layer(mesh, activations, cotangent, w_in, *rest):
    seqs, block, width = activations.shape
    n = Sizes(mesh, seqs, block, width, w_in.shape[2])
    if w_in.shape[0] == 1 and n.fits():
        return fused_layer(n, activations, cotangent, w_in, *rest)
    return general_layer(activations, cotangent, w_in, *rest)


BOTH = ("batch", "seq")


def solution(mesh):
    in_specs = (
        P(*BOTH, None),
        P(*BOTH, None),
        P(None, BOTH, None),
        P(None, None, BOTH),
        P(None, BOTH),
        P(None, None, BOTH),
        P(None, BOTH, None),
        P(None, BOTH, None),
        P(None, None, BOTH),
        P(None, None, BOTH),
        P(None, BOTH),
        P(None, BOTH),
        P(None, None, BOTH),
        P(None, None, BOTH),
    )
    out_specs = (
        P(*BOTH, None),
        P(*BOTH, None),
        P(),
        P(None, BOTH, None),
        P(None, BOTH, None),
        P(None, BOTH, None),
        P(None, None, BOTH),
        P(None, None, BOTH),
        P(None, None, BOTH),
        P(None, BOTH),
        P(None, BOTH),
        P(None, BOTH),
        P(None, None, BOTH),
        P(None, None, BOTH),
        P(None, None, BOTH),
    )
    return jax.shard_map(
        functools.partial(local_layer, mesh), mesh=mesh, in_specs=in_specs, out_specs=out_specs, check_vma=False)
```
